32 devices in a mesh: dp: 8 (over y, x, core), tensor: 4 (over z).
Axes of the slice: x: 2, y: 2, z: 4, core: 2. Of those that a mesh axis runs over, the one named last changes fastest.
Arguments:
- layer_input: bfloat16 [32768, 1024], P(('dp', 'tensor')), may hold values from -15 to 15
- grad_output: bfloat16 [32768, 1024], P(('dp', 'tensor')), may hold values from -6 to 6
- doc_lengths: int32 [64, 4], P('dp'), may hold values from 1 to 256, 512 in all within a row
- ranges: float32 [4], replicated, may hold values from 0.5 to 6
- w_qkv: bfloat16 [3, 1024, 1024], P(None, None, 'tensor'), may hold values from -0.1875 to 0.1875
- bias_qv: bfloat16 [2, 1024], P(None, 'tensor'), may hold values from -3 to 3
- w_out: bfloat16 [1024, 1024], P('tensor'), may hold values from -0.75 to 0.75
- b_out: bfloat16 [1024], replicated, may hold values from -3 to 3
- gain_one: bfloat16 [1024], replicated, may hold values from 0.5 to 1.5
- shift_one: bfloat16 [1024], replicated, may hold values from -3 to 3
- w_in: bfloat16 [1024, 4096], P(None, 'tensor'), may hold values from -0.1875 to 0.1875
- b_in: bfloat16 [4096], P('tensor'), may hold values from -3 to 3
- w_down: bfloat16 [4096, 1024], P('tensor'), may hold values from -0.1875 to 0.1875
- b_down: bfloat16 [1024], replicated, may hold values from -3 to 3
- gain_two: bfloat16 [1024], replicated, may hold values from 0.5 to 1.5
- shift_two: bfloat16 [1024], replicated, may hold values from -3 to 3
Outputs:
- output: bfloat16 [32768, 1024], P(('dp', 'tensor'))
- grad_x: bfloat16 [32768, 1024], P(('dp', 'tensor'))
- grad_w_qkv: float32 [3, 1024, 1024], P(None, None, 'tensor')
- grad_bias_qv: float32 [2, 1024], P(None, 'tensor')
- grad_w_out: float32 [1024, 1024], P('tensor')
- grad_b_out: float32 [1024], replicated
- grad_gain_one: float32 [1024], replicated
- grad_shift_one: float32 [1024], replicated
- grad_w_in: float32 [1024, 4096], P(None, 'tensor')
- grad_b_in: float32 [4096], P('tensor')
- grad_w_down: float32 [4096, 1024], P('tensor')
- grad_b_down: float32 [1024], replicated
- grad_gain_two: float32 [1024], replicated
- grad_shift_two: float32 [1024], replicated
- new_ranges: float32 [4], replicated
The draws below stay inside these ranges and needn't reach their ends.
Inputs may be any that keep to these rules, and one draw needn't show every extreme that they name: `doc_lengths`: each packed row holds 4 documents whose lengths sum to 512.
All inputs are finite; a program needn't handle non-finite values. Where the reference program divides by a largest or mean magnitude, that divisor is 1e-20 or more.
Results may differ from the reference program's by a relative error of at most 0.013.
The reference program's roundings to bfloat16 on the way count: a program that leaves them out, or rounds other values in their place, can miss the bound.
Values may be sent and summed in bfloat16 or wider, within the bound.
A program may use at most 320 MiB of HBM per device.

```python
import math
import jax
import jax.numpy as jnp
import numpy as np
from jax import lax

D = 1024
HEADS = 16
HD = 64
FF = 4096
SEQ = 512
DOCS = 4
GROUP_SEQS = 8
SEQUENCES = 64
TOKENS = 32768


def draw_layer_input(key, part):
    key = jax.random.fold_in(key, 11)
    base_key = jax.random.fold_in(key, 1)
    column_key = jax.random.fold_in(key, 2)
    sign_key = jax.random.fold_in(key, 3)
    rows = jnp.arange(TOKENS, dtype=jnp.float32)[:, None]
    place = rows / max(TOKENS - 1, 1)
    rising = 1.0 + 2.0 * place
    base = jnp.clip(jax.random.normal(base_key, (TOKENS, D), jnp.float32), -5.0, 5.0)
    spike_column = jax.random.randint(column_key, (TOKENS, 1), 0, D)
    spike_sign = 2.0 * jax.random.randint(sign_key, (TOKENS, 1), 0, 2).astype(jnp.float32) - 1.0
    columns = jnp.arange(D, dtype=jnp.int32)[None, :]
    spike = jnp.where(columns == spike_column, 14.0 * place * spike_sign, 0.0)
    return jnp.clip(base * rising + spike, -15.0, 15.0).astype(jnp.bfloat16)


def shard_levels(own_key, dims, cuts, low, largest):
    loudness, own = 1.0, jax.random.fold_in(own_key, 6)
    for dim, parts in cuts:
        steps = jnp.exp(jax.random.uniform(jax.random.fold_in(own, dim), (parts,), jnp.float32, low / len(cuts), largest / len(cuts)))
        loudness = loudness * jnp.repeat(steps, dims[dim] // parts).reshape([-1 if axis == dim else 1 for axis in range(len(dims))])
    return loudness


def split_up(amount, total, reach, skew):
    portions = [(1 << 20) // math.isqrt(grade ** skew) + 1 for grade in range(2, amount + 1)]
    surplus, given = total - reach - (amount - 1), [1] * (amount - 1)
    while surplus > 0:
        movable = [i for i in range(amount - 1) if given[i] < reach]
        whole, remaining = sum([portions[i] for i in movable]), surplus
        for i in movable:
            more = min(reach - given[i], max(1, remaining * portions[i] // whole), surplus)
            given[i] = given[i] + more
            surplus = surplus - more
    return np.array([reach] + given)


def uneven(own_key, count, total, bound, lean):
    if count == 2:
        one = jax.random.randint(own_key, (), max(1, total - bound), min(bound, total - 1) + 1)
        return jnp.stack([one, total - one])
    tallies = jnp.asarray(split_up(count, total, bound, lean), jnp.int32)
    twos = (count - 1) // 2
    donor, taker = tallies[1:1 + 2 * twos:2], tallies[2:2 + 2 * twos:2]
    room = jnp.minimum(donor - 1, bound - taker)
    shifted = jax.random.randint(jax.random.fold_in(own_key, 1), (twos,), 0, 1 << 20) % (room + 1)
    tallies = tallies.at[1:1 + 2 * twos:2].set(donor - shifted).at[2:2 + 2 * twos:2].set(taker + shifted)
    return tallies[jax.random.permutation(jax.random.fold_in(own_key, 2), count)]


def noise(rng, dims, deviation, reach, pieces=(), kind=jnp.bfloat16):
    gain = shard_levels(rng, dims, pieces, -0.22, 0.18) if pieces else 1.0
    values = jax.random.normal(rng, dims, jnp.float32) * deviation * gain
    return jnp.minimum(jnp.maximum(values, -reach), reach).astype(kind)


def setup_inputs(seed: int = 0) -> dict:
    keys = jax.random.split(jax.random.key(seed), 17)
    return {
        "layer_input": draw_layer_input(jax.random.fold_in(keys[16], 71), 0),
        "grad_output": noise(keys[1], (TOKENS, D), 1.0, 6.0, ((0, 32),)),
        "doc_lengths": jax.vmap(lambda own: uneven(own, DOCS, SEQ, SEQ // 2, 2))(jax.random.split(keys[2], SEQUENCES)).reshape((SEQUENCES, DOCS)).astype(jnp.int32),
        "ranges": jnp.clip(jnp.exp(jax.random.uniform(keys[3], (4,), jnp.float32, math.log(0.5), math.log(6.0))), 0.5, 6.0),
        "w_qkv": noise(keys[4], (3, D, D), D ** -0.5, 0.1875, ((2, 4),)),
        "bias_qv": noise(keys[5], (2, D), 0.5, 3.0, ((1, 4),)),
        "w_out": noise(keys[6], (D, D), (D // 16) ** -0.5, 0.75, ((0, 4),)),
        "b_out": noise(keys[7], (D,), 0.5, 3.0),
        "gain_one": jnp.clip(1.0 + 0.1 * jax.random.normal(keys[8], (D,), jnp.float32), 0.5, 1.5).astype(jnp.bfloat16),
        "shift_one": noise(keys[9], (D,), 0.5, 3.0),
        "w_in": noise(keys[10], (D, FF), D ** -0.5, 0.1875, ((1, 4),)),
        "b_in": noise(keys[11], (FF,), 0.5, 3.0, ((0, 4),)),
        "w_down": noise(keys[12], (FF, D), (FF // 4) ** -0.5, 0.1875, ((0, 4),)),
        "b_down": noise(keys[13], (D,), 0.5, 3.0),
        "gain_two": jnp.clip(1.0 + 0.1 * jax.random.normal(keys[14], (D,), jnp.float32), 0.5, 1.5).astype(jnp.bfloat16),
        "shift_two": noise(keys[15], (D,), 0.5, 3.0),
    }


EPS = 1e-06
DECAY = 0.9
HIGH = lax.Precision.HIGHEST

@jax.custom_vjp
def low(v):
    return lax.optimization_barrier(v.astype(jnp.bfloat16)).astype(jnp.float32)

@jax.custom_vjp
def low_back(v):
    return v

def low_keep(v):
    return (low(v), None)

def low_pass(kept, grad):
    return (grad,)

def back_keep(v):
    return (v, None)

def back_low(kept, grad):
    return (low(grad),)
low.defvjp(low_keep, low_pass)
low_back.defvjp(back_keep, back_low)

def soft_clip(values, clip_level):
    return clip_level * jnp.tanh(values / clip_level)

def matmul(first_operand, second_operand):
    return jnp.dot(first_operand, second_operand, precision=HIGH)

def layer_norm(summed, norm_gain, norm_shift):
    center = summed - lax.optimization_barrier(jnp.mean(summed, axis=-1, keepdims=True))
    spread = lax.optimization_barrier(jnp.mean(center * center, axis=-1, keepdims=True))
    return center * lax.rsqrt(spread + EPS) * norm_gain + norm_shift

def segment_ids(doc_lengths):
    doc_ends = jnp.cumsum(doc_lengths, axis=1, dtype=jnp.int32)
    places = jnp.arange(SEQ, dtype=jnp.int32)
    return lax.optimization_barrier(jnp.sum((places[None, :, None] >= doc_ends[:, None, :]).astype(jnp.int32), axis=2, dtype=jnp.int32))

def attend(queries, key_rows, value_rows, segments):
    raw_scores = low_back(jnp.einsum('bqhd,bkhd->bhqk', queries, key_rows, precision=HIGH))
    scores = raw_scores * HD ** (-0.5)
    same_doc = segments[:, None, :, None] == segments[:, None, None, :]
    scores = jnp.where(same_doc, scores, -1e+30)
    row_max = lax.optimization_barrier(jnp.max(scores, axis=-1, keepdims=True))
    exponent = jnp.exp(scores - row_max)
    attn_probs = low(exponent / lax.optimization_barrier(jnp.sum(exponent, axis=-1, keepdims=True)))
    return jnp.einsum('bhqk,bkhd->bqhd', attn_probs, value_rows, precision=HIGH)

def quantize(values, previous, fixed_levels, position):
    if fixed_levels is None:
        clip_level = DECAY * previous + (1.0 - DECAY) * jnp.max(jnp.abs(values))
    else:
        clip_level = fixed_levels[position]
    return (low(soft_clip(values, clip_level)), clip_level)

def forward(inputs, doc_lengths, ranges, weight_levels, params, fixed_levels):
    w_qkv, bias_qv, w_out, b_out, gain_one, shift_one, w_in, b_in, w_down, b_down, gain_two, shift_two = params
    quant_input, level_input = quantize(inputs, ranges[0], fixed_levels, 0)
    quant_qkv = low(soft_clip(w_qkv, weight_levels[:3][:, None, None]))
    queries = low_back(low(matmul(quant_input, quant_qkv[0]) + bias_qv[0]))
    key_rows = low_back(low(matmul(quant_input, quant_qkv[1])))
    value_rows = low_back(low(matmul(quant_input, quant_qkv[2]) + bias_qv[1]))
    blocked = (-1, GROUP_SEQS, SEQ, HEADS, HD)
    segments = segment_ids(doc_lengths).reshape(-1, GROUP_SEQS, SEQ)

    def one_group(carried, group_items):
        return (carried, jax.checkpoint(attend)(*group_items))
    _, context = lax.scan(one_group, jnp.zeros((), jnp.float32), (queries.reshape(blocked), key_rows.reshape(blocked), value_rows.reshape(blocked), segments))
    context = low_back(context.reshape(inputs.shape))
    quant_context, level_context = quantize(context, ranges[1], fixed_levels, 1)
    attention_out = low_back(matmul(quant_context, low(soft_clip(w_out, weight_levels[3])))) + b_out
    normed = layer_norm(inputs + attention_out, gain_one, shift_one)
    quant_normed, level_normed = quantize(normed, ranges[2], fixed_levels, 2)
    hidden = low_back(matmul(quant_normed, low(soft_clip(w_in, weight_levels[4]))) + b_in)
    active = jax.nn.gelu(hidden, approximate=False)
    quant_active, level_active = quantize(active, ranges[3], fixed_levels, 3)
    branch = low_back(matmul(quant_active, low(soft_clip(w_down, weight_levels[5])))) + b_down
    result = layer_norm(normed + branch, gain_two, shift_two)
    return (result, jnp.stack([level_input, level_context, level_normed, level_active]))

def reference(layer_input, grad_output, doc_lengths, ranges, w_qkv, bias_qv, w_out, b_out, gain_one, shift_one, w_in, b_in, w_down, b_down, gain_two, shift_two):
    params = tuple((entry.astype(jnp.float32) for entry in (w_qkv, bias_qv, w_out, b_out, gain_one, shift_one, w_in, b_in, w_down, b_down, gain_two, shift_two)))
    weight_levels = 0.5 * jnp.stack([jnp.max(jnp.abs(params[0][0])), jnp.max(jnp.abs(params[0][1])), jnp.max(jnp.abs(params[0][2])), jnp.max(jnp.abs(params[2])), jnp.max(jnp.abs(params[6])), jnp.max(jnp.abs(params[8]))])
    inputs = layer_input.astype(jnp.float32)
    _, new_ranges = forward(inputs, doc_lengths, ranges, weight_levels, params, None)

    def run_layer(inputs, params):
        return forward(inputs, doc_lengths, ranges, weight_levels, params, new_ranges)[0]
    result, pullback = jax.vjp(run_layer, inputs, params)
    grad_x, gradients = pullback(grad_output.astype(jnp.float32))
    return (result.astype(jnp.bfloat16), grad_x.astype(jnp.bfloat16), gradients[0], gradients[1], gradients[2], gradients[3], gradients[4], gradients[5], gradients[6], gradients[7], gradients[8], gradients[9], gradients[10], gradients[11], new_ranges)
```

```python
from functools import partial

import jax
import jax.numpy as jnp
from jax import lax
from jax.experimental import pallas as pl
from jax.experimental.pallas import tpu as pltpu
from jax.sharding import PartitionSpec as P

HD = 64
SEQ = 512
LANES = 128

EPS = 1e-06
DECAY = 0.9
MASKED = -1e30
MESH = pl.DeviceIdType.MESH
F32 = jnp.float32
BF16 = jnp.bfloat16
MIB = 1024 * 1024


def shape_of(dims, kind):
    return jax.ShapeDtypeStruct(dims, kind)


def params(mib=48, **rest):
    return pltpu.CompilerParams(vmem_limit_bytes=mib * MIB, **rest)


def in_smem():
    return pl.BlockSpec(memory_space=pltpu.SMEM)


def cost(flops, moved):
    return pl.CostEstimate(flops=int(flops), bytes_accessed=int(moved), transcendentals=0)


def dot(first, second):
    return jnp.dot(first, second, preferred_element_type=F32)


def dot_cols(first, second):
    return lax.dot_general(first, second, (((1,), (1,)), ((), ())), preferred_element_type=F32)


def dot_rows(first, second):
    return lax.dot_general(first, second, (((0,), (0,)), ((), ())), preferred_element_type=F32)


def flat(block):
    return block.reshape(block.shape[0] * block.shape[1], block.shape[2])


def exchange_kernel(kind, x_ref, range_ref, o_ref, near, far, mid, near_send, near_recv, far_send, far_recv):
    data, part = lax.axis_index("dp"), lax.axis_index("tensor")
    datas, parts = lax.axis_size("dp"), lax.axis_size("tensor")
    barrier = pltpu.get_barrier_semaphore()

    def to_data(step):
        return (lax.rem(data + step, datas), part)

    def to_part(step):
        return (data, lax.rem(part + step, parts))

    def greet(target):
        def run(step, carry):
            pl.semaphore_signal(barrier, inc=1, device_id=target(step), device_id_type=MESH)
            return carry

        return run

    lax.fori_loop(1, datas, greet(to_data), 0)
    lax.fori_loop(1, parts, greet(to_part), 0)
    pl.semaphore_wait(barrier, datas + parts - 2)

    def exchange(source, slots, send, recv, target, count):
        def copy(step):
            return pltpu.make_async_remote_copy(
                src_ref=source,
                dst_ref=slots.at[step],
                send_sem=send.at[step],
                recv_sem=recv.at[step],
                device_id=target(step),
                device_id_type=MESH,
            )

        def start(step, carry):
            copy(step).start()
            return carry

        def finish(step, carry):
            copy(step).wait()
            return carry

        lax.fori_loop(1, count, start, 0)
        slots[0] = source[...]
        lax.fori_loop(1, count, finish, 0)
        if kind == "sum":
            return jnp.sum(slots[...], axis=0)
        return jnp.max(slots[...], axis=0)

    mid[...] = exchange(x_ref, near, near_send, near_recv, to_data, datas)
    total = exchange(mid, far, far_send, far_recv, to_part, parts)
    if kind == "rows":
        total = jnp.broadcast_to(jnp.max(total, axis=1, keepdims=True), total.shape)
    if kind == "level":
        peak = jnp.max(total, keepdims=True)
        total = jnp.broadcast_to(DECAY * range_ref[0] + (1.0 - DECAY) * peak, total.shape)
    o_ref[...] = total


def exchange_all(values, mesh, kind, previous):
    datas, parts = mesh.shape["dp"], mesh.shape["tensor"]
    dims = values.shape
    copies = pltpu.SemaphoreType.DMA
    return pl.pallas_call(
        partial(exchange_kernel, kind),
        out_shape=shape_of(dims, F32),
        in_specs=[pl.BlockSpec(memory_space=pltpu.VMEM), in_smem()],
        out_specs=pl.BlockSpec(memory_space=pltpu.VMEM),
        scratch_shapes=[
            pltpu.VMEM((datas,) + dims, F32),
            pltpu.VMEM((parts,) + dims, F32),
            pltpu.VMEM(dims, F32),
            copies((datas,)),
            copies((datas,)),
            copies((parts,)),
            copies((parts,)),
        ],
        compiler_params=pltpu.CompilerParams(
            collective_id={"rows": 0, "level": 1, "sum": 2}[kind], has_side_effects=True
        ),
        name="exchange_" + kind,
    )(values, previous)


def swap(values, axis, bit):
    count = lax.axis_size(axis)
    return lax.ppermute(values, axis, [(i, i ^ (1 << bit)) for i in range(count)])


def bits_of(axis):
    return lax.axis_size(axis).bit_length() - 1


def plane_orders():
    plane = list(range(1, bits_of("dp")))
    return plane, (plane[::-1], plane)


def spread_plane(values, order):
    held = []
    for bit in order:
        other = swap(values, "dp", bit)
        place = sum(1 for seen in held if seen > bit)
        values = jnp.stack([values, other], axis=place)
        held.append(bit)
    return values.reshape((-1,) + values.shape[len(held) :])


def gather(piece):
    held = piece[None]
    for bit in reversed(range(bits_of("tensor"))):
        other = swap(held, "tensor", bit)
        held = jnp.stack([held, other], axis=1).reshape((-1,) + piece.shape)
    half = held.shape[0] // 2
    _, orders = plane_orders()
    sides = [spread_plane(held[:half], orders[0]), spread_plane(held[half:], orders[1])]
    near = jnp.concatenate(sides, axis=1)
    return near, swap(near, "dp", 0)


def low(values):
    return values.astype(BF16)


def scatter_side(values, order):
    plane, _ = plane_orders()
    values = values.reshape((2,) * len(plane) + values.shape[1:])
    left = plane[::-1]
    for bit in order:
        place = left.index(bit)
        keep = lax.index_in_dim(values, 0, place, keepdims=False)
        send = lax.index_in_dim(values, 1, place, keepdims=False)
        values = keep + swap(low(send), "dp", bit).astype(F32)
        left.remove(bit)
    for bit in range(bits_of("tensor") - 1):
        pairs = values.reshape((-1, 2) + values.shape[1:])
        values = pairs[:, 0] + swap(low(pairs[:, 1]), "tensor", bit).astype(F32)
    return values[0]


def scatter(keep, send):
    summed = keep + swap(send, "dp", 0).astype(F32)
    half = summed.shape[1] // 2
    _, orders = plane_orders()
    near = scatter_side(summed[:, :half], orders[0])
    far = scatter_side(summed[:, half:], orders[1])
    return near + swap(low(far), "tensor", bits_of("tensor") - 1).astype(F32)


def spread(piece):
    half = piece.shape[1] // 2
    _, orders = plane_orders()
    sides = [spread_plane(piece[:, :half], orders[0]), spread_plane(piece[:, half:], orders[1])]
    near = jnp.concatenate(sides, axis=2)
    return jnp.concatenate([near, swap(near, "dp", 0)], axis=0)


def take_blocks(ref, order_ref):
    return jnp.concatenate(
        [
            ref[:, pl.ds(pl.multiple_of(order_ref[j] * LANES, LANES), LANES)]
            for j in range(ref.shape[1] // LANES)
        ],
        axis=1,
    )


def put_blocks(ref, order_ref, values):
    for j in range(ref.shape[1] // LANES):
        ref[:, pl.ds(pl.multiple_of(order_ref[j] * LANES, LANES), LANES)] = values[
            :, j * LANES : (j + 1) * LANES
        ]


def fold_peak(values):
    return jnp.max(jnp.abs(values).reshape(-1, 8, LANES), axis=0)


def column_peak(values):
    peak = fold_peak(values[:, :LANES])
    for j in range(1, values.shape[1] // LANES):
        peak = jnp.maximum(peak, fold_peak(values[:, j * LANES : (j + 1) * LANES]))
    return peak


def quant_kernel(order_ref, x_ref, level_ref, o_ref):
    level = level_ref[0:1, 0:1]
    x = take_blocks(x_ref, order_ref).astype(F32)
    o_ref[...] = low(level * jnp.tanh(x / level))


def quant_rows(x, level, order):
    tokens, width = x.shape
    rows = 256
    return pl.pallas_call(
        quant_kernel,
        grid=(tokens // rows,),
        in_specs=[
            in_smem(),
            pl.BlockSpec((rows, width), lambda t: (t, 0)),
            pl.BlockSpec((8, LANES), lambda t: (0, 0)),
        ],
        out_specs=pl.BlockSpec((rows, width), lambda t: (t, 0)),
        out_shape=shape_of((tokens, width), BF16),
        compiler_params=params(32),
        name="quant_input",
    )(order, x, level)


def qkv_kernel(x_ref, near_ref, far_ref, b_ref, o_ref):
    half = x_ref.shape[1] // 2
    total = dot(x_ref[:, :half], flat(near_ref[...])) + dot(x_ref[:, half:], flat(far_ref[...]))
    o_ref[...] = low(total + b_ref[...])


def qkv_rows(x, weights, bias):
    near, far = weights
    plane, parts, kinds, rows, c = near.shape
    tokens, width = x.shape
    weight_spec = pl.BlockSpec((plane, None, None, rows, c), lambda r, i: (0, r, i, 0, 0))
    return pl.pallas_call(
        qkv_kernel,
        grid=(parts, kinds),
        in_specs=[
            pl.BlockSpec((tokens, width), lambda r, i: (0, 0)),
            weight_spec,
            weight_spec,
            pl.BlockSpec((None, 1, c), lambda r, i: (i, 0, r)),
        ],
        out_specs=pl.BlockSpec((None, tokens, c), lambda r, i: (i, 0, r)),
        out_shape=shape_of((kinds, tokens, parts * c), BF16),
        compiler_params=params(32),
        cost_estimate=cost(2 * tokens * width * kinds * parts * c, 14 * MIB),
        name="qkv",
    )(x, near, far, bias)


def fill_mask(mask_ref, col_ref, row_ref):
    mask_ref[...] = jnp.where(col_ref[...] == row_ref[...], 0.0, MASKED).astype(F32)


def attend_kernel(q_ref, k_ref, v_ref, col_ref, row_ref, o_ref, lse_ref, peak_ref, mask_ref, sums_ref):
    row, pair = pl.program_id(0), pl.program_id(1)
    factor = HD ** (-0.5)

    @pl.when(pair == 0)
    def _():
        fill_mask(mask_ref, col_ref, row_ref)
        sums_ref[...] = jnp.zeros_like(sums_ref)

    @pl.when((pair == 0) & (row == 0))
    def _():
        peak_ref[...] = jnp.zeros_like(peak_ref)

    rows = 256
    lanes = lax.broadcasted_iota(jnp.int32, (rows, LANES), 1)
    for start in range(0, SEQ, rows):
        here = pl.ds(start, rows)
        q = q_ref[here, :] * jnp.asarray(factor, BF16)
        parts = []
        sums = sums_ref[here, :]
        for head in range(LANES // HD):
            own = lanes // HD == head
            scores = dot_cols(jnp.where(own, q, jnp.zeros_like(q)), k_ref[...]) + mask_ref[here, :]
            row_max = jnp.max(scores, axis=-1, keepdims=True)
            exponent = jnp.exp(scores - row_max)
            totals = jnp.sum(exponent, axis=-1, keepdims=True)
            probs = low(exponent * (1.0 / totals))
            parts.append(dot(probs, v_ref[...]))
            sums = jnp.where(lanes == pair * (LANES // HD) + head, row_max + jnp.log(totals), sums)
        context = parts[0]
        for head in range(1, LANES // HD):
            context = jnp.where(lanes // HD == head, parts[head], context)
        o_ref[here, :] = context
        sums_ref[here, :] = sums
        peak_ref[...] = jnp.maximum(peak_ref[...], fold_peak(context))

    @pl.when(pair == pl.num_programs(1) - 1)
    def _():
        lse_ref[...] = sums_ref[...].T


def attend(qkv, cols, rows):
    _, tokens, width = qkv.shape
    held = tokens // SEQ

    def side(i):
        return pl.BlockSpec((None, SEQ, LANES), lambda r, j: (i, r, j))

    return pl.pallas_call(
        attend_kernel,
        grid=(held, width // LANES),
        in_specs=[
            side(0),
            side(1),
            side(2),
            pl.BlockSpec((None, SEQ, 1), lambda r, j: (r, 0, 0)),
            pl.BlockSpec((None, 1, SEQ), lambda r, j: (r, 0, 0)),
        ],
        out_specs=[
            pl.BlockSpec((SEQ, LANES), lambda r, j: (r, j)),
            pl.BlockSpec((None, LANES, SEQ), lambda r, j: (r, 0, 0)),
            pl.BlockSpec((8, LANES), lambda r, j: (0, 0)),
        ],
        out_shape=[
            shape_of((tokens, width), F32),
            shape_of((held, LANES, SEQ), F32),
            shape_of((8, LANES), F32),
        ],
        scratch_shapes=[pltpu.VMEM((SEQ, SEQ), F32), pltpu.VMEM((SEQ, LANES), F32)],
        compiler_params=params(40),
        cost_estimate=cost(30e9, 16 * MIB),
        name="attend",
    )(qkv, qkv, qkv, cols, rows)


def attend_back_kernel(
    q_ref, k_ref, v_ref, g_ref, col_ref, row_ref, lse_ref, dq_ref, dk_ref, dv_ref, sum_ref, mask_ref
):
    pair = pl.program_id(1)
    factor = HD ** (-0.5)

    @pl.when(pair == 0)
    def _():
        fill_mask(mask_ref, col_ref, row_ref)

    lanes = lax.broadcasted_iota(jnp.int32, (SEQ, LANES), 1)
    q, k, v, g = q_ref[...], k_ref[...], v_ref[...], g_ref[...]
    q_sums, k_sums, v_sums = [], [], []
    for head in range(LANES // HD):
        own = lanes // HD == head
        zero = jnp.zeros_like(q)
        q_own = jnp.where(own, q * jnp.asarray(factor, BF16), zero)
        g_own = jnp.where(own, g, zero)
        logsum = lse_ref[pl.ds(pair * (LANES // HD) + head, 1), :]
        probs = jnp.exp(dot_cols(k, q_own) + mask_ref[...] - logsum)
        v_sums.append(dot(low(probs), g))
        grad_probs = dot_cols(v, g_own)
        mean_grad = jnp.sum(probs * grad_probs, axis=0, keepdims=True)
        grad_scores = low(factor * probs * (grad_probs - mean_grad))
        k_sums.append(dot(grad_scores, q))
        q_sums.append(dot_rows(grad_scores, k))

    def join(parts):
        joined = parts[0]
        for head in range(1, LANES // HD):
            joined = jnp.where(lanes // HD == head, parts[head], joined)
        return low(joined)

    dq, dv = join(q_sums), join(v_sums)
    dq_ref[...] = dq
    dk_ref[...] = join(k_sums)
    dv_ref[...] = dv
    sum_ref[0:1, :] = jnp.sum(dq.astype(F32), axis=0, keepdims=True)
    sum_ref[1:2, :] = jnp.sum(dv.astype(F32), axis=0, keepdims=True)


def attend_back(qkv, grad, cols, rows, lse):
    _, tokens, width = qkv.shape
    held = tokens // SEQ

    def side(i):
        return pl.BlockSpec((None, SEQ, LANES), lambda r, j: (i, r, j))

    block = pl.BlockSpec((SEQ, LANES), lambda r, j: (r, j))
    return pl.pallas_call(
        attend_back_kernel,
        grid=(held, width // LANES),
        in_specs=[
            side(0),
            side(1),
            side(2),
            block,
            pl.BlockSpec((None, SEQ, 1), lambda r, j: (r, 0, 0)),
            pl.BlockSpec((None, 1, SEQ), lambda r, j: (r, 0, 0)),
            pl.BlockSpec((None, LANES, SEQ), lambda r, j: (r, 0, 0)),
        ],
        out_specs=[block, block, block, pl.BlockSpec((None, 8, LANES), lambda r, j: (r, 0, j))],
        out_shape=[shape_of((tokens, width), BF16)] * 3 + [shape_of((held, 8, width), F32)],
        scratch_shapes=[pltpu.VMEM((SEQ, SEQ), F32)],
        compiler_params=params(40),
        cost_estimate=cost(60e9, 16 * MIB),
        name="attend_back",
    )(qkv, qkv, qkv, grad, cols, rows, lse)


def project(values, near_ref, far_ref):
    parts, c = near_ref.shape[1], near_ref.shape[3]
    halves = []
    for ref in (near_ref, far_ref):
        total = None
        for r in range(parts):
            term = dot_cols(values[:, r * c : (r + 1) * c], flat(ref[:, r]))
            total = term if total is None else total + term
        halves.append(total)
    return jnp.concatenate(halves, axis=1)


def norm_parts(summed):
    center = summed - jnp.mean(summed, axis=-1, keepdims=True)
    inverse = lax.rsqrt(jnp.mean(center * center, axis=-1, keepdims=True) + EPS)
    return center * inverse, inverse


def norm_back(upstream, normal, inverse, gain):
    scaled = upstream * gain
    return inverse * (
        scaled
        - jnp.mean(scaled, axis=-1, keepdims=True)
        - normal * jnp.mean(scaled * normal, axis=-1, keepdims=True)
    )


def add_sums(ref, sums):
    @pl.when(pl.program_id(0) == 0)
    def _():
        ref[...] = jnp.zeros_like(ref)

    for i, values in enumerate(sums):
        ref[i : i + 1, :] += jnp.sum(values, axis=0, keepdims=True)


def first_norm_kernel(
    order_ref, ctx_ref, level_ref, near_ref, far_ref, x_ref, row_ref, quant_ref, normed_ref, normal_ref,
    inverse_ref, peak_ref
):
    level = level_ref[0:1, 0:1]
    quant = low(level * jnp.tanh(ctx_ref[...] / level))
    quant_ref[...] = quant
    summed = take_blocks(x_ref, order_ref).astype(F32) + project(quant, near_ref, far_ref)
    normal, inverse = norm_parts(summed + row_ref[0:1, :])
    normed = normal * row_ref[1:2, :] + row_ref[2:3, :]
    normed_ref[...] = normed
    normal_ref[...] = normal
    inverse_ref[...] = inverse

    @pl.when(pl.program_id(0) == 0)
    def _():
        peak_ref[...] = jnp.zeros_like(peak_ref)

    peak_ref[...] = jnp.maximum(peak_ref[...], column_peak(normed))


def whole(values):
    dims = values.shape
    return pl.BlockSpec(dims, lambda *steps: (0,) * len(dims))


def first_norm(context, level, weights, x, vectors, order):
    near, far = weights
    tokens, width = x.shape
    inner = context.shape[1]
    rows = 256

    def block(columns):
        return pl.BlockSpec((rows, columns), lambda t: (t, 0))

    return pl.pallas_call(
        first_norm_kernel,
        grid=(tokens // rows,),
        in_specs=[
            in_smem(),
            block(inner),
            whole(level),
            whole(near),
            whole(far),
            block(width),
            whole(vectors),
        ],
        out_specs=[
            block(inner),
            block(width),
            block(width),
            block(1),
            pl.BlockSpec((8, LANES), lambda t: (0, 0)),
        ],
        out_shape=[
            shape_of((tokens, inner), BF16),
            shape_of((tokens, width), F32),
            shape_of((tokens, width), F32),
            shape_of((tokens, 1), F32),
            shape_of((8, LANES), F32),
        ],
        compiler_params=params(48),
        cost_estimate=cost(2 * tokens * width * inner, 20 * MIB),
        name="first_norm",
    )(order, context, level, near, far, x, vectors)


def hidden_kernel(normed_ref, level_ref, near_ref, far_ref, b_ref, quant_ref, act_ref, slope_ref, peak_ref):
    tokens, width = normed_ref.shape
    half = width // 2
    rows = 128

    @pl.when(pl.program_id(0) == 0)
    def _():
        peak_ref[...] = jnp.zeros_like(peak_ref)
        level = level_ref[0:1, 0:1]

        @pl.loop(0, tokens // rows)
        def _(step):
            here = pl.ds(step * rows, rows)
            quant_ref[here, :] = low(level * jnp.tanh(normed_ref[here, :] / level))

    @pl.loop(0, tokens // rows)
    def _(step):
        here = pl.ds(pl.multiple_of(step * rows, rows), rows)
        hidden = dot(quant_ref[here, :half], flat(near_ref[...]))
        hidden = hidden + dot(quant_ref[here, half:], flat(far_ref[...])) + b_ref[...]
        share = 0.5 + 0.5 * lax.erf(hidden * (0.5**0.5))
        active = hidden * share
        act_ref[here, :] = active
        slope_ref[here, :] = share + hidden * (
            (0.5 / jnp.pi) ** 0.5 * jnp.exp(-0.5 * hidden * hidden)
        )
        peak_ref[...] = jnp.maximum(peak_ref[...], column_peak(active))


def hidden_rows(normed, level, weights, bias):
    near, far = weights
    plane, parts, rows, c = near.shape
    tokens, width = normed.shape
    step = min(c, 512)
    cuts = c // step
    weight_spec = pl.BlockSpec((plane, None, rows, step), lambda s: (0, s // cuts, 0, s % cuts))
    block = pl.BlockSpec((tokens, step), lambda s: (0, s))
    return pl.pallas_call(
        hidden_kernel,
        grid=(parts * cuts,),
        in_specs=[
            whole(normed),
            whole(level),
            weight_spec,
            weight_spec,
            pl.BlockSpec((1, step), lambda s: (0, s)),
        ],
        out_specs=[
            pl.BlockSpec((tokens, width), lambda s: (0, 0)),
            block,
            block,
            pl.BlockSpec((8, LANES), lambda s: (0, 0)),
        ],
        out_shape=[
            shape_of((tokens, width), BF16),
            shape_of((tokens, parts * c), F32),
            shape_of((tokens, parts * c), F32),
            shape_of((8, LANES), F32),
        ],
        compiler_params=params(48),
        cost_estimate=cost(2 * tokens * width * parts * c, 50 * MIB),
        name="hidden",
    )(normed, level, near, far, bias)


def second_norm_kernel(
    order_ref, act_ref, slope_ref, level_ref, near_ref, far_ref, normed_ref, grad_ref, row_ref,
    quant_ref, back_ref, out_ref, sum_ref, branch_ref, terms_ref
):
    level = level_ref[0:1, 0:1]
    tangent = jnp.tanh(act_ref[...] / level)
    quant = low(level * tangent)
    quant_ref[...] = quant
    back_ref[...] = (1.0 - tangent * tangent) * slope_ref[...]
    summed = normed_ref[...] + project(quant, near_ref, far_ref) + row_ref[0:1, :]
    normal, inverse = norm_parts(summed)
    gain = row_ref[1:2, :]
    put_blocks(out_ref, order_ref, low(normal * gain + row_ref[2:3, :]))
    upstream = take_blocks(grad_ref, order_ref).astype(F32)
    grad_sum = norm_back(upstream, normal, inverse, gain)
    sum_ref[...] = grad_sum
    branch_ref[...] = low(grad_sum)
    add_sums(terms_ref, (grad_sum, upstream * normal, upstream))


def second_norm(active, slope, level, weights, normed, grad, vectors, order):
    near, far = weights
    tokens, width = normed.shape
    inner = active.shape[1]
    rows = 128

    def block(columns):
        return pl.BlockSpec((rows, columns), lambda t: (t, 0))

    return pl.pallas_call(
        second_norm_kernel,
        grid=(tokens // rows,),
        in_specs=[
            in_smem(),
            block(inner),
            block(inner),
            whole(level),
            whole(near),
            whole(far),
            block(width),
            block(width),
            whole(vectors),
        ],
        out_specs=[
            block(inner),
            block(inner),
            block(width),
            block(width),
            block(width),
            pl.BlockSpec((8, width), lambda t: (0, 0)),
        ],
        out_shape=[
            shape_of((tokens, inner), BF16),
            shape_of((tokens, inner), F32),
            shape_of((tokens, width), BF16),
            shape_of((tokens, width), F32),
            shape_of((tokens, width), BF16),
            shape_of((8, width), F32),
        ],
        compiler_params=params(56),
        cost_estimate=cost(2 * tokens * width * inner, 80 * MIB),
        name="second_norm",
    )(order, active, slope, level, near, far, normed, grad, vectors)


def weight_grad_kernel(count, x_ref, *refs):
    h_refs, (keep_ref, send_ref, turned_ref) = refs[:count], refs[count:]
    half = turned_ref.shape[0] // 2

    @pl.when((pl.program_id(0) == 0) & (pl.program_id(1) == 0))
    def _():
        turned_ref[...] = x_ref[...].T

    for i, h_ref in enumerate(h_refs):
        h = h_ref[...]
        keep_ref[:, i] = dot(turned_ref[:half, :], h).reshape(keep_ref.shape[0], -1, h.shape[1])
        send_ref[:, i] = low(dot(turned_ref[half:, :], h)).reshape(keep_ref.shape[0], -1, h.shape[1])


def weight_grad(x, grads, parts, plane):
    tokens, width = x.shape
    count = len(grads)
    c = grads[0].shape[1] // parts
    rows = width // (2 * plane)
    step = min(c, 512)
    cuts = c // step
    dims = (plane, parts, count, rows, c)
    out_spec = pl.BlockSpec((plane, None, count, rows, step), lambda r, j: (0, r, 0, 0, j))
    return pl.pallas_call(
        partial(weight_grad_kernel, count),
        grid=(parts, cuts),
        in_specs=[whole(x)]
        + [pl.BlockSpec((tokens, step), lambda r, j: (0, r * cuts + j))] * count,
        out_specs=[out_spec, out_spec],
        out_shape=[shape_of(dims, F32), shape_of(dims, BF16)],
        scratch_shapes=[pltpu.VMEM((width, tokens), BF16)],
        compiler_params=params(48),
        cost_estimate=cost(2 * tokens * width * parts * c * count, 8 * width * parts * c * count),
        name="weight_grad",
    )(x, *grads)


def grad_hidden_kernel(g_ref, near_ref, far_ref, back_ref, o_ref, sum_ref):
    tokens, width = g_ref.shape
    half = width // 2
    rows = 256
    sum_ref[...] = jnp.zeros_like(sum_ref)

    @pl.loop(0, tokens // rows)
    def _(step):
        here = pl.ds(pl.multiple_of(step * rows, rows), rows)
        grad = dot(g_ref[here, :half], flat(near_ref[...]))
        grad = grad + dot(g_ref[here, half:], flat(far_ref[...]))
        grad = low(grad * back_ref[here, :])
        o_ref[here, :] = grad
        sum_ref[...] += jnp.sum(grad.astype(F32), axis=0, keepdims=True)


def grad_hidden_rows(grad, weights, back):
    near, far = weights
    plane, parts, rows, c = near.shape
    tokens, width = grad.shape
    step = min(c, 512)
    cuts = c // step
    weight_spec = pl.BlockSpec((plane, None, rows, step), lambda s: (0, s // cuts, 0, s % cuts))
    block = pl.BlockSpec((tokens, step), lambda s: (0, s))
    return pl.pallas_call(
        grad_hidden_kernel,
        grid=(parts * cuts,),
        in_specs=[whole(grad), weight_spec, weight_spec, block],
        out_specs=[block, pl.BlockSpec((1, step), lambda s: (0, s))],
        out_shape=[shape_of((tokens, parts * c), BF16), shape_of((1, parts * c), F32)],
        compiler_params=params(48),
        cost_estimate=cost(2 * tokens * width * parts * c, 34 * MIB),
        name="grad_hidden",
    )(grad, near, far, back)


def first_back_kernel(
    g_ref, near_ref, far_ref, normed_ref, normal_ref, inverse_ref, sum_two_ref, level_ref, row_ref,
    sum_ref, low_ref, terms_ref
):
    level = level_ref[0:1, 0:1]
    tangent = jnp.tanh(normed_ref[...] / level)
    grad = project(g_ref[...], near_ref, far_ref) * (1.0 - tangent * tangent) + sum_two_ref[...]
    normal = normal_ref[...]
    grad_sum = norm_back(grad, normal, inverse_ref[...], row_ref[1:2, :])
    sum_ref[...] = grad_sum
    low_ref[...] = low(grad_sum)
    add_sums(terms_ref, (grad_sum, grad * normal, grad))


def first_back(grad, weights, normed, normal, inverse, sum_two, level, vectors):
    near, far = weights
    tokens, width = normed.shape
    inner = grad.shape[1]
    rows = 256

    def block(columns):
        return pl.BlockSpec((rows, columns), lambda t: (t, 0))

    return pl.pallas_call(
        first_back_kernel,
        grid=(tokens // rows,),
        in_specs=[
            block(inner),
            whole(near),
            whole(far),
            block(width),
            block(width),
            block(1),
            block(width),
            whole(level),
            whole(vectors),
        ],
        out_specs=[block(width), block(width), pl.BlockSpec((8, width), lambda t: (0, 0))],
        out_shape=[
            shape_of((tokens, width), F32),
            shape_of((tokens, width), BF16),
            shape_of((8, width), F32),
        ],
        compiler_params=params(56),
        cost_estimate=cost(2 * tokens * width * inner, 36 * MIB),
        name="first_back",
    )(grad, near, far, normed, normal, inverse, sum_two, level, vectors)


def grad_context_kernel(g_ref, near_ref, far_ref, ctx_ref, level_ref, o_ref):
    half = g_ref.shape[1] // 2
    level = level_ref[0:1, 0:1]
    tangent = jnp.tanh(ctx_ref[...] / level)
    grad = dot(g_ref[:, :half], flat(near_ref[...])) + dot(g_ref[:, half:], flat(far_ref[...]))
    o_ref[...] = low(grad * (1.0 - tangent * tangent))


def grad_context_rows(grad, weights, context, level):
    near, far = weights
    plane, parts, rows, c = near.shape
    tokens, width = grad.shape
    weight_spec = pl.BlockSpec((plane, None, rows, c), lambda r: (0, r, 0, 0))
    block = pl.BlockSpec((tokens, c), lambda r: (0, r))
    return pl.pallas_call(
        grad_context_kernel,
        grid=(parts,),
        in_specs=[whole(grad), weight_spec, weight_spec, block, whole(level)],
        out_specs=block,
        out_shape=shape_of((tokens, parts * c), BF16),
        compiler_params=params(40),
        cost_estimate=cost(2 * tokens * width * parts * c, 10 * MIB),
        name="grad_context",
    )(grad, near, far, context, level)


def grad_input_kernel(order_ref, q_ref, k_ref, v_ref, near_ref, far_ref, sum_ref, x_ref, level_ref, o_ref):
    level = level_ref[0:1, 0:1]
    total = None
    for i, ref in enumerate((q_ref, k_ref, v_ref)):
        term = project(ref[...], near_ref.at[:, :, i], far_ref.at[:, :, i])
        total = term if total is None else total + term
    tangent = jnp.tanh(take_blocks(x_ref, order_ref).astype(F32) / level)
    put_blocks(o_ref, order_ref, low(sum_ref[...] + total * (1.0 - tangent * tangent)))


def grad_input(grads, weights, grad_sum, x, level, order):
    near, far = weights
    tokens, width = x.shape
    inner = grads[0].shape[1]
    rows = 256

    def block(columns):
        return pl.BlockSpec((rows, columns), lambda t: (t, 0))

    return pl.pallas_call(
        grad_input_kernel,
        grid=(tokens // rows,),
        in_specs=[
            in_smem(),
            block(inner),
            block(inner),
            block(inner),
            whole(near),
            whole(far),
            block(width),
            block(width),
            whole(level),
        ],
        out_specs=block(width),
        out_shape=shape_of((tokens, width), BF16),
        compiler_params=params(48),
        cost_estimate=cost(6 * tokens * width * inner, 20 * MIB),
        name="grad_input",
    )(order, *grads, near, far, grad_sum, x, level)


def doc_segments(doc_lengths, length):
    doc_ends = jnp.cumsum(doc_lengths, axis=1, dtype=jnp.int32)
    places = jnp.arange(length, dtype=jnp.int32)
    return jnp.sum(
        (places[None, :, None] >= doc_ends[:, None, :]).astype(jnp.int32), axis=2, dtype=jnp.int32
    )


def soft_clip(values, clip_level):
    return clip_level * jnp.tanh(values / clip_level)


def clip_slope(values, clip_level):
    tangent = jnp.tanh(values / clip_level)
    return 1.0 - tangent * tangent


def by_distance(values, axis_name, axis):
    count, me = lax.axis_size(axis_name), lax.axis_index(axis_name)
    dims = values.shape
    split = values.reshape(dims[:axis] + (count, dims[axis] // count) + dims[axis + 1 :])
    moved = jnp.take(split, me ^ jnp.arange(count), axis=axis)
    return moved.reshape(dims)


def own_block(values, axis):
    rows = values.shape[axis] // lax.axis_size("dp")
    return lax.dynamic_slice_in_dim(values, lax.axis_index("dp") * rows, rows, axis)


def local(
    mesh, layer_input, grad_output, doc_lengths, ranges, w_qkv, bias_qv, w_out, b_out, gain_one,
    shift_one, w_in, b_in, w_down, b_down, gain_two, shift_two
):
    datas, parts = lax.axis_size("dp"), lax.axis_size("tensor")
    data, part = lax.axis_index("dp"), lax.axis_index("tensor")
    plane = datas // 2
    tokens, width = layer_input.shape
    rows = width // datas

    places = jnp.arange(datas)
    distance = (places % plane) * 2 + places // plane
    blocks = data ^ distance
    if rows % LANES == 0:
        per_block = rows // LANES
        order = (blocks[:, None] * per_block + jnp.arange(per_block)).reshape(-1).astype(jnp.int32)
    else:
        order = jnp.arange(width // LANES, dtype=jnp.int32)

    def arrange(values):
        split = values.reshape(values.shape[:-1] + (datas, rows))
        return jnp.take(split, blocks, axis=-2).reshape(values.shape)

    def restore(values):
        split = values.reshape(values.shape[:-1] + (datas, rows))
        back = jnp.zeros((datas,), jnp.int32).at[blocks].set(places.astype(jnp.int32))
        return jnp.take(split, back, axis=-2).reshape(values.shape)

    def arrange_rows(values):
        return values if rows % LANES == 0 else arrange(values)

    def restore_rows(values):
        return values if rows % LANES == 0 else restore(values)

    x = arrange_rows(layer_input)
    upstream = arrange_rows(grad_output)
    vectors_one = jnp.zeros((8, width), F32).at[:3].set(
        arrange(jnp.stack([b_out, gain_one, shift_one]).astype(F32))
    )
    vectors_two = jnp.zeros((8, width), F32).at[:3].set(
        arrange(jnp.stack([b_down, gain_two, shift_two]).astype(F32))
    )

    own = [
        own_block(w_qkv, 1),
        own_block(w_out, 1).T[None],
        own_block(w_in, 0)[None],
        own_block(w_down, 1).T[None],
    ]
    own = [values.astype(F32) for values in own]
    peaks = [jnp.max(jnp.abs(own[0][i]), axis=0) for i in range(3)]
    peaks += [jnp.max(jnp.abs(values[0]), axis=0) for values in own[1:]]
    peaks += [jnp.max(jnp.abs(x.astype(F32)), axis=0)]
    peaks = [jnp.max(values.reshape(-1, LANES), axis=0) for values in peaks]
    peaks = jnp.stack(peaks + [jnp.zeros_like(peaks[0])])
    reached = exchange_all(peaks, mesh, "rows", ranges[:1])
    weight_levels = 0.5 * reached[:6, 0]
    level_input = DECAY * ranges[0] + (1.0 - DECAY) * reached[6:7, 0:1]
    level_input = jnp.broadcast_to(level_input, (8, LANES))
    own_levels = [weight_levels[:3][:, None, None]] + [weight_levels[i] for i in (3, 4, 5)]
    quant_own = [low(soft_clip(values, level)) for values, level in zip(own, own_levels)]
    slopes = [clip_slope(values, level) for values, level in zip(own, own_levels)]

    weights_qkv = gather(quant_own[0])
    weights_out, weights_in, weights_down = [
        tuple(side[:, :, 0] for side in gather(values)) for values in quant_own[1:]
    ]
    biases = jnp.concatenate([bias_qv.reshape(-1), b_in]).astype(BF16)[None]
    for bit in reversed(range(bits_of("tensor"))):
        other = swap(biases, "tensor", bit)
        biases = jnp.stack([biases, other], axis=1).reshape(-1, biases.shape[1])
    columns = bias_qv.shape[1]
    bias_q = biases[:, :columns].reshape(1, -1)
    bias_v = biases[:, columns : 2 * columns].reshape(1, -1)
    bias_qkv = jnp.stack([bias_q, jnp.zeros_like(bias_q), bias_v]).astype(F32)
    bias_hidden = biases[:, 2 * columns :].reshape(1, -1).astype(F32)

    held = tokens // SEQ
    lengths_here = lax.dynamic_slice_in_dim(doc_lengths, part * held, held, 0)
    segments = doc_segments(lengths_here, SEQ).astype(F32)
    seg_cols, seg_rows = segments[:, :, None], segments[:, None, :]

    quant_input = quant_rows(x, level_input, order)
    qkv = qkv_rows(quant_input, weights_qkv, bias_qkv)
    context, lse, peak = attend(qkv, seg_cols, seg_rows)
    level_context = exchange_all(peak, mesh, "level", ranges[1:2])
    quant_context, normed, normal_one, inverse_one, peak = first_norm(
        context, level_context, weights_out, x, vectors_one, order
    )
    level_normed = exchange_all(peak, mesh, "level", ranges[2:3])
    quant_normed, active, slope, peak = hidden_rows(normed, level_normed, weights_in, bias_hidden)
    level_active = exchange_all(peak, mesh, "level", ranges[3:4])
    quant_active, back, output, grad_sum_two, grad_branch, terms_two = second_norm(
        active, slope, level_active, weights_down, normed, upstream, vectors_two, order
    )

    def finish(keep, send, slope):
        return spread(low(scatter(keep, send) * slope))

    down = finish(*weight_grad(grad_branch, [quant_active], parts, plane), slopes[3])
    grad_hidden, sum_hidden = grad_hidden_rows(grad_branch, weights_down, back)
    inner = finish(*weight_grad(quant_normed, [grad_hidden], parts, plane), slopes[2])
    grad_sum_one, grad_attention, terms_one = first_back(
        grad_hidden, weights_in, normed, normal_one, inverse_one, grad_sum_two, level_normed, vectors_one
    )
    outer = finish(*weight_grad(grad_attention, [quant_context], parts, plane), slopes[1])
    grad_context = grad_context_rows(grad_attention, weights_out, context, level_context)
    *grads, sum_qv = attend_back(qkv, grad_context, seg_cols, seg_rows, lse)
    first = finish(*weight_grad(quant_input, grads, parts, plane), slopes[0])
    grad_x = grad_input(grads, weights_qkv, grad_sum_one, x, level_input, order)

    back_order = (data ^ jnp.arange(datas)).astype(jnp.int32)
    back_order = (back_order % 2) * plane + back_order // 2

    def own_order(values):
        return jnp.take(values, back_order, axis=0).astype(F32)

    grad_w_qkv = own_order(first).transpose(1, 0, 2, 3).reshape(w_qkv.shape)
    grad_w_in = own_order(inner).reshape(w_in.shape)
    grad_w_out = own_order(outer).reshape(width, -1).T
    grad_w_down = own_order(down).reshape(width, -1).T

    sums = jnp.concatenate([restore(terms_one[:3]), restore(terms_two[:3])])
    sum_qv = jnp.sum(sum_qv, axis=0)[:2]
    sum_qv = by_distance(sum_qv, "tensor", 1)
    sum_hidden = by_distance(sum_hidden, "tensor", 1).reshape(-1, width)
    sums = jnp.concatenate([sums, sum_qv, sum_hidden])
    padded = jnp.zeros((-(-sums.shape[0] // 8) * 8, width), F32).at[: sums.shape[0]].set(sums)
    sums = exchange_all(padded, mesh, "sum", ranges[:1])
    hidden_all = sums[8 : 8 + sum_hidden.shape[0]].reshape(-1)
    grad_bias_qv = lax.dynamic_slice_in_dim(sums[6:8], part * columns, columns, 1)
    grad_b_in = lax.dynamic_slice_in_dim(hidden_all, part * b_in.shape[0], b_in.shape[0], 0)
    new_ranges = jnp.stack(
        [level_input[0, 0], level_context[0, 0], level_normed[0, 0], level_active[0, 0]]
    )
    return (
        restore_rows(output),
        restore_rows(grad_x),
        grad_w_qkv,
        grad_bias_qv,
        grad_w_out,
        sums[0],
        sums[1],
        sums[2],
        grad_w_in,
        grad_b_in,
        grad_w_down,
        sums[3],
        sums[4],
        sums[5],
        new_ranges,
    )


def solution(mesh):
    in_specs = (
        P(("dp", "tensor"), None),
        P(("dp", "tensor"), None),
        P("dp", None),
        P(),
        P(None, None, "tensor"),
        P(None, "tensor"),
        P("tensor", None),
        P(),
        P(),
        P(),
        P(None, "tensor"),
        P("tensor"),
        P("tensor", None),
        P(),
        P(),
        P(),
    )
    out_specs = (
        P(("dp", "tensor"), None),
        P(("dp", "tensor"), None),
        P(None, None, "tensor"),
        P(None, "tensor"),
        P("tensor", None),
        P(),
        P(),
        P(),
        P(None, "tensor"),
        P("tensor"),
        P("tensor", None),
        P(),
        P(),
        P(),
        P(),
    )
    return jax.shard_map(
        partial(local, mesh), mesh=mesh, in_specs=in_specs, out_specs=out_specs, check_vma=False
    )
```

```python
from functools import partial

import jax
import jax.numpy as jnp
from jax import lax
from jax.experimental import pallas as pl
from jax.experimental.pallas import tpu as pltpu
from jax.sharding import PartitionSpec as P

HD = 64
SEQ = 512
LANES = 128

EPS = 1e-06
DECAY = 0.9
MASKED = -1e30
MESH = pl.DeviceIdType.MESH
F32 = jnp.float32
BF16 = jnp.bfloat16
MIB = 1024 * 1024


def shape_of(dims, kind):
    return jax.ShapeDtypeStruct(dims, kind)


def params(mib=48, **rest):
    return pltpu.CompilerParams(vmem_limit_bytes=mib * MIB, **rest)


def in_smem():
    return pl.BlockSpec(memory_space=pltpu.SMEM)


def cost(flops, moved):
    return pl.CostEstimate(flops=int(flops), bytes_accessed=int(moved), transcendentals=0)


def dot(first, second):
    return jnp.dot(first, second, preferred_element_type=F32)


def dot_cols(first, second):
    return lax.dot_general(first, second, (((1,), (1,)), ((), ())), preferred_element_type=F32)


def dot_rows(first, second):
    return lax.dot_general(first, second, (((0,), (0,)), ((), ())), preferred_element_type=F32)


def flat(block):
    return block.reshape(block.shape[0] * block.shape[1], block.shape[2])


def exchange_kernel(kind, x_ref, range_ref, o_ref, near, far, mid, near_send, near_recv, far_send, far_recv):
    data, part = lax.axis_index("dp"), lax.axis_index("tensor")
    datas, parts = lax.axis_size("dp"), lax.axis_size("tensor")
    barrier = pltpu.get_barrier_semaphore()

    def to_data(step):
        return (lax.rem(data + step, datas), part)

    def to_part(step):
        return (data, lax.rem(part + step, parts))

    def greet(target):
        def run(step, carry):
            pl.semaphore_signal(barrier, inc=1, device_id=target(step), device_id_type=MESH)
            return carry

        return run

    lax.fori_loop(1, datas, greet(to_data), 0)
    lax.fori_loop(1, parts, greet(to_part), 0)
    pl.semaphore_wait(barrier, datas + parts - 2)

    def exchange(source, slots, send, recv, target, count):
        def copy(step):
            return pltpu.make_async_remote_copy(
                src_ref=source,
                dst_ref=slots.at[step],
                send_sem=send.at[step],
                recv_sem=recv.at[step],
                device_id=target(step),
                device_id_type=MESH,
            )

        def start(step, carry):
            copy(step).start()
            return carry

        def finish(step, carry):
            copy(step).wait()
            return carry

        lax.fori_loop(1, count, start, 0)
        slots[0] = source[...]
        lax.fori_loop(1, count, finish, 0)
        return jnp.max(slots[...], axis=0)

    mid[...] = exchange(x_ref, near, near_send, near_recv, to_data, datas)
    total = exchange(mid, far, far_send, far_recv, to_part, parts)
    if kind == "rows":
        total = jnp.broadcast_to(jnp.max(total, axis=1, keepdims=True), total.shape)
    if kind == "level":
        peak = jnp.max(total, keepdims=True)
        total = jnp.broadcast_to(DECAY * range_ref[0] + (1.0 - DECAY) * peak, total.shape)
    o_ref[...] = total


def exchange_all(values, mesh, kind, previous):
    datas, parts = mesh.shape["dp"], mesh.shape["tensor"]
    dims = values.shape
    copies = pltpu.SemaphoreType.DMA
    return pl.pallas_call(
        partial(exchange_kernel, kind),
        out_shape=shape_of(dims, F32),
        in_specs=[pl.BlockSpec(memory_space=pltpu.VMEM), in_smem()],
        out_specs=pl.BlockSpec(memory_space=pltpu.VMEM),
        scratch_shapes=[
            pltpu.VMEM((datas,) + dims, F32),
            pltpu.VMEM((parts,) + dims, F32),
            pltpu.VMEM(dims, F32),
            copies((datas,)),
            copies((datas,)),
            copies((parts,)),
            copies((parts,)),
        ],
        compiler_params=pltpu.CompilerParams(
            collective_id={"rows": 0, "level": 1}[kind], has_side_effects=True
        ),
        name="exchange_" + kind,
    )(values, previous)


def tie(values, others):
    return lax.optimization_barrier((values, *others))[0]


def swap(values, axis, bit, token=None):
    count = lax.axis_size(axis)
    other = lax.ppermute(values, axis, [(i, i ^ (1 << bit)) for i in range(count)])
    return other if token is None else tie(other, [token])


def bits_of(axis):
    return lax.axis_size(axis).bit_length() - 1


def plane_orders():
    plane = list(range(1, bits_of("dp")))
    return plane, (plane[::-1], plane)


def run_all(chain, token=None):
    try:
        chain.send(token)
        while True:
            next(chain)
    except StopIteration as done:
        return done.value


def low(values):
    return values.astype(BF16)


def scatter_plane(keep, send):
    plane, orders = plane_orders()
    token = yield [send]
    values = keep + swap(send, "dp", 0, token).astype(F32)
    half = values.shape[1] // 2
    sides = [values[:, :half], values[:, half:]]
    sides = [side.reshape((2,) * len(plane) + side.shape[1:]) for side in sides]
    left = [plane[::-1], plane[::-1]]
    for step in range(len(plane)):
        places = [left[i].index(orders[i][step]) for i in range(2)]
        sends = [low(lax.index_in_dim(sides[i], 1, places[i], keepdims=False)) for i in range(2)]
        token = yield sends
        for i in range(2):
            bit = orders[i][step]
            keep = lax.index_in_dim(sides[i], 0, places[i], keepdims=False)
            sides[i] = keep + swap(sends[i], "dp", bit, token).astype(F32)
            left[i].remove(bit)
    return sides


def scatter_all(keep, send):
    sides = yield from scatter_plane(keep, send)
    for bit in range(bits_of("tensor") - 1):
        pairs = [values.reshape((-1, 2) + values.shape[1:]) for values in sides]
        sends = [low(values[:, 1]) for values in pairs]
        token = yield sends
        sides = [
            values[:, 0] + swap(send, "tensor", bit, token).astype(F32)
            for values, send in zip(pairs, sends)
        ]
    send = low(sides[1][0])
    token = yield [send]
    return sides[0][0] + swap(send, "tensor", bits_of("tensor") - 1, token).astype(F32)


def at_distance(axis, r):
    me, index = lax.axis_index(axis), 0
    for bit in range(bits_of(axis)):
        index = index + (me // (1 << bit) + (r >> bit)) % 2 * (1 << bit)
    return index


def plane_moves():
    plane = 1 << (bits_of("dp") - 1)
    if plane == 4:
        return [(1, 2), (2, 4)], [(3, 1, 4, 0), (3, 2, 2, 1)]
    return [(slot, 2 * slot) for slot in range(1, plane)], []


class Mover:
    def __init__(self, send, recv, local):
        self.send, self.recv, self.local = send, recv, local
        self.count, self.local_count = 0, 0

    def remote(self, source, target, axis, r):
        i = self.count
        self.count += 1
        return pltpu.make_async_remote_copy(
            src_ref=source,
            dst_ref=target,
            send_sem=self.send.at[i],
            recv_sem=self.recv.at[i],
            device_id={axis: at_distance(axis, r)},
            device_id_type=MESH,
        )

    def own(self, source, target):
        i = self.local_count
        self.local_count += 1
        return pltpu.make_async_copy(source, target, self.local.at[i])


def greet(distances):
    barrier = pltpu.get_barrier_semaphore()
    for axis, r in distances:
        pl.semaphore_signal(
            barrier, inc=1, device_id={axis: at_distance(axis, r)}, device_id_type=MESH
        )
    pl.semaphore_wait(barrier, len(distances))


def part_distances():
    return [("tensor", r) for r in range(1, 1 << bits_of("tensor"))]


def plane_distances():
    first, second = plane_moves()
    apart = sorted({move[1] for move in first} | {move[2] for move in second} | {1})
    return [("dp", r) for r in apart]


def halves_of(ref, half):
    rows = ref.shape[-2] // 2
    return ref.at[..., half * rows : (half + 1) * rows, :]


class AlongParts:
    def __init__(self, mover, own, held):
        self.copy = mover.own(own, held.at[0])
        self.moves = [mover.remote(own, held.at[r], axis, r) for axis, r in part_distances()]

    def start(self):
        self.copy.start()
        for move in self.moves:
            move.start()

    def finish(self):
        self.copy.wait()
        for move in self.moves:
            move.wait()


class OverPlane:
    def __init__(self, mover, held, near, far):
        first, second = plane_moves()
        self.copy = mover.own(held, near.at[0])
        self.first = [mover.remote(held, near.at[slot], "dp", r) for slot, r in first]
        self.second = [
            mover.remote(halves_of(near.at[source], half), halves_of(near.at[slot], half), "dp", r)
            for slot, source, r, half in second
        ]
        sources = [held] + [near.at[slot] for slot in range(1, near.shape[0])]
        self.cores = [mover.remote(source, far.at[i], "dp", 1) for i, source in enumerate(sources)]
        self.early = 1 + len(first)

    def start(self):
        self.copy.start()
        for move in self.first:
            move.start()
        self.cores[0].start()

    def relay(self):
        for move in self.first:
            move.wait_recv()
        for move in self.second + self.cores[1 : self.early]:
            move.start()

    def finish(self):
        for move in self.second:
            move.wait_recv()
        for move in self.cores[self.early :]:
            move.start()
        self.copy.wait()
        for move in self.first + self.second:
            move.wait_send()
        for move in self.cores:
            move.wait()


def copy_counts(plans):
    first, second = plane_moves()
    parts, plane = 1 << bits_of("tensor"), 1 << (bits_of("dp") - 1)
    remote = sum(parts - 1 if kind == "parts" else len(first) + len(second) + plane for kind in plans)
    return remote, len(plans)


def copy_semaphores(remote, local):
    copies = pltpu.SemaphoreType.DMA
    return [copies((remote,)), copies((remote,)), copies((local,))]


def anywhere():
    return pl.BlockSpec(memory_space=pl.ANY)


def hosting(body, counts, plans, relay_step):
    ins, outs = counts

    def kernel(*refs):
        extra = sum(1 if kind == "parts" else 2 for kind in plans)
        body_ins, sources = refs[:ins], list(refs[ins : ins + len(plans)])
        rest = refs[ins + len(plans) :]
        body_outs, targets = rest[:outs], list(rest[outs : outs + extra])
        scratch = rest[outs + extra :]
        body_scratch, semaphores = scratch[:-3], scratch[-3:]
        mover = Mover(*semaphores)
        moves = []
        for kind in plans:
            if kind == "parts":
                moves.append(AlongParts(mover, sources.pop(0), targets.pop(0)))
            else:
                moves.append(OverPlane(mover, sources.pop(0), targets.pop(0), targets.pop(0)))
        step, steps = 0, 1
        for i in range(HOST_RANK[body]):
            step = step * pl.num_programs(i) + pl.program_id(i)
            steps = steps * pl.num_programs(i)
        apart = plane_distances() if "plane" in plans else []
        apart = apart + (part_distances() if "parts" in plans else [])

        @pl.when(step == 0)
        def _():
            greet(apart)
            for move in moves:
                move.start()

        @pl.when(step == relay_step)
        def _():
            for move in moves:
                if isinstance(move, OverPlane):
                    move.relay()

        body(*body_ins, *body_outs, *body_scratch)

        @pl.when(step == steps - 1)
        def _():
            for move in moves:
                move.finish()

    return kernel


def gather_shapes(kind, values):
    parts, plane = 1 << bits_of("tensor"), 1 << (bits_of("dp") - 1)
    if kind == "parts":
        return [shape_of((parts,) + values.shape, values.dtype)]
    return [shape_of((plane,) + values.shape, values.dtype)] * 2


def hosted_call(body, plans, sources, relay_step, cid, *, grid, in_specs, out_specs, out_shape, scratch_shapes=(), mib, **rest):
    extra = [shape for kind, values in zip(plans, sources) for shape in gather_shapes(kind, values)]
    counts = (len(in_specs), len(out_specs))
    call = pl.pallas_call(
        hosting(body, counts, plans, relay_step),
        grid=grid,
        in_specs=in_specs + [anywhere()] * len(sources),
        out_specs=out_specs + [anywhere()] * len(extra),
        out_shape=out_shape + extra,
        scratch_shapes=list(scratch_shapes) + copy_semaphores(*copy_counts(plans)),
        compiler_params=params(mib, collective_id=cid, has_side_effects=True),
        **rest,
    )

    def run(*args):
        results = call(*args, *sources)
        return results[: counts[1]], results[counts[1] :]

    return run


def first_gather_kernel(first_ref, out_ref, in_ref, near, far, held_out, held_in, send, recv, own):
    mover = Mover(send, recv, own)
    parts, plane = near.shape[1], near.shape[0]
    moves, relays = plane_moves()
    keep = mover.own(first_ref, near.at[0, 0])
    along = [mover.remote(first_ref, near.at[0, r], axis, r) for axis, r in part_distances()]
    sources = [first_ref] + [near.at[0, r] for r in range(1, parts)]
    over = [[mover.remote(sources[r], near.at[slot, r], "dp", d) for slot, d in moves] for r in range(parts)]
    again = [
        [
            mover.remote(halves_of(near.at[source, r], half), halves_of(near.at[slot, r], half), "dp", d)
            for slot, source, d, half in relays
        ]
        for r in range(parts)
    ]
    cores = [
        [mover.remote(sources[r] if slot == 0 else near.at[slot, r], far.at[slot, r], "dp", 1) for slot in range(plane)]
        for r in range(parts)
    ]
    later = [AlongParts(mover, out_ref, held_out), AlongParts(mover, in_ref, held_in)]
    greet(part_distances() + plane_distances())
    for move in along + over[0]:
        move.start()
    cores[0][0].start()
    keep.start()
    for r in range(1, parts):
        along[r - 1].wait_recv()
        for move in over[r] + cores[r][:1]:
            move.start()
    for move in along:
        move.wait_send()
    for move in later:
        move.start()
    for r in range(parts):
        for i, (slot, _) in enumerate(moves):
            over[r][i].wait_recv()
            cores[r][slot].start()
        for move in again[r]:
            move.start()
    for r in range(parts):
        for move in again[r]:
            move.wait_recv()
        for slot in range(1 + len(moves), plane):
            cores[r][slot].start()
    keep.wait()
    for r in range(parts):
        for move in over[r] + again[r]:
            move.wait_send()
        for move in cores[r]:
            move.wait()
    for move in later:
        move.finish()


def first_gather(first, outer, inner):
    parts, plane = 1 << bits_of("tensor"), 1 << (bits_of("dp") - 1)
    moves, relays = plane_moves()
    remote = 3 * (parts - 1) + parts * (len(moves) + len(relays) + plane)
    return pl.pallas_call(
        first_gather_kernel,
        in_specs=[anywhere()] * 3,
        out_specs=[anywhere()] * 4,
        out_shape=[shape_of((plane, parts) + first.shape, BF16)] * 2
        + [shape_of((parts,) + values.shape, BF16) for values in (outer, inner)],
        scratch_shapes=copy_semaphores(remote, 3),
        compiler_params=params(16, collective_id=3, has_side_effects=True),
        name="first_gather",
    )(first, outer, inner)


class PartSum:
    def __init__(self, mover, send, recv, slope, piece, near, far):
        self.moves = [mover.remote(send.at[r - 1], recv.at[r - 1], axis, r) for axis, r in part_distances()]
        self.over = OverPlane(mover, piece, near, far)
        self.send, self.recv, self.slope, self.piece = send, recv, slope, piece

    def push(self, r, values):
        self.send[r - 1] = low(values)
        self.moves[r - 1].start()

    def reach(self, own):
        for move in self.moves:
            move.wait_recv()
        total = own + jnp.sum(self.recv[...].astype(F32), axis=0)
        self.piece[...] = low(total * self.slope[...])
        self.over.start()

    def relay(self):
        self.over.relay()

    def finish(self):
        self.over.finish()
        for move in self.moves:
            move.wait_send()


def finale_kernel(
    down_ref, in_a, in_b, out_a, out_b, q_a, q_b, keep_ref, send_ref, slope_in, slope_out, slope_q, sums_ref,
    near_d, far_d, near_i, far_i, near_o, far_o, near_q, far_q, sums_out,
    send_i, recv_i, piece_i, send_o, recv_o, piece_o, send_q, recv_q, piece_q, core_recv, plane_send,
    plane_recv, sums_near, sums_mid, sums_far, send, recv, own
):
    mover = Mover(send, recv, own)
    plane, half = keep_ref.shape[0], keep_ref.shape[1]
    parts = 2 * half
    quarter = half // 2
    datas = sums_near.shape[0]
    core = mover.remote(send_ref, core_recv, "dp", 1)
    planes = [
        mover.remote(plane_send.at[r - 1], plane_recv.at[r - 1], "dp", 2 * r) for r in range(1, plane)
    ]
    down = OverPlane(mover, down_ref, near_d, far_d)
    inner = PartSum(mover, send_i, recv_i, slope_in, piece_i, near_i, far_i)
    outer = PartSum(mover, send_o, recv_o, slope_out, piece_o, near_o, far_o)
    first = PartSum(mover, send_q, recv_q, slope_q, piece_q, near_q, far_q)
    sum_data = [mover.remote(sums_ref, sums_near.at[r], "dp", r) for r in range(1, datas)]
    sum_part = [mover.remote(sums_mid, sums_far.at[r], axis, r) for axis, r in part_distances()]

    greet([("dp", r) for r in range(1, datas)] + part_distances())
    core.start()
    down.start()
    for move in sum_data:
        move.start()
    for r in range(1, half):
        first.push(r, (q_a if r < quarter else q_b)[r % quarter])
    for r in range(1, parts):
        outer.push(r, (out_a if r < half else out_b)[r % half])
    for r in range(1, parts):
        inner.push(r, (in_a if r < half else in_b)[r % half])

    core.wait_recv()
    for r in range(1, plane):
        plane_send[r - 1] = low(keep_ref[r] + core_recv[r].astype(F32))
        planes[r - 1].start()
    for move in sum_data:
        move.wait()
    sums_near[0] = sums_ref[...]
    sums_mid[...] = jnp.sum(sums_near[...], axis=0)
    for move in sum_part:
        move.start()
    down.relay()
    outer.reach(out_a[0])
    for move in planes:
        move.wait_recv()
    for r in range(half):
        total = keep_ref[0, r] + core_recv[0, r].astype(F32)
        for i in range(plane - 1):
            total = total + plane_recv[i, r].astype(F32)
        first.push(half + r, total)
    down.finish()
    outer.relay()
    inner.reach(in_a[0])
    outer.finish()
    for move in sum_part:
        move.wait()
    sums_far[0] = sums_mid[...]
    sums_out[...] = jnp.sum(sums_far[...], axis=0)
    first.reach(q_a[0])
    inner.relay()
    first.relay()
    inner.finish()
    first.finish()
    core.wait_send()
    for move in planes:
        move.wait_send()


def finale(down, inner, outer, first, raw, slopes, sums):
    parts, plane, datas = 1 << bits_of("tensor"), 1 << (bits_of("dp") - 1), 1 << bits_of("dp")
    keep, send = raw
    pieces = [down, slopes[1], slopes[2], slopes[0]]
    first_moves, second_moves = plane_moves()
    per_plane = len(first_moves) + len(second_moves) + plane
    remote = 1 + plane - 1 + 4 * per_plane + 4 * (parts - 1) + datas - 1
    vmem = pl.BlockSpec(memory_space=pltpu.VMEM)
    scratch = []
    for piece in pieces[1:]:
        scratch += [pltpu.VMEM((parts - 1,) + piece.shape, BF16)] * 2 + [pltpu.VMEM(piece.shape, BF16)]
    scratch += [pltpu.VMEM(keep.shape, BF16)] + [pltpu.VMEM((plane - 1,) + keep.shape[1:], BF16)] * 2
    scratch += [
        pltpu.VMEM((datas,) + sums.shape, F32),
        pltpu.VMEM(sums.shape, F32),
        pltpu.VMEM((parts,) + sums.shape, F32),
    ]
    out_shape = []
    for piece in pieces:
        out_shape += [shape_of((plane,) + piece.shape, BF16)] * 2
    args = (down, *inner, *outer, *first, keep, send, slopes[1], slopes[2], slopes[0], sums)
    results = pl.pallas_call(
        finale_kernel,
        in_specs=[vmem] * 8 + [anywhere()] + [vmem] * 4,
        out_specs=[anywhere()] * 8 + [vmem],
        out_shape=out_shape + [shape_of(sums.shape, F32)],
        scratch_shapes=scratch + copy_semaphores(remote, 4),
        compiler_params=params(48, collective_id=2, has_side_effects=True),
        name="finale",
    )(*args)
    return [results[2 * i : 2 * i + 2] for i in range(4)], results[8]


def take_blocks(ref, order_ref):
    return jnp.concatenate(
        [
            ref[:, pl.ds(pl.multiple_of(order_ref[j] * LANES, LANES), LANES)]
            for j in range(ref.shape[1] // LANES)
        ],
        axis=1,
    )


def put_blocks(ref, order_ref, values):
    for j in range(ref.shape[1] // LANES):
        ref[:, pl.ds(pl.multiple_of(order_ref[j] * LANES, LANES), LANES)] = values[
            :, j * LANES : (j + 1) * LANES
        ]


def fold_peak(values):
    return jnp.max(jnp.abs(values).reshape(-1, 8, LANES), axis=0)


def column_peak(values):
    peak = fold_peak(values[:, :LANES])
    for j in range(1, values.shape[1] // LANES):
        peak = jnp.maximum(peak, fold_peak(values[:, j * LANES : (j + 1) * LANES]))
    return peak


def quant_kernel(order_ref, x_ref, level_ref, o_ref):
    level = level_ref[0:1, 0:1]
    x = take_blocks(x_ref, order_ref).astype(F32)
    o_ref[...] = low(level * jnp.tanh(x / level))


def quant_rows(x, level, order):
    tokens, width = x.shape
    rows = 256
    return pl.pallas_call(
        quant_kernel,
        grid=(tokens // rows,),
        in_specs=[
            in_smem(),
            pl.BlockSpec((rows, width), lambda t: (t, 0)),
            pl.BlockSpec((8, LANES), lambda t: (0, 0)),
        ],
        out_specs=pl.BlockSpec((rows, width), lambda t: (t, 0)),
        out_shape=shape_of((tokens, width), BF16),
        compiler_params=params(32),
        name="quant_input",
    )(order, x, level)


def qkv_kernel(x_ref, near_ref, far_ref, b_ref, o_ref):
    half = x_ref.shape[1] // 2
    total = dot(x_ref[:, :half], flat(near_ref[...])) + dot(x_ref[:, half:], flat(far_ref[...]))
    o_ref[...] = low(total + b_ref[...])


def qkv_rows(x, weights, bias, held_out):
    near, far = weights
    plane, parts, kinds, rows, c = near.shape
    tokens, width = x.shape
    weight_spec = pl.BlockSpec((plane, None, None, rows, c), lambda r, i: (0, r, i, 0, 0))
    run = hosted_call(
        qkv_kernel,
        ["plane"],
        [held_out],
        parts * kinds // 2,
        4,
        grid=(parts, kinds),
        in_specs=[
            pl.BlockSpec((tokens, width), lambda r, i: (0, 0)),
            weight_spec,
            weight_spec,
            pl.BlockSpec((None, 1, c), lambda r, i: (i, 0, r)),
        ],
        out_specs=[pl.BlockSpec((None, tokens, c), lambda r, i: (i, 0, r))],
        out_shape=[shape_of((kinds, tokens, parts * c), BF16)],
        mib=32,
        cost_estimate=cost(2 * tokens * width * kinds * parts * c, 14 * MIB),
        name="qkv",
    )
    return run(x, near, far, bias)


def fill_mask(mask_ref, col_ref, row_ref):
    mask_ref[...] = jnp.where(col_ref[...] == row_ref[...], 0.0, MASKED).astype(F32)


def attend_kernel(q_ref, k_ref, v_ref, col_ref, row_ref, o_ref, lse_ref, peak_ref, mask_ref, sums_ref):
    row, pair = pl.program_id(0), pl.program_id(1)
    factor = HD ** (-0.5)

    @pl.when(pair == 0)
    def _():
        fill_mask(mask_ref, col_ref, row_ref)
        sums_ref[...] = jnp.zeros_like(sums_ref)

    @pl.when((pair == 0) & (row == 0))
    def _():
        peak_ref[...] = jnp.zeros_like(peak_ref)

    rows = 256
    lanes = lax.broadcasted_iota(jnp.int32, (rows, LANES), 1)
    for start in range(0, SEQ, rows):
        here = pl.ds(start, rows)
        q = q_ref[here, :] * jnp.asarray(factor, BF16)
        parts = []
        sums = sums_ref[here, :]
        for head in range(LANES // HD):
            own = lanes // HD == head
            scores = dot_cols(jnp.where(own, q, jnp.zeros_like(q)), k_ref[...]) + mask_ref[here, :]
            row_max = jnp.max(scores, axis=-1, keepdims=True)
            exponent = jnp.exp(scores - row_max)
            totals = jnp.sum(exponent, axis=-1, keepdims=True)
            probs = low(exponent * (1.0 / totals))
            parts.append(dot(probs, v_ref[...]))
            sums = jnp.where(lanes == pair * (LANES // HD) + head, row_max + jnp.log(totals), sums)
        context = parts[0]
        for head in range(1, LANES // HD):
            context = jnp.where(lanes // HD == head, parts[head], context)
        o_ref[here, :] = context
        sums_ref[here, :] = sums
        peak_ref[...] = jnp.maximum(peak_ref[...], fold_peak(context))

    @pl.when(pair == pl.num_programs(1) - 1)
    def _():
        lse_ref[...] = sums_ref[...].T


def attend(qkv, cols, rows, held_in, own_down):
    _, tokens, width = qkv.shape
    held = tokens // SEQ

    def side(i):
        return pl.BlockSpec((None, SEQ, LANES), lambda r, j: (i, r, j))

    run = hosted_call(
        attend_kernel,
        ["plane", "parts"],
        [held_in, own_down],
        held * width // LANES * 3 // 4,
        5,
        grid=(held, width // LANES),
        in_specs=[
            side(0),
            side(1),
            side(2),
            pl.BlockSpec((None, SEQ, 1), lambda r, j: (r, 0, 0)),
            pl.BlockSpec((None, 1, SEQ), lambda r, j: (r, 0, 0)),
        ],
        out_specs=[
            pl.BlockSpec((SEQ, LANES), lambda r, j: (r, j)),
            pl.BlockSpec((None, LANES, SEQ), lambda r, j: (r, 0, 0)),
            pl.BlockSpec((8, LANES), lambda r, j: (0, 0)),
        ],
        out_shape=[
            shape_of((tokens, width), F32),
            shape_of((held, LANES, SEQ), F32),
            shape_of((8, LANES), F32),
        ],
        scratch_shapes=[pltpu.VMEM((SEQ, SEQ), F32), pltpu.VMEM((SEQ, LANES), F32)],
        mib=40,
        cost_estimate=cost(30e9, 80 * MIB),
        name="attend",
    )
    return run(qkv, qkv, qkv, cols, rows)


def attend_back_kernel(
    c, first, order_ref, q_ref, k_ref, v_ref, g_ref, col_ref, row_ref, lse_ref, before_ref, dq_ref, dk_ref,
    dv_ref, sum_ref, mask_ref
):
    pair = pl.program_id(1)

    @pl.when((pair == 0) & (pl.program_id(0) == 0))
    def _():
        sum_ref[...] = before_ref[...]

    factor = HD ** (-0.5)

    @pl.when(pair == 0)
    def _():
        fill_mask(mask_ref, col_ref, row_ref)

    lanes = lax.broadcasted_iota(jnp.int32, (SEQ, LANES), 1)
    q, k, v, g = q_ref[...], k_ref[...], v_ref[...], g_ref[...]
    q_sums, k_sums, v_sums = [], [], []
    for head in range(LANES // HD):
        own = lanes // HD == head
        zero = jnp.zeros_like(q)
        q_own = jnp.where(own, q * jnp.asarray(factor, BF16), zero)
        g_own = jnp.where(own, g, zero)
        logsum = lse_ref[pl.ds((pair + first // LANES) * (LANES // HD) + head, 1), :]
        probs = jnp.exp(dot_cols(k, q_own) + mask_ref[...] - logsum)
        v_sums.append(dot(low(probs), g))
        grad_probs = dot_cols(v, g_own)
        mean_grad = jnp.sum(probs * grad_probs, axis=0, keepdims=True)
        grad_scores = low(factor * probs * (grad_probs - mean_grad))
        k_sums.append(dot(grad_scores, q))
        q_sums.append(dot_rows(grad_scores, k))

    def join(parts):
        joined = parts[0]
        for head in range(1, LANES // HD):
            joined = jnp.where(lanes // HD == head, parts[head], joined)
        return low(joined)

    dq, dv = join(q_sums), join(v_sums)
    dq_ref[...] = dq
    dk_ref[...] = join(k_sums)
    dv_ref[...] = dv
    column = first + pair * LANES
    place = order_ref[column // c] * c + column % c
    here = pl.ds(pl.multiple_of(place, LANES), LANES)
    sum_ref[0:1, here] += jnp.sum(dq.astype(F32), axis=0, keepdims=True)
    sum_ref[1:2, here] += jnp.sum(dv.astype(F32), axis=0, keepdims=True)


def attend_back(qkv, grad, cols, rows, lse, before, part_order, c, first):
    _, tokens, inner = qkv.shape
    width = grad.shape[1]
    held = tokens // SEQ
    skip = first // LANES

    def side(i):
        return pl.BlockSpec((None, SEQ, LANES), lambda r, j: (i, r, j + skip))

    block = pl.BlockSpec((SEQ, LANES), lambda r, j: (r, j))
    sums = pl.BlockSpec((8, inner), lambda r, j: (0, 0))
    return pl.pallas_call(
        partial(attend_back_kernel, c, first),
        grid=(held, width // LANES),
        in_specs=[
            in_smem(),
            side(0),
            side(1),
            side(2),
            block,
            pl.BlockSpec((None, SEQ, 1), lambda r, j: (r, 0, 0)),
            pl.BlockSpec((None, 1, SEQ), lambda r, j: (r, 0, 0)),
            pl.BlockSpec((None, LANES, SEQ), lambda r, j: (r, 0, 0)),
            sums,
        ],
        out_specs=[block, block, block, sums],
        out_shape=[shape_of((tokens, width), BF16)] * 3 + [shape_of((8, inner), F32)],
        scratch_shapes=[pltpu.VMEM((SEQ, SEQ), F32)],
        compiler_params=params(40),
        cost_estimate=cost(15e9, 50 * MIB),
        name="attend_back",
    )(part_order, qkv, qkv, qkv, grad, cols, rows, lse, before)


def project(values, near_ref, far_ref):
    parts, c = near_ref.shape[1], near_ref.shape[3]
    halves = []
    for ref in (near_ref, far_ref):
        total = None
        for r in range(parts):
            term = dot_cols(values[:, r * c : (r + 1) * c], flat(ref[:, r]))
            total = term if total is None else total + term
        halves.append(total)
    return jnp.concatenate(halves, axis=1)


def norm_parts(summed):
    center = summed - jnp.mean(summed, axis=-1, keepdims=True)
    inverse = lax.rsqrt(jnp.mean(center * center, axis=-1, keepdims=True) + EPS)
    return center * inverse, inverse


def norm_back(upstream, normal, inverse, gain):
    scaled = upstream * gain
    return inverse * (
        scaled
        - jnp.mean(scaled, axis=-1, keepdims=True)
        - normal * jnp.mean(scaled * normal, axis=-1, keepdims=True)
    )


def add_sums(ref, order_ref, sums):
    @pl.when(pl.program_id(0) == 0)
    def _():
        ref[...] = jnp.zeros_like(ref)

    for i, values in enumerate(sums):
        total = jnp.sum(values, axis=0, keepdims=True)
        for j in range(ref.shape[1] // LANES):
            here = pl.ds(pl.multiple_of(order_ref[j] * LANES, LANES), LANES)
            ref[i : i + 1, here] += total[:, j * LANES : (j + 1) * LANES]


def first_norm_kernel(
    order_ref, ctx_ref, level_ref, near_ref, far_ref, x_ref, row_ref, quant_ref, normed_ref, normal_ref,
    inverse_ref, peak_ref
):
    level = level_ref[0:1, 0:1]
    quant = low(level * jnp.tanh(ctx_ref[...] / level))
    quant_ref[...] = quant
    vectors = take_blocks(row_ref, order_ref)
    summed = take_blocks(x_ref, order_ref).astype(F32) + project(quant, near_ref, far_ref)
    normal, inverse = norm_parts(summed + vectors[0:1, :])
    normed = normal * vectors[1:2, :] + vectors[2:3, :]
    normed_ref[...] = normed
    normal_ref[...] = normal
    inverse_ref[...] = inverse

    @pl.when(pl.program_id(0) == 0)
    def _():
        peak_ref[...] = jnp.zeros_like(peak_ref)

    peak_ref[...] = jnp.maximum(peak_ref[...], column_peak(normed))


def whole(values):
    dims = values.shape
    return pl.BlockSpec(dims, lambda *steps: (0,) * len(dims))


def first_norm(context, level, weights, x, vectors, order):
    near, far = weights
    tokens, width = x.shape
    inner = context.shape[1]
    rows = 256

    def block(columns):
        return pl.BlockSpec((rows, columns), lambda t: (t, 0))

    return pl.pallas_call(
        first_norm_kernel,
        grid=(tokens // rows,),
        in_specs=[
            in_smem(),
            block(inner),
            whole(level),
            whole(near),
            whole(far),
            block(width),
            whole(vectors),
        ],
        out_specs=[
            block(inner),
            block(width),
            block(width),
            block(1),
            pl.BlockSpec((8, LANES), lambda t: (0, 0)),
        ],
        out_shape=[
            shape_of((tokens, inner), BF16),
            shape_of((tokens, width), F32),
            shape_of((tokens, width), F32),
            shape_of((tokens, 1), F32),
            shape_of((8, LANES), F32),
        ],
        compiler_params=params(48),
        cost_estimate=cost(2 * tokens * width * inner, 20 * MIB),
        name="first_norm",
    )(order, context, level, near, far, x, vectors)


def hidden_kernel(normed_ref, level_ref, near_ref, far_ref, b_ref, quant_ref, act_ref, slope_ref, peak_ref):
    tokens, width = normed_ref.shape
    half = width // 2
    rows = 128

    @pl.when(pl.program_id(0) == 0)
    def _():
        peak_ref[...] = jnp.zeros_like(peak_ref)
        level = level_ref[0:1, 0:1]

        @pl.loop(0, tokens // rows)
        def _(step):
            here = pl.ds(step * rows, rows)
            quant_ref[here, :] = low(level * jnp.tanh(normed_ref[here, :] / level))

    @pl.loop(0, tokens // rows)
    def _(step):
        here = pl.ds(pl.multiple_of(step * rows, rows), rows)
        hidden = dot(quant_ref[here, :half], flat(near_ref[...]))
        hidden = hidden + dot(quant_ref[here, half:], flat(far_ref[...])) + b_ref[...]
        share = 0.5 + 0.5 * lax.erf(hidden * (0.5**0.5))
        active = hidden * share
        act_ref[here, :] = active
        slope_ref[here, :] = share + hidden * (
            (0.5 / jnp.pi) ** 0.5 * jnp.exp(-0.5 * hidden * hidden)
        )
        peak_ref[...] = jnp.maximum(peak_ref[...], column_peak(active))


def hidden_rows(normed, level, weights, bias, held_down):
    near, far = weights
    plane, parts, rows, c = near.shape
    tokens, width = normed.shape
    step = min(c, 512)
    cuts = c // step
    weight_spec = pl.BlockSpec((plane, None, rows, step), lambda s: (0, s // cuts, 0, s % cuts))
    block = pl.BlockSpec((tokens, step), lambda s: (0, s))
    run = hosted_call(
        hidden_kernel,
        ["plane"],
        [held_down],
        parts * cuts * 3 // 4,
        6,
        grid=(parts * cuts,),
        in_specs=[
            whole(normed),
            whole(level),
            weight_spec,
            weight_spec,
            pl.BlockSpec((1, step), lambda s: (0, s)),
        ],
        out_specs=[
            pl.BlockSpec((tokens, width), lambda s: (0, 0)),
            block,
            block,
            pl.BlockSpec((8, LANES), lambda s: (0, 0)),
        ],
        out_shape=[
            shape_of((tokens, width), BF16),
            shape_of((tokens, parts * c), F32),
            shape_of((tokens, parts * c), F32),
            shape_of((8, LANES), F32),
        ],
        mib=48,
        cost_estimate=cost(2 * tokens * width * parts * c, 50 * MIB),
        name="hidden",
    )
    return run(normed, level, near, far, bias)


def second_norm_kernel(
    order_ref, act_ref, slope_ref, level_ref, near_ref, far_ref, normed_ref, grad_ref, row_ref,
    quant_ref, back_ref, out_ref, sum_ref, branch_ref, terms_ref
):
    level = level_ref[0:1, 0:1]
    tangent = jnp.tanh(act_ref[...] / level)
    quant = low(level * tangent)
    quant_ref[...] = quant
    back_ref[...] = (1.0 - tangent * tangent) * slope_ref[...]
    vectors = take_blocks(row_ref, order_ref)
    summed = normed_ref[...] + project(quant, near_ref, far_ref) + vectors[3:4, :]
    normal, inverse = norm_parts(summed)
    gain = vectors[4:5, :]
    put_blocks(out_ref, order_ref, low(normal * gain + vectors[5:6, :]))
    upstream = take_blocks(grad_ref, order_ref).astype(F32)
    grad_sum = norm_back(upstream, normal, inverse, gain)
    sum_ref[...] = grad_sum
    branch_ref[...] = low(grad_sum)
    add_sums(terms_ref, order_ref, (grad_sum, upstream * normal, upstream))


def second_norm(active, slope, level, weights, normed, grad, vectors, order):
    near, far = weights
    tokens, width = normed.shape
    inner = active.shape[1]
    rows = 128

    def block(columns):
        return pl.BlockSpec((rows, columns), lambda t: (t, 0))

    return pl.pallas_call(
        second_norm_kernel,
        grid=(tokens // rows,),
        in_specs=[
            in_smem(),
            block(inner),
            block(inner),
            whole(level),
            whole(near),
            whole(far),
            block(width),
            block(width),
            whole(vectors),
        ],
        out_specs=[
            block(inner),
            block(inner),
            block(width),
            block(width),
            block(width),
            pl.BlockSpec((8, width), lambda t: (0, 0)),
        ],
        out_shape=[
            shape_of((tokens, inner), BF16),
            shape_of((tokens, inner), F32),
            shape_of((tokens, width), BF16),
            shape_of((tokens, width), F32),
            shape_of((tokens, width), BF16),
            shape_of((8, width), F32),
        ],
        compiler_params=params(56),
        cost_estimate=cost(2 * tokens * width * inner, 80 * MIB),
        name="second_norm",
    )(order, active, slope, level, near, far, normed, grad, vectors)


def weight_grad_kernel(count, x_ref, *refs):
    h_refs, (keep_ref, send_ref, turned_ref) = refs[:count], refs[count:]
    half = turned_ref.shape[0] // 2

    @pl.when((pl.program_id(0) == 0) & (pl.program_id(1) == 0))
    def _():
        turned_ref[...] = x_ref[...].T

    for i, h_ref in enumerate(h_refs):
        h = h_ref[...]
        keep_ref[:, i] = dot(turned_ref[:half, :], h).reshape(keep_ref.shape[0], -1, h.shape[1])
        send_ref[:, i] = low(dot(turned_ref[half:, :], h)).reshape(keep_ref.shape[0], -1, h.shape[1])


def weight_grad(x, grads, parts, plane):
    tokens, width = x.shape
    count = len(grads)
    c = grads[0].shape[1] // parts
    rows = width // (2 * plane)
    step = min(c, 512)
    cuts = c // step
    dims = (plane, parts, count, rows, c)
    out_spec = pl.BlockSpec((plane, None, count, rows, step), lambda r, j: (0, r, 0, 0, j))
    return pl.pallas_call(
        partial(weight_grad_kernel, count),
        grid=(parts, cuts),
        in_specs=[whole(x)]
        + [pl.BlockSpec((tokens, step), lambda r, j: (0, r * cuts + j))] * count,
        out_specs=[out_spec, out_spec],
        out_shape=[shape_of(dims, F32), shape_of(dims, BF16)],
        scratch_shapes=[pltpu.VMEM((width, tokens), BF16)],
        compiler_params=params(48),
        cost_estimate=cost(2 * tokens * width * parts * c * count, 10 * width * parts * c * count),
        name="weight_grad",
    )(x, *grads)


def grad_hidden_kernel(cuts, order_ref, g_ref, near_ref, far_ref, back_ref, o_ref, sum_ref):
    tokens, width = g_ref.shape
    half = width // 2
    rows = 256
    block = pl.program_id(0)
    columns = back_ref.shape[1]

    @pl.when(block == 0)
    def _():
        sum_ref[...] = jnp.zeros_like(sum_ref)

    def run(step, total):
        here = pl.ds(pl.multiple_of(step * rows, rows), rows)
        grad = dot(g_ref[here, :half], flat(near_ref[...]))
        grad = grad + dot(g_ref[here, half:], flat(far_ref[...]))
        grad = low(grad * back_ref[here, :])
        o_ref[here, :] = grad
        return total + jnp.sum(grad.astype(F32), axis=0, keepdims=True)

    total = lax.fori_loop(0, tokens // rows, run, jnp.zeros((1, columns), F32))
    start = pl.multiple_of((block % cuts) * columns, LANES)
    sum_ref[pl.ds(order_ref[block // cuts], 1), pl.ds(start, columns)] = total


def grad_hidden_rows(grad, weights, back, part_order):
    near, far = weights
    plane, parts, rows, c = near.shape
    tokens, width = grad.shape
    step = min(c, 512)
    cuts = c // step
    weight_spec = pl.BlockSpec((plane, None, rows, step), lambda s: (0, s // cuts, 0, s % cuts))
    block = pl.BlockSpec((tokens, step), lambda s: (0, s))
    return pl.pallas_call(
        partial(grad_hidden_kernel, cuts),
        grid=(parts * cuts,),
        in_specs=[in_smem(), whole(grad), weight_spec, weight_spec, block],
        out_specs=[block, pl.BlockSpec((parts, c), lambda s: (0, 0))],
        out_shape=[shape_of((tokens, parts * c), BF16), shape_of((parts, c), F32)],
        compiler_params=params(48),
        cost_estimate=cost(2 * tokens * width * parts * c, 34 * MIB),
        name="grad_hidden",
    )(part_order, grad, near, far, back)


def first_back_kernel(
    order_ref, g_ref, near_ref, far_ref, normed_ref, normal_ref, inverse_ref, sum_two_ref, level_ref, row_ref,
    sum_ref, low_ref, terms_ref
):
    level = level_ref[0:1, 0:1]
    tangent = jnp.tanh(normed_ref[...] / level)
    grad = project(g_ref[...], near_ref, far_ref) * (1.0 - tangent * tangent) + sum_two_ref[...]
    normal = normal_ref[...]
    gain = take_blocks(row_ref, order_ref)[1:2, :]
    grad_sum = norm_back(grad, normal, inverse_ref[...], gain)
    sum_ref[...] = grad_sum
    low_ref[...] = low(grad_sum)
    add_sums(terms_ref, order_ref, (grad_sum, grad * normal, grad))


def first_back(grad, weights, normed, normal, inverse, sum_two, level, vectors, order):
    near, far = weights
    tokens, width = normed.shape
    inner = grad.shape[1]
    rows = 256

    def block(columns):
        return pl.BlockSpec((rows, columns), lambda t: (t, 0))

    return pl.pallas_call(
        first_back_kernel,
        grid=(tokens // rows,),
        in_specs=[
            in_smem(),
            block(inner),
            whole(near),
            whole(far),
            block(width),
            block(width),
            block(1),
            block(width),
            whole(level),
            whole(vectors),
        ],
        out_specs=[block(width), block(width), pl.BlockSpec((8, width), lambda t: (0, 0))],
        out_shape=[
            shape_of((tokens, width), F32),
            shape_of((tokens, width), BF16),
            shape_of((8, width), F32),
        ],
        compiler_params=params(56),
        cost_estimate=cost(2 * tokens * width * inner, 36 * MIB),
        name="first_back",
    )(order, grad, near, far, normed, normal, inverse, sum_two, level, vectors)


def grad_context_kernel(g_ref, near_ref, far_ref, ctx_ref, level_ref, o_ref):
    half = g_ref.shape[1] // 2
    level = level_ref[0:1, 0:1]
    tangent = jnp.tanh(ctx_ref[...] / level)
    grad = dot(g_ref[:, :half], flat(near_ref[...])) + dot(g_ref[:, half:], flat(far_ref[...]))
    o_ref[...] = low(grad * (1.0 - tangent * tangent))


def grad_context_rows(grad, weights, context, level, first):
    near, far = weights
    plane, parts, rows, c = near.shape
    parts = parts // 2
    tokens, width = grad.shape
    weight_spec = pl.BlockSpec((plane, None, rows, c), lambda r: (0, r + first, 0, 0))
    block = pl.BlockSpec((tokens, c), lambda r: (0, r))
    return pl.pallas_call(
        grad_context_kernel,
        grid=(parts,),
        in_specs=[
            whole(grad),
            weight_spec,
            weight_spec,
            pl.BlockSpec((tokens, c), lambda r: (0, r + first)),
            whole(level),
        ],
        out_specs=block,
        out_shape=shape_of((tokens, parts * c), BF16),
        compiler_params=params(40),
        cost_estimate=cost(2 * tokens * width * parts * c, 10 * MIB),
        name="grad_context",
    )(grad, near, far, context, level)


def grad_input_kernel(order_ref, *refs):
    g_refs, (near_ref, far_ref, sum_ref, x_ref, level_ref, o_ref) = refs[:6], refs[6:]
    level = level_ref[0:1, 0:1]
    half = near_ref.shape[1] // 2
    total = None
    for side in range(2):
        for i in range(3):
            term = project(
                g_refs[side * 3 + i][...],
                near_ref.at[:, side * half : (side + 1) * half, i],
                far_ref.at[:, side * half : (side + 1) * half, i],
            )
            total = term if total is None else total + term
    tangent = jnp.tanh(take_blocks(x_ref, order_ref).astype(F32) / level)
    put_blocks(o_ref, order_ref, low(sum_ref[...] + total * (1.0 - tangent * tangent)))


def grad_input(grads, weights, grad_sum, x, level, order):
    near, far = weights
    tokens, width = x.shape
    inner = grads[0].shape[1]
    rows = 256

    def block(columns):
        return pl.BlockSpec((rows, columns), lambda t: (t, 0))

    return pl.pallas_call(
        grad_input_kernel,
        grid=(tokens // rows,),
        in_specs=[in_smem()]
        + [block(inner)] * 6
        + [whole(near), whole(far), block(width), block(width), whole(level)],
        out_specs=block(width),
        out_shape=shape_of((tokens, width), BF16),
        compiler_params=params(48),
        cost_estimate=cost(12 * tokens * width * inner, 20 * MIB),
        name="grad_input",
    )(order, *grads, near, far, grad_sum, x, level)


def place_kernel(turn, order_ref, near_ref, far_ref, o_ref):
    plane, kinds, rows, c = near_ref.shape
    for core, ref in enumerate((near_ref, far_ref)):
        for j in range(plane):
            here = pl.ds(pl.multiple_of(order_ref[core * plane + j] * rows, rows), rows)
            if turn:
                o_ref[:, here] = ref[j, 0].astype(F32).T
            else:
                for i in range(kinds):
                    o_ref[i, here, :] = ref[j, i].astype(F32)


def place_grad(sides, blocks, turn):
    near, far = sides
    plane, kinds, rows, c = near.shape
    width = 2 * plane * rows
    if turn and rows % LANES:
        split = jnp.concatenate([near, far], axis=0)[:, 0]
        back = jnp.zeros((2 * plane,), jnp.int32).at[blocks].set(jnp.arange(2 * plane, dtype=jnp.int32))
        return jnp.take(split, back, axis=0).astype(F32).reshape(width, c).T
    dims = (c, width) if turn else (kinds, width, c)
    return pl.pallas_call(
        partial(place_kernel, turn),
        grid=(1,),
        in_specs=[in_smem(), whole(near), whole(far)],
        out_specs=pl.BlockSpec(dims, lambda s: (0,) * len(dims)),
        out_shape=shape_of(dims, F32),
        compiler_params=params(32),
        name="place_grad",
    )(blocks.astype(jnp.int32), near, far)


HOST_RANK = {qkv_kernel: 2, attend_kernel: 2, hidden_kernel: 1}


def doc_segments(doc_lengths, length):
    doc_ends = jnp.cumsum(doc_lengths, axis=1, dtype=jnp.int32)
    places = jnp.arange(length, dtype=jnp.int32)
    return jnp.sum(
        (places[None, :, None] >= doc_ends[:, None, :]).astype(jnp.int32), axis=2, dtype=jnp.int32
    )


def soft_clip(values, clip_level):
    return clip_level * jnp.tanh(values / clip_level)


def clip_slope(values, clip_level):
    tangent = jnp.tanh(values / clip_level)
    return 1.0 - tangent * tangent


def own_block(values, axis):
    rows = values.shape[axis] // lax.axis_size("dp")
    return lax.dynamic_slice_in_dim(values, lax.axis_index("dp") * rows, rows, axis)


def local(
    mesh, layer_input, grad_output, doc_lengths, ranges, w_qkv, bias_qv, w_out, b_out, gain_one,
    shift_one, w_in, b_in, w_down, b_down, gain_two, shift_two
):
    datas, parts = lax.axis_size("dp"), lax.axis_size("tensor")
    data, part = lax.axis_index("dp"), lax.axis_index("tensor")
    plane = datas // 2
    tokens, width = layer_input.shape
    rows = width // datas

    places = jnp.arange(datas)
    distance = (places % plane) * 2 + places // plane
    blocks = data ^ distance
    if rows % LANES == 0:
        per_block = rows // LANES
        order = (blocks[:, None] * per_block + jnp.arange(per_block)).reshape(-1).astype(jnp.int32)
    else:
        order = jnp.arange(width // LANES, dtype=jnp.int32)

    def arrange(values):
        split = values.reshape(values.shape[:-1] + (datas, rows))
        return jnp.take(split, blocks, axis=-2).reshape(values.shape)

    def restore(values):
        split = values.reshape(values.shape[:-1] + (datas, rows))
        back = jnp.zeros((datas,), jnp.int32).at[blocks].set(places.astype(jnp.int32))
        return jnp.take(split, back, axis=-2).reshape(values.shape)

    def arrange_rows(values):
        return values if rows % LANES == 0 else arrange(values)

    def restore_rows(values):
        return values if rows % LANES == 0 else restore(values)

    part_order = (part ^ jnp.arange(parts)).astype(jnp.int32)
    x = arrange_rows(layer_input)
    upstream = arrange_rows(grad_output)
    vectors = jnp.stack([b_out, gain_one, shift_one, b_down, gain_two, shift_two, b_out, b_out])
    vectors = arrange_rows(vectors).astype(F32)

    own = [
        own_block(w_qkv, 1),
        own_block(w_out, 1).T[None],
        own_block(w_in, 0)[None],
        own_block(w_down, 1).T[None],
    ]
    own = [values.astype(F32) for values in own]
    peaks = [jnp.max(jnp.abs(own[0][i]), axis=0) for i in range(3)]
    peaks += [jnp.max(jnp.abs(values[0]), axis=0) for values in own[1:]]
    peaks += [jnp.max(jnp.abs(x.astype(F32)), axis=0)]
    peaks = [jnp.max(values.reshape(-1, LANES), axis=0) for values in peaks]
    peaks = jnp.stack(peaks + [jnp.zeros_like(peaks[0])])
    reached = exchange_all(peaks, mesh, "rows", ranges[:1])
    weight_levels = 0.5 * reached[:6, 0]
    level_input = DECAY * ranges[0] + (1.0 - DECAY) * reached[6:7, 0:1]
    level_input = jnp.broadcast_to(level_input, (8, LANES))
    own_levels = [weight_levels[:3][:, None, None]] + [weight_levels[i] for i in (3, 4, 5)]
    quant_own = [low(soft_clip(values, level)) for values, level in zip(own, own_levels)]
    slopes = [clip_slope(values, level) for values, level in zip(own, own_levels)]

    *weights_qkv, held_out, held_in = first_gather(*quant_own[:3])
    biases = jnp.concatenate([bias_qv.reshape(-1), b_in]).astype(BF16)[None]
    for bit in reversed(range(bits_of("tensor"))):
        other = swap(biases, "tensor", bit)
        biases = jnp.stack([biases, other], axis=1).reshape(-1, biases.shape[1])
    columns = bias_qv.shape[1]
    bias_q = biases[:, :columns].reshape(1, -1)
    bias_v = biases[:, columns : 2 * columns].reshape(1, -1)
    bias_qkv = jnp.stack([bias_q, jnp.zeros_like(bias_q), bias_v]).astype(F32)
    bias_hidden = biases[:, 2 * columns :].reshape(1, -1).astype(F32)

    held = tokens // SEQ
    lengths_here = lax.dynamic_slice_in_dim(doc_lengths, part * held, held, 0)
    segments = doc_segments(lengths_here, SEQ).astype(F32)
    seg_cols, seg_rows = segments[:, :, None], segments[:, None, :]
    half = parts // 2 * columns

    quant_input = quant_rows(x, level_input, order)
    (qkv,), weights_out = qkv_rows(quant_input, weights_qkv, bias_qkv, held_out)
    (context, lse, peak), (*weights_in, held_down) = attend(
        qkv, seg_cols, seg_rows, held_in, quant_own[3]
    )
    level_context = exchange_all(peak, mesh, "level", ranges[1:2])
    weights_out = tuple(side[:, :, 0] for side in weights_out)
    weights_in = tuple(side[:, :, 0] for side in weights_in)
    quant_context, normed, normal_one, inverse_one, peak = first_norm(
        context, level_context, weights_out, x, vectors, order
    )
    level_normed = exchange_all(peak, mesh, "level", ranges[2:3])
    (quant_normed, active, slope, peak), weights_down = hidden_rows(
        normed, level_normed, weights_in, bias_hidden, held_down
    )
    level_active = exchange_all(peak, mesh, "level", ranges[3:4])
    weights_down = tuple(side[:, :, 0] for side in weights_down)
    quant_active, back, output, grad_sum_two, grad_branch, terms_two = second_norm(
        active, slope, level_active, weights_down, normed, upstream, vectors, order
    )

    down = scatter_all(*weight_grad(grad_branch, [quant_active], parts, plane))
    grad_branch = tie(grad_branch, next(down))
    grad_hidden, sum_hidden = grad_hidden_rows(grad_branch, weights_down, back, part_order)
    grad_hidden = tie(grad_hidden, down.send(sum_hidden))
    inner = scatter_plane(*weight_grad(quant_normed, [grad_hidden], parts, plane))
    grad_hidden = tie(grad_hidden, next(inner))
    grad_sum_one, grad_attention, terms_one = first_back(
        grad_hidden, weights_in, normed, normal_one, inverse_one, grad_sum_two, level_normed, vectors, order
    )
    grad_attention = tie(grad_attention, inner.send(terms_one) + down.send(terms_one))
    outer = scatter_plane(*weight_grad(grad_attention, [quant_context], parts, plane))
    grad_attention = tie(grad_attention, next(outer))
    grad_a = grad_context_rows(grad_attention, weights_out, context, level_context, 0)
    grad_b = grad_context_rows(grad_attention, weights_out, context, level_context, parts // 2)
    sums_before = jnp.zeros((8, 2 * half), F32)
    *grads_a, token = attend_back(qkv, grad_a, seg_cols, seg_rows, lse, sums_before, part_order, columns, 0)
    grads_a[0] = tie(grads_a[0], down.send(token) + outer.send(token))
    first = scatter_plane(*weight_grad(quant_input, grads_a, parts // 2, plane))
    grad_b = tie(grad_b, next(first))
    *grads_b, token = attend_back(qkv, grad_b, seg_cols, seg_rows, lse, token, part_order, columns, half)
    sum_qv = token
    grads_b[0] = tie(
        grads_b[0], inner.send(token) + down.send(token) + outer.send(token) + first.send(token)
    )
    raw = weight_grad(quant_input, grads_b, parts // 2, plane)
    grads_b[0] = tie(grads_b[0], first.send(raw[1]))
    grad_x = grad_input(grads_a + grads_b, weights_qkv, grad_sum_one, x, level_input, order)

    sums = [terms_one[:3], terms_two[:3], sum_qv[:2], sum_hidden.reshape(-1, width)]
    if rows % LANES:
        sums[0], sums[1] = restore(sums[0]), restore(sums[1])
    sums = jnp.concatenate(sums)
    padded = jnp.pad(sums, ((0, -sums.shape[0] % 8), (0, 0)))
    down, inner, outer, first = [run_all(chain, grad_x) for chain in (down, inner, outer, first)]
    (down, inner, outer, first), sums = finale(
        low(down * slopes[3]), inner, outer, first, raw, [slopes[0], slopes[2], slopes[1]], padded
    )
    hidden_all = sums[8 : 8 + sum_hidden.size // width].reshape(-1)
    grad_bias_qv = lax.dynamic_slice_in_dim(sums[6:8], part * columns, columns, 1)
    grad_b_in = lax.dynamic_slice_in_dim(hidden_all, part * b_in.shape[0], b_in.shape[0], 0)
    grad_w_down = place_grad(down, blocks, True)
    grad_w_out = place_grad(outer, blocks, True)
    grad_w_in = place_grad(inner, blocks, False)[0]
    grad_w_qkv = place_grad(first, blocks, False)
    new_ranges = jnp.stack(
        [level_input[0, 0], level_context[0, 0], level_normed[0, 0], level_active[0, 0]]
    )
    return (
        restore_rows(output),
        restore_rows(grad_x),
        grad_w_qkv,
        grad_bias_qv,
        grad_w_out,
        sums[0],
        sums[1],
        sums[2],
        grad_w_in,
        grad_b_in,
        grad_w_down,
        sums[3],
        sums[4],
        sums[5],
        new_ranges,
    )


def solution(mesh):
    in_specs = (
        P(("dp", "tensor"), None),
        P(("dp", "tensor"), None),
        P("dp", None),
        P(),
        P(None, None, "tensor"),
        P(None, "tensor"),
        P("tensor", None),
        P(),
        P(),
        P(),
        P(None, "tensor"),
        P("tensor"),
        P("tensor", None),
        P(),
        P(),
        P(),
    )
    out_specs = (
        P(("dp", "tensor"), None),
        P(("dp", "tensor"), None),
        P(None, None, "tensor"),
        P(None, "tensor"),
        P("tensor", None),
        P(),
        P(),
        P(),
        P(None, "tensor"),
        P("tensor"),
        P("tensor", None),
        P(),
        P(),
        P(),
        P(),
    )
    return jax.shard_map(
        partial(local, mesh), mesh=mesh, in_specs=in_specs, out_specs=out_specs, check_vma=False
    )
```

```python
from functools import partial

import jax
import jax.numpy as jnp
from jax import lax
from jax.experimental import pallas as pl
from jax.experimental.pallas import tpu as pltpu
from jax.sharding import PartitionSpec as P

HD = 64
SEQ = 512
LANES = 128

EPS = 1e-06
DECAY = 0.9
MASKED = -1e30
MESH = pl.DeviceIdType.MESH
F32 = jnp.float32
BF16 = jnp.bfloat16
MIB = 1024 * 1024


def shape_of(dims, kind):
    return jax.ShapeDtypeStruct(dims, kind)


def params(**rest):
    return pltpu.CompilerParams(vmem_limit_bytes=60 * MIB, **rest)


def in_smem():
    return pl.BlockSpec(memory_space=pltpu.SMEM)


def cost(flops, moved):
    return pl.CostEstimate(flops=int(flops), bytes_accessed=int(moved), transcendentals=0)


def dot(first, second):
    return jnp.dot(first, second, preferred_element_type=F32)


def dot_cols(first, second):
    return lax.dot_general(first, second, (((1,), (1,)), ((), ())), preferred_element_type=F32)


def dot_rows(first, second):
    return lax.dot_general(first, second, (((0,), (0,)), ((), ())), preferred_element_type=F32)


def flat(block):
    return block.reshape(block.shape[0] * block.shape[1], block.shape[2])


def exchange_kernel(
    kind, x_ref, range_ref, level_ref, o_ref, near, far, mid, near_send, near_recv, far_send, far_recv
):
    data, part = lax.axis_index("dp"), lax.axis_index("tensor")
    datas, parts = lax.axis_size("dp"), lax.axis_size("tensor")
    barrier = pltpu.get_barrier_semaphore()

    def to_data(step):
        return (lax.rem(data + step, datas), part)

    def to_part(step):
        return (data, lax.rem(part + step, parts))

    def greet(target):
        def run(step, carry):
            pl.semaphore_signal(barrier, inc=1, device_id=target(step), device_id_type=MESH)
            return carry

        return run

    lax.fori_loop(1, datas, greet(to_data), 0)
    lax.fori_loop(1, parts, greet(to_part), 0)
    pl.semaphore_wait(barrier, datas + parts - 2)

    def exchange(source, slots, send, recv, target, count):
        def copy(step):
            return pltpu.make_async_remote_copy(
                src_ref=source,
                dst_ref=slots.at[step],
                send_sem=send.at[step],
                recv_sem=recv.at[step],
                device_id=target(step),
                device_id_type=MESH,
            )

        def start(step, carry):
            copy(step).start()
            return carry

        def finish(step, carry):
            copy(step).wait()
            return carry

        lax.fori_loop(1, count, start, 0)
        slots[0] = source[...]
        lax.fori_loop(1, count, finish, 0)
        return jnp.max(slots[...], axis=0)

    mid[...] = exchange(x_ref, near, near_send, near_recv, to_data, datas)
    total = exchange(mid, far, far_send, far_recv, to_part, parts)
    if kind == "rows":
        total = jnp.broadcast_to(jnp.max(total, axis=1, keepdims=True), total.shape)
    if kind != "rows":
        peak = jnp.max(total, keepdims=True)
        level = DECAY * range_ref[kind] + (1.0 - DECAY) * peak
        places = lax.broadcasted_iota(jnp.int32, total.shape, 0)
        total = jnp.where(places == kind, level, level_ref[...])
    o_ref[...] = total


def exchange_all(values, mesh, kind, previous, levels):
    datas, parts = mesh.shape["dp"], mesh.shape["tensor"]
    dims = values.shape
    copies = pltpu.SemaphoreType.DMA
    vmem = pl.BlockSpec(memory_space=pltpu.VMEM)
    return pl.pallas_call(
        partial(exchange_kernel, kind),
        out_shape=shape_of(dims, F32),
        in_specs=[vmem, in_smem(), vmem],
        out_specs=vmem,
        scratch_shapes=[
            pltpu.VMEM((datas,) + dims, F32),
            pltpu.VMEM((parts,) + dims, F32),
            pltpu.VMEM(dims, F32),
            copies((datas,)),
            copies((datas,)),
            copies((parts,)),
            copies((parts,)),
        ],
        compiler_params=params(
            collective_id={"rows": 0, 1: 1, 2: 7, 3: 8}[kind], has_side_effects=True
        ),
        name="exchange",
    )(values, previous, levels)


def tie(values, others):
    return lax.optimization_barrier((values, *others))[0]


def swap(values, axis, bit, token=None):
    count = lax.axis_size(axis)
    other = lax.ppermute(values, axis, [(i, i ^ (1 << bit)) for i in range(count)])
    return other if token is None else tie(other, [token])


def far_swap(values, r):
    count = lax.axis_size("dp")
    return lax.ppermute(values, "dp", [(i, i ^ r) for i in range(count)])


def bits_of(axis):
    return lax.axis_size(axis).bit_length() - 1


def plane_orders():
    plane = list(range(1, bits_of("dp")))
    return plane, (plane[::-1], plane)


def run_all(chain, token=None):
    try:
        chain.send(token)
        while True:
            next(chain)
    except StopIteration as done:
        return done.value


def low(values):
    return values.astype(BF16)


def first_split(plane_bits):
    _, orders = plane_orders()
    split = []
    for order in orders:
        bit = order[0] - 1
        split.append([[s for s in range(1 << plane_bits) if (s >> bit) & 1 == away] for away in (0, 1)])
    return split


def scatter_plane(keeps, sends, but_last=False):
    plane, orders = plane_orders()
    left = [[bit for bit in plane[::-1] if bit != order[0]] for order in orders]
    sides = [keep.reshape((2,) * len(left[0]) + keep.shape[1:]) for keep in keeps]
    token = yield list(sends)
    for i in range(2):
        other = swap(sends[i], "dp", orders[i][0], token)
        sides[i] = sides[i] + other.reshape(sides[i].shape).astype(F32)
    for step in range(1, len(plane)):
        places = [left[i].index(orders[i][step]) for i in range(2)]
        sends = [low(lax.index_in_dim(sides[i], 1, places[i], keepdims=False)) for i in range(2)]
        if but_last and step == len(plane) - 1:
            return [(lax.index_in_dim(sides[i], 0, places[i], keepdims=False), sends[i]) for i in range(2)]
        token = yield sends
        for i in range(2):
            bit = orders[i][step]
            keep = lax.index_in_dim(sides[i], 0, places[i], keepdims=False)
            sides[i] = keep + swap(sends[i], "dp", bit, token).astype(F32)
            left[i].remove(bit)
    return sides


def scatter_part(keeps, sends):
    sides = yield from scatter_plane(keeps, sends)
    for bit in range(bits_of("tensor") - 1):
        pairs = [values.reshape((-1, 2) + values.shape[1:]) for values in sides]
        sends = [low(values[:, 1]) for values in pairs]
        token = yield sends
        sides = [
            values[:, 0] + swap(send, "tensor", bit, token).astype(F32)
            for values, send in zip(pairs, sends)
        ]
    return [side[0] for side in sides]


def scatter_all(keeps, sends):
    sides = yield from scatter_part(keeps, sends)
    send = low(sides[1])
    token = yield [send]
    return sides[0] + swap(send, "tensor", bits_of("tensor") - 1, token).astype(F32)


def at_distance(axis, r):
    me, index = lax.axis_index(axis), 0
    for bit in range(bits_of(axis)):
        index = index + (me // (1 << bit) + (r >> bit)) % 2 * (1 << bit)
    return index


def plane_moves():
    plane = 1 << (bits_of("dp") - 1)
    if plane == 4:
        return [(1, 2), (2, 4)], [(3, 1, 4, 0), (3, 2, 2, 1)]
    return [(slot, 2 * slot) for slot in range(1, plane)], []


class Mover:
    def __init__(self, send, recv, local):
        self.send, self.recv, self.local = send, recv, local
        self.count, self.local_count = 0, 0

    def remote(self, source, target, axis, r):
        i = self.count
        self.count += 1
        return pltpu.make_async_remote_copy(
            src_ref=source,
            dst_ref=target,
            send_sem=self.send.at[i],
            recv_sem=self.recv.at[i],
            device_id={axis: at_distance(axis, r)},
            device_id_type=MESH,
        )

    def own(self, source, target):
        i = self.local_count
        self.local_count += 1
        return pltpu.make_async_copy(source, target, self.local.at[i])


def greet(distances):
    barrier = pltpu.get_barrier_semaphore()
    for axis, r in distances:
        pl.semaphore_signal(
            barrier, inc=1, device_id={axis: at_distance(axis, r)}, device_id_type=MESH
        )
    pl.semaphore_wait(barrier, len(distances))


def part_distances():
    return [("tensor", r) for r in range(1, 1 << bits_of("tensor"))]


def plane_distances():
    first, second = plane_moves()
    apart = sorted({move[1] for move in first} | {move[2] for move in second} | {1})
    return [("dp", r) for r in apart]


def halves_of(ref, half):
    rows = ref.shape[-2] // 2
    return ref.at[..., half * rows : (half + 1) * rows, :]


def slots(ref, *inner):
    return lambda slot: ref.at[(slot,) + inner]


def low_bit(r):
    return r & -r


class AlongParts:
    def __init__(self, mover, own, place):
        parts = 1 << bits_of("tensor")
        self.copy = mover.own(own, place(0))
        self.moves, self.there = {}, {0}
        for r in range(1, parts):
            rest = r - low_bit(r)
            source = own if rest == 0 else place(rest)
            self.moves[r] = mover.remote(source, place(r), "tensor", low_bit(r))
        self.order = sorted(self.moves, key=lambda r: (bin(r).count("1"), -r))

    def start(self):
        self.copy.start()
        for r in self.order:
            if r == low_bit(r):
                self.moves[r].start()

    def arrive(self, r):
        if r not in self.there:
            self.moves[r].wait_recv()
            self.there.add(r)

    def hand_on(self):
        for r in self.order:
            if r != low_bit(r):
                self.arrive(r - low_bit(r))
                self.moves[r].start()

    def finish(self):
        self.copy.wait()
        for r, move in self.moves.items():
            self.arrive(r)
            move.wait_send()


class OverPlane:
    def __init__(self, mover, held, near, far, given=(), via=None):
        first, second = plane_moves()
        plane = 1 << (bits_of("dp") - 1)
        sources = [held] + (list(given) or [near(slot) for slot, _ in first])
        here = [held] + list(given)
        self.loads = [] if via is None else [mover.own(here[i], via.at[i]) for i in range(len(here))]
        self.copies = [
            mover.own(here[i] if via is None else via.at[i], near(i)) for i in range(len(here))
        ]
        self.first = [] if given else [mover.remote(held, near(slot), "dp", r) for slot, r in first]
        self.second = [
            mover.remote(halves_of(sources[source], half), halves_of(near(slot), half), "dp", r)
            for slot, source, r, half in second
        ]
        sources += [near(slot) for slot in range(len(sources), plane)]
        self.cores = [mover.remote(values, far(i), "dp", 1) for i, values in enumerate(sources)]
        self.early = 1 + len(first)

    def start(self):
        for copy in self.loads or self.copies:
            copy.start()
        for move in self.first:
            move.start()
        self.cores[0].start()

    def relay(self):
        for move in self.first:
            move.wait_recv()
        for move in self.second + self.cores[1 : self.early]:
            move.start()

    def settle(self):
        for load, copy in zip(self.loads, self.copies):
            load.wait()
            copy.start()

    def finish(self):
        for move in self.second:
            move.wait_recv()
        for move in self.cores[self.early :]:
            move.start()
        for move in self.first + self.second:
            move.wait_send()
        for move in self.cores:
            move.wait()
        for copy in self.copies:
            copy.wait()


def plane_counts(given):
    first, second = plane_moves()
    plane = 1 << (bits_of("dp") - 1)
    return len(second) + plane + (0 if given else len(first)), 2 + 2 * given


def copy_semaphores(remote, local):
    copies = pltpu.SemaphoreType.DMA
    return [copies((remote,)), copies((remote,)), copies((local,))]


def anywhere():
    return pl.BlockSpec(memory_space=pltpu.HBM)


def hosting(body, counts, given):
    ins, outs = counts
    sources = sum(1 + count for count in given)

    def kernel(*refs):
        body_ins, held = refs[:ins], list(refs[ins : ins + sources])
        rest = refs[ins + sources :]
        body_outs, sides = rest[:outs], rest[outs : outs + 2 * len(given)]
        body_scratch = rest[outs + 2 * len(given) : -3 - len(given)]
        vias, mover = rest[-3 - len(given) : -3], Mover(*rest[-3:])
        weights = []
        for i, count in enumerate(given):
            own, *there = [held.pop(0) for _ in range(1 + count)]
            near, far = slots(sides[2 * i]), slots(sides[2 * i + 1])
            weights.append((OverPlane(mover, own, near, far, there, vias[i]), count))
        step, steps = 0, 1
        for i in range(HOST_RANK[body]):
            step = step * pl.num_programs(i) + pl.program_id(i)
            steps = steps * pl.num_programs(i)

        @pl.when(step == 0)
        def _():
            greet(plane_distances())
            for weight, count in weights:
                weight.start()
                if count:
                    weight.relay()

        @pl.when(step == steps * 3 // 4)
        def _():
            for weight, count in weights:
                weight.settle()
                if not count:
                    weight.relay()

        body(*body_ins, *body_outs, *body_scratch)

        @pl.when(step == steps - 1)
        def _():
            for weight, _ in weights:
                weight.finish()

    return kernel


def hosted_call(body, weights, cid, *, grid, in_specs, out_specs, out_shape, scratch_shapes=(), **rest):
    plane = 1 << (bits_of("dp") - 1)
    counts = (len(in_specs), len(out_specs))
    given = [len(there) for _, there in weights]
    totals = [sum(column) for column in zip(*[plane_counts(count) for count in given])]
    out_shape, vias, sources = list(out_shape), [], []
    for held, there in weights:
        out_shape += [shape_of((plane,) + held.shape, held.dtype)] * 2
        vias.append(pltpu.VMEM((1 + len(there),) + held.shape, held.dtype))
        sources += [held] + list(there)
    call = pl.pallas_call(
        hosting(body, counts, given),
        grid=grid,
        in_specs=in_specs + [anywhere()] * len(sources),
        out_specs=out_specs + [anywhere()] * 2 * len(weights),
        out_shape=out_shape,
        scratch_shapes=list(scratch_shapes) + vias + copy_semaphores(*totals),
        compiler_params=params(collective_id=cid, has_side_effects=True),
        **rest,
    )

    def run(*args):
        results = call(*args, *sources)
        return results[: counts[1]], results[counts[1] :]

    return run


def first_gather_kernel(
    first_ref, bias_ref, out_ref, in_ref, near, far, held_bias, near_out, far_out, held_in, held_out, send, recv, own
):
    mover = Mover(send, recv, own)
    parts, plane = near.shape[1], near.shape[0]
    moves, relays = plane_moves()
    along = AlongParts(mover, first_ref, lambda r: near.at[0, r])
    sources = [first_ref] + [near.at[0, r] for r in range(1, parts)]
    over = [[mover.remote(sources[r], near.at[slot, r], "dp", d) for slot, d in moves] for r in range(parts)]
    again = [
        [
            mover.remote(halves_of(near.at[source, r], half), halves_of(near.at[slot, r], half), "dp", d)
            for slot, source, d, half in relays
        ]
        for r in range(parts)
    ]
    cores = [
        [mover.remote(sources[r] if slot == 0 else near.at[slot, r], far.at[slot, r], "dp", 1) for slot in range(plane)]
        for r in range(parts)
    ]
    later = [
        AlongParts(mover, source, lambda r, held=held: held.at[r])
        for source, held in ((bias_ref, held_bias), (out_ref, held_out), (in_ref, held_in))
    ]
    outer = OverPlane(mover, held_out, slots(near_out), slots(far_out))
    greet(part_distances() + plane_distances())
    along.start()
    for move in over[0] + cores[0][:1]:
        move.start()
    along.hand_on()
    for units in later[:2]:
        units.start()
    for r in along.order:
        along.arrive(r)
        for move in over[r] + cores[r][:1]:
            move.start()
    for units in later[:2]:
        units.hand_on()
    later[2].start()
    later[1].finish()
    outer.start()
    later[2].hand_on()
    order = [0] + along.order
    for r in order:
        for i, (slot, _) in enumerate(moves):
            over[r][i].wait_recv()
            cores[r][slot].start()
        for move in again[r]:
            move.start()
    outer.relay()
    for r in order:
        for move in again[r]:
            move.wait_recv()
        for slot in range(1 + len(moves), plane):
            cores[r][slot].start()
    along.finish()
    for r in range(parts):
        for move in over[r] + again[r]:
            move.wait_send()
        for move in cores[r]:
            move.wait()
    outer.finish()
    for units in (later[0], later[2]):
        units.finish()


def first_gather(first, biases, outer, inner):
    parts, plane = 1 << bits_of("tensor"), 1 << (bits_of("dp") - 1)
    moves, relays = plane_moves()
    remote = 4 * (parts - 1) + parts * (len(moves) + len(relays) + plane) + plane_counts(0)[0]
    return pl.pallas_call(
        first_gather_kernel,
        in_specs=[pl.BlockSpec(memory_space=pltpu.VMEM)] * 4,
        out_specs=[anywhere()] * 6,
        out_shape=[shape_of((plane, parts) + first.shape, BF16)] * 2
        + [shape_of((parts,) + biases.shape, BF16)]
        + [shape_of((plane, parts) + outer.shape, BF16)] * 2
        + [shape_of((parts,) + inner.shape, BF16)],
        scratch_shapes=[pltpu.VMEM((parts,) + outer.shape, BF16)] + copy_semaphores(remote, 5),
        compiler_params=params(collective_id=3, has_side_effects=True),
        name="first_gather",
    )(first, biases, outer, inner)


class PartSum:
    def __init__(self, mover, distances, send, recv, slope, piece, near, far):
        self.moves = [
            mover.remote(send.at[i], recv.at[i], "tensor", r) for i, r in enumerate(distances)
        ]
        self.over = OverPlane(mover, piece, slots(near), slots(far))
        self.send, self.recv, self.slope, self.piece = send, recv, slope, piece
        self.distances = list(distances)

    def push(self, r, values):
        i = self.distances.index(r)
        self.send[i] = low(values)
        self.moves[i].start()

    def reach(self, own):
        for move in self.moves:
            move.wait_recv()
        total = own + jnp.sum(self.recv[...].astype(F32), axis=0)
        self.piece[...] = low(total * self.slope[...])
        self.over.start()

    def relay(self):
        self.over.relay()

    def finish(self):
        self.over.finish()
        for move in self.moves:
            move.wait_send()


def finale_kernel(
    down_ref, in_a, in_b, out_a, out_b, keep_0, keep_1, keep_2, keep_3, send_0, send_1, send_2, send_3,
    slope_in, slope_out, slope_q, sums_ref, near_d, far_d, near_i, far_i, near_o, far_o, near_q, far_q, sums_out,
    send_i, recv_i, piece_i, send_o, recv_o, piece_o, send_q, recv_q, piece_q, recv_0, recv_1, recv_2, recv_3,
    sums_near, sums_mid, sums_far, send, recv, own
):
    mover = Mover(send, recv, own)
    _, orders = plane_orders()
    quarter = keep_0.shape[0]
    half, parts = 2 * quarter, 4 * quarter
    datas = sums_near.shape[0]
    keeps, sends = (keep_0, keep_1, keep_2, keep_3), (send_0, send_1, send_2, send_3)
    recvs = (recv_0, recv_1, recv_2, recv_3)
    steps = [mover.remote(sends[i], recvs[i], "dp", 1 << orders[i % 2][-1]) for i in range(4)]
    down = OverPlane(mover, down_ref, slots(near_d), slots(far_d))
    inner = PartSum(mover, [half], send_i, recv_i, slope_in, piece_i, near_i, far_i)
    outer = PartSum(mover, range(1, parts), send_o, recv_o, slope_out, piece_o, near_o, far_o)
    first = PartSum(mover, range(1, parts), send_q, recv_q, slope_q, piece_q, near_q, far_q)
    sum_data = [mover.remote(sums_ref, sums_near.at[r], "dp", r) for r in range(1, datas)]
    sum_part = [mover.remote(sums_mid, sums_far.at[r], axis, r) for axis, r in part_distances()]

    def block(r):
        return keeps[r // quarter][r % quarter] + recvs[r // quarter][r % quarter].astype(F32)

    greet([("dp", r) for r in range(1, datas)] + part_distances())
    for step in steps:
        step.start()
    inner.push(half, in_b[...])
    for r in range(1, parts):
        outer.push(r, (out_a if r < half else out_b)[r % half])
    for i in (3, 2, 1, 0):
        steps[i].wait_recv()
        for r in range(i * quarter, (i + 1) * quarter):
            if r:
                first.push(r, block(r))
    down.start()
    for move in sum_data:
        move.start()
    inner.reach(in_a[...])
    outer.reach(out_a[0])
    for move in sum_data:
        move.wait()
    sums_near[0] = sums_ref[...]
    sums_mid[...] = jnp.sum(sums_near[...], axis=0)
    for move in sum_part:
        move.start()
    down.relay()
    inner.relay()
    outer.relay()
    first.reach(block(0))
    for move in sum_part:
        move.wait()
    sums_far[0] = sums_mid[...]
    sums_out[...] = jnp.sum(sums_far[...], axis=0)
    down.finish()
    inner.finish()
    outer.finish()
    first.relay()
    first.finish()
    for step in steps:
        step.wait_send()


def finale(down, inner, outer, first, slopes, sums):
    parts, plane, datas = 1 << bits_of("tensor"), 1 << (bits_of("dp") - 1), 1 << bits_of("dp")
    pieces = [down, slopes[1], slopes[2], slopes[0]]
    remote = 4 + 4 * plane_counts(0)[0] + 3 * (parts - 1) + 1 + datas - 1
    vmem = pl.BlockSpec(memory_space=pltpu.VMEM)
    scratch = []
    for piece, count in zip(pieces[1:], (1, parts - 1, parts - 1)):
        scratch += [pltpu.VMEM((count,) + piece.shape, BF16)] * 2 + [pltpu.VMEM(piece.shape, BF16)]
    scratch += [pltpu.VMEM(first[0][1].shape, BF16)] * 4
    scratch += [
        pltpu.VMEM((datas,) + sums.shape, F32),
        pltpu.VMEM(sums.shape, F32),
        pltpu.VMEM((parts,) + sums.shape, F32),
    ]
    out_shape = []
    for piece in pieces:
        out_shape += [shape_of((plane,) + piece.shape, BF16)] * 2
    keeps, sends = [side[0] for side in first], [side[1] for side in first]
    args = (down, *inner, *outer, *keeps, *sends, slopes[1], slopes[2], slopes[0], sums)
    results = pl.pallas_call(
        finale_kernel,
        in_specs=[vmem] * 9 + [anywhere()] * 4 + [vmem] * 4,
        out_specs=[anywhere()] * 8 + [vmem],
        out_shape=out_shape + [shape_of(sums.shape, F32)],
        scratch_shapes=scratch + copy_semaphores(remote, 4),
        compiler_params=params(collective_id=2, has_side_effects=True),
        name="finale",
    )(*args)
    return [results[2 * i : 2 * i + 2] for i in range(4)], results[8]


def take_blocks(ref, order_ref, here=slice(None)):
    return jnp.concatenate(
        [
            ref[here, pl.ds(pl.multiple_of(order_ref[j] * LANES, LANES), LANES)]
            for j in range(ref.shape[1] // LANES)
        ],
        axis=1,
    )


def put_blocks(ref, order_ref, values):
    for j in range(ref.shape[1] // LANES):
        ref[:, pl.ds(pl.multiple_of(order_ref[j] * LANES, LANES), LANES)] = values[
            :, j * LANES : (j + 1) * LANES
        ]


def fold_peak(values):
    return jnp.max(jnp.abs(values).reshape(-1, 8, LANES), axis=0)


def column_peak(values):
    peak = fold_peak(values[:, :LANES])
    for j in range(1, values.shape[1] // LANES):
        peak = jnp.maximum(peak, fold_peak(values[:, j * LANES : (j + 1) * LANES]))
    return peak


def prepare_kernel(
    order_ref, range_ref, peak_ref, x_ref, qkv_ref, out_ref, in_ref, down_ref, level_ref, quant_ref,
    *refs
):
    level = DECAY * range_ref[0] + (1.0 - DECAY) * peak_ref[6:7, 0:1]
    level_ref[...] = jnp.broadcast_to(level, level_ref.shape)
    for i, ref in enumerate((qkv_ref, out_ref, in_ref, down_ref)):
        for j in range(ref.shape[0]):
            place = j if i == 0 else i + 2
            own = 0.5 * peak_ref[place : place + 1, 0:1]
            tangent = jnp.tanh(ref[j].astype(F32) / own)
            refs[2 * i][j] = low(own * tangent)
            refs[2 * i + 1][j] = 1.0 - tangent * tangent
    rows = 256

    @pl.loop(0, x_ref.shape[0] // rows)
    def _(step):
        here = pl.ds(pl.multiple_of(step * rows, rows), rows)
        x = take_blocks(x_ref, order_ref, here).astype(F32)
        quant_ref[here, :] = low(level * jnp.tanh(x / level))


def prepare(peaks, previous, x, own, order):
    vmem = pl.BlockSpec(memory_space=pltpu.VMEM)
    out_shape = [shape_of((8, LANES), F32), shape_of(x.shape, BF16)]
    for values in own:
        out_shape += [shape_of(values.shape, BF16), shape_of(values.shape, F32)]
    levels, quant, *rest = pl.pallas_call(
        prepare_kernel,
        in_specs=[in_smem(), in_smem()] + [vmem] * 6,
        out_specs=[vmem] * 10,
        out_shape=out_shape,
        compiler_params=params(),
        name="prepare",
    )(order, previous, peaks, x, *own)
    return levels, quant, rest[::2], rest[1::2]


def qkv_kernel(x_ref, near_ref, far_ref, b_ref, o_ref):
    half = x_ref.shape[1] // 2
    total = dot(x_ref[:, :half], flat(near_ref[...])) + dot(x_ref[:, half:], flat(far_ref[...]))
    o_ref[...] = low(total + b_ref[...])


def qkv_rows(x, weights, bias):
    near, far = weights
    plane, parts, kinds, rows, c = near.shape
    tokens, width = x.shape
    weight_spec = pl.BlockSpec((plane, None, None, rows, c), lambda r, i: (0, r, i, 0, 0))
    return pl.pallas_call(
        qkv_kernel,
        grid=(parts, kinds),
        in_specs=[
            pl.BlockSpec((tokens, width), lambda r, i: (0, 0)),
            weight_spec,
            weight_spec,
            pl.BlockSpec((None, 1, c), lambda r, i: (i, 0, r)),
        ],
        out_specs=pl.BlockSpec((None, tokens, c), lambda r, i: (i, 0, r)),
        out_shape=shape_of((kinds, tokens, parts * c), BF16),
        compiler_params=params(),
        cost_estimate=cost(2 * tokens * width * kinds * parts * c, 14 * MIB),
        name="qkv",
    )(x, near, far, bias)


def fill_mask(mask_ref, col_ref, row_ref):
    mask_ref[...] = jnp.where(col_ref[...] == row_ref[...], 0.0, MASKED).astype(F32)


def attend_kernel(
    skip, q_ref, k_ref, v_ref, col_ref, row_ref, lse_before, peak_before, *refs
):
    o_ref, lse_ref, peak_ref, mask_ref, sums_ref = refs[-5:]
    row, pair = pl.program_id(0), pl.program_id(1)
    factor = HD ** (-0.5)

    @pl.when(pair == 0)
    def _():
        fill_mask(mask_ref, col_ref, row_ref)
        sums_ref[...] = lse_before[...].T

    @pl.when((pair == 0) & (row == 0))
    def _():
        peak_ref[...] = peak_before[...]

    rows = 256
    lanes = lax.broadcasted_iota(jnp.int32, (rows, LANES), 1)
    for start in range(0, SEQ, rows):
        here = pl.ds(start, rows)
        q = q_ref[here, :] * jnp.asarray(factor, BF16)
        parts = []
        sums = sums_ref[here, :]
        for head in range(LANES // HD):
            own = lanes // HD == head
            scores = dot_cols(jnp.where(own, q, jnp.zeros_like(q)), k_ref[...]) + mask_ref[here, :]
            row_max = jnp.max(scores, axis=-1, keepdims=True)
            exponent = jnp.exp(scores - row_max)
            totals = jnp.sum(exponent, axis=-1, keepdims=True)
            probs = low(exponent * (1.0 / totals))
            parts.append(dot(probs, v_ref[...]))
            sums = jnp.where(lanes == (pair + skip) * (LANES // HD) + head, row_max + jnp.log(totals), sums)
        context = parts[0]
        for head in range(1, LANES // HD):
            context = jnp.where(lanes // HD == head, parts[head], context)
        o_ref[here, :] = context
        sums_ref[here, :] = sums
        peak_ref[...] = jnp.maximum(peak_ref[...], fold_peak(context))

    @pl.when(pair == pl.num_programs(1) - 1)
    def _():
        lse_ref[...] = sums_ref[...].T


def attend_first_kernel(*refs):
    attend_kernel(0, *refs)


def attend_last_kernel(*refs):
    attend_kernel(pl.num_programs(1), *refs)


def attend(qkv, cols, rows, lse, peak, context=None, weights=()):
    _, tokens, width = qkv.shape
    held = tokens // SEQ
    last = context is not None
    skip = width // LANES // 2 if last else 0

    def side(i):
        return pl.BlockSpec((None, SEQ, LANES), lambda r, j: (i, r, j + skip))

    sums = pl.BlockSpec((None, LANES, SEQ), lambda r, j: (r, 0, 0))
    small = pl.BlockSpec((8, LANES), lambda r, j: (0, 0))
    setup = dict(
        grid=(held, width // LANES // 2),
        in_specs=[
            side(0),
            side(1),
            side(2),
            pl.BlockSpec((None, SEQ, 1), lambda r, j: (r, 0, 0)),
            pl.BlockSpec((None, 1, SEQ), lambda r, j: (r, 0, 0)),
            sums,
            small,
        ],
        out_specs=[pl.BlockSpec((SEQ, LANES), lambda r, j: (r, j + skip)), sums, small],
        out_shape=[
            shape_of((tokens, width), F32),
            shape_of((held, LANES, SEQ), F32),
            shape_of((8, LANES), F32),
        ],
        scratch_shapes=[pltpu.VMEM((SEQ, SEQ), F32), pltpu.VMEM((SEQ, LANES), F32)],
        cost_estimate=cost(15e9, 40 * MIB),
        name="attend",
    )
    args = (qkv, qkv, qkv, cols, rows, lse, peak)
    if not last:
        return pl.pallas_call(attend_first_kernel, compiler_params=params(), **setup)(*args)
    setup["in_specs"].append(anywhere())
    run = hosted_call(
        attend_last_kernel, weights, 5, input_output_aliases={len(args): 0}, **setup
    )
    return run(*args, context)


def attend_back_kernel(
    c, first, order_ref, q_ref, k_ref, v_ref, g_ref, col_ref, row_ref, lse_ref, before_ref, dq_ref, dk_ref,
    dv_ref, sum_ref, mask_ref
):
    pair = pl.program_id(1)

    @pl.when((pair == 0) & (pl.program_id(0) == 0))
    def _():
        sum_ref[...] = before_ref[...]

    factor = HD ** (-0.5)

    @pl.when(pair == 0)
    def _():
        fill_mask(mask_ref, col_ref, row_ref)

    lanes = lax.broadcasted_iota(jnp.int32, (SEQ, LANES), 1)
    q, k, v, g = q_ref[...], k_ref[...], v_ref[...], g_ref[...]
    q_sums, k_sums, v_sums = [], [], []
    for head in range(LANES // HD):
        own = lanes // HD == head
        zero = jnp.zeros_like(q)
        q_own = jnp.where(own, q * jnp.asarray(factor, BF16), zero)
        g_own = jnp.where(own, g, zero)
        logsum = lse_ref[pl.ds((pair + first // LANES) * (LANES // HD) + head, 1), :]
        probs = jnp.exp(dot_cols(k, q_own) + mask_ref[...] - logsum)
        v_sums.append(dot(low(probs), g))
        grad_probs = dot_cols(v, g_own)
        mean_grad = jnp.sum(probs * grad_probs, axis=0, keepdims=True)
        grad_scores = low(factor * probs * (grad_probs - mean_grad))
        k_sums.append(dot(grad_scores, q))
        q_sums.append(dot_rows(grad_scores, k))

    def join(parts):
        joined = parts[0]
        for head in range(1, LANES // HD):
            joined = jnp.where(lanes // HD == head, parts[head], joined)
        return low(joined)

    dq, dv = join(q_sums), join(v_sums)
    dq_ref[...] = dq
    dk_ref[...] = join(k_sums)
    dv_ref[...] = dv
    column = first + pair * LANES
    place = order_ref[column // c] * c + column % c
    here = pl.ds(pl.multiple_of(place, LANES), LANES)
    sum_ref[0:1, here] += jnp.sum(dq.astype(F32), axis=0, keepdims=True)
    sum_ref[1:2, here] += jnp.sum(dv.astype(F32), axis=0, keepdims=True)


def attend_back(qkv, grad, cols, rows, lse, before, part_order, c, first):
    _, tokens, inner = qkv.shape
    width = grad.shape[1]
    held = tokens // SEQ
    skip = first // LANES

    def side(i):
        return pl.BlockSpec((None, SEQ, LANES), lambda r, j: (i, r, j + skip))

    block = pl.BlockSpec((SEQ, LANES), lambda r, j: (r, j))
    sums = pl.BlockSpec((8, inner), lambda r, j: (0, 0))
    return pl.pallas_call(
        partial(attend_back_kernel, c, first),
        grid=(held, width // LANES),
        in_specs=[
            in_smem(),
            side(0),
            side(1),
            side(2),
            block,
            pl.BlockSpec((None, SEQ, 1), lambda r, j: (r, 0, 0)),
            pl.BlockSpec((None, 1, SEQ), lambda r, j: (r, 0, 0)),
            pl.BlockSpec((None, LANES, SEQ), lambda r, j: (r, 0, 0)),
            sums,
        ],
        out_specs=[block, block, block, sums],
        out_shape=[shape_of((tokens, width), BF16)] * 3 + [shape_of((8, inner), F32)],
        scratch_shapes=[pltpu.VMEM((SEQ, SEQ), F32)],
        compiler_params=params(),
        cost_estimate=cost(15e9, 50 * MIB),
        name="attend_back",
    )(part_order, qkv, qkv, qkv, grad, cols, rows, lse, before)


def project(values, *sides):
    halves = []
    for refs in (sides[::2], sides[1::2]):
        total, place = None, 0
        for ref in refs:
            c = ref.shape[3]
            for r in range(ref.shape[1]):
                term = dot_cols(values[:, place : place + c], flat(ref[:, r]))
                total = term if total is None else total + term
                place += c
        halves.append(total)
    return jnp.concatenate(halves, axis=1)


def norm_parts(summed):
    center = summed - jnp.mean(summed, axis=-1, keepdims=True)
    inverse = lax.rsqrt(jnp.mean(center * center, axis=-1, keepdims=True) + EPS)
    return center * inverse, inverse


def norm_back(upstream, normal, inverse, gain):
    scaled = upstream * gain
    return inverse * (
        scaled
        - jnp.mean(scaled, axis=-1, keepdims=True)
        - normal * jnp.mean(scaled * normal, axis=-1, keepdims=True)
    )


def add_sums(ref, order_ref, sums):
    @pl.when(pl.program_id(0) == 0)
    def _():
        ref[...] = jnp.zeros_like(ref)

    for i, values in enumerate(sums):
        total = jnp.sum(values, axis=0, keepdims=True)
        for j in range(ref.shape[1] // LANES):
            here = pl.ds(pl.multiple_of(order_ref[j] * LANES, LANES), LANES)
            ref[i : i + 1, here] += total[:, j * LANES : (j + 1) * LANES]


def first_norm_kernel(
    order_ref, ctx_ref, level_ref, near_ref, far_ref, x_ref, row_ref, quant_ref, normed_ref, normal_ref,
    inverse_ref, peak_ref
):
    level = level_ref[1:2, 0:1]
    quant = low(level * jnp.tanh(ctx_ref[...] / level))
    quant_ref[...] = quant
    vectors = take_blocks(row_ref, order_ref)
    summed = take_blocks(x_ref, order_ref).astype(F32) + project(quant, near_ref, far_ref)
    normal, inverse = norm_parts(summed + vectors[0:1, :])
    normed = normal * vectors[1:2, :] + vectors[2:3, :]
    normed_ref[...] = normed
    normal_ref[...] = normal
    inverse_ref[...] = inverse

    @pl.when(pl.program_id(0) == 0)
    def _():
        peak_ref[...] = jnp.zeros_like(peak_ref)

    peak_ref[...] = jnp.maximum(peak_ref[...], column_peak(normed))


def whole(values):
    dims = values.shape
    return pl.BlockSpec(dims, lambda *steps: (0,) * len(dims))


def first_norm(context, level, weights, x, vectors, order):
    near, far = weights
    tokens, width = x.shape
    inner = context.shape[1]
    rows = 512

    def block(columns):
        return pl.BlockSpec((rows, columns), lambda t: (t, 0))

    return pl.pallas_call(
        first_norm_kernel,
        grid=(tokens // rows,),
        in_specs=[
            in_smem(),
            block(inner),
            whole(level),
            whole(near),
            whole(far),
            block(width),
            whole(vectors),
        ],
        out_specs=[
            block(inner),
            block(width),
            block(width),
            block(1),
            pl.BlockSpec((8, LANES), lambda t: (0, 0)),
        ],
        out_shape=[
            shape_of((tokens, inner), BF16),
            shape_of((tokens, width), F32),
            shape_of((tokens, width), F32),
            shape_of((tokens, 1), F32),
            shape_of((8, LANES), F32),
        ],
        compiler_params=params(),
        cost_estimate=cost(2 * tokens * width * inner, 20 * MIB),
        name="first_norm",
    )(order, context, level, near, far, x, vectors)


def hidden_kernel(normed_ref, level_ref, near_ref, far_ref, b_ref, quant_ref, act_ref, slope_ref, peak_ref):
    half = normed_ref.shape[1] // 2

    @pl.when(pl.program_id(0) == 0)
    def _():
        peak_ref[...] = jnp.zeros_like(peak_ref)
        level = level_ref[2:3, 0:1]
        quant_ref[...] = low(level * jnp.tanh(normed_ref[...] / level))

    hidden = dot(quant_ref[:, :half], flat(near_ref[...]))
    hidden = hidden + dot(quant_ref[:, half:], flat(far_ref[...])) + b_ref[...]
    share = 0.5 + 0.5 * lax.erf(hidden * (0.5**0.5))
    active = hidden * share
    act_ref[...] = active
    slope_ref[...] = share + hidden * ((0.5 / jnp.pi) ** 0.5 * jnp.exp(-0.5 * hidden * hidden))
    peak_ref[...] = jnp.maximum(peak_ref[...], column_peak(active))


def hidden_rows(normed, level, weights, bias, held_down):
    near, far = weights
    plane, parts, rows, c = near.shape
    tokens, width = normed.shape
    step = min(c, 512)
    cuts = c // step
    weight_spec = pl.BlockSpec((plane, None, rows, step), lambda s: (0, s // cuts, 0, s % cuts))
    block = pl.BlockSpec((tokens, step), lambda s: (0, s))
    run = hosted_call(
        hidden_kernel,
        [(held_down, ())],
        6,
        grid=(parts * cuts,),
        in_specs=[
            whole(normed),
            whole(level),
            weight_spec,
            weight_spec,
            pl.BlockSpec((1, step), lambda s: (0, s)),
        ],
        out_specs=[
            pl.BlockSpec((tokens, width), lambda s: (0, 0)),
            block,
            block,
            pl.BlockSpec((8, LANES), lambda s: (0, 0)),
        ],
        out_shape=[
            shape_of((tokens, width), BF16),
            shape_of((tokens, parts * c), F32),
            shape_of((tokens, parts * c), F32),
            shape_of((8, LANES), F32),
        ],
        cost_estimate=cost(2 * tokens * width * parts * c, 50 * MIB),
        name="hidden",
    )
    return run(normed, level, near, far, bias)


def second_norm_kernel(
    order_ref, act_ref, slope_ref, level_ref, near_a, far_a, near_b, far_b, normed_ref, grad_ref, row_ref,
    quant_ref, back_ref, out_ref, sum_ref, branch_ref, terms_ref
):
    level = level_ref[3:4, 0:1]
    tangent = jnp.tanh(act_ref[...] / level)
    quant = low(level * tangent)
    quant_ref[...] = quant
    back_ref[...] = (1.0 - tangent * tangent) * slope_ref[...]
    vectors = take_blocks(row_ref, order_ref)
    summed = normed_ref[...] + project(quant, near_a, far_a, near_b, far_b) + vectors[3:4, :]
    normal, inverse = norm_parts(summed)
    gain = vectors[4:5, :]
    put_blocks(out_ref, order_ref, low(normal * gain + vectors[5:6, :]))
    upstream = take_blocks(grad_ref, order_ref).astype(F32)
    grad_sum = norm_back(upstream, normal, inverse, gain)
    sum_ref[...] = grad_sum
    branch_ref[...] = low(grad_sum)
    add_sums(terms_ref, order_ref, (grad_sum, upstream * normal, upstream))


def second_norm(active, slope, level, weights, normed, grad, vectors, order):
    tokens, width = normed.shape
    inner = active.shape[1]
    rows = 256

    def block(columns):
        return pl.BlockSpec((rows, columns), lambda t: (t, 0))

    return pl.pallas_call(
        second_norm_kernel,
        grid=(tokens // rows,),
        in_specs=[
            in_smem(),
            block(inner),
            block(inner),
            whole(level),
            *[whole(side) for side in weights],
            block(width),
            block(width),
            whole(vectors),
        ],
        out_specs=[
            block(inner),
            block(inner),
            block(width),
            block(width),
            block(width),
            pl.BlockSpec((8, width), lambda t: (0, 0)),
        ],
        out_shape=[
            shape_of((tokens, inner), BF16),
            shape_of((tokens, inner), F32),
            shape_of((tokens, width), BF16),
            shape_of((tokens, width), F32),
            shape_of((tokens, width), BF16),
            shape_of((8, width), F32),
        ],
        compiler_params=params(),
        cost_estimate=cost(2 * tokens * width * inner, 80 * MIB),
        name="second_norm",
    )(order, active, slope, level, *weights, normed, grad, vectors)


def weight_grad_specs(x, grads, parts, plane):
    tokens, width = x.shape
    count = len(grads)
    c = grads[0].shape[1] // parts
    step = min(c, 1024)
    cuts = c // step
    dims = (plane, parts, count, width // (2 * plane), c)
    in_specs = [pl.BlockSpec((tokens, step), lambda r, j: (0, r * cuts + j))] * count
    out_spec = pl.BlockSpec((plane, None, count, dims[3], step), lambda r, j: (0, r, 0, 0, j))
    return dims, (parts, cuts), in_specs, out_spec, 2 * tokens * width * parts * c * count


def weight_send_kernel(count, x_ref, *refs):
    h_refs, (send_ref, turned_ref) = refs[:count], refs[count:]

    @pl.when((pl.program_id(0) == 0) & (pl.program_id(1) == 0))
    def _():
        turned_ref[...] = x_ref[...].T

    for i, h_ref in enumerate(h_refs):
        h = h_ref[...]
        send_ref[:, i] = low(dot(turned_ref[...], h)).reshape(send_ref.shape[0], -1, h.shape[1])


def weight_send(x, grads, parts, plane):
    dims, grid, in_specs, out_spec, flops = weight_grad_specs(x, grads, parts, plane)
    tokens, width = x.shape
    return pl.pallas_call(
        partial(weight_send_kernel, len(grads)),
        grid=grid,
        in_specs=[pl.BlockSpec((tokens, width // 2), lambda r, j: (0, 1))] + in_specs,
        out_specs=out_spec,
        out_shape=shape_of(dims, BF16),
        scratch_shapes=[pltpu.VMEM((width // 2, tokens), BF16)],
        compiler_params=params(),
        cost_estimate=cost(flops / 2, 16 * MIB),
        name="weight_send",
    )(x, *grads)


def weight_keep_kernel(count, split, x_ref, other_ref, *refs):
    h_refs, outs, turned_ref = refs[:count], refs[count:-1], refs[-1]
    half = pl.num_programs(0) // 2

    @pl.when((pl.program_id(0) == 0) & (pl.program_id(1) == 0))
    def _():
        turned_ref[...] = x_ref[...].T

    for side in range(2):

        @pl.when(pl.program_id(0) // half == side)
        def _(side=side):
            keep_ref, send_ref = outs[2 * side : 2 * side + 2]
            for i, h_ref in enumerate(h_refs):
                h = h_ref[...]
                total = dot(turned_ref[...], h).reshape(other_ref.shape[0], -1, h.shape[1])
                for j, slot in enumerate(split[side][0]):
                    keep_ref[j, i] = total[slot] + other_ref[slot, i].astype(F32)
                for j, slot in enumerate(split[side][1]):
                    send_ref[j, i] = low(total[slot] + other_ref[slot, i].astype(F32))


def weight_keep(x, grads, other, parts, plane):
    dims, (_, cuts), in_specs, out_spec, flops = weight_grad_specs(x, grads, parts, plane)
    tokens, width = x.shape
    half = parts // 2
    block = (plane // 2, None, len(grads), dims[3], dims[4] // cuts)
    near = pl.BlockSpec(
        block, lambda r, j: (0, jnp.minimum(r, half - 1), 0, 0, jnp.where(r < half, j, cuts - 1))
    )
    far = pl.BlockSpec(block, lambda r, j: (0, jnp.maximum(r - half, 0), 0, 0, jnp.where(r < half, 0, j)))
    small = (plane // 2, half) + dims[2:]
    keep_a, send_a, keep_b, send_b = pl.pallas_call(
        partial(weight_keep_kernel, len(grads), first_split(bits_of("dp") - 1)),
        grid=(parts, cuts),
        in_specs=[pl.BlockSpec((tokens, width // 2), lambda r, j: (0, 0)), out_spec] + in_specs,
        out_specs=[near, near, far, far],
        out_shape=[shape_of(small, F32), shape_of(small, BF16)] * 2,
        scratch_shapes=[pltpu.VMEM((width // 2, tokens), BF16)],
        compiler_params=params(),
        cost_estimate=cost(flops / 2, 24 * MIB),
        name="weight_keep",
    )(x, other, *grads)
    return [keep_a, keep_b], [send_a, send_b]


def grad_hidden_kernel(cuts, order_ref, g_ref, near_a, far_a, near_b, far_b, back_ref, o_ref, sum_ref):
    half = g_ref.shape[1] // 2
    block = pl.program_id(0)
    columns = back_ref.shape[1]

    @pl.when(block == 0)
    def _():
        sum_ref[...] = jnp.zeros_like(sum_ref)

    for side, (near_ref, far_ref) in enumerate(((near_a, far_a), (near_b, far_b))):

        @pl.when(block * 2 // pl.num_programs(0) == side)
        def _(near_ref=near_ref, far_ref=far_ref):
            grad = dot(g_ref[:, :half], flat(near_ref[...])) + dot(g_ref[:, half:], flat(far_ref[...]))
            grad = low(grad * back_ref[...])
            o_ref[...] = grad
            total = jnp.sum(grad.astype(F32), axis=0, keepdims=True)
            start = pl.multiple_of((block % cuts) * columns, LANES)
            sum_ref[pl.ds(order_ref[block // cuts], 1), pl.ds(start, columns)] = total


def grad_hidden_rows(grad, weights, back, part_order):
    plane, half, rows, c = weights[0].shape
    parts = 2 * half
    tokens, width = grad.shape
    step = min(c, 1024)
    cuts = c // step
    block = (plane, None, rows, step)
    first = pl.BlockSpec(
        block,
        lambda s: (0, jnp.minimum(s // cuts, half - 1), 0, jnp.where(s < half * cuts, s % cuts, cuts - 1)),
    )
    last = pl.BlockSpec(
        block,
        lambda s: (0, jnp.maximum(s // cuts - half, 0), 0, jnp.where(s < half * cuts, 0, s % cuts)),
    )
    block = pl.BlockSpec((tokens, step), lambda s: (0, s))
    return pl.pallas_call(
        partial(grad_hidden_kernel, cuts),
        grid=(parts * cuts,),
        in_specs=[in_smem(), whole(grad), first, first, last, last, block],
        out_specs=[block, pl.BlockSpec((parts, c), lambda s: (0, 0))],
        out_shape=[shape_of((tokens, parts * c), BF16), shape_of((parts, c), F32)],
        compiler_params=params(),
        cost_estimate=cost(2 * tokens * width * parts * c, 34 * MIB),
        name="grad_hidden",
    )(part_order, grad, *weights, back)


def first_back_kernel(
    order_ref, g_ref, near_ref, far_ref, normed_ref, normal_ref, inverse_ref, sum_two_ref, level_ref, row_ref,
    sum_ref, low_ref, terms_ref
):
    level = level_ref[2:3, 0:1]
    tangent = jnp.tanh(normed_ref[...] / level)
    grad = project(g_ref[...], near_ref, far_ref) * (1.0 - tangent * tangent) + sum_two_ref[...]
    normal = normal_ref[...]
    gain = take_blocks(row_ref, order_ref)[1:2, :]
    grad_sum = norm_back(grad, normal, inverse_ref[...], gain)
    sum_ref[...] = grad_sum
    low_ref[...] = low(grad_sum)
    add_sums(terms_ref, order_ref, (grad_sum, grad * normal, grad))


def first_back(grad, weights, normed, normal, inverse, sum_two, level, vectors, order):
    near, far = weights
    tokens, width = normed.shape
    inner = grad.shape[1]
    rows = 256

    def block(columns):
        return pl.BlockSpec((rows, columns), lambda t: (t, 0))

    return pl.pallas_call(
        first_back_kernel,
        grid=(tokens // rows,),
        in_specs=[
            in_smem(),
            block(inner),
            whole(near),
            whole(far),
            block(width),
            block(width),
            block(1),
            block(width),
            whole(level),
            whole(vectors),
        ],
        out_specs=[block(width), block(width), pl.BlockSpec((8, width), lambda t: (0, 0))],
        out_shape=[
            shape_of((tokens, width), F32),
            shape_of((tokens, width), BF16),
            shape_of((8, width), F32),
        ],
        compiler_params=params(),
        cost_estimate=cost(2 * tokens * width * inner, 36 * MIB),
        name="first_back",
    )(order, grad, near, far, normed, normal, inverse, sum_two, level, vectors)


def grad_context_kernel(g_ref, near_ref, far_ref, ctx_ref, level_ref, o_ref):
    half = g_ref.shape[1] // 2
    level = level_ref[1:2, 0:1]
    tangent = jnp.tanh(ctx_ref[...] / level)
    grad = dot(g_ref[:, :half], flat(near_ref[...])) + dot(g_ref[:, half:], flat(far_ref[...]))
    o_ref[...] = low(grad * (1.0 - tangent * tangent))


def grad_context_rows(grad, weights, context, level, first):
    near, far = weights
    plane, parts, rows, c = near.shape
    parts = parts // 2
    tokens, width = grad.shape
    weight_spec = pl.BlockSpec((plane, None, rows, c), lambda r: (0, r + first, 0, 0))
    block = pl.BlockSpec((tokens, c), lambda r: (0, r))
    return pl.pallas_call(
        grad_context_kernel,
        grid=(parts,),
        in_specs=[
            whole(grad),
            weight_spec,
            weight_spec,
            pl.BlockSpec((tokens, c), lambda r: (0, r + first)),
            whole(level),
        ],
        out_specs=block,
        out_shape=shape_of((tokens, parts * c), BF16),
        compiler_params=params(),
        cost_estimate=cost(2 * tokens * width * parts * c, 10 * MIB),
        name="grad_context",
    )(grad, near, far, context, level)


def grad_input_kernel(order_ref, *refs):
    g_refs, (near_ref, far_ref, sum_ref, x_ref, level_ref, o_ref) = refs[:6], refs[6:]
    level = level_ref[0:1, 0:1]
    half = near_ref.shape[1] // 2
    total = None
    for side in range(2):
        for i in range(3):
            term = project(
                g_refs[side * 3 + i][...],
                near_ref.at[:, side * half : (side + 1) * half, i],
                far_ref.at[:, side * half : (side + 1) * half, i],
            )
            total = term if total is None else total + term
    tangent = jnp.tanh(take_blocks(x_ref, order_ref).astype(F32) / level)
    put_blocks(o_ref, order_ref, low(sum_ref[...] + total * (1.0 - tangent * tangent)))


def grad_input(grads, weights, grad_sum, x, level, order):
    near, far = weights
    tokens, width = x.shape
    inner = grads[0].shape[1]
    rows = 256

    def block(columns):
        return pl.BlockSpec((rows, columns), lambda t: (t, 0))

    return pl.pallas_call(
        grad_input_kernel,
        grid=(tokens // rows,),
        in_specs=[in_smem()]
        + [block(inner)] * 6
        + [whole(near), whole(far), block(width), block(width), whole(level)],
        out_specs=block(width),
        out_shape=shape_of((tokens, width), BF16),
        compiler_params=params(),
        cost_estimate=cost(12 * tokens * width * inner, 20 * MIB),
        name="grad_input",
    )(order, *grads, near, far, grad_sum, x, level)


def place_kernel(turns, order_ref, *refs):
    ins, outs = refs[: 2 * len(turns)], refs[2 * len(turns) :]
    core = pl.program_id(0) * 2 // pl.num_programs(0)
    for side in range(2):

        @pl.when(core == side)
        def _(side=side):
            for i, turn in enumerate(turns):
                values = ins[2 * i + side]
                if turn:
                    outs[i][...] = values[0].astype(F32).T
                else:
                    outs[i][...] = values[...].astype(F32)


def place_grads(groups, turns, blocks):
    plane, _, rows, _ = groups[0][0].shape
    width = 2 * plane * rows
    results = [None] * len(groups)
    if rows % LANES:
        back = jnp.zeros((2 * plane,), jnp.int32).at[blocks].set(jnp.arange(2 * plane, dtype=jnp.int32))
        for i, (near, far) in enumerate(groups):
            if turns[i]:
                split = jnp.concatenate([near, far], axis=0)[:, 0]
                results[i] = jnp.take(split, back, axis=0).astype(F32).reshape(width, -1).T
    todo = [i for i in range(len(groups)) if results[i] is None]
    in_specs, out_specs, out_shape, args = [], [], [], []
    for i in todo:
        near, far = groups[i]
        _, kinds, _, c = near.shape
        block = (None, kinds, rows, c)
        in_specs.append(pl.BlockSpec(block, lambda p, order: (jnp.minimum(p, plane - 1), 0, 0, 0)))
        in_specs.append(pl.BlockSpec(block, lambda p, order: (jnp.maximum(p - plane, 0), 0, 0, 0)))
        args += [near, far]
        if turns[i]:
            out_specs.append(pl.BlockSpec((c, rows), lambda p, order: (0, order[p])))
            out_shape.append(shape_of((c, width), F32))
        else:
            out_specs.append(pl.BlockSpec((kinds, rows, c), lambda p, order: (0, order[p], 0)))
            out_shape.append(shape_of((kinds, width, c), F32))
    placed = pl.pallas_call(
        partial(place_kernel, [turns[i] for i in todo]),
        grid_spec=pltpu.PrefetchScalarGridSpec(
            num_scalar_prefetch=1, grid=(2 * plane,), in_specs=in_specs, out_specs=out_specs
        ),
        out_shape=out_shape,
        compiler_params=params(),
        name="place_grads",
    )(blocks.astype(jnp.int32), *args)
    for i, values in zip(todo, placed):
        results[i] = values
    return results


def but_last(keeps, sends):
    return scatter_plane(keeps, sends, True)


def scatter_plane_of(chain, x, grads, other, token, parts, plane):
    return chain(*weight_keep(tie(x, [token]), grads, other, parts, plane))


HOST_RANK = {attend_last_kernel: 2, hidden_kernel: 1}


def doc_segments(doc_lengths, length):
    doc_ends = jnp.cumsum(doc_lengths, axis=1, dtype=jnp.int32)
    places = jnp.arange(length, dtype=jnp.int32)
    return jnp.sum(
        (places[None, :, None] >= doc_ends[:, None, :]).astype(jnp.int32), axis=2, dtype=jnp.int32
    )


def soft_clip(values, clip_level):
    return clip_level * jnp.tanh(values / clip_level)


def clip_slope(values, clip_level):
    tangent = jnp.tanh(values / clip_level)
    return 1.0 - tangent * tangent


def own_block(values, axis):
    rows = values.shape[axis] // lax.axis_size("dp")
    return lax.dynamic_slice_in_dim(values, lax.axis_index("dp") * rows, rows, axis)


def local(
    mesh, layer_input, grad_output, doc_lengths, ranges, w_qkv, bias_qv, w_out, b_out, gain_one,
    shift_one, w_in, b_in, w_down, b_down, gain_two, shift_two
):
    datas, parts = lax.axis_size("dp"), lax.axis_size("tensor")
    data, part = lax.axis_index("dp"), lax.axis_index("tensor")
    plane = datas // 2
    tokens, width = layer_input.shape
    rows = width // datas

    places = jnp.arange(datas)
    distance = (places % plane) * 2 + places // plane
    blocks = data ^ distance
    if rows % LANES == 0:
        per_block = rows // LANES
        order = (blocks[:, None] * per_block + jnp.arange(per_block)).reshape(-1).astype(jnp.int32)
    else:
        order = jnp.arange(width // LANES, dtype=jnp.int32)

    def arrange(values):
        split = values.reshape(values.shape[:-1] + (datas, rows))
        return jnp.take(split, blocks, axis=-2).reshape(values.shape)

    def restore(values):
        split = values.reshape(values.shape[:-1] + (datas, rows))
        back = jnp.zeros((datas,), jnp.int32).at[blocks].set(places.astype(jnp.int32))
        return jnp.take(split, back, axis=-2).reshape(values.shape)

    def arrange_rows(values):
        return values if rows % LANES == 0 else arrange(values)

    def restore_rows(values):
        return values if rows % LANES == 0 else restore(values)

    part_order = (part ^ jnp.arange(parts)).astype(jnp.int32)
    x = arrange_rows(layer_input)
    upstream = arrange_rows(grad_output)
    vectors = jnp.stack([b_out, gain_one, shift_one, b_down, gain_two, shift_two, b_out, b_out])
    vectors = arrange_rows(vectors).astype(F32)

    own = [
        own_block(w_qkv, 1),
        own_block(w_out, 1).T[None],
        own_block(w_in, 0)[None],
        own_block(w_down, 1).T[None],
    ]
    peaks = [jnp.max(jnp.abs(own[0][i].astype(F32)), axis=0) for i in range(3)]
    peaks += [jnp.max(jnp.abs(values[0].astype(F32)), axis=0) for values in own[1:]]
    peaks += [jnp.max(jnp.abs(x.astype(F32)), axis=0)]
    peaks = [jnp.max(values.reshape(-1, LANES), axis=0) for values in peaks]
    peaks = jnp.stack(peaks + [jnp.zeros_like(peaks[0])])
    reached = exchange_all(peaks, mesh, "rows", ranges, peaks)
    levels, quant_input, quant_own, slopes = prepare(reached, ranges, x, own, order)
    biases = jnp.concatenate([bias_qv.reshape(-1), b_in])
    count = biases.shape[0]
    biases = jnp.pad(biases, (0, -count % (16 * LANES))).reshape(-1, LANES)
    near, far, biases, near_out, far_out, held_in = first_gather(quant_own[0], biases, *quant_own[1:3])
    weights_qkv, weights_out = (near, far), (near_out, far_out)
    biases = biases.reshape(parts, -1)[:, :count]
    columns = bias_qv.shape[1]
    bias_q = biases[:, :columns].reshape(1, -1)
    bias_v = biases[:, columns : 2 * columns].reshape(1, -1)
    bias_qkv = jnp.stack([bias_q, jnp.zeros_like(bias_q), bias_v]).astype(F32)
    bias_hidden = biases[:, 2 * columns :].reshape(1, -1).astype(F32)

    held = tokens // SEQ
    lengths_here = lax.dynamic_slice_in_dim(doc_lengths, part * held, held, 0)
    segments = doc_segments(lengths_here, SEQ).astype(F32)
    seg_cols, seg_rows = segments[:, :, None], segments[:, None, :]
    half = parts // 2 * columns

    first_moves, _ = plane_moves()

    def over_plane(values, token):
        values = tie(values, [token])
        return [far_swap(values, r) for _, r in first_moves]

    zero = jnp.zeros((8, LANES), F32)
    there_in = over_plane(held_in, biases)
    held_a = tie(quant_own[3], [biases])[None]
    for bit in reversed(range(bits_of("tensor") - 1)):
        other = swap(held_a, "tensor", bit)
        held_a = jnp.stack([held_a, other], axis=1).reshape((-1,) + held_a.shape[1:])
    qkv = qkv_rows(quant_input, weights_qkv, bias_qkv)
    held_a = tie(held_a, [qkv])
    there_a = over_plane(held_a, qkv)
    held_b = swap(held_a, "tensor", bits_of("tensor") - 1)
    context, lse, peak = attend(qkv, seg_cols, seg_rows, jnp.zeros((held, LANES, SEQ), F32), zero)
    there_in, there_a = [tie(values, [peak]) for values in there_in], [tie(values, [peak]) for values in there_a]
    (context, lse, peak), (*weights_in, near_a, far_a) = attend(
        qkv, seg_cols, seg_rows, lse, peak, context, [(held_in, there_in), (held_a, there_a)]
    )
    weights_in = tuple(side[:, :, 0] for side in weights_in)
    levels = exchange_all(peak, mesh, 1, ranges, levels)
    weights_out = tuple(side[:, :, 0] for side in weights_out)
    quant_context, normed, normal_one, inverse_one, peak = first_norm(
        context, levels, weights_out, x, vectors, order
    )
    levels = exchange_all(peak, mesh, 2, ranges, levels)
    held_b = tie(held_b, [levels])
    (quant_normed, active, slope, peak), (near_b, far_b) = hidden_rows(
        normed, levels, weights_in, bias_hidden, held_b
    )
    levels = exchange_all(peak, mesh, 3, ranges, levels)
    weights_down = [side[:, :, 0] for side in (near_a, far_a, near_b, far_b)]
    quant_active, back, output, grad_sum_two, grad_branch, terms_two = second_norm(
        active, slope, levels, weights_down, normed, upstream, vectors, order
    )

    other = weight_send(grad_branch, [quant_active], parts, plane)
    grad_branch = tie(grad_branch, [other])
    other = swap(other, "dp", 0)
    grad_hidden, sum_hidden = grad_hidden_rows(grad_branch, weights_down, back, part_order)
    down = scatter_plane_of(scatter_all, grad_branch, [quant_active], other, sum_hidden, parts, plane)
    grad_hidden = tie(grad_hidden, next(down))
    other = weight_send(quant_normed, [grad_hidden], parts, plane)
    grad_branch = tie(grad_hidden, [other])
    other = swap(other, "dp", 0)
    grad_sum_one, grad_attention, terms_one = first_back(
        grad_branch, weights_in, normed, normal_one, inverse_one, grad_sum_two, levels, vectors, order
    )
    grad_hidden = tie(grad_hidden, down.send(terms_one))
    inner = scatter_plane_of(scatter_part, quant_normed, [grad_hidden], other, terms_one, parts, plane)
    grad_attention = tie(grad_attention, next(inner))
    other = weight_send(grad_attention, [quant_context], parts, plane)
    grad_context = tie(grad_attention, [other])
    other = swap(other, "dp", 0)
    grad_a = grad_context_rows(grad_context, weights_out, context, levels, 0)
    grad_b = grad_context_rows(grad_context, weights_out, context, levels, parts // 2)
    sums_before = jnp.zeros((8, 2 * half), F32)
    *grads_a, token = attend_back(qkv, grad_a, seg_cols, seg_rows, lse, sums_before, part_order, columns, 0)
    grads_a[0] = tie(grads_a[0], down.send(token))
    outer = scatter_plane_of(scatter_plane, grad_attention, [quant_context], other, token, parts, plane)
    grads_a[0] = tie(grads_a[0], next(outer))
    other = weight_send(quant_input, grads_a, parts // 2, plane)
    grad_b = tie(grad_b, [other])
    other = swap(other, "dp", 0)
    *grads_b, token = attend_back(qkv, grad_b, seg_cols, seg_rows, lse, token, part_order, columns, half)
    sum_qv = token
    grads_b[0] = tie(grads_b[0], inner.send(token) + down.send(token) + outer.send(token))
    other_b = weight_send(quant_input, grads_b, parts // 2, plane)
    grads_a[0] = tie(grads_a[0], [other_b])
    other_b = swap(other_b, "dp", 0)
    first_a = scatter_plane_of(but_last, quant_input, grads_a, other, grads_a[0], parts // 2, plane)
    grads_b[0] = tie(grads_b[0], next(first_a))
    first_b = scatter_plane_of(but_last, quant_input, grads_b, other_b, grads_b[0], parts // 2, plane)
    started = next(first_b) + inner.send(grads_b[0])
    grads_b[0] = tie(grads_b[0], started)
    grad_x = grad_input(grads_a + grads_b, weights_qkv, grad_sum_one, x, levels, order)

    sums = [terms_one[:3], terms_two[:3], sum_qv[:2], sum_hidden.reshape(-1, width)]
    if rows % LANES:
        sums[0], sums[1] = restore(sums[0]), restore(sums[1])
    sums = jnp.concatenate(sums)
    padded = jnp.pad(sums, ((0, -sums.shape[0] % 8), (0, 0)))
    down, inner, outer, first_a, first_b = [
        run_all(chain, grad_x) for chain in (down, inner, outer, first_a, first_b)
    ]
    (down, inner, outer, first), sums = finale(
        low(down * slopes[3]), inner, outer, first_a + first_b, [slopes[0], slopes[2], slopes[1]], padded
    )
    hidden_all = sums[8 : 8 + sum_hidden.size // width].reshape(-1)
    grad_bias_qv = lax.dynamic_slice_in_dim(sums[6:8], part * columns, columns, 1)
    grad_b_in = lax.dynamic_slice_in_dim(hidden_all, part * b_in.shape[0], b_in.shape[0], 0)
    grad_w_down, grad_w_out, grad_w_in, grad_w_qkv = place_grads(
        [down, outer, inner, first], [True, True, False, False], blocks
    )
    grad_w_in = grad_w_in[0]
    new_ranges = levels[:4, 0]
    return (
        restore_rows(output),
        restore_rows(grad_x),
        grad_w_qkv,
        grad_bias_qv,
        grad_w_out,
        sums[0],
        sums[1],
        sums[2],
        grad_w_in,
        grad_b_in,
        grad_w_down,
        sums[3],
        sums[4],
        sums[5],
        new_ranges,
    )


def solution(mesh):
    in_specs = (
        P(("dp", "tensor"), None),
        P(("dp", "tensor"), None),
        P("dp", None),
        P(),
        P(None, None, "tensor"),
        P(None, "tensor"),
        P("tensor", None),
        P(),
        P(),
        P(),
        P(None, "tensor"),
        P("tensor"),
        P("tensor", None),
        P(),
        P(),
        P(),
    )
    out_specs = (
        P(("dp", "tensor"), None),
        P(("dp", "tensor"), None),
        P(None, None, "tensor"),
        P(None, "tensor"),
        P("tensor", None),
        P(),
        P(),
        P(),
        P(None, "tensor"),
        P("tensor"),
        P("tensor", None),
        P(),
        P(),
        P(),
        P(),
    )
    return jax.shard_map(
        partial(local, mesh), mesh=mesh, in_specs=in_specs, out_specs=out_specs, check_vma=False
    )
```

```python
from functools import partial

import jax
import jax.numpy as jnp
from jax import lax
from jax.experimental import pallas as pl
from jax.experimental.pallas import tpu as pltpu
from jax.sharding import PartitionSpec as P

HD = 64
SEQ = 512
LANES = 128

EPS = 1e-06
DECAY = 0.9
MASKED = -1e30
MESH = pl.DeviceIdType.MESH
F32 = jnp.float32
BF16 = jnp.bfloat16
MIB = 1024 * 1024


def shape_of(dims, kind):
    return jax.ShapeDtypeStruct(dims, kind)


def params(**rest):
    return pltpu.CompilerParams(vmem_limit_bytes=60 * MIB, **rest)


def in_smem():
    return pl.BlockSpec(memory_space=pltpu.SMEM)


def cost(flops, moved):
    return pl.CostEstimate(flops=int(flops) // 1000, bytes_accessed=int(moved) // 1000, transcendentals=0)


def dot(first, second):
    return jnp.dot(first, second, preferred_element_type=F32)


def dot_cols(first, second):
    return lax.dot_general(first, second, (((1,), (1,)), ((), ())), preferred_element_type=F32)


def dot_rows(first, second):
    return lax.dot_general(first, second, (((0,), (0,)), ((), ())), preferred_element_type=F32)


def flat(block):
    return block.reshape(block.shape[0] * block.shape[1], block.shape[2])


def tie(values, others):
    return lax.optimization_barrier((values, *others))[0]


def swap(values, axis, bit, token=None):
    count = lax.axis_size(axis)
    other = lax.ppermute(values, axis, [(i, i ^ (1 << bit)) for i in range(count)])
    return other if token is None else tie(other, [token])


def far_swap(values, r):
    count = lax.axis_size("dp")
    return lax.ppermute(values, "dp", [(i, i ^ r) for i in range(count)])


def bits_of(axis):
    return lax.axis_size(axis).bit_length() - 1


def plane_orders():
    plane = list(range(1, bits_of("dp")))
    return plane, (plane[::-1], plane)


def run_all(chain, token=None):
    try:
        chain.send(token)
        while True:
            next(chain)
    except StopIteration as done:
        return done.value


def low(values):
    return values.astype(BF16)


def first_split(plane_bits):
    _, orders = plane_orders()
    split = []
    for order in orders:
        bit = order[0] - 1
        split.append([[s for s in range(1 << plane_bits) if (s >> bit) & 1 == away] for away in (0, 1)])
    return split


def scatter_plane(keeps, sends, left_over=False):
    plane, orders = plane_orders()
    left = [[bit for bit in plane[::-1] if bit != order[0]] for order in orders]
    sides = [keep.reshape((2,) * len(left[0]) + keep.shape[1:]) for keep in keeps]
    sends = [send.reshape(side.shape) for side, send in zip(sides, sends)]
    for step in range(len(plane)):
        if step:
            places = [left[i].index(orders[i][step]) for i in range(2)]
            sends = [low(lax.index_in_dim(sides[i], 1, places[i], keepdims=False)) for i in range(2)]
            sides = [lax.index_in_dim(sides[i], 0, places[i], keepdims=False) for i in range(2)]
            for i in range(2):
                left[i].remove(orders[i][step])
        token = yield sends
        others = [swap(sends[i], "dp", orders[i][step], token) for i in range(2)]
        if left_over and step == len(plane) - 2:
            return list(zip(sides, others))
        sides = [side + other.astype(F32) for side, other in zip(sides, others)]
    return sides


def scatter_all(keeps, sends):
    sides = yield from scatter_plane(keeps, sends)
    last = bits_of("tensor") - 1
    for bit in range(last):
        pairs = [values.reshape((-1, 2) + values.shape[1:]) for values in sides]
        sends = [low(values[:, 1]) for values in pairs]
        token = yield sends
        others = [swap(send, "tensor", bit, token) for send in sends]
        sides = [values[:, 0] + other.astype(F32) for values, other in zip(pairs, others)]
    send = low(sides[1][0])
    token = yield [send]
    return sides[0][0], swap(send, "tensor", last, token)


def at_distance(axis, r):
    me, index = lax.axis_index(axis), 0
    for bit in range(bits_of(axis)):
        index = index + (me // (1 << bit) + (r >> bit)) % 2 * (1 << bit)
    return index


def plane_moves():
    plane = 1 << (bits_of("dp") - 1)
    if plane == 4:
        return [(1, 2), (2, 4)], [(3, 1, 4, 0), (3, 2, 2, 1)]
    return [(slot, 2 * slot) for slot in range(1, plane)], []


class Mover:
    def __init__(self, send, recv, local):
        self.send, self.recv, self.local = send, recv, local
        self.count, self.local_count = 0, 0

    def remote(self, source, target, axis, r):
        i = self.count
        self.count += 1
        return pltpu.make_async_remote_copy(
            src_ref=source,
            dst_ref=target,
            send_sem=self.send.at[i],
            recv_sem=self.recv.at[i],
            device_id={axis: at_distance(axis, r)},
            device_id_type=MESH,
        )

    def own(self, source, target):
        i = self.local_count
        self.local_count += 1
        return pltpu.make_async_copy(source, target, self.local.at[i])


def greet(distances):
    barrier = pltpu.get_barrier_semaphore()
    for axis, r in distances:
        pl.semaphore_signal(
            barrier, inc=1, device_id={axis: at_distance(axis, r)}, device_id_type=MESH
        )
    pl.semaphore_wait(barrier, len(distances))


def part_distances():
    return [("tensor", r) for r in range(1, 1 << bits_of("tensor"))]


def plane_distances():
    first, second = plane_moves()
    apart = sorted({move[1] for move in first} | {move[2] for move in second} | {1})
    return [("dp", r) for r in apart]


def halves_of(ref, half):
    rows = ref.shape[-2] // 2
    return ref.at[..., half * rows : (half + 1) * rows, :]


def slots(ref, *inner):
    return lambda slot: ref.at[(slot,) + inner]


def low_bit(r):
    return r & -r


class AlongParts:
    def __init__(self, mover, own, place):
        parts = 1 << bits_of("tensor")
        self.copy = mover.own(own, place(0))
        self.moves, self.there = {}, {0}
        for r in range(1, parts):
            rest = r - low_bit(r)
            source = own if rest == 0 else place(rest)
            self.moves[r] = mover.remote(source, place(r), "tensor", low_bit(r))
        self.order = sorted(self.moves, key=lambda r: (bin(r).count("1"), -r))

    def start(self):
        self.copy.start()
        for r in self.order:
            if r == low_bit(r):
                self.moves[r].start()

    def arrive(self, r):
        if r not in self.there:
            self.moves[r].wait_recv()
            self.there.add(r)

    def hand_on(self):
        for r in self.order:
            if r != low_bit(r):
                self.arrive(r - low_bit(r))
                self.moves[r].start()

    def finish(self):
        self.copy.wait()
        for r, move in self.moves.items():
            self.arrive(r)
            move.wait_send()


class OverPlane:
    def __init__(self, mover, held, near, far, given=(), via=None):
        first, second = plane_moves()
        plane = 1 << (bits_of("dp") - 1)
        sources = [held] + (list(given) or [near(slot) for slot, _ in first])
        here = [held] + list(given)
        self.loads = [] if via is None else [mover.own(here[i], via.at[i]) for i in range(len(here))]
        self.copies = [
            mover.own(here[i] if via is None else via.at[i], near(i)) for i in range(len(here))
        ]
        self.first = [] if given else [mover.remote(held, near(slot), "dp", r) for slot, r in first]
        self.second = [
            mover.remote(halves_of(sources[source], half), halves_of(near(slot), half), "dp", r)
            for slot, source, r, half in second
        ]
        sources += [near(slot) for slot in range(len(sources), plane)]
        self.cores = [mover.remote(values, far(i), "dp", 1) for i, values in enumerate(sources)]
        self.early = 1 + len(first)

    def start(self):
        for copy in self.loads or self.copies:
            copy.start()
        for move in self.first:
            move.start()
        self.cores[0].start()

    def relay(self):
        for move in self.first:
            move.wait_recv()
        for move in self.second + self.cores[1 : self.early]:
            move.start()

    def settle(self):
        for load, copy in zip(self.loads, self.copies):
            load.wait()
            copy.start()

    def finish(self):
        for move in self.second:
            move.wait_recv()
        for move in self.cores[self.early :]:
            move.start()
        for move in self.first + self.second:
            move.wait_send()
        for move in self.cores:
            move.wait()
        for copy in self.copies:
            copy.wait()


def plane_counts(given):
    first, second = plane_moves()
    plane = 1 << (bits_of("dp") - 1)
    return len(second) + plane + (0 if given else len(first)), 2 + 2 * given


def copy_semaphores(remote, local):
    copies = pltpu.SemaphoreType.DMA
    return [copies((remote,)), copies((remote,)), copies((local,))]


def anywhere():
    return pl.BlockSpec(memory_space=pltpu.HBM)


def all_distances():
    return [("dp", r) for r in range(1, 1 << bits_of("dp"))] + part_distances()


class Peaks:
    def __init__(self, mover, mine, near, mid, far):
        self.mine, self.near, self.mid, self.far = mine, near, mid, far
        self.first = [mover.remote(mine, near.at[r], "dp", r) for r in range(1, near.shape[0])]
        self.second = [mover.remote(mid, far.at[r], axis, r) for axis, r in part_distances()]

    def reach(self, values):
        self.mine[...] = values
        for moves, source, held in (
            (self.first, self.mine, self.near),
            (self.second, self.mid, self.far),
        ):
            for move in moves:
                move.start()
            held[0] = source[...]
            for move in moves:
                move.wait()
            values = jnp.max(held[...], axis=0)
            self.mid[...] = values
        return values


def peak_scratch():
    datas, parts = 1 << bits_of("dp"), 1 << bits_of("tensor")
    tile = (8, LANES)
    return [pltpu.VMEM(dims, F32) for dims in (tile, (datas,) + tile, tile, (parts,) + tile)]


def peak_moves():
    return (1 << bits_of("dp")) + (1 << bits_of("tensor")) - 2


def hosting(body, counts, given, row, peak):
    ins, outs = counts
    sources = sum(1 + count for count in given)

    def kernel(*refs):
        body_ins, (range_ref, before_ref) = refs[:ins], refs[ins : ins + 2]
        held, rest = list(refs[ins + 2 : ins + 2 + sources]), refs[ins + 2 + sources :]
        body_outs, level_ref = rest[:outs], rest[outs]
        sides, rest = rest[outs + 1 : outs + 1 + 2 * len(given)], rest[outs + 1 + 2 * len(given) :]
        body_scratch, vias = rest[: -7 - len(given)], rest[-7 - len(given) : -7]
        mover = Mover(*rest[-3:])
        peaks = Peaks(mover, *rest[-7:-3])
        weights = []
        for i, count in enumerate(given):
            own, *there = [held.pop(0) for _ in range(1 + count)]
            near, far = slots(sides[2 * i]), slots(sides[2 * i + 1])
            weights.append((OverPlane(mover, own, near, far, there, vias[i]), count))
        step, steps = 0, 1
        for i in range(HOST_RANK[body]):
            step = step * pl.num_programs(i) + pl.program_id(i)
            steps = steps * pl.num_programs(i)

        @pl.when(step == 0)
        def _():
            greet(all_distances())
            for weight, count in weights:
                weight.start()
                if count:
                    weight.relay()

        @pl.when(step == steps * 3 // 4)
        def _():
            for weight, count in weights:
                weight.settle()
                if not count:
                    weight.relay()

        body(*body_ins, *body_outs, *body_scratch)

        @pl.when(step == steps - 1)
        def _():
            for weight, _ in weights:
                weight.finish()
            largest = jnp.max(peaks.reach(body_outs[peak][...]), keepdims=True)
            level = DECAY * range_ref[row] + (1.0 - DECAY) * largest
            places = lax.broadcasted_iota(jnp.int32, level_ref.shape, 0)
            level_ref[...] = jnp.where(places == row, level, before_ref[...])

    return kernel


def hosted_call(body, weights, cid, ranges, levels, row, peak, *, grid, in_specs, out_specs, out_shape, scratch_shapes=(), **rest):
    plane = 1 << (bits_of("dp") - 1)
    counts = (len(in_specs), len(out_specs))
    given = [len(there) for _, there in weights]
    totals = [sum(column) for column in zip((peak_moves(), 1), *[plane_counts(count) for count in given])]
    small = pl.BlockSpec((8, LANES), lambda *steps: (0, 0))
    out_shape, vias, sources = out_shape + [shape_of((8, LANES), F32)], [], []
    for held, there in weights:
        out_shape += [shape_of((plane,) + held.shape, held.dtype)] * 2
        vias.append(pltpu.VMEM((1 + len(there),) + held.shape, held.dtype))
        sources += [held] + list(there)
    call = pl.pallas_call(
        hosting(body, counts, given, row, peak),
        grid=grid,
        in_specs=in_specs + [in_smem(), small] + [anywhere()] * len(sources),
        out_specs=out_specs + [small] + [anywhere()] * 2 * len(weights),
        out_shape=out_shape,
        scratch_shapes=list(scratch_shapes) + vias + peak_scratch() + copy_semaphores(*totals),
        compiler_params=params(collective_id=cid, has_side_effects=True),
        **rest,
    )

    def run(*args):
        results = call(*args, ranges, levels, *sources)
        return results[: counts[1]], results[counts[1]], results[counts[1] + 1 :]

    return run


def first_gather_kernel(
    first_ref, bias_ref, out_ref, in_ref, near, far, held_bias, near_out, far_out, held_in, held_out, send, recv, own
):
    mover = Mover(send, recv, own)
    parts, plane = near.shape[1], near.shape[0]
    moves, relays = plane_moves()
    along = AlongParts(mover, first_ref, lambda r: near.at[0, r])
    sources = [first_ref] + [near.at[0, r] for r in range(1, parts)]
    over = [[mover.remote(sources[r], near.at[slot, r], "dp", d) for slot, d in moves] for r in range(parts)]
    again = [
        [
            mover.remote(halves_of(near.at[source, r], half), halves_of(near.at[slot, r], half), "dp", d)
            for slot, source, d, half in relays
        ]
        for r in range(parts)
    ]
    cores = [
        [mover.remote(sources[r] if slot == 0 else near.at[slot, r], far.at[slot, r], "dp", 1) for slot in range(plane)]
        for r in range(parts)
    ]
    later = [
        AlongParts(mover, source, lambda r, held=held: held.at[r])
        for source, held in ((bias_ref, held_bias), (out_ref, held_out), (in_ref, held_in))
    ]
    outer = OverPlane(mover, held_out, slots(near_out), slots(far_out))
    greet(part_distances() + plane_distances())
    along.start()
    for move in over[0] + cores[0][:1]:
        move.start()
    along.hand_on()
    for units in later[:2]:
        units.start()
    for r in along.order:
        along.arrive(r)
        for move in over[r] + cores[r][:1]:
            move.start()
    for units in later[:2]:
        units.hand_on()
    later[2].start()
    later[1].finish()
    outer.start()
    later[2].hand_on()
    order = [0] + along.order
    for r in order:
        for i, (slot, _) in enumerate(moves):
            over[r][i].wait_recv()
            cores[r][slot].start()
        for move in again[r]:
            move.start()
    outer.relay()
    for r in order:
        for move in again[r]:
            move.wait_recv()
        for slot in range(1 + len(moves), plane):
            cores[r][slot].start()
    along.finish()
    for r in range(parts):
        for move in over[r] + again[r]:
            move.wait_send()
        for move in cores[r]:
            move.wait()
    outer.finish()
    for units in (later[0], later[2]):
        units.finish()


def first_gather(first, biases, outer, inner):
    parts, plane = 1 << bits_of("tensor"), 1 << (bits_of("dp") - 1)
    moves, relays = plane_moves()
    remote = 4 * (parts - 1) + parts * (len(moves) + len(relays) + plane) + plane_counts(0)[0]
    return pl.pallas_call(
        first_gather_kernel,
        in_specs=[pl.BlockSpec(memory_space=pltpu.VMEM)] * 4,
        out_specs=[anywhere()] * 6,
        out_shape=[shape_of((plane, parts) + first.shape, BF16)] * 2
        + [shape_of((parts,) + biases.shape, BF16)]
        + [shape_of((plane, parts) + outer.shape, BF16)] * 2
        + [shape_of((parts,) + inner.shape, BF16)],
        scratch_shapes=[pltpu.VMEM((parts,) + outer.shape, BF16)] + copy_semaphores(remote, 5),
        compiler_params=params(collective_id=3, has_side_effects=True),
        name="first_gather",
    )(first, biases, outer, inner)


CHUNK = 2


def finale_kernel(
    down_sum, down_more, in_sum, in_more, keep_0, more_0, keep_1, more_1, keep_2, more_2, keep_3, more_3,
    slope_q, slope_in, slope_down, sums_ref, near_d, far_d, near_i, far_i, near_q, far_q, sums_out,
    piece_d, piece_i, send_q, recv_q, piece_q, send_p, recv_p, sums_near, sums_mid, sums_far, send, recv, own
):
    mover = Mover(send, recv, own)
    _, orders = plane_orders()
    keeps, mores = (keep_0, keep_1, keep_2, keep_3), (more_0, more_1, more_2, more_3)
    quarter, kinds = keep_0.shape[1:3]
    parts, datas, chunks = 4 * quarter, sums_near.shape[0], kinds // CHUNK
    steps = [
        [mover.remote(send_p.at[k, i], recv_p.at[k, i], "dp", 1 << orders[i % 2][-1]) for i in range(4)]
        for k in range(chunks)
    ]
    along = [
        [mover.remote(send_q.at[k, r - 1], recv_q.at[k, r - 1], axis, r) for axis, r in part_distances()]
        for k in range(chunks)
    ]
    down = OverPlane(mover, piece_d, slots(near_d), slots(far_d))
    inner = OverPlane(mover, piece_i, slots(near_i), slots(far_i))
    first = [
        OverPlane(
            mover,
            piece_q.at[k],
            slots(near_q, pl.ds(k * CHUNK, CHUNK)),
            slots(far_q, pl.ds(k * CHUNK, CHUNK)),
        )
        for k in range(chunks)
    ]
    me = lax.axis_index("dp")
    sum_data = [
        mover.remote(sums_ref.at[at_distance("dp", r)], sums_near.at[r], "dp", r) for r in range(1, datas)
    ]
    sum_back = [mover.remote(sums_out.at[me], sums_out.at[me], "dp", r) for r in range(1, datas)]
    sum_part = [mover.remote(sums_mid, sums_far.at[r], axis, r) for axis, r in part_distances()]

    def kinds_of(k):
        return slice(k * CHUNK, (k + 1) * CHUNK)

    def block(k, r):
        i, j = r // quarter, r % quarter
        here = keeps[i][0, j, kinds_of(k)] + mores[i][0, j, kinds_of(k)].astype(F32)
        return here + recv_p[k, i, j].astype(F32)

    def reach(k):
        total = block(k, 0)
        for r in range(1, parts):
            along[k][r - 1].wait_recv()
            total = total + recv_q[k, r - 1].astype(F32)
        piece_q[k] = low(total * slope_q[kinds_of(k)])
        first[k].start()

    greet([("dp", r) for r in range(1, datas)] + part_distances())
    for move in sum_data:
        move.start()
    for k in range(chunks):
        for i in (3, 2, 1, 0):
            more = mores[i][1, :, kinds_of(k)].astype(F32)
            send_p[k, i] = low(keeps[i][1, :, kinds_of(k)] + more)
            steps[k][i].start()
    piece_d[...] = low((down_sum[...] + down_more[...].astype(F32)) * slope_down[...])
    piece_i[...] = low((in_sum[...] + in_more[...].astype(F32)) * slope_in[...])
    for k in range(chunks):
        for i in (3, 2, 1, 0):
            steps[k][i].wait_recv()
            for r in range(i * quarter, (i + 1) * quarter):
                if r:
                    send_q[k, r - 1] = low(block(k, r))
                    along[k][r - 1].start()
    down.start()
    inner.start()
    for move in sum_data:
        move.wait()
    sums_near[0] = sums_ref[me]
    sums_mid[...] = jnp.sum(sums_near[...], axis=0)
    for move in sum_part:
        move.start()
    reach(0)
    down.relay()
    inner.relay()
    for k in range(1, chunks):
        reach(k)
        first[k - 1].relay()
    for move in sum_part:
        move.wait()
    sums_far[0] = sums_mid[...]
    sums_out[me] = jnp.sum(sums_far[...], axis=0)
    for move in sum_back:
        move.start()
    down.finish()
    inner.finish()
    first[chunks - 1].relay()
    for move in sum_back:
        move.wait()
    for unit in first:
        unit.finish()
    for group in steps + along:
        for move in group:
            move.wait_send()


def finale(down, inner, first, slopes, sums):
    parts, plane, datas = 1 << bits_of("tensor"), 1 << (bits_of("dp") - 1), 1 << bits_of("dp")
    pieces = [slopes[2], slopes[1], slopes[0]]
    _, quarter, kinds, rows, c = first[0][0].shape
    chunks = kinds // CHUNK
    remote = chunks * (4 + parts - 1) + (2 + chunks) * plane_counts(0)[0] + 2 * (datas - 1) + parts - 1
    dims = sums.shape
    sums = sums.reshape(datas, -1, LANES)
    own = sums.shape[1:]
    vmem = pl.BlockSpec(memory_space=pltpu.VMEM)
    scratch = [pltpu.VMEM(piece.shape, BF16) for piece in pieces[:2]]
    scratch += [pltpu.VMEM((chunks, parts - 1, CHUNK, rows, c), BF16)] * 2
    scratch += [pltpu.VMEM((chunks, CHUNK, rows, c), BF16)]
    scratch += [pltpu.VMEM((chunks, 4, quarter, CHUNK, rows, c), BF16)] * 2
    scratch += [
        pltpu.VMEM(sums.shape, F32),
        pltpu.VMEM(own, F32),
        pltpu.VMEM((parts,) + own, F32),
    ]
    out_shape = []
    for piece in pieces:
        out_shape += [shape_of((plane,) + piece.shape, BF16)] * 2
    args = [*down, *inner]
    for pair in first:
        args += list(pair)
    args += [*slopes, sums]
    results = pl.pallas_call(
        finale_kernel,
        in_specs=[vmem] * len(args),
        out_specs=[anywhere()] * 6 + [vmem],
        out_shape=out_shape + [shape_of(sums.shape, F32)],
        scratch_shapes=scratch + copy_semaphores(remote, 2 + chunks),
        compiler_params=params(collective_id=2, has_side_effects=True),
        name="finale",
    )(*args)
    return [results[2 * i : 2 * i + 2] for i in range(3)], results[6].reshape(dims)


class Order:
    def __init__(self, width):
        self.rows = width // (1 << bits_of("dp"))

    def __getitem__(self, j):
        if self.rows % LANES:
            return j
        plane, each = 1 << (bits_of("dp") - 1), self.rows // LANES
        place = j // each
        return at_distance("dp", place % plane * 2 + place // plane) * each + j % each


def take_blocks(ref, order_ref, here=slice(None)):
    return jnp.concatenate(
        [
            ref[here, pl.ds(pl.multiple_of(order_ref[j] * LANES, LANES), LANES)]
            for j in range(ref.shape[1] // LANES)
        ],
        axis=1,
    )


def put_blocks(ref, order_ref, values):
    for j in range(ref.shape[1] // LANES):
        ref[:, pl.ds(pl.multiple_of(order_ref[j] * LANES, LANES), LANES)] = values[
            :, j * LANES : (j + 1) * LANES
        ]


def fold_peak(values):
    return jnp.max(jnp.abs(values).reshape(-1, 8, LANES), axis=0)


def column_peak(values):
    peak = fold_peak(values[:, :LANES])
    for j in range(1, values.shape[1] // LANES):
        peak = jnp.maximum(peak, fold_peak(values[:, j * LANES : (j + 1) * LANES]))
    return peak


def lane_peak(values):
    return jnp.max(column_peak(values), axis=0, keepdims=True)


def prepare_kernel(
    range_ref, x_ref, qkv_ref, out_ref, in_ref, down_ref, level_ref, quant_ref, *refs
):
    peaks = Peaks(Mover(*refs[-3:-1], None), *refs[-7:-3])
    greet(all_distances())
    order = Order(x_ref.shape[1])
    rows = 256
    steps = x_ref.shape[0] // rows

    def largest(step, peak):
        here = pl.ds(pl.multiple_of(step * rows, rows), rows)
        return jnp.maximum(peak, column_peak(x_ref[here, :].astype(F32)))

    own = [qkv_ref[j].astype(F32) for j in range(3)]
    own += [ref[0].astype(F32) for ref in (out_ref, in_ref, down_ref)]
    found = [lane_peak(values) for values in own]
    inputs = lax.fori_loop(0, steps, largest, jnp.zeros((8, LANES), F32))
    found.append(jnp.max(inputs, axis=0, keepdims=True))
    found.append(jnp.zeros((1, LANES), F32))
    reached = jnp.max(peaks.reach(jnp.concatenate(found, axis=0)), axis=1, keepdims=True)
    level = DECAY * range_ref[0] + (1.0 - DECAY) * reached[6:7, :]
    level_ref[...] = jnp.broadcast_to(level, level_ref.shape)
    for i, values in enumerate(own):
        bound = 0.5 * reached[i : i + 1, :]
        tangent = jnp.tanh(values / bound)
        quant, slope = low(bound * tangent), 1.0 - tangent * tangent
        if i < 4:
            refs[4][i] = slope
        else:
            refs[1 + i][0] = slope
        if i < 3:
            refs[0][i] = quant
        else:
            refs[i - 2][0] = quant

    @pl.loop(0, steps)
    def _(step):
        here = pl.ds(pl.multiple_of(step * rows, rows), rows)
        x = take_blocks(x_ref, order, here).astype(F32)
        quant_ref[here, :] = low(level * jnp.tanh(x / level))


def prepare(ranges, x, own):
    vmem = pl.BlockSpec(memory_space=pltpu.VMEM)
    out_shape = [shape_of((8, LANES), F32), shape_of(x.shape, BF16)]
    out_shape += [shape_of(values.shape, BF16) for values in own]
    out_shape += [shape_of((4,) + own[0].shape[1:], F32)]
    out_shape += [shape_of(values.shape, F32) for values in own[2:]]
    levels, quant, *rest = pl.pallas_call(
        prepare_kernel,
        in_specs=[in_smem()] + [vmem] * 5,
        out_specs=[vmem] * 9,
        out_shape=out_shape,
        scratch_shapes=peak_scratch() + copy_semaphores(peak_moves(), 1),
        compiler_params=params(collective_id=0, has_side_effects=True),
        name="prepare",
    )(ranges, x, *own)
    return levels, quant, rest[:4], rest[4:]


def qkv_kernel(x_ref, near_ref, far_ref, b_ref, o_ref):
    half = x_ref.shape[1] // 2
    total = dot(x_ref[:, :half], flat(near_ref[...])) + dot(x_ref[:, half:], flat(far_ref[...]))
    o_ref[...] = low(total + b_ref[...])


def qkv_rows(x, weights, bias):
    near, far = weights
    plane, parts, kinds, rows, c = near.shape
    tokens, width = x.shape
    weight_spec = pl.BlockSpec((plane, None, None, rows, c), lambda r, i: (0, r, i, 0, 0))
    return pl.pallas_call(
        qkv_kernel,
        grid=(parts, kinds),
        in_specs=[
            pl.BlockSpec((tokens, width), lambda r, i: (0, 0)),
            weight_spec,
            weight_spec,
            pl.BlockSpec((None, 1, c), lambda r, i: (i, 0, r)),
        ],
        out_specs=pl.BlockSpec((None, tokens, c), lambda r, i: (i, 0, r)),
        out_shape=shape_of((kinds, tokens, parts * c), BF16),
        compiler_params=params(),
        cost_estimate=cost(2 * tokens * width * kinds * parts * c, 14 * MIB),
        name="qkv",
    )(x, near, far, bias)


def fill_mask(mask_ref, ends_ref):
    row = pl.program_id(0)

    def segments(dims, axis):
        places = lax.broadcasted_iota(jnp.int32, dims, axis)
        count = jnp.zeros(dims, jnp.int32)
        for j in range(ends_ref.shape[1]):
            count = count + (places >= ends_ref[row, j]).astype(jnp.int32)
        return count

    same = segments((SEQ, 1), 0) == segments((1, SEQ), 1)
    mask_ref[...] = jnp.where(same, 0.0, MASKED).astype(F32)


def attend_kernel(
    skip, ends_ref, q_ref, k_ref, v_ref, *refs
):
    o_ref, lse_ref, peak_ref, mask_ref, sums_ref = refs[-5:]
    row, pair = pl.program_id(0), pl.program_id(1)
    factor = HD ** (-0.5)

    @pl.when(pair == 0)
    def _():
        fill_mask(mask_ref, ends_ref)
        sums_ref[...] = jnp.zeros_like(sums_ref) if skip == 0 else refs[0][...].T

    @pl.when((pair == 0) & (row == 0))
    def _():
        peak_ref[...] = jnp.zeros_like(peak_ref) if skip == 0 else refs[1][...]

    rows = 256
    lanes = lax.broadcasted_iota(jnp.int32, (rows, LANES), 1)
    for start in range(0, SEQ, rows):
        here = pl.ds(start, rows)
        q = q_ref[here, :] * jnp.asarray(factor, BF16)
        parts = []
        sums = sums_ref[here, :]
        for head in range(LANES // HD):
            own = lanes // HD == head
            scores = dot_cols(jnp.where(own, q, jnp.zeros_like(q)), k_ref[...]) + mask_ref[here, :]
            row_max = jnp.max(scores, axis=-1, keepdims=True)
            exponent = jnp.exp(scores - row_max)
            totals = jnp.sum(exponent, axis=-1, keepdims=True)
            probs = low(exponent * (1.0 / totals))
            parts.append(dot(probs, v_ref[...]))
            sums = jnp.where(lanes == (pair + skip) * (LANES // HD) + head, row_max + jnp.log(totals), sums)
        context = parts[0]
        for head in range(1, LANES // HD):
            context = jnp.where(lanes // HD == head, parts[head], context)
        o_ref[here, :] = context
        sums_ref[here, :] = sums
        peak_ref[...] = jnp.maximum(peak_ref[...], fold_peak(context))

    @pl.when(pair == pl.num_programs(1) - 1)
    def _():
        lse_ref[...] = sums_ref[...].T


def attend_first_kernel(*refs):
    attend_kernel(0, *refs)


def attend_last_kernel(*refs):
    attend_kernel(pl.num_programs(1), *refs)


def attend(qkv, ends, lse=None, peak=None, context=None, weights=(), ranges=None, levels=None):
    _, tokens, width = qkv.shape
    held = tokens // SEQ
    last = context is not None
    skip = width // LANES // 2 if last else 0

    def side(i):
        return pl.BlockSpec((None, SEQ, LANES), lambda r, j: (i, r, j + skip))

    sums = pl.BlockSpec((None, LANES, SEQ), lambda r, j: (r, 0, 0))
    small = pl.BlockSpec((8, LANES), lambda r, j: (0, 0))
    setup = dict(
        grid=(held, width // LANES // 2),
        in_specs=[in_smem(), side(0), side(1), side(2)],
        out_specs=[pl.BlockSpec((SEQ, LANES), lambda r, j: (r, j + skip)), sums, small],
        out_shape=[
            shape_of((tokens, width), F32),
            shape_of((held, LANES, SEQ), F32),
            shape_of((8, LANES), F32),
        ],
        scratch_shapes=[pltpu.VMEM((SEQ, SEQ), F32), pltpu.VMEM((SEQ, LANES), F32)],
        cost_estimate=cost(15e9, 40 * MIB),
        name="attend",
    )
    args = (ends, qkv, qkv, qkv)
    if not last:
        return pl.pallas_call(attend_first_kernel, compiler_params=params(), **setup)(*args)
    setup["in_specs"] += [sums, small, anywhere()]
    run = hosted_call(
        attend_last_kernel, weights, 5, ranges, levels, 1, 2, input_output_aliases={6: 0}, **setup
    )
    return run(*args, lse, peak, context)


def attend_back_kernel(
    c, first, order_ref, ends_ref, q_ref, k_ref, v_ref, g_ref, lse_ref, before_ref, dq_ref, dk_ref,
    dv_ref, sum_ref, mask_ref
):
    pair = pl.program_id(1)

    @pl.when((pair == 0) & (pl.program_id(0) == 0))
    def _():
        sum_ref[...] = before_ref[...]

    factor = HD ** (-0.5)

    @pl.when(pair == 0)
    def _():
        fill_mask(mask_ref, ends_ref)

    lanes = lax.broadcasted_iota(jnp.int32, (SEQ, LANES), 1)
    q, k, v, g = q_ref[...], k_ref[...], v_ref[...], g_ref[...]
    q_sums, k_sums, v_sums = [], [], []
    for head in range(LANES // HD):
        own = lanes // HD == head
        zero = jnp.zeros_like(q)
        q_own = jnp.where(own, q * jnp.asarray(factor, BF16), zero)
        g_own = jnp.where(own, g, zero)
        logsum = lse_ref[pl.ds((pair + first // LANES) * (LANES // HD) + head, 1), :]
        probs = jnp.exp(dot_cols(k, q_own) + mask_ref[...] - logsum)
        v_sums.append(dot(low(probs), g))
        grad_probs = dot_cols(v, g_own)
        mean_grad = jnp.sum(probs * grad_probs, axis=0, keepdims=True)
        grad_scores = low(factor * probs * (grad_probs - mean_grad))
        k_sums.append(dot(grad_scores, q))
        q_sums.append(dot_rows(grad_scores, k))

    def join(parts):
        joined = parts[0]
        for head in range(1, LANES // HD):
            joined = jnp.where(lanes // HD == head, parts[head], joined)
        return low(joined)

    dq, dv = join(q_sums), join(v_sums)
    dq_ref[...] = dq
    dk_ref[...] = join(k_sums)
    dv_ref[...] = dv
    column = first + pair * LANES
    place = order_ref[column // c] * c + column % c
    here = pl.ds(pl.multiple_of(place, LANES), LANES)
    sum_ref[0:1, here] += jnp.sum(dq.astype(F32), axis=0, keepdims=True)
    sum_ref[1:2, here] += jnp.sum(dv.astype(F32), axis=0, keepdims=True)


def attend_back(qkv, grad, ends, lse, before, part_order, c, first):
    _, tokens, inner = qkv.shape
    width = inner // 2
    held = tokens // SEQ
    skip = first // LANES

    def side(i):
        return pl.BlockSpec((None, SEQ, LANES), lambda r, j: (i, r, j + skip))

    block = pl.BlockSpec((SEQ, LANES), lambda r, j: (r, j))
    sums = pl.BlockSpec((8, inner), lambda r, j: (0, 0))
    return pl.pallas_call(
        partial(attend_back_kernel, c, first),
        grid=(held, width // LANES),
        in_specs=[
            in_smem(),
            in_smem(),
            side(0),
            side(1),
            side(2),
            pl.BlockSpec((SEQ, LANES), lambda r, j: (r, j + skip)),
            pl.BlockSpec((None, LANES, SEQ), lambda r, j: (r, 0, 0)),
            sums,
        ],
        out_specs=[block, block, block, sums],
        out_shape=[shape_of((tokens, width), BF16)] * 3 + [shape_of((8, inner), F32)],
        scratch_shapes=[pltpu.VMEM((SEQ, SEQ), F32)],
        compiler_params=params(),
        cost_estimate=cost(15e9, 50 * MIB),
        name="attend_back",
    )(part_order, ends, qkv, qkv, qkv, grad, lse, before)


def project(values, *sides):
    halves = []
    for refs in (sides[::2], sides[1::2]):
        total, place = None, 0
        for ref in refs:
            c = ref.shape[3]
            for r in range(ref.shape[1]):
                term = dot_cols(values[:, place : place + c], flat(ref[:, r]))
                total = term if total is None else total + term
                place += c
        halves.append(total)
    return jnp.concatenate(halves, axis=1)


def norm_parts(summed):
    center = summed - jnp.mean(summed, axis=-1, keepdims=True)
    inverse = lax.rsqrt(jnp.mean(center * center, axis=-1, keepdims=True) + EPS)
    return center * inverse, inverse


def norm_back(upstream, normal, inverse, gain):
    scaled = upstream * gain
    return inverse * (
        scaled
        - jnp.mean(scaled, axis=-1, keepdims=True)
        - normal * jnp.mean(scaled * normal, axis=-1, keepdims=True)
    )


def add_sums(ref, order_ref, sums):
    @pl.when(pl.program_id(0) == 0)
    def _():
        ref[...] = jnp.zeros_like(ref)

    for i, values in enumerate(sums):
        total = jnp.sum(values, axis=0, keepdims=True)
        for j in range(ref.shape[1] // LANES):
            here = pl.ds(pl.multiple_of(order_ref[j] * LANES, LANES), LANES)
            ref[i : i + 1, here] += total[:, j * LANES : (j + 1) * LANES]


def first_norm_kernel(
    ctx_ref, level_ref, near_ref, far_ref, x_ref, row_ref, quant_ref, normed_ref, normal_ref,
    inverse_ref, peak_ref
):
    level = level_ref[1:2, 0:1]
    quant = low(level * jnp.tanh(ctx_ref[...] / level))
    quant_ref[...] = quant
    order = Order(x_ref.shape[1])
    vectors = take_blocks(row_ref, order)
    summed = take_blocks(x_ref, order).astype(F32) + project(quant, near_ref, far_ref)
    normal, inverse = norm_parts(summed + vectors[0:1, :])
    normed = normal * vectors[1:2, :] + vectors[2:3, :]
    normed_ref[...] = normed
    normal_ref[...] = normal
    inverse_ref[...] = inverse

    @pl.when(pl.program_id(0) == 0)
    def _():
        peak_ref[...] = jnp.zeros_like(peak_ref)

    peak_ref[...] = jnp.maximum(peak_ref[...], column_peak(normed))


def whole(values):
    dims = values.shape
    return pl.BlockSpec(dims, lambda *steps: (0,) * len(dims))


def first_norm(context, level, weights, x, vectors, ranges):
    near, far = weights
    tokens, width = x.shape
    inner = context.shape[1]
    rows = 512

    def block(columns):
        return pl.BlockSpec((rows, columns), lambda t: (t, 0))

    run = hosted_call(
        first_norm_kernel,
        [],
        7,
        ranges,
        level,
        2,
        4,
        grid=(tokens // rows,),
        in_specs=[
            block(inner),
            whole(level),
            whole(near),
            whole(far),
            block(width),
            whole(vectors),
        ],
        out_specs=[
            block(inner),
            block(width),
            block(width),
            block(1),
            pl.BlockSpec((8, LANES), lambda t: (0, 0)),
        ],
        out_shape=[
            shape_of((tokens, inner), BF16),
            shape_of((tokens, width), F32),
            shape_of((tokens, width), F32),
            shape_of((tokens, 1), F32),
            shape_of((8, LANES), F32),
        ],
        cost_estimate=cost(2 * tokens * width * inner, 20 * MIB),
        name="first_norm",
    )
    return run(context, level, near, far, x, vectors)


def hidden_kernel(normed_ref, level_ref, near_ref, far_ref, b_ref, quant_ref, act_ref, slope_ref, peak_ref):
    half = normed_ref.shape[1] // 2

    @pl.when(pl.program_id(0) == 0)
    def _():
        peak_ref[...] = jnp.zeros_like(peak_ref)
        level = level_ref[2:3, 0:1]
        quant_ref[...] = low(level * jnp.tanh(normed_ref[...] / level))

    hidden = dot(quant_ref[:, :half], flat(near_ref[...]))
    hidden = hidden + dot(quant_ref[:, half:], flat(far_ref[...])) + b_ref[...]
    share = 0.5 + 0.5 * lax.erf(hidden * (0.5**0.5))
    active = hidden * share
    act_ref[...] = active
    slope_ref[...] = share + hidden * ((0.5 / jnp.pi) ** 0.5 * jnp.exp(-0.5 * hidden * hidden))
    peak_ref[...] = jnp.maximum(peak_ref[...], column_peak(active))


def hidden_rows(normed, level, weights, bias, held_down, ranges):
    near, far = weights
    plane, parts, rows, c = near.shape
    tokens, width = normed.shape
    step = min(c, 512)
    cuts = c // step
    weight_spec = pl.BlockSpec((plane, None, rows, step), lambda s: (0, s // cuts, 0, s % cuts))
    block = pl.BlockSpec((tokens, step), lambda s: (0, s))
    run = hosted_call(
        hidden_kernel,
        [(held_down, ())],
        6,
        ranges,
        level,
        3,
        3,
        grid=(parts * cuts,),
        in_specs=[
            whole(normed),
            whole(level),
            weight_spec,
            weight_spec,
            pl.BlockSpec((1, step), lambda s: (0, s)),
        ],
        out_specs=[
            pl.BlockSpec((tokens, width), lambda s: (0, 0)),
            block,
            block,
            pl.BlockSpec((8, LANES), lambda s: (0, 0)),
        ],
        out_shape=[
            shape_of((tokens, width), BF16),
            shape_of((tokens, parts * c), F32),
            shape_of((tokens, parts * c), F32),
            shape_of((8, LANES), F32),
        ],
        cost_estimate=cost(2 * tokens * width * parts * c, 50 * MIB),
        name="hidden",
    )
    return run(normed, level, near, far, bias)


def second_norm_kernel(
    order_ref, act_ref, slope_ref, level_ref, near_a, far_a, near_b, far_b, normed_ref, grad_ref, row_ref,
    quant_ref, back_ref, out_ref, sum_ref, branch_ref, terms_ref
):
    level = level_ref[3:4, 0:1]
    tangent = jnp.tanh(act_ref[...] / level)
    quant = low(level * tangent)
    quant_ref[...] = quant
    back_ref[...] = (1.0 - tangent * tangent) * slope_ref[...]
    vectors = take_blocks(row_ref, order_ref)
    summed = normed_ref[...] + project(quant, near_a, far_a, near_b, far_b) + vectors[3:4, :]
    normal, inverse = norm_parts(summed)
    gain = vectors[4:5, :]
    put_blocks(out_ref, order_ref, low(normal * gain + vectors[5:6, :]))
    upstream = take_blocks(grad_ref, order_ref).astype(F32)
    grad_sum = norm_back(upstream, normal, inverse, gain)
    sum_ref[...] = grad_sum
    branch_ref[...] = low(grad_sum)
    add_sums(terms_ref, order_ref, (grad_sum, upstream * normal, upstream))


def second_norm(active, slope, level, weights, normed, grad, vectors, order):
    tokens, width = normed.shape
    inner = active.shape[1]
    rows = 256

    def block(columns):
        return pl.BlockSpec((rows, columns), lambda t: (t, 0))

    return pl.pallas_call(
        second_norm_kernel,
        grid=(tokens // rows,),
        in_specs=[
            in_smem(),
            block(inner),
            block(inner),
            whole(level),
            *[whole(side) for side in weights],
            block(width),
            block(width),
            whole(vectors),
        ],
        out_specs=[
            block(inner),
            block(inner),
            block(width),
            block(width),
            block(width),
            pl.BlockSpec((8, width), lambda t: (0, 0)),
        ],
        out_shape=[
            shape_of((tokens, inner), BF16),
            shape_of((tokens, inner), F32),
            shape_of((tokens, width), BF16),
            shape_of((tokens, width), F32),
            shape_of((tokens, width), BF16),
            shape_of((8, width), F32),
        ],
        compiler_params=params(),
        cost_estimate=cost(2 * tokens * width * inner, 80 * MIB),
        name="second_norm",
    )(order, active, slope, level, *weights, normed, grad, vectors)


def weight_specs(xs, products, parts, plane, c):
    tokens, width = xs[0].shape
    count = len(products)
    step = min(c, 1024)
    cuts = c // step
    dims = (plane, parts, count, width // (2 * plane), c)
    in_specs = [
        pl.BlockSpec((tokens, step), lambda r, j, first=first: (0, (r + first) * cuts + j))
        for _, _, first in products
    ]
    out_spec = pl.BlockSpec((plane, None, count, dims[3], step), lambda r, j: (0, r, 0, 0, j))
    estimate = cost(tokens * width * parts * c * count, 20 * MIB)
    return dims, (parts, cuts), in_specs, out_spec, estimate


def turn_once(x_refs, turned_refs):
    @pl.when((pl.program_id(0) == 0) & (pl.program_id(1) == 0))
    def _():
        for x_ref, turned_ref in zip(x_refs, turned_refs):
            turned_ref[...] = x_ref[...].T


def weight_send_kernel(count, which, *refs):
    x_refs, h_refs = refs[:count], refs[count : count + len(which)]
    send_ref, turned = refs[count + len(which)], refs[count + len(which) + 1 :]
    turn_once(x_refs, turned)
    for i, h_ref in enumerate(h_refs):
        h = h_ref[...]
        total = dot(turned[which[i]][...], h)
        send_ref[:, i] = low(total).reshape(send_ref.shape[0], -1, h.shape[1])


def weight_send(xs, products, parts, plane, c):
    dims, grid, in_specs, out_spec, estimate = weight_specs(xs, products, parts, plane, c)
    tokens, width = xs[0].shape
    return pl.pallas_call(
        partial(weight_send_kernel, len(xs), [product[0] for product in products]),
        grid=grid,
        in_specs=[pl.BlockSpec((tokens, width // 2), lambda r, j: (0, 1))] * len(xs) + in_specs,
        out_specs=out_spec,
        out_shape=shape_of(dims, BF16),
        scratch_shapes=[pltpu.VMEM((width // 2, tokens), BF16)] * len(xs),
        compiler_params=params(),
        cost_estimate=estimate,
        name="weight_send",
    )(*xs, *[product[1] for product in products])


def weight_keep_kernel(count, which, split, *refs):
    x_refs, other_ref = refs[:count], refs[count]
    h_refs = refs[count + 1 : count + 1 + len(which)]
    outs, turned = refs[count + 1 + len(which) : -count], refs[-count:]
    half = pl.num_programs(0) // 2
    turn_once(x_refs, turned)
    for side in range(2):

        @pl.when(pl.program_id(0) // half == side)
        def _(side=side):
            keep_ref, send_ref = outs[2 * side : 2 * side + 2]
            for i, h_ref in enumerate(h_refs):
                h = h_ref[...]
                total = dot(turned[which[i]][...], h).reshape(other_ref.shape[0], -1, h.shape[1])
                for j, slot in enumerate(split[side][0]):
                    keep_ref[j, i] = total[slot] + other_ref[slot, i].astype(F32)
                for j, slot in enumerate(split[side][1]):
                    send_ref[j, i] = low(total[slot] + other_ref[slot, i].astype(F32))


def weight_keep(xs, products, other, parts, plane, c):
    dims, (_, cuts), in_specs, out_spec, estimate = weight_specs(xs, products, parts, plane, c)
    tokens, width = xs[0].shape
    half = parts // 2
    block = (plane // 2, None, dims[2], dims[3], c // cuts)
    near = pl.BlockSpec(
        block, lambda r, j: (0, jnp.minimum(r, half - 1), 0, 0, jnp.where(r < half, j, cuts - 1))
    )
    far = pl.BlockSpec(block, lambda r, j: (0, jnp.maximum(r - half, 0), 0, 0, jnp.where(r < half, 0, j)))
    small = (plane // 2, half) + dims[2:]
    which = [product[0] for product in products]
    keep_a, send_a, keep_b, send_b = pl.pallas_call(
        partial(weight_keep_kernel, len(xs), which, first_split(bits_of("dp") - 1)),
        grid=(parts, cuts),
        in_specs=[pl.BlockSpec((tokens, width // 2), lambda r, j: (0, 0))] * len(xs)
        + [out_spec]
        + in_specs,
        out_specs=[near, near, far, far],
        out_shape=[shape_of(small, F32), shape_of(small, BF16)] * 2,
        scratch_shapes=[pltpu.VMEM((width // 2, tokens), BF16)] * len(xs),
        compiler_params=params(),
        cost_estimate=estimate,
        name="weight_keep",
    )(*xs, other, *[product[1] for product in products])
    return [keep_a, keep_b], [send_a, send_b]


def grad_hidden_kernel(cuts, order_ref, g_ref, near_a, far_a, near_b, far_b, back_ref, o_ref, sum_ref):
    half = g_ref.shape[1] // 2
    block = pl.program_id(0)
    columns = back_ref.shape[1]

    @pl.when(block == 0)
    def _():
        sum_ref[...] = jnp.zeros_like(sum_ref)

    for side, (near_ref, far_ref) in enumerate(((near_a, far_a), (near_b, far_b))):

        @pl.when(block * 2 // pl.num_programs(0) == side)
        def _(near_ref=near_ref, far_ref=far_ref):
            grad = dot(g_ref[:, :half], flat(near_ref[...])) + dot(g_ref[:, half:], flat(far_ref[...]))
            grad = low(grad * back_ref[...])
            o_ref[...] = grad
            total = jnp.sum(grad.astype(F32), axis=0, keepdims=True)
            start = pl.multiple_of((block % cuts) * columns, LANES)
            sum_ref[pl.ds(order_ref[block // cuts], 1), pl.ds(start, columns)] = total


def grad_hidden_rows(grad, weights, back, part_order):
    plane, half, rows, c = weights[0].shape
    parts = 2 * half
    tokens, width = grad.shape
    step = min(c, 1024)
    cuts = c // step
    block = (plane, None, rows, step)
    first = pl.BlockSpec(
        block,
        lambda s: (0, jnp.minimum(s // cuts, half - 1), 0, jnp.where(s < half * cuts, s % cuts, cuts - 1)),
    )
    last = pl.BlockSpec(
        block,
        lambda s: (0, jnp.maximum(s // cuts - half, 0), 0, jnp.where(s < half * cuts, 0, s % cuts)),
    )
    block = pl.BlockSpec((tokens, step), lambda s: (0, s))
    return pl.pallas_call(
        partial(grad_hidden_kernel, cuts),
        grid=(parts * cuts,),
        in_specs=[in_smem(), whole(grad), first, first, last, last, block],
        out_specs=[block, pl.BlockSpec((parts, c), lambda s: (0, 0))],
        out_shape=[shape_of((tokens, parts * c), BF16), shape_of((parts, c), F32)],
        compiler_params=params(),
        cost_estimate=cost(2 * tokens * width * parts * c, 34 * MIB),
        name="grad_hidden",
    )(part_order, grad, *weights, back)


def first_back_kernel(
    order_ref, g_ref, near_ref, far_ref, normed_ref, normal_ref, inverse_ref, sum_two_ref, level_ref, row_ref,
    sum_ref, low_ref, terms_ref
):
    level = level_ref[2:3, 0:1]
    tangent = jnp.tanh(normed_ref[...] / level)
    grad = project(g_ref[...], near_ref, far_ref) * (1.0 - tangent * tangent) + sum_two_ref[...]
    normal = normal_ref[...]
    gain = take_blocks(row_ref, order_ref)[1:2, :]
    grad_sum = norm_back(grad, normal, inverse_ref[...], gain)
    sum_ref[...] = grad_sum
    low_ref[...] = low(grad_sum)
    add_sums(terms_ref, order_ref, (grad_sum, grad * normal, grad))


def first_back(grad, weights, normed, normal, inverse, sum_two, level, vectors, order):
    near, far = weights
    tokens, width = normed.shape
    inner = grad.shape[1]
    rows = 256

    def block(columns):
        return pl.BlockSpec((rows, columns), lambda t: (t, 0))

    return pl.pallas_call(
        first_back_kernel,
        grid=(tokens // rows,),
        in_specs=[
            in_smem(),
            block(inner),
            whole(near),
            whole(far),
            block(width),
            block(width),
            block(1),
            block(width),
            whole(level),
            whole(vectors),
        ],
        out_specs=[block(width), block(width), pl.BlockSpec((8, width), lambda t: (0, 0))],
        out_shape=[
            shape_of((tokens, width), F32),
            shape_of((tokens, width), BF16),
            shape_of((8, width), F32),
        ],
        compiler_params=params(),
        cost_estimate=cost(2 * tokens * width * inner, 36 * MIB),
        name="first_back",
    )(order, grad, near, far, normed, normal, inverse, sum_two, level, vectors)


def grad_context_kernel(g_ref, near_ref, far_ref, ctx_ref, level_ref, o_ref):
    half = g_ref.shape[1] // 2
    level = level_ref[1:2, 0:1]
    tangent = jnp.tanh(ctx_ref[...] / level)
    grad = dot(g_ref[:, :half], flat(near_ref[...])) + dot(g_ref[:, half:], flat(far_ref[...]))
    o_ref[...] = low(grad * (1.0 - tangent * tangent))


def grad_context_rows(grad, weights, context, level):
    near, far = weights
    plane, parts, rows, c = near.shape
    tokens, width = grad.shape
    weight_spec = pl.BlockSpec((plane, None, rows, c), lambda r: (0, r, 0, 0))
    block = pl.BlockSpec((tokens, c), lambda r: (0, r))
    return pl.pallas_call(
        grad_context_kernel,
        grid=(parts,),
        in_specs=[
            whole(grad),
            weight_spec,
            weight_spec,
            block,
            whole(level),
        ],
        out_specs=block,
        out_shape=shape_of((tokens, parts * c), BF16),
        compiler_params=params(),
        cost_estimate=cost(2 * tokens * width * parts * c, 10 * MIB),
        name="grad_context",
    )(grad, near, far, context, level)


def grad_input_kernel(order_ref, *refs):
    g_refs, (near_ref, far_ref, sum_ref, x_ref, level_ref, o_ref) = refs[:6], refs[6:]
    level = level_ref[0:1, 0:1]
    half = near_ref.shape[1] // 2
    total = None
    for side in range(2):
        for i in range(3):
            term = project(
                g_refs[side * 3 + i][...],
                near_ref.at[:, side * half : (side + 1) * half, i],
                far_ref.at[:, side * half : (side + 1) * half, i],
            )
            total = term if total is None else total + term
    tangent = jnp.tanh(take_blocks(x_ref, order_ref).astype(F32) / level)
    put_blocks(o_ref, order_ref, low(sum_ref[...] + total * (1.0 - tangent * tangent)))


def grad_input(grads, weights, grad_sum, x, level, order):
    near, far = weights
    tokens, width = x.shape
    inner = grads[0].shape[1]
    rows = 256

    def block(columns):
        return pl.BlockSpec((rows, columns), lambda t: (t, 0))

    return pl.pallas_call(
        grad_input_kernel,
        grid=(tokens // rows,),
        in_specs=[in_smem()]
        + [block(inner)] * 6
        + [whole(near), whole(far), block(width), block(width), whole(level)],
        out_specs=block(width),
        out_shape=shape_of((tokens, width), BF16),
        compiler_params=params(),
        cost_estimate=cost(12 * tokens * width * inner, 20 * MIB),
        name="grad_input",
    )(order, *grads, near, far, grad_sum, x, level)


def place_kernel(turned, order_ref, *refs):
    d_refs, i_refs, q_refs = refs[:2], refs[2:4], refs[4:6]
    in_out, qkv_out, *turned_outs = refs[6:]
    step = pl.program_id(0)
    plane, _, rows, _ = i_refs[0].shape
    for core in range(2):
        for j in range(plane):
            here = pl.ds(pl.multiple_of(order_ref[core * plane + j] * rows, rows), rows)
            in_out[0, here, :] = i_refs[core][j, 0].astype(F32)
            if turned:
                turned_outs[0][:, here] = d_refs[core][j, 0].astype(F32).T

            @pl.when(step < 3)
            def _(core=core, j=j, here=here):
                qkv_out[0, here, :] = q_refs[core][j, 0].astype(F32)

            if turned:

                @pl.when(step == 3)
                def _(core=core, j=j, here=here):
                    turned_outs[1][:, here] = q_refs[core][j, 0].astype(F32).T


def place_grads(down, inner, first, blocks):
    plane, _, rows, c = inner[0].shape
    columns = first[0].shape[3]
    width = 2 * plane * rows
    turned = rows % LANES == 0
    cut = c // 4

    def piece(size, index):
        return [pl.BlockSpec((plane, 1, rows, size), index)] * 2

    out_specs = [
        pl.BlockSpec((1, width, cut), lambda p: (0, 0, p)),
        pl.BlockSpec((1, width, columns), lambda p: (jnp.minimum(p, 2), 0, 0)),
    ]
    out_shape = [shape_of((1, width, c), F32), shape_of((3, width, columns), F32)]
    if turned:
        out_specs.append(pl.BlockSpec((cut, width), lambda p: (p, 0)))
        out_specs.append(pl.BlockSpec((columns, width), lambda p: (0, 0)))
        out_shape += [shape_of((c, width), F32), shape_of((columns, width), F32)]
    inner_grad, qkv_grad, *rest = pl.pallas_call(
        partial(place_kernel, turned),
        grid=(4,),
        in_specs=[in_smem()]
        + piece(cut, lambda p: (0, 0, 0, p)) * 2
        + piece(columns, lambda p: (0, p, 0, 0)),
        out_specs=out_specs,
        out_shape=out_shape,
        compiler_params=params(),
        name="place_grads",
    )(blocks.astype(jnp.int32), *down, *inner, *first)
    if not turned:
        back = jnp.zeros((2 * plane,), jnp.int32).at[blocks].set(jnp.arange(2 * plane, dtype=jnp.int32))
        for near, far in (down, [side[:, 3:] for side in first]):
            split = jnp.concatenate([near, far], axis=0)[:, 0]
            rest.append(jnp.take(split, back, axis=0).astype(F32).reshape(width, -1).T)
    return inner_grad[0], qkv_grad, rest[0], rest[1]


def left_over(keeps, sends):
    return scatter_plane(keeps, sends, True)


def scatter_grad(chain, xs, products, other, token, parts, plane, c):
    return chain(*weight_keep([tie(xs[0], [token])] + xs[1:], products, other, parts, plane, c))


HOST_RANK = {first_norm_kernel: 1, attend_last_kernel: 2, hidden_kernel: 1}


def own_block(values, axis):
    rows = values.shape[axis] // lax.axis_size("dp")
    return lax.dynamic_slice_in_dim(values, lax.axis_index("dp") * rows, rows, axis)


def local(
    mesh, layer_input, grad_output, doc_lengths, ranges, w_qkv, bias_qv, w_out, b_out, gain_one,
    shift_one, w_in, b_in, w_down, b_down, gain_two, shift_two
):
    datas, parts = lax.axis_size("dp"), lax.axis_size("tensor")
    data, part = lax.axis_index("dp"), lax.axis_index("tensor")
    plane = datas // 2
    tokens, width = layer_input.shape
    rows = width // datas

    places = jnp.arange(datas)
    distance = (places % plane) * 2 + places // plane
    blocks = data ^ distance
    if rows % LANES == 0:
        per_block = rows // LANES
        order = (blocks[:, None] * per_block + jnp.arange(per_block)).reshape(-1).astype(jnp.int32)
    else:
        order = jnp.arange(width // LANES, dtype=jnp.int32)

    def arrange(values):
        split = values.reshape(values.shape[:-1] + (datas, rows))
        return jnp.take(split, blocks, axis=-2).reshape(values.shape)

    def restore(values):
        split = values.reshape(values.shape[:-1] + (datas, rows))
        back = jnp.zeros((datas,), jnp.int32).at[blocks].set(places.astype(jnp.int32))
        return jnp.take(split, back, axis=-2).reshape(values.shape)

    def arrange_rows(values):
        return values if rows % LANES == 0 else arrange(values)

    def restore_rows(values):
        return values if rows % LANES == 0 else restore(values)

    part_order = (part ^ jnp.arange(parts)).astype(jnp.int32)
    x = arrange_rows(layer_input)
    upstream = arrange_rows(grad_output)
    vectors = jnp.stack([b_out, gain_one, shift_one, b_down, gain_two, shift_two, b_out, b_out])
    vectors = arrange_rows(vectors).astype(F32)

    own = [
        own_block(w_qkv, 1),
        own_block(w_out, 1).T[None],
        own_block(w_in, 0)[None],
        own_block(w_down, 1).T[None],
    ]
    levels, quant_input, quant_own, slopes = prepare(ranges, x, own)
    biases = jnp.concatenate([bias_qv.reshape(-1), b_in])
    count = biases.shape[0]
    biases = jnp.pad(biases, (0, -count % (16 * LANES))).reshape(-1, LANES)
    near, far, biases, near_out, far_out, held_in = first_gather(quant_own[0], biases, *quant_own[1:3])
    weights_qkv, weights_out = (near, far), (near_out, far_out)
    biases = biases.reshape(parts, -1)[:, :count]
    columns = bias_qv.shape[1]
    bias_q = biases[:, :columns].reshape(1, -1)
    bias_v = biases[:, columns : 2 * columns].reshape(1, -1)
    bias_qkv = jnp.stack([bias_q, jnp.zeros_like(bias_q), bias_v]).astype(F32)
    bias_hidden = biases[:, 2 * columns :].reshape(1, -1).astype(F32)

    held = tokens // SEQ
    lengths_here = lax.dynamic_slice_in_dim(doc_lengths, part * held, held, 0)
    ends = jnp.cumsum(lengths_here, axis=1, dtype=jnp.int32)
    half = parts // 2 * columns

    first_moves, _ = plane_moves()

    def over_plane(values, token):
        values = tie(values, [token])
        return [far_swap(values, r) for _, r in first_moves]

    there_in = over_plane(held_in, biases)
    held_a = tie(quant_own[3], [biases])[None]
    for bit in reversed(range(bits_of("tensor") - 1)):
        other = swap(held_a, "tensor", bit)
        held_a = jnp.stack([held_a, other], axis=1).reshape((-1,) + held_a.shape[1:])
    qkv = qkv_rows(quant_input, weights_qkv, bias_qkv)
    held_a = tie(held_a, [qkv])
    there_a = over_plane(held_a, qkv)
    held_b = swap(held_a, "tensor", bits_of("tensor") - 1)
    context, lse, peak = attend(qkv, ends)
    there_in, there_a = [tie(values, [peak]) for values in there_in], [tie(values, [peak]) for values in there_a]
    (context, lse, _), levels, (*weights_in, near_a, far_a) = attend(
        qkv, ends, lse, peak, context, [(held_in, there_in), (held_a, there_a)], ranges, levels
    )
    weights_in = tuple(side[:, :, 0] for side in weights_in)
    weights_out = tuple(side[:, :, 0] for side in weights_out)
    (quant_context, normed, normal_one, inverse_one, _), levels, _ = first_norm(
        context, levels, weights_out, x, vectors, ranges
    )
    held_b = tie(held_b, [levels])
    (quant_normed, active, slope, _), levels, (near_b, far_b) = hidden_rows(
        normed, levels, weights_in, bias_hidden, held_b, ranges
    )
    weights_down = [side[:, :, 0] for side in (near_a, far_a, near_b, far_b)]
    quant_active, back, output, grad_sum_two, grad_branch, terms_two = second_norm(
        active, slope, levels, weights_down, normed, upstream, vectors, order
    )

    wide = b_in.shape[0]
    other = weight_send([grad_branch], [(0, quant_active, 0)], parts, plane, wide)
    grad_after = tie(grad_branch, [other])
    other = swap(other, "dp", 0)
    grad_hidden, sum_hidden = grad_hidden_rows(grad_after, weights_down, back, part_order)
    down = scatter_grad(
        scatter_all, [grad_branch], [(0, quant_active, 0)], other, sum_hidden, parts, plane, wide
    )
    grad_hidden = tie(grad_hidden, next(down))
    other = weight_send([quant_normed], [(0, grad_hidden, 0)], parts, plane, wide)
    grad_after = tie(grad_hidden, [other])
    other = swap(other, "dp", 0)
    grad_sum_one, grad_attention, terms_one = first_back(
        grad_after, weights_in, normed, normal_one, inverse_one, grad_sum_two, levels, vectors, order
    )
    grad_hidden = tie(grad_hidden, down.send(terms_one))
    inner = scatter_grad(
        scatter_all, [quant_normed], [(0, grad_hidden, 0)], other, terms_one, parts, plane, wide
    )
    grad_after = tie(grad_attention, next(inner))
    grad_context = grad_context_rows(grad_after, weights_out, context, levels)
    grad_context = tie(grad_context, down.send(grad_context))
    sums_before = jnp.zeros((8, 2 * half), F32)
    *grads, token = attend_back(
        qkv, grad_context, ends, lse, sums_before, part_order, columns, 0
    )
    grads_a = grads
    xs = [quant_input, grad_attention]
    products_a = [(0, grad, 0) for grad in grads] + [(1, quant_context, 0)]
    other_a = weight_send(xs, products_a, parts // 2, plane, columns)
    token_a = other_a
    grad_context = tie(grad_context, inner.send(token_a) + down.send(token_a))
    other_a = swap(other_a, "dp", 0)
    *grads, token = attend_back(
        qkv, grad_context, ends, lse, token, part_order, columns, half
    )
    sum_qv = token
    down = run_all(down, token)
    grads[0] = tie(grads[0], inner.send(token) + [down[1]])
    products_b = [(0, grad, 0) for grad in grads] + [(1, quant_context, parts // 2)]
    other_b = weight_send(xs, products_b, parts // 2, plane, columns)
    token = other_b
    other_b = swap(other_b, "dp", 0)
    first_a = scatter_grad(left_over, xs, products_a, other_a, token, parts // 2, plane, columns)
    started = next(first_a)
    first_b = scatter_grad(left_over, xs, products_b, other_b, started[0], parts // 2, plane, columns)
    started = next(first_b) + inner.send(started[0])
    grads[0] = tie(grads[0], started)
    grad_x = grad_input(grads_a + grads, weights_qkv, grad_sum_one, x, levels, order)

    sums = [terms_one[:3], terms_two[:3], sum_qv[:2], sum_hidden.reshape(-1, width)]
    if rows % LANES:
        sums[0], sums[1] = restore(sums[0]), restore(sums[1])
    sums = jnp.concatenate(sums)
    padded = jnp.pad(sums, ((0, -sums.shape[0] % 8), (0, 0)))
    inner, first_a, first_b = [run_all(chain, grad_x) for chain in (inner, first_a, first_b)]
    (down, inner, first), sums = finale(down, inner, first_a + first_b, slopes, padded)
    hidden_all = sums[8 : 8 + sum_hidden.size // width].reshape(-1)
    grad_bias_qv = lax.dynamic_slice_in_dim(sums[6:8], part * columns, columns, 1)
    grad_b_in = lax.dynamic_slice_in_dim(hidden_all, part * b_in.shape[0], b_in.shape[0], 0)
    grad_w_in, grad_w_qkv, grad_w_down, grad_w_out = place_grads(down, inner, first, blocks)
    new_ranges = levels[:4, 0]
    return (
        restore_rows(output),
        restore_rows(grad_x),
        grad_w_qkv,
        grad_bias_qv,
        grad_w_out,
        sums[0],
        sums[1],
        sums[2],
        grad_w_in,
        grad_b_in,
        grad_w_down,
        sums[3],
        sums[4],
        sums[5],
        new_ranges,
    )


def solution(mesh):
    in_specs = (
        P(("dp", "tensor"), None),
        P(("dp", "tensor"), None),
        P("dp", None),
        P(),
        P(None, None, "tensor"),
        P(None, "tensor"),
        P("tensor", None),
        P(),
        P(),
        P(),
        P(None, "tensor"),
        P("tensor"),
        P("tensor", None),
        P(),
        P(),
        P(),
    )
    out_specs = (
        P(("dp", "tensor"), None),
        P(("dp", "tensor"), None),
        P(None, None, "tensor"),
        P(None, "tensor"),
        P("tensor", None),
        P(),
        P(),
        P(),
        P(None, "tensor"),
        P("tensor"),
        P("tensor", None),
        P(),
        P(),
        P(),
        P(),
    )
    return jax.shard_map(
        partial(local, mesh), mesh=mesh, in_specs=in_specs, out_specs=out_specs, check_vma=False
    )
```

```python
from functools import partial

import jax
import jax.numpy as jnp
from jax import lax
from jax.experimental import pallas as pl
from jax.experimental.pallas import tpu as pltpu
from jax.sharding import PartitionSpec as P

HD = 64
SEQ = 512
LANES = 128

EPS = 1e-06
DECAY = 0.9
MASKED = -1e30
MESH = pl.DeviceIdType.MESH
F32 = jnp.float32
BF16 = jnp.bfloat16
MIB = 1024 * 1024


def shape_of(dims, kind):
    return jax.ShapeDtypeStruct(dims, kind)


def params(**rest):
    return pltpu.CompilerParams(vmem_limit_bytes=60 * MIB, **rest)


def in_smem():
    return pl.BlockSpec(memory_space=pltpu.SMEM)


def cost(flops, moved):
    return pl.CostEstimate(flops=int(flops) // 1000, bytes_accessed=int(moved) // 1000, transcendentals=0)


def dot(first, second):
    return jnp.dot(first, second, preferred_element_type=F32)


def dot_cols(first, second):
    return lax.dot_general(first, second, (((1,), (1,)), ((), ())), preferred_element_type=F32)


def dot_rows(first, second):
    return lax.dot_general(first, second, (((0,), (0,)), ((), ())), preferred_element_type=F32)


def flat(block):
    return block.reshape(block.shape[0] * block.shape[1], block.shape[2])


def tie(values, others):
    return lax.optimization_barrier((values, *others))[0]


def swap(values, axis, bit, token=None):
    count = lax.axis_size(axis)
    other = lax.ppermute(values, axis, [(i, i ^ (1 << bit)) for i in range(count)])
    return other if token is None else tie(other, [token])


def far_swap(values, r):
    count = lax.axis_size("dp")
    return lax.ppermute(values, "dp", [(i, i ^ r) for i in range(count)])


def bits_of(axis):
    return lax.axis_size(axis).bit_length() - 1


def plane_orders():
    plane = list(range(1, bits_of("dp")))
    return plane, (plane[::-1], plane)


def run_all(chain, token=None):
    try:
        chain.send(token)
        while True:
            next(chain)
    except StopIteration as done:
        return done.value


def low(values):
    return values.astype(BF16)


def first_split(plane_bits):
    _, orders = plane_orders()
    split = []
    for order in orders:
        bit = order[0] - 1
        split.append([[s for s in range(1 << plane_bits) if (s >> bit) & 1 == away] for away in (0, 1)])
    return split


def scatter_plane(keeps, sends, left_over=False):
    plane, orders = plane_orders()
    left = [[bit for bit in plane[::-1] if bit != order[0]] for order in orders]
    sides = [keep.reshape((2,) * len(left[0]) + keep.shape[1:]) for keep in keeps]
    sends = [send.reshape(side.shape) for side, send in zip(sides, sends)]
    for step in range(len(plane)):
        if step:
            places = [left[i].index(orders[i][step]) for i in range(2)]
            sends = [low(lax.index_in_dim(sides[i], 1, places[i], keepdims=False)) for i in range(2)]
            sides = [lax.index_in_dim(sides[i], 0, places[i], keepdims=False) for i in range(2)]
            for i in range(2):
                left[i].remove(orders[i][step])
        token = yield sends
        others = [swap(sends[i], "dp", orders[i][step], token) for i in range(2)]
        if left_over and step == len(plane) - 2:
            return list(zip(sides, others))
        sides = [side + other.astype(F32) for side, other in zip(sides, others)]
    return sides


def scatter_all(keeps, sends):
    sides = yield from scatter_plane(keeps, sends)
    last = bits_of("tensor") - 1
    for bit in range(last):
        pairs = [values.reshape((-1, 2) + values.shape[1:]) for values in sides]
        send = jnp.concatenate([low(values[:, 1]) for values in pairs])
        token = yield [send]
        others = jnp.split(swap(send, "tensor", bit, token), 2)
        sides = [values[:, 0] + other.astype(F32) for values, other in zip(pairs, others)]
    send = low(sides[1][0])
    token = yield [send]
    return sides[0][0], swap(send, "tensor", last, token)


def at_distance(axis, r):
    me, index = lax.axis_index(axis), 0
    for bit in range(bits_of(axis)):
        index = index + (me // (1 << bit) + (r >> bit)) % 2 * (1 << bit)
    return index


def plane_moves():
    plane = 1 << (bits_of("dp") - 1)
    if plane == 4:
        return [(1, 2), (2, 4)], [(3, 1, 4, 0), (3, 2, 2, 1)]
    return [(slot, 2 * slot) for slot in range(1, plane)], []


class Mover:
    def __init__(self, send, recv, local):
        self.send, self.recv, self.local = send, recv, local
        self.count, self.local_count = 0, 0

    def remote(self, source, target, axis, r):
        i = self.count
        self.count += 1
        return pltpu.make_async_remote_copy(
            src_ref=source,
            dst_ref=target,
            send_sem=self.send.at[i],
            recv_sem=self.recv.at[i],
            device_id={axis: at_distance(axis, r)},
            device_id_type=MESH,
        )

    def own(self, source, target):
        i = self.local_count
        self.local_count += 1
        return pltpu.make_async_copy(source, target, self.local.at[i])


def greet(distances):
    barrier = pltpu.get_barrier_semaphore()
    for axis, r in distances:
        pl.semaphore_signal(
            barrier, inc=1, device_id={axis: at_distance(axis, r)}, device_id_type=MESH
        )
    pl.semaphore_wait(barrier, len(distances))


def part_distances():
    return [("tensor", r) for r in range(1, 1 << bits_of("tensor"))]


def plane_distances():
    first, second = plane_moves()
    apart = sorted({move[1] for move in first} | {move[2] for move in second} | {1})
    return [("dp", r) for r in apart]


def halves_of(ref, half):
    rows = ref.shape[-2] // 2
    return ref.at[..., half * rows : (half + 1) * rows, :]


def slots(ref, *inner):
    return lambda slot: ref.at[(slot,) + inner]


def low_bit(r):
    return r & -r


class AlongParts:
    def __init__(self, mover, own, place):
        parts = 1 << bits_of("tensor")
        self.copy = mover.own(own, place(0))
        self.moves, self.there = {}, {0}
        for r in range(1, parts):
            rest = r - low_bit(r)
            source = own if rest == 0 else place(rest)
            self.moves[r] = mover.remote(source, place(r), "tensor", low_bit(r))
        self.order = sorted(self.moves, key=lambda r: (bin(r).count("1"), -r))

    def start(self):
        self.copy.start()
        for r in self.order:
            if r == low_bit(r):
                self.moves[r].start()

    def arrive(self, r):
        if r not in self.there:
            self.moves[r].wait_recv()
            self.there.add(r)

    def hand_on(self):
        for r in self.order:
            if r != low_bit(r):
                self.arrive(r - low_bit(r))
                self.moves[r].start()

    def finish(self):
        self.copy.wait()
        for r, move in self.moves.items():
            self.arrive(r)
            move.wait_send()


class OverPlane:
    def __init__(self, mover, held, near, far, given=(), via=None):
        first, second = plane_moves()
        plane = 1 << (bits_of("dp") - 1)
        sources = [held] + (list(given) or [near(slot) for slot, _ in first])
        here = [held] + list(given)
        self.loads = [] if via is None else [mover.own(here[i], via.at[i]) for i in range(len(here))]
        self.copies = [
            mover.own(here[i] if via is None else via.at[i], near(i)) for i in range(len(here))
        ]
        self.first = [] if given else [mover.remote(held, near(slot), "dp", r) for slot, r in first]
        self.second = [
            mover.remote(halves_of(sources[source], half), halves_of(near(slot), half), "dp", r)
            for slot, source, r, half in second
        ]
        sources += [near(slot) for slot in range(len(sources), plane)]
        self.cores = [mover.remote(values, far(i), "dp", 1) for i, values in enumerate(sources)]
        self.early = 1 + len(first)

    def start(self):
        for copy in self.loads or self.copies:
            copy.start()
        for move in self.first:
            move.start()
        self.cores[0].start()

    def relay(self):
        for move in self.first:
            move.wait_recv()
        for move in self.second + self.cores[1 : self.early]:
            move.start()

    def settle(self):
        for load, copy in zip(self.loads, self.copies):
            load.wait()
            copy.start()

    def finish(self):
        for move in self.second:
            move.wait_recv()
        for move in self.cores[self.early :]:
            move.start()
        for move in self.first + self.second:
            move.wait_send()
        for move in self.cores:
            move.wait()
        for copy in self.copies:
            copy.wait()


def plane_counts(given):
    first, second = plane_moves()
    plane = 1 << (bits_of("dp") - 1)
    return len(second) + plane + (0 if given else len(first)), 2 + 2 * given


def copy_semaphores(remote, local):
    copies = pltpu.SemaphoreType.DMA
    return [copies((remote,)), copies((remote,)), copies((local,))]


def anywhere():
    return pl.BlockSpec(memory_space=pltpu.HBM)


def all_distances():
    return [("dp", r) for r in range(1, 1 << bits_of("dp"))] + part_distances()


class Peaks:
    def __init__(self, mover, mine, near, mid, far):
        self.mine, self.near, self.mid, self.far = mine, near, mid, far
        self.first = [mover.remote(mine, near.at[r], "dp", r) for r in range(1, near.shape[0])]
        self.second = [mover.remote(mid, far.at[r], axis, r) for axis, r in part_distances()]

    def reach(self, values):
        self.mine[...] = values
        for moves, source, held in (
            (self.first, self.mine, self.near),
            (self.second, self.mid, self.far),
        ):
            for move in moves:
                move.start()
            held[0] = source[...]
            for move in moves:
                move.wait()
            values = jnp.max(held[...], axis=0)
            self.mid[...] = values
        return values


def peak_scratch():
    datas, parts = 1 << bits_of("dp"), 1 << bits_of("tensor")
    tile = (8, LANES)
    return [pltpu.VMEM(dims, F32) for dims in (tile, (datas,) + tile, tile, (parts,) + tile)]


def peak_moves():
    return (1 << bits_of("dp")) + (1 << bits_of("tensor")) - 2


def hosting(body, counts, given, row, peak):
    ins, outs = counts
    sources = sum(1 + count for count in given)

    def kernel(*refs):
        body_ins, (range_ref, before_ref) = refs[:ins], refs[ins : ins + 2]
        held, rest = list(refs[ins + 2 : ins + 2 + sources]), refs[ins + 2 + sources :]
        body_outs, level_ref = rest[:outs], rest[outs]
        sides, rest = rest[outs + 1 : outs + 1 + 2 * len(given)], rest[outs + 1 + 2 * len(given) :]
        body_scratch, vias = rest[: -7 - len(given)], rest[-7 - len(given) : -7]
        mover = Mover(*rest[-3:])
        peaks = Peaks(mover, *rest[-7:-3])
        weights = []
        for i, count in enumerate(given):
            own, *there = [held.pop(0) for _ in range(1 + count)]
            near, far = slots(sides[2 * i]), slots(sides[2 * i + 1])
            weights.append((OverPlane(mover, own, near, far, there, vias[i]), count))
        step, steps = 0, 1
        for i in range(HOST_RANK[body]):
            step = step * pl.num_programs(i) + pl.program_id(i)
            steps = steps * pl.num_programs(i)

        @pl.when(step == 0)
        def _():
            greet(all_distances())
            for weight, count in weights:
                weight.start()
                if count:
                    weight.relay()

        @pl.when(step == steps * 3 // 4)
        def _():
            for weight, count in weights:
                weight.settle()
                if not count:
                    weight.relay()

        body(*body_ins, *body_outs, *body_scratch)

        @pl.when(step == steps - 1)
        def _():
            for weight, _ in weights:
                weight.finish()
            largest = jnp.max(peaks.reach(body_outs[peak][...]), keepdims=True)
            level = DECAY * range_ref[row] + (1.0 - DECAY) * largest
            places = lax.broadcasted_iota(jnp.int32, level_ref.shape, 0)
            level_ref[...] = jnp.where(places == row, level, before_ref[...])

    return kernel


def hosted_call(body, weights, cid, ranges, levels, row, peak, *, grid, in_specs, out_specs, out_shape, scratch_shapes=(), **rest):
    plane = 1 << (bits_of("dp") - 1)
    counts = (len(in_specs), len(out_specs))
    given = [len(there) for _, there in weights]
    totals = [sum(column) for column in zip((peak_moves(), 1), *[plane_counts(count) for count in given])]
    small = pl.BlockSpec((8, LANES), lambda *steps: (0, 0))
    out_shape, vias, sources = out_shape + [shape_of((8, LANES), F32)], [], []
    for held, there in weights:
        out_shape += [shape_of((plane,) + held.shape, held.dtype)] * 2
        vias.append(pltpu.VMEM((1 + len(there),) + held.shape, held.dtype))
        sources += [held] + list(there)
    call = pl.pallas_call(
        hosting(body, counts, given, row, peak),
        grid=grid,
        in_specs=in_specs + [in_smem(), small] + [anywhere()] * len(sources),
        out_specs=out_specs + [small] + [anywhere()] * 2 * len(weights),
        out_shape=out_shape,
        scratch_shapes=list(scratch_shapes) + vias + peak_scratch() + copy_semaphores(*totals),
        compiler_params=params(collective_id=cid, has_side_effects=True),
        **rest,
    )

    def run(*args):
        results = call(*args, ranges, levels, *sources)
        return results[: counts[1]], results[counts[1]], results[counts[1] + 1 :]

    return run


def first_gather_kernel(
    first_ref, bias_ref, out_ref, in_ref, near, far, held_bias, near_out, far_out, held_in, held_out, send, recv, own
):
    mover = Mover(send, recv, own)
    parts, plane = near.shape[1], near.shape[0]
    moves, relays = plane_moves()
    along = AlongParts(mover, first_ref, lambda r: near.at[0, r])
    sources = [first_ref] + [near.at[0, r] for r in range(1, parts)]
    over = [[mover.remote(sources[r], near.at[slot, r], "dp", d) for slot, d in moves] for r in range(parts)]
    again = [
        [
            mover.remote(halves_of(near.at[source, r], half), halves_of(near.at[slot, r], half), "dp", d)
            for slot, source, d, half in relays
        ]
        for r in range(parts)
    ]
    cores = [
        [mover.remote(sources[r] if slot == 0 else near.at[slot, r], far.at[slot, r], "dp", 1) for slot in range(plane)]
        for r in range(parts)
    ]
    later = [
        AlongParts(mover, source, lambda r, held=held: held.at[r])
        for source, held in ((bias_ref, held_bias), (out_ref, held_out), (in_ref, held_in))
    ]
    outer = OverPlane(mover, held_out, slots(near_out), slots(far_out))
    greet(part_distances() + plane_distances())
    along.start()
    for move in over[0] + cores[0][:1]:
        move.start()
    along.hand_on()
    for units in later[:2]:
        units.start()
    for r in along.order:
        along.arrive(r)
        for move in over[r] + cores[r][:1]:
            move.start()
    for units in later[:2]:
        units.hand_on()
    later[2].start()
    later[1].finish()
    outer.start()
    later[2].hand_on()
    order = [0] + along.order
    for r in order:
        for i, (slot, _) in enumerate(moves):
            over[r][i].wait_recv()
            cores[r][slot].start()
        for move in again[r]:
            move.start()
    outer.relay()
    for r in order:
        for move in again[r]:
            move.wait_recv()
        for slot in range(1 + len(moves), plane):
            cores[r][slot].start()
    along.finish()
    for r in range(parts):
        for move in over[r] + again[r]:
            move.wait_send()
        for move in cores[r]:
            move.wait()
    outer.finish()
    for units in (later[0], later[2]):
        units.finish()


def first_gather(first, biases, outer, inner):
    parts, plane = 1 << bits_of("tensor"), 1 << (bits_of("dp") - 1)
    moves, relays = plane_moves()
    remote = 4 * (parts - 1) + parts * (len(moves) + len(relays) + plane) + plane_counts(0)[0]
    return pl.pallas_call(
        first_gather_kernel,
        in_specs=[pl.BlockSpec(memory_space=pltpu.VMEM)] * 4,
        out_specs=[anywhere()] * 6,
        out_shape=[shape_of((plane, parts) + first.shape, BF16)] * 2
        + [shape_of((parts,) + biases.shape, BF16)]
        + [shape_of((plane, parts) + outer.shape, BF16)] * 2
        + [shape_of((parts,) + inner.shape, BF16)],
        scratch_shapes=[pltpu.VMEM((parts,) + outer.shape, BF16)] + copy_semaphores(remote, 5),
        compiler_params=params(collective_id=3, has_side_effects=True),
        name="first_gather",
    )(first, biases, outer, inner)


CHUNK = 2


def finale_kernel(
    down_sum, down_more, in_sum, in_more, keep_0, more_0, keep_1, more_1, keep_2, more_2, keep_3, more_3,
    slope_q, slope_in, slope_down, sums_ref, near_d, far_d, near_i, far_i, near_q, far_q, sums_out,
    piece_d, piece_i, send_q, recv_q, piece_q, send_p, recv_p, sums_near, sums_mid, sums_far, send, recv, own
):
    mover = Mover(send, recv, own)
    _, orders = plane_orders()
    keeps, mores = (keep_0, keep_1, keep_2, keep_3), (more_0, more_1, more_2, more_3)
    quarter, kinds = keep_0.shape[1:3]
    parts, datas, chunks = 4 * quarter, sums_near.shape[0], kinds // CHUNK
    steps = [
        [mover.remote(send_p.at[k, i], recv_p.at[k, i], "dp", 1 << orders[i % 2][-1]) for i in range(4)]
        for k in range(chunks)
    ]
    along = [
        [mover.remote(send_q.at[k, r - 1], recv_q.at[k, r - 1], axis, r) for axis, r in part_distances()]
        for k in range(chunks)
    ]
    down = OverPlane(mover, piece_d, slots(near_d), slots(far_d))
    inner = OverPlane(mover, piece_i, slots(near_i), slots(far_i))
    first = [
        OverPlane(
            mover,
            piece_q.at[k],
            slots(near_q, pl.ds(k * CHUNK, CHUNK)),
            slots(far_q, pl.ds(k * CHUNK, CHUNK)),
        )
        for k in range(chunks)
    ]
    me = lax.axis_index("dp")
    sum_data = [
        mover.remote(sums_ref.at[at_distance("dp", r)], sums_near.at[r], "dp", r) for r in range(1, datas)
    ]
    sum_back = [mover.remote(sums_out.at[me], sums_out.at[me], "dp", r) for r in range(1, datas)]
    sum_part = [mover.remote(sums_mid, sums_far.at[r], axis, r) for axis, r in part_distances()]

    def kinds_of(k):
        return slice(k * CHUNK, (k + 1) * CHUNK)

    def block(k, r):
        i, j = r // quarter, r % quarter
        here = keeps[i][0, j, kinds_of(k)] + mores[i][0, j, kinds_of(k)].astype(F32)
        return here + recv_p[k, i, j].astype(F32)

    def reach(k):
        total = block(k, 0)
        for r in range(1, parts):
            along[k][r - 1].wait_recv()
            total = total + recv_q[k, r - 1].astype(F32)
        piece_q[k] = low(total * slope_q[kinds_of(k)])
        first[k].start()

    greet([("dp", r) for r in range(1, datas)] + part_distances())
    for move in sum_data:
        move.start()
    for k in range(chunks):
        for i in (3, 2, 1, 0):
            more = mores[i][1, :, kinds_of(k)].astype(F32)
            send_p[k, i] = low(keeps[i][1, :, kinds_of(k)] + more)
            steps[k][i].start()
    piece_d[...] = low((down_sum[...] + down_more[...].astype(F32)) * slope_down[...])
    piece_i[...] = low((in_sum[...] + in_more[...].astype(F32)) * slope_in[...])
    for k in range(chunks):
        for i in (3, 2, 1, 0):
            steps[k][i].wait_recv()
            for r in range(i * quarter, (i + 1) * quarter):
                if r:
                    send_q[k, r - 1] = low(block(k, r))
                    along[k][r - 1].start()
    down.start()
    inner.start()
    for move in sum_data:
        move.wait()
    sums_near[0] = sums_ref[me]
    sums_mid[...] = jnp.sum(sums_near[...], axis=0)
    for move in sum_part:
        move.start()
    reach(0)
    down.relay()
    inner.relay()
    for k in range(1, chunks):
        reach(k)
        first[k - 1].relay()
    for move in sum_part:
        move.wait()
    sums_far[0] = sums_mid[...]
    sums_out[me] = jnp.sum(sums_far[...], axis=0)
    for move in sum_back:
        move.start()
    down.finish()
    inner.finish()
    first[chunks - 1].relay()
    for move in sum_back:
        move.wait()
    for unit in first:
        unit.finish()
    for group in steps + along:
        for move in group:
            move.wait_send()


def finale(down, inner, first, slopes, sums):
    parts, plane, datas = 1 << bits_of("tensor"), 1 << (bits_of("dp") - 1), 1 << bits_of("dp")
    pieces = [slopes[2], slopes[1], slopes[0]]
    _, quarter, kinds, rows, c = first[0][0].shape
    chunks = kinds // CHUNK
    remote = chunks * (4 + parts - 1) + (2 + chunks) * plane_counts(0)[0] + 2 * (datas - 1) + parts - 1
    dims = sums.shape
    sums = sums.reshape(datas, -1, LANES)
    own = sums.shape[1:]
    vmem = pl.BlockSpec(memory_space=pltpu.VMEM)
    scratch = [pltpu.VMEM(piece.shape, BF16) for piece in pieces[:2]]
    scratch += [pltpu.VMEM((chunks, parts - 1, CHUNK, rows, c), BF16)] * 2
    scratch += [pltpu.VMEM((chunks, CHUNK, rows, c), BF16)]
    scratch += [pltpu.VMEM((chunks, 4, quarter, CHUNK, rows, c), BF16)] * 2
    scratch += [
        pltpu.VMEM(sums.shape, F32),
        pltpu.VMEM(own, F32),
        pltpu.VMEM((parts,) + own, F32),
    ]
    out_shape = []
    for piece in pieces:
        out_shape += [shape_of((plane,) + piece.shape, BF16)] * 2
    args = [*down, *inner]
    for pair in first:
        args += list(pair)
    args += [*slopes, sums]
    results = pl.pallas_call(
        finale_kernel,
        in_specs=[vmem] * len(args),
        out_specs=[anywhere()] * 6 + [vmem],
        out_shape=out_shape + [shape_of(sums.shape, F32)],
        scratch_shapes=scratch + copy_semaphores(remote, 2 + chunks),
        compiler_params=params(collective_id=2, has_side_effects=True),
        name="finale",
    )(*args)
    return [results[2 * i : 2 * i + 2] for i in range(3)], results[6].reshape(dims)


class Order:
    def __init__(self, width):
        self.rows = width // (1 << bits_of("dp"))

    def __getitem__(self, j):
        if self.rows % LANES:
            return j
        plane, each = 1 << (bits_of("dp") - 1), self.rows // LANES
        place = j // each
        return at_distance("dp", place % plane * 2 + place // plane) * each + j % each


def take_blocks(ref, order_ref, here=slice(None)):
    return jnp.concatenate(
        [
            ref[here, pl.ds(pl.multiple_of(order_ref[j] * LANES, LANES), LANES)]
            for j in range(ref.shape[1] // LANES)
        ],
        axis=1,
    )


def put_blocks(ref, order_ref, values):
    for j in range(ref.shape[1] // LANES):
        ref[:, pl.ds(pl.multiple_of(order_ref[j] * LANES, LANES), LANES)] = values[
            :, j * LANES : (j + 1) * LANES
        ]


def fold_peak(values):
    return jnp.max(jnp.abs(values).reshape(-1, 8, LANES), axis=0)


def column_peak(values):
    peak = fold_peak(values[:, :LANES])
    for j in range(1, values.shape[1] // LANES):
        peak = jnp.maximum(peak, fold_peak(values[:, j * LANES : (j + 1) * LANES]))
    return peak


def lane_peak(values):
    return jnp.max(column_peak(values), axis=0, keepdims=True)


def prepare_kernel(
    range_ref, x_ref, qkv_ref, out_ref, in_ref, down_ref, level_ref, quant_ref, *refs
):
    peaks = Peaks(Mover(*refs[-3:-1], None), *refs[-7:-3])
    greet(all_distances())
    order = Order(x_ref.shape[1])
    rows = 256
    steps = x_ref.shape[0] // rows

    def largest(step, peak):
        here = pl.ds(pl.multiple_of(step * rows, rows), rows)
        return jnp.maximum(peak, column_peak(x_ref[here, :].astype(F32)))

    own = [qkv_ref[j].astype(F32) for j in range(3)]
    own += [ref[0].astype(F32) for ref in (out_ref, in_ref, down_ref)]
    found = [lane_peak(values) for values in own]
    inputs = lax.fori_loop(0, steps, largest, jnp.zeros((8, LANES), F32))
    found.append(jnp.max(inputs, axis=0, keepdims=True))
    found.append(jnp.zeros((1, LANES), F32))
    reached = jnp.max(peaks.reach(jnp.concatenate(found, axis=0)), axis=1, keepdims=True)
    level = DECAY * range_ref[0] + (1.0 - DECAY) * reached[6:7, :]
    level_ref[...] = jnp.broadcast_to(level, level_ref.shape)
    for i, values in enumerate(own):
        bound = 0.5 * reached[i : i + 1, :]
        tangent = jnp.tanh(values / bound)
        quant, slope = low(bound * tangent), 1.0 - tangent * tangent
        if i < 4:
            refs[4][i] = slope
        else:
            refs[1 + i][0] = slope
        if i < 3:
            refs[0][i] = quant
        else:
            refs[i - 2][0] = quant

    @pl.loop(0, steps)
    def _(step):
        here = pl.ds(pl.multiple_of(step * rows, rows), rows)
        x = take_blocks(x_ref, order, here).astype(F32)
        quant_ref[here, :] = low(level * jnp.tanh(x / level))


def prepare(ranges, x, own):
    vmem = pl.BlockSpec(memory_space=pltpu.VMEM)
    out_shape = [shape_of((8, LANES), F32), shape_of(x.shape, BF16)]
    out_shape += [shape_of(values.shape, BF16) for values in own]
    out_shape += [shape_of((4,) + own[0].shape[1:], F32)]
    out_shape += [shape_of(values.shape, F32) for values in own[2:]]
    levels, quant, *rest = pl.pallas_call(
        prepare_kernel,
        in_specs=[in_smem()] + [vmem] * 5,
        out_specs=[vmem] * 9,
        out_shape=out_shape,
        scratch_shapes=peak_scratch() + copy_semaphores(peak_moves(), 1),
        compiler_params=params(collective_id=0, has_side_effects=True),
        name="prepare",
    )(ranges, x, *own)
    return levels, quant, rest[:4], rest[4:]


def qkv_kernel(x_ref, near_ref, far_ref, b_ref, o_ref):
    half = x_ref.shape[1] // 2
    total = dot(x_ref[:, :half], flat(near_ref[...])) + dot(x_ref[:, half:], flat(far_ref[...]))
    o_ref[...] = low(total + b_ref[...])


def qkv_rows(x, weights, bias):
    near, far = weights
    plane, parts, kinds, rows, c = near.shape
    tokens, width = x.shape
    weight_spec = pl.BlockSpec((plane, None, None, rows, c), lambda r, i: (0, r, i, 0, 0))
    return pl.pallas_call(
        qkv_kernel,
        grid=(parts, kinds),
        in_specs=[
            pl.BlockSpec((tokens, width), lambda r, i: (0, 0)),
            weight_spec,
            weight_spec,
            pl.BlockSpec((None, 1, c), lambda r, i: (i, 0, r)),
        ],
        out_specs=pl.BlockSpec((None, tokens, c), lambda r, i: (i, 0, r)),
        out_shape=shape_of((kinds, tokens, parts * c), BF16),
        compiler_params=params(),
        cost_estimate=cost(2 * tokens * width * kinds * parts * c, 14 * MIB),
        name="qkv",
    )(x, near, far, bias)


def fill_mask(mask_ref, ends_ref):
    row = pl.program_id(0)

    def segments(dims, axis):
        places = lax.broadcasted_iota(jnp.int32, dims, axis)
        count = jnp.zeros(dims, jnp.int32)
        for j in range(ends_ref.shape[1]):
            count = count + (places >= ends_ref[row, j]).astype(jnp.int32)
        return count

    same = segments((SEQ, 1), 0) == segments((1, SEQ), 1)
    mask_ref[...] = jnp.where(same, 0.0, MASKED).astype(F32)


def attend_kernel(
    skip, ends_ref, q_ref, k_ref, v_ref, *refs
):
    o_ref, lse_ref, peak_ref, mask_ref, sums_ref = refs[-5:]
    row, pair = pl.program_id(0), pl.program_id(1)
    factor = HD ** (-0.5)

    @pl.when(pair == 0)
    def _():
        fill_mask(mask_ref, ends_ref)
        sums_ref[...] = jnp.zeros_like(sums_ref) if skip == 0 else refs[0][...].T

    @pl.when((pair == 0) & (row == 0))
    def _():
        peak_ref[...] = jnp.zeros_like(peak_ref) if skip == 0 else refs[1][...]

    rows = SEQ
    lanes = lax.broadcasted_iota(jnp.int32, (rows, LANES), 1)
    for start in range(0, SEQ, rows):
        here = pl.ds(start, rows)
        q = q_ref[here, :] * jnp.asarray(factor, BF16)
        parts = []
        sums = sums_ref[here, :]
        for head in range(LANES // HD):
            own = lanes // HD == head
            scores = dot_cols(jnp.where(own, q, jnp.zeros_like(q)), k_ref[...]) + mask_ref[here, :]
            row_max = jnp.max(scores, axis=-1, keepdims=True)
            exponent = jnp.exp(scores - row_max)
            totals = jnp.sum(exponent, axis=-1, keepdims=True)
            probs = low(exponent * (1.0 / totals))
            parts.append(dot(probs, v_ref[...]))
            sums = jnp.where(lanes == (pair + skip) * (LANES // HD) + head, row_max + jnp.log(totals), sums)
        context = parts[0]
        for head in range(1, LANES // HD):
            context = jnp.where(lanes // HD == head, parts[head], context)
        o_ref[here, :] = context
        sums_ref[here, :] = sums
        peak_ref[...] = jnp.maximum(peak_ref[...], fold_peak(context))

    @pl.when(pair == pl.num_programs(1) - 1)
    def _():
        lse_ref[...] = sums_ref[...].T


def attend_first_kernel(*refs):
    attend_kernel(0, *refs)


def attend_last_kernel(*refs):
    attend_kernel(pl.num_programs(1), *refs)


def attend(qkv, ends, lse=None, peak=None, context=None, weights=(), ranges=None, levels=None):
    _, tokens, width = qkv.shape
    held = tokens // SEQ
    last = context is not None
    skip = width // LANES // 2 if last else 0

    def side(i):
        return pl.BlockSpec((None, SEQ, LANES), lambda r, j: (i, r, j + skip))

    sums = pl.BlockSpec((None, LANES, SEQ), lambda r, j: (r, 0, 0))
    small = pl.BlockSpec((8, LANES), lambda r, j: (0, 0))
    setup = dict(
        grid=(held, width // LANES // 2),
        in_specs=[in_smem(), side(0), side(1), side(2)],
        out_specs=[pl.BlockSpec((SEQ, LANES), lambda r, j: (r, j + skip)), sums, small],
        out_shape=[
            shape_of((tokens, width), F32),
            shape_of((held, LANES, SEQ), F32),
            shape_of((8, LANES), F32),
        ],
        scratch_shapes=[pltpu.VMEM((SEQ, SEQ), F32), pltpu.VMEM((SEQ, LANES), F32)],
        cost_estimate=cost(15e9, 40 * MIB),
        name="attend",
    )
    args = (ends, qkv, qkv, qkv)
    if not last:
        return pl.pallas_call(attend_first_kernel, compiler_params=params(), **setup)(*args)
    setup["in_specs"] += [sums, small, anywhere()]
    run = hosted_call(
        attend_last_kernel, weights, 5, ranges, levels, 1, 2, input_output_aliases={6: 0}, **setup
    )
    return run(*args, lse, peak, context)


def attend_back_kernel(
    c, first, order_ref, ends_ref, q_ref, k_ref, v_ref, g_ref, lse_ref, before_ref, dq_ref, dk_ref,
    dv_ref, sum_ref, mask_ref
):
    pair = pl.program_id(1)

    @pl.when((pair == 0) & (pl.program_id(0) == 0))
    def _():
        sum_ref[...] = before_ref[...]

    factor = HD ** (-0.5)

    @pl.when(pair == 0)
    def _():
        fill_mask(mask_ref, ends_ref)

    lanes = lax.broadcasted_iota(jnp.int32, (SEQ, LANES), 1)
    q, k, v, g = q_ref[...], k_ref[...], v_ref[...], g_ref[...]
    heads, zero = LANES // HD, jnp.zeros((SEQ, LANES), BF16)
    probs, grad_scores = [], []
    for head in range(heads):
        own = lanes // HD == head
        q_own = jnp.where(own, q * jnp.asarray(factor, BF16), zero)
        g_own = jnp.where(own, g, zero)
        logsum = lse_ref[pl.ds((pair + first // LANES) * heads + head, 1), :]
        prob = jnp.exp(dot_cols(k, q_own) + mask_ref[...] - logsum)
        grad_probs = dot_cols(v, g_own)
        mean_grad = jnp.sum(prob * grad_probs, axis=0, keepdims=True)
        probs.append(low(prob))
        grad_scores.append(low(factor * prob * (grad_probs - mean_grad)))
    v_sums = dot(jnp.concatenate(probs, axis=0), g)
    k_sums = dot(jnp.concatenate(grad_scores, axis=0), q)
    q_sums = dot_rows(jnp.concatenate(grad_scores, axis=1), k)

    def join(parts):
        joined = parts[:SEQ]
        for head in range(1, heads):
            joined = jnp.where(lanes // HD == head, parts[head * SEQ : (head + 1) * SEQ], joined)
        return low(joined)

    dq, dv = join(q_sums), join(v_sums)
    dq_ref[...] = dq
    dk_ref[...] = join(k_sums)
    dv_ref[...] = dv
    column = first + pair * LANES
    place = order_ref[column // c] * c + column % c
    here = pl.ds(pl.multiple_of(place, LANES), LANES)
    sum_ref[0:1, here] += jnp.sum(dq.astype(F32), axis=0, keepdims=True)
    sum_ref[1:2, here] += jnp.sum(dv.astype(F32), axis=0, keepdims=True)


def attend_back(qkv, grad, ends, lse, before, part_order, c, first):
    _, tokens, inner = qkv.shape
    width = inner // 2
    held = tokens // SEQ
    skip = first // LANES

    def side(i):
        return pl.BlockSpec((None, SEQ, LANES), lambda r, j: (i, r, j + skip))

    block = pl.BlockSpec((SEQ, LANES), lambda r, j: (r, j))
    sums = pl.BlockSpec((8, inner), lambda r, j: (0, 0))
    return pl.pallas_call(
        partial(attend_back_kernel, c, first),
        grid=(held, width // LANES),
        in_specs=[
            in_smem(),
            in_smem(),
            side(0),
            side(1),
            side(2),
            pl.BlockSpec((SEQ, LANES), lambda r, j: (r, j + skip)),
            pl.BlockSpec((None, LANES, SEQ), lambda r, j: (r, 0, 0)),
            sums,
        ],
        out_specs=[block, block, block, sums],
        out_shape=[shape_of((tokens, width), BF16)] * 3 + [shape_of((8, inner), F32)],
        scratch_shapes=[pltpu.VMEM((SEQ, SEQ), F32)],
        compiler_params=params(),
        cost_estimate=cost(15e9, 50 * MIB),
        name="attend_back",
    )(part_order, ends, qkv, qkv, qkv, grad, lse, before)


def project(values, *sides):
    halves = []
    for refs in (sides[::2], sides[1::2]):
        total, place = None, 0
        for ref in refs:
            c = ref.shape[3]
            for r in range(ref.shape[1]):
                term = dot_cols(values[:, place : place + c], flat(ref[:, r]))
                total = term if total is None else total + term
                place += c
        halves.append(total)
    return jnp.concatenate(halves, axis=1)


def norm_parts(summed):
    center = summed - jnp.mean(summed, axis=-1, keepdims=True)
    inverse = lax.rsqrt(jnp.mean(center * center, axis=-1, keepdims=True) + EPS)
    return center * inverse, inverse


def norm_back(upstream, normal, inverse, gain):
    scaled = upstream * gain
    return inverse * (
        scaled
        - jnp.mean(scaled, axis=-1, keepdims=True)
        - normal * jnp.mean(scaled * normal, axis=-1, keepdims=True)
    )


def add_sums(ref, order_ref, sums):
    @pl.when(pl.program_id(0) == 0)
    def _():
        ref[...] = jnp.zeros_like(ref)

    for i, values in enumerate(sums):
        total = jnp.sum(values, axis=0, keepdims=True)
        for j in range(ref.shape[1] // LANES):
            here = pl.ds(pl.multiple_of(order_ref[j] * LANES, LANES), LANES)
            ref[i : i + 1, here] += total[:, j * LANES : (j + 1) * LANES]


def first_norm_kernel(
    ctx_ref, level_ref, near_ref, far_ref, x_ref, row_ref, quant_ref, normed_ref, normal_ref,
    inverse_ref, peak_ref
):
    level = level_ref[1:2, 0:1]
    quant = low(level * jnp.tanh(ctx_ref[...] / level))
    quant_ref[...] = quant
    order = Order(x_ref.shape[1])
    vectors = take_blocks(row_ref, order)
    summed = take_blocks(x_ref, order).astype(F32) + project(quant, near_ref, far_ref)
    normal, inverse = norm_parts(summed + vectors[0:1, :])
    normed = normal * vectors[1:2, :] + vectors[2:3, :]
    normed_ref[...] = normed
    normal_ref[...] = normal
    inverse_ref[...] = inverse

    @pl.when(pl.program_id(0) == 0)
    def _():
        peak_ref[...] = jnp.zeros_like(peak_ref)

    peak_ref[...] = jnp.maximum(peak_ref[...], column_peak(normed))


def whole(values):
    dims = values.shape
    return pl.BlockSpec(dims, lambda *steps: (0,) * len(dims))


def first_norm(context, level, weights, x, vectors, ranges):
    near, far = weights
    tokens, width = x.shape
    inner = context.shape[1]
    rows = 512

    def block(columns):
        return pl.BlockSpec((rows, columns), lambda t: (t, 0))

    run = hosted_call(
        first_norm_kernel,
        [],
        7,
        ranges,
        level,
        2,
        4,
        grid=(tokens // rows,),
        in_specs=[
            block(inner),
            whole(level),
            whole(near),
            whole(far),
            block(width),
            whole(vectors),
        ],
        out_specs=[
            block(inner),
            block(width),
            block(width),
            block(1),
            pl.BlockSpec((8, LANES), lambda t: (0, 0)),
        ],
        out_shape=[
            shape_of((tokens, inner), BF16),
            shape_of((tokens, width), F32),
            shape_of((tokens, width), F32),
            shape_of((tokens, 1), F32),
            shape_of((8, LANES), F32),
        ],
        cost_estimate=cost(2 * tokens * width * inner, 20 * MIB),
        name="first_norm",
    )
    return run(context, level, near, far, x, vectors)


def hidden_kernel(normed_ref, level_ref, near_ref, far_ref, b_ref, quant_ref, act_ref, slope_ref, peak_ref):
    half = normed_ref.shape[1] // 2

    @pl.when(pl.program_id(0) == 0)
    def _():
        peak_ref[...] = jnp.zeros_like(peak_ref)
        level = level_ref[2:3, 0:1]
        quant_ref[...] = low(level * jnp.tanh(normed_ref[...] / level))

    hidden = dot(quant_ref[:, :half], flat(near_ref[...]))
    hidden = hidden + dot(quant_ref[:, half:], flat(far_ref[...])) + b_ref[...]
    share = 0.5 + 0.5 * lax.erf(hidden * (0.5**0.5))
    active = hidden * share
    act_ref[...] = active
    slope_ref[...] = share + hidden * ((0.5 / jnp.pi) ** 0.5 * jnp.exp(-0.5 * hidden * hidden))
    peak_ref[...] = jnp.maximum(peak_ref[...], column_peak(active))


def hidden_rows(normed, level, weights, bias, held_down, ranges):
    near, far = weights
    plane, parts, rows, c = near.shape
    tokens, width = normed.shape
    step = min(c, 512)
    cuts = c // step
    weight_spec = pl.BlockSpec((plane, None, rows, step), lambda s: (0, s // cuts, 0, s % cuts))
    block = pl.BlockSpec((tokens, step), lambda s: (0, s))
    run = hosted_call(
        hidden_kernel,
        [(held_down, ())],
        6,
        ranges,
        level,
        3,
        3,
        grid=(parts * cuts,),
        in_specs=[
            whole(normed),
            whole(level),
            weight_spec,
            weight_spec,
            pl.BlockSpec((1, step), lambda s: (0, s)),
        ],
        out_specs=[
            pl.BlockSpec((tokens, width), lambda s: (0, 0)),
            block,
            block,
            pl.BlockSpec((8, LANES), lambda s: (0, 0)),
        ],
        out_shape=[
            shape_of((tokens, width), BF16),
            shape_of((tokens, parts * c), F32),
            shape_of((tokens, parts * c), F32),
            shape_of((8, LANES), F32),
        ],
        cost_estimate=cost(2 * tokens * width * parts * c, 50 * MIB),
        name="hidden",
    )
    return run(normed, level, near, far, bias)


def second_norm_kernel(
    order_ref, act_ref, level_ref, near_a, far_a, near_b, far_b, normed_ref, grad_ref, row_ref,
    quant_ref, out_ref, sum_ref, branch_ref, terms_ref
):
    level = level_ref[3:4, 0:1]
    quant = low(level * jnp.tanh(act_ref[...] / level))
    quant_ref[...] = quant
    vectors = take_blocks(row_ref, order_ref)
    summed = normed_ref[...] + project(quant, near_a, far_a, near_b, far_b) + vectors[3:4, :]
    normal, inverse = norm_parts(summed)
    gain = vectors[4:5, :]
    put_blocks(out_ref, order_ref, low(normal * gain + vectors[5:6, :]))
    upstream = take_blocks(grad_ref, order_ref).astype(F32)
    grad_sum = norm_back(upstream, normal, inverse, gain)
    sum_ref[...] = grad_sum
    branch_ref[...] = low(grad_sum)
    add_sums(terms_ref, order_ref, (grad_sum, upstream * normal, upstream))


def second_norm(active, level, weights, normed, grad, vectors, order):
    tokens, width = normed.shape
    inner = active.shape[1]
    rows = 256

    def block(columns):
        return pl.BlockSpec((rows, columns), lambda t: (t, 0))

    return pl.pallas_call(
        second_norm_kernel,
        grid=(tokens // rows,),
        in_specs=[
            in_smem(),
            block(inner),
            whole(level),
            *[whole(side) for side in weights],
            block(width),
            block(width),
            whole(vectors),
        ],
        out_specs=[
            block(inner),
            block(width),
            block(width),
            block(width),
            pl.BlockSpec((8, width), lambda t: (0, 0)),
        ],
        out_shape=[
            shape_of((tokens, inner), BF16),
            shape_of((tokens, width), BF16),
            shape_of((tokens, width), F32),
            shape_of((tokens, width), BF16),
            shape_of((8, width), F32),
        ],
        compiler_params=params(),
        cost_estimate=cost(2 * tokens * width * inner, 80 * MIB),
        name="second_norm",
    )(order, active, level, *weights, normed, grad, vectors)


def weight_specs(xs, products, parts, plane, c):
    tokens, width = xs[0].shape
    count = len(products)
    step = min(c, 1024)
    cuts = c // step
    dims = (plane, parts, count, width // (2 * plane), c)
    in_specs = [
        pl.BlockSpec((tokens, step), lambda r, j, first=first: (0, (r + first) * cuts + j))
        for _, _, first in products
    ]
    out_spec = pl.BlockSpec((plane, None, count, dims[3], step), lambda r, j: (0, r, 0, 0, j))
    estimate = cost(tokens * width * parts * c * count, 20 * MIB)
    return dims, (parts, cuts), in_specs, out_spec, estimate


def turn_once(x_refs, turned_refs):
    @pl.when((pl.program_id(0) == 0) & (pl.program_id(1) == 0))
    def _():
        for x_ref, turned_ref in zip(x_refs, turned_refs):
            turned_ref[...] = x_ref[...].T


def weight_send_kernel(count, which, *refs):
    x_refs, h_refs = refs[:count], refs[count : count + len(which)]
    send_ref, turned = refs[count + len(which)], refs[count + len(which) + 1 :]
    turn_once(x_refs, turned)
    for i, h_ref in enumerate(h_refs):
        h = h_ref[...]
        total = dot(turned[which[i]][...], h)
        send_ref[:, i] = low(total).reshape(send_ref.shape[0], -1, h.shape[1])


def weight_send(xs, products, parts, plane, c):
    dims, grid, in_specs, out_spec, estimate = weight_specs(xs, products, parts, plane, c)
    tokens, width = xs[0].shape
    return pl.pallas_call(
        partial(weight_send_kernel, len(xs), [product[0] for product in products]),
        grid=grid,
        in_specs=[pl.BlockSpec((tokens, width // 2), lambda r, j: (0, 1))] * len(xs) + in_specs,
        out_specs=out_spec,
        out_shape=shape_of(dims, BF16),
        scratch_shapes=[pltpu.VMEM((width // 2, tokens), BF16)] * len(xs),
        compiler_params=params(),
        cost_estimate=estimate,
        name="weight_send",
    )(*xs, *[product[1] for product in products])


def weight_keep_kernel(count, which, split, *refs):
    x_refs, other_ref = refs[:count], refs[count]
    h_refs = refs[count + 1 : count + 1 + len(which)]
    outs, turned = refs[count + 1 + len(which) : -count], refs[-count:]
    half = pl.num_programs(0) // 2
    turn_once(x_refs, turned)
    for side in range(2):

        @pl.when(pl.program_id(0) // half == side)
        def _(side=side):
            keep_ref, send_ref = outs[2 * side : 2 * side + 2]
            for i, h_ref in enumerate(h_refs):
                h = h_ref[...]
                total = dot(turned[which[i]][...], h).reshape(other_ref.shape[0], -1, h.shape[1])
                for j, slot in enumerate(split[side][0]):
                    keep_ref[j, i] = total[slot] + other_ref[slot, i].astype(F32)
                for j, slot in enumerate(split[side][1]):
                    send_ref[j, i] = low(total[slot] + other_ref[slot, i].astype(F32))


def weight_keep(xs, products, other, parts, plane, c):
    dims, (_, cuts), in_specs, out_spec, estimate = weight_specs(xs, products, parts, plane, c)
    tokens, width = xs[0].shape
    half = parts // 2
    block = (plane // 2, None, dims[2], dims[3], c // cuts)
    near = pl.BlockSpec(
        block, lambda r, j: (0, jnp.minimum(r, half - 1), 0, 0, jnp.where(r < half, j, cuts - 1))
    )
    far = pl.BlockSpec(block, lambda r, j: (0, jnp.maximum(r - half, 0), 0, 0, jnp.where(r < half, 0, j)))
    small = (plane // 2, half) + dims[2:]
    which = [product[0] for product in products]
    keep_a, send_a, keep_b, send_b = pl.pallas_call(
        partial(weight_keep_kernel, len(xs), which, first_split(bits_of("dp") - 1)),
        grid=(parts, cuts),
        in_specs=[pl.BlockSpec((tokens, width // 2), lambda r, j: (0, 0))] * len(xs)
        + [out_spec]
        + in_specs,
        out_specs=[near, near, far, far],
        out_shape=[shape_of(small, F32), shape_of(small, BF16)] * 2,
        scratch_shapes=[pltpu.VMEM((width // 2, tokens), BF16)] * len(xs),
        compiler_params=params(),
        cost_estimate=estimate,
        name="weight_keep",
    )(*xs, other, *[product[1] for product in products])
    return [keep_a, keep_b], [send_a, send_b]


def grad_hidden_kernel(
    cuts, order_ref, g_ref, near_a, far_a, near_b, far_b, act_ref, slope_ref, level_ref, o_ref, sum_ref
):
    half = g_ref.shape[1] // 2
    block = pl.program_id(0)
    columns = act_ref.shape[1]
    level = level_ref[3:4, 0:1]

    @pl.when(block == 0)
    def _():
        sum_ref[...] = jnp.zeros_like(sum_ref)

    for side, (near_ref, far_ref) in enumerate(((near_a, far_a), (near_b, far_b))):

        @pl.when(block * 2 // pl.num_programs(0) == side)
        def _(near_ref=near_ref, far_ref=far_ref):
            grad = dot(g_ref[:, :half], flat(near_ref[...])) + dot(g_ref[:, half:], flat(far_ref[...]))
            tangent = jnp.tanh(act_ref[...] / level)
            grad = low(grad * ((1.0 - tangent * tangent) * slope_ref[...]))
            o_ref[...] = grad
            total = jnp.sum(grad.astype(F32), axis=0, keepdims=True)
            start = pl.multiple_of((block % cuts) * columns, LANES)
            sum_ref[pl.ds(order_ref[block // cuts], 1), pl.ds(start, columns)] = total


def grad_hidden_rows(grad, weights, active, slope, level, part_order):
    plane, half, rows, c = weights[0].shape
    parts = 2 * half
    tokens, width = grad.shape
    step = min(c, 1024)
    cuts = c // step
    block = (plane, None, rows, step)
    first = pl.BlockSpec(
        block,
        lambda s: (0, jnp.minimum(s // cuts, half - 1), 0, jnp.where(s < half * cuts, s % cuts, cuts - 1)),
    )
    last = pl.BlockSpec(
        block,
        lambda s: (0, jnp.maximum(s // cuts - half, 0), 0, jnp.where(s < half * cuts, 0, s % cuts)),
    )
    block = pl.BlockSpec((tokens, step), lambda s: (0, s))
    return pl.pallas_call(
        partial(grad_hidden_kernel, cuts),
        grid=(parts * cuts,),
        in_specs=[in_smem(), whole(grad), first, first, last, last, block, block, whole(level)],
        out_specs=[block, pl.BlockSpec((parts, c), lambda s: (0, 0))],
        out_shape=[shape_of((tokens, parts * c), BF16), shape_of((parts, c), F32)],
        compiler_params=params(),
        cost_estimate=cost(2 * tokens * width * parts * c, 34 * MIB),
        name="grad_hidden",
    )(part_order, grad, *weights, active, slope, level)


def first_back_kernel(
    order_ref, g_ref, near_ref, far_ref, normed_ref, normal_ref, inverse_ref, sum_two_ref, level_ref, row_ref,
    sum_ref, low_ref, terms_ref
):
    level = level_ref[2:3, 0:1]
    tangent = jnp.tanh(normed_ref[...] / level)
    grad = project(g_ref[...], near_ref, far_ref) * (1.0 - tangent * tangent) + sum_two_ref[...]
    normal = normal_ref[...]
    gain = take_blocks(row_ref, order_ref)[1:2, :]
    grad_sum = norm_back(grad, normal, inverse_ref[...], gain)
    sum_ref[...] = grad_sum
    low_ref[...] = low(grad_sum)
    add_sums(terms_ref, order_ref, (grad_sum, grad * normal, grad))


def first_back(grad, weights, normed, normal, inverse, sum_two, level, vectors, order):
    near, far = weights
    tokens, width = normed.shape
    inner = grad.shape[1]
    rows = 256

    def block(columns):
        return pl.BlockSpec((rows, columns), lambda t: (t, 0))

    return pl.pallas_call(
        first_back_kernel,
        grid=(tokens // rows,),
        in_specs=[
            in_smem(),
            block(inner),
            whole(near),
            whole(far),
            block(width),
            block(width),
            block(1),
            block(width),
            whole(level),
            whole(vectors),
        ],
        out_specs=[block(width), block(width), pl.BlockSpec((8, width), lambda t: (0, 0))],
        out_shape=[
            shape_of((tokens, width), F32),
            shape_of((tokens, width), BF16),
            shape_of((8, width), F32),
        ],
        compiler_params=params(),
        cost_estimate=cost(2 * tokens * width * inner, 36 * MIB),
        name="first_back",
    )(order, grad, near, far, normed, normal, inverse, sum_two, level, vectors)


def grad_context_kernel(g_ref, near_ref, far_ref, ctx_ref, level_ref, o_ref):
    half = g_ref.shape[1] // 2
    level = level_ref[1:2, 0:1]
    tangent = jnp.tanh(ctx_ref[...] / level)
    grad = dot(g_ref[:, :half], flat(near_ref[...])) + dot(g_ref[:, half:], flat(far_ref[...]))
    o_ref[...] = low(grad * (1.0 - tangent * tangent))


def grad_context_rows(grad, weights, context, level):
    near, far = weights
    plane, parts, rows, c = near.shape
    tokens, width = grad.shape
    weight_spec = pl.BlockSpec((plane, None, rows, c), lambda r: (0, r, 0, 0))
    block = pl.BlockSpec((tokens, c), lambda r: (0, r))
    return pl.pallas_call(
        grad_context_kernel,
        grid=(parts,),
        in_specs=[
            whole(grad),
            weight_spec,
            weight_spec,
            block,
            whole(level),
        ],
        out_specs=block,
        out_shape=shape_of((tokens, parts * c), BF16),
        compiler_params=params(),
        cost_estimate=cost(2 * tokens * width * parts * c, 10 * MIB),
        name="grad_context",
    )(grad, near, far, context, level)


def grad_input_kernel(order_ref, *refs):
    g_refs, (near_ref, far_ref, sum_ref, x_ref, level_ref, o_ref) = refs[:6], refs[6:]
    level = level_ref[0:1, 0:1]
    half = near_ref.shape[1] // 2
    total = None
    for side in range(2):
        for i in range(3):
            term = project(
                g_refs[side * 3 + i][...],
                near_ref.at[:, side * half : (side + 1) * half, i],
                far_ref.at[:, side * half : (side + 1) * half, i],
            )
            total = term if total is None else total + term
    tangent = jnp.tanh(take_blocks(x_ref, order_ref).astype(F32) / level)
    put_blocks(o_ref, order_ref, low(sum_ref[...] + total * (1.0 - tangent * tangent)))


def grad_input(grads, weights, grad_sum, x, level, order):
    near, far = weights
    tokens, width = x.shape
    inner = grads[0].shape[1]
    rows = 256

    def block(columns):
        return pl.BlockSpec((rows, columns), lambda t: (t, 0))

    return pl.pallas_call(
        grad_input_kernel,
        grid=(tokens // rows,),
        in_specs=[in_smem()]
        + [block(inner)] * 6
        + [whole(near), whole(far), block(width), block(width), whole(level)],
        out_specs=block(width),
        out_shape=shape_of((tokens, width), BF16),
        compiler_params=params(),
        cost_estimate=cost(12 * tokens * width * inner, 20 * MIB),
        name="grad_input",
    )(order, *grads, near, far, grad_sum, x, level)


def place_kernel(turned, order_ref, *refs):
    d_refs, i_refs, q_refs = refs[:2], refs[2:4], refs[4:6]
    in_out, qkv_out, *turned_outs = refs[6:]
    step = pl.program_id(0)
    plane, _, rows, _ = i_refs[0].shape
    for core in range(2):
        for j in range(plane):
            here = pl.ds(pl.multiple_of(order_ref[core * plane + j] * rows, rows), rows)
            in_out[0, here, :] = i_refs[core][j, 0].astype(F32)
            if turned:
                turned_outs[0][:, here] = d_refs[core][j, 0].astype(F32).T

            @pl.when(step < 3)
            def _(core=core, j=j, here=here):
                qkv_out[0, here, :] = q_refs[core][j, 0].astype(F32)

            if turned:

                @pl.when(step == 3)
                def _(core=core, j=j, here=here):
                    turned_outs[1][:, here] = q_refs[core][j, 0].astype(F32).T


def place_grads(down, inner, first, blocks):
    plane, _, rows, c = inner[0].shape
    columns = first[0].shape[3]
    width = 2 * plane * rows
    turned = rows % LANES == 0
    cut = c // 4

    def piece(size, index):
        return [pl.BlockSpec((plane, 1, rows, size), index)] * 2

    out_specs = [
        pl.BlockSpec((1, width, cut), lambda p: (0, 0, p)),
        pl.BlockSpec((1, width, columns), lambda p: (jnp.minimum(p, 2), 0, 0)),
    ]
    out_shape = [shape_of((1, width, c), F32), shape_of((3, width, columns), F32)]
    if turned:
        out_specs.append(pl.BlockSpec((cut, width), lambda p: (p, 0)))
        out_specs.append(pl.BlockSpec((columns, width), lambda p: (0, 0)))
        out_shape += [shape_of((c, width), F32), shape_of((columns, width), F32)]
    inner_grad, qkv_grad, *rest = pl.pallas_call(
        partial(place_kernel, turned),
        grid=(4,),
        in_specs=[in_smem()]
        + piece(cut, lambda p: (0, 0, 0, p)) * 2
        + piece(columns, lambda p: (0, p, 0, 0)),
        out_specs=out_specs,
        out_shape=out_shape,
        compiler_params=params(),
        name="place_grads",
    )(blocks.astype(jnp.int32), *down, *inner, *first)
    if not turned:
        back = jnp.zeros((2 * plane,), jnp.int32).at[blocks].set(jnp.arange(2 * plane, dtype=jnp.int32))
        for near, far in (down, [side[:, 3:] for side in first]):
            split = jnp.concatenate([near, far], axis=0)[:, 0]
            rest.append(jnp.take(split, back, axis=0).astype(F32).reshape(width, -1).T)
    return inner_grad[0], qkv_grad, rest[0], rest[1]


def left_over(keeps, sends):
    return scatter_plane(keeps, sends, True)


def scatter_grad(chain, xs, products, other, token, parts, plane, c):
    return chain(*weight_keep([tie(xs[0], [token])] + xs[1:], products, other, parts, plane, c))


HOST_RANK = {first_norm_kernel: 1, attend_last_kernel: 2, hidden_kernel: 1}


def own_block(values, axis):
    rows = values.shape[axis] // lax.axis_size("dp")
    return lax.dynamic_slice_in_dim(values, lax.axis_index("dp") * rows, rows, axis)


def local(
    mesh, layer_input, grad_output, doc_lengths, ranges, w_qkv, bias_qv, w_out, b_out, gain_one,
    shift_one, w_in, b_in, w_down, b_down, gain_two, shift_two
):
    datas, parts = lax.axis_size("dp"), lax.axis_size("tensor")
    data, part = lax.axis_index("dp"), lax.axis_index("tensor")
    plane = datas // 2
    tokens, width = layer_input.shape
    rows = width // datas

    places = jnp.arange(datas)
    distance = (places % plane) * 2 + places // plane
    blocks = data ^ distance
    if rows % LANES == 0:
        per_block = rows // LANES
        order = (blocks[:, None] * per_block + jnp.arange(per_block)).reshape(-1).astype(jnp.int32)
    else:
        order = jnp.arange(width // LANES, dtype=jnp.int32)

    def arrange(values):
        split = values.reshape(values.shape[:-1] + (datas, rows))
        return jnp.take(split, blocks, axis=-2).reshape(values.shape)

    def restore(values):
        split = values.reshape(values.shape[:-1] + (datas, rows))
        back = jnp.zeros((datas,), jnp.int32).at[blocks].set(places.astype(jnp.int32))
        return jnp.take(split, back, axis=-2).reshape(values.shape)

    def arrange_rows(values):
        return values if rows % LANES == 0 else arrange(values)

    def restore_rows(values):
        return values if rows % LANES == 0 else restore(values)

    part_order = (part ^ jnp.arange(parts)).astype(jnp.int32)
    x = arrange_rows(layer_input)
    upstream = arrange_rows(grad_output)
    vectors = jnp.stack([b_out, gain_one, shift_one, b_down, gain_two, shift_two, b_out, b_out])
    vectors = arrange_rows(vectors).astype(F32)

    own = [
        own_block(w_qkv, 1),
        own_block(w_out, 1).T[None],
        own_block(w_in, 0)[None],
        own_block(w_down, 1).T[None],
    ]
    levels, quant_input, quant_own, slopes = prepare(ranges, x, own)
    biases = jnp.concatenate([bias_qv.reshape(-1), b_in])
    count = biases.shape[0]
    biases = jnp.pad(biases, (0, -count % (16 * LANES))).reshape(-1, LANES)
    near, far, biases, near_out, far_out, held_in = first_gather(quant_own[0], biases, *quant_own[1:3])
    weights_qkv, weights_out = (near, far), (near_out, far_out)
    biases = biases.reshape(parts, -1)[:, :count]
    columns = bias_qv.shape[1]
    bias_q = biases[:, :columns].reshape(1, -1)
    bias_v = biases[:, columns : 2 * columns].reshape(1, -1)
    bias_qkv = jnp.stack([bias_q, jnp.zeros_like(bias_q), bias_v]).astype(F32)
    bias_hidden = biases[:, 2 * columns :].reshape(1, -1).astype(F32)

    held = tokens // SEQ
    lengths_here = lax.dynamic_slice_in_dim(doc_lengths, part * held, held, 0)
    ends = jnp.cumsum(lengths_here, axis=1, dtype=jnp.int32)
    half = parts // 2 * columns

    first_moves, _ = plane_moves()

    def over_plane(values, token):
        values = tie(values, [token])
        return [far_swap(values, r) for _, r in first_moves]

    there_in = over_plane(held_in, biases)
    held_a = tie(quant_own[3], [biases])[None]
    for bit in reversed(range(bits_of("tensor") - 1)):
        other = swap(held_a, "tensor", bit)
        held_a = jnp.stack([held_a, other], axis=1).reshape((-1,) + held_a.shape[1:])
    qkv = qkv_rows(quant_input, weights_qkv, bias_qkv)
    held_a = tie(held_a, [qkv])
    there_a = over_plane(held_a, qkv)
    held_b = swap(held_a, "tensor", bits_of("tensor") - 1)
    context, lse, peak = attend(qkv, ends)
    there_in, there_a = [tie(values, [peak]) for values in there_in], [tie(values, [peak]) for values in there_a]
    (context, lse, _), levels, (*weights_in, near_a, far_a) = attend(
        qkv, ends, lse, peak, context, [(held_in, there_in), (held_a, there_a)], ranges, levels
    )
    weights_in = tuple(side[:, :, 0] for side in weights_in)
    weights_out = tuple(side[:, :, 0] for side in weights_out)
    (quant_context, normed, normal_one, inverse_one, _), levels, _ = first_norm(
        context, levels, weights_out, x, vectors, ranges
    )
    held_b = tie(held_b, [levels])
    (quant_normed, active, slope, _), levels, (near_b, far_b) = hidden_rows(
        normed, levels, weights_in, bias_hidden, held_b, ranges
    )
    weights_down = [side[:, :, 0] for side in (near_a, far_a, near_b, far_b)]
    quant_active, output, grad_sum_two, grad_branch, terms_two = second_norm(
        active, levels, weights_down, normed, upstream, vectors, order
    )

    wide = b_in.shape[0]
    other = weight_send([grad_branch], [(0, quant_active, 0)], parts, plane, wide)
    grad_after = tie(grad_branch, [other])
    other = swap(other, "dp", 0)
    grad_hidden, sum_hidden = grad_hidden_rows(
        grad_after, weights_down, active, slope, levels, part_order
    )
    down = scatter_grad(
        scatter_all, [grad_branch], [(0, quant_active, 0)], other, sum_hidden, parts, plane, wide
    )
    grad_hidden = tie(grad_hidden, next(down))
    other = weight_send([quant_normed], [(0, grad_hidden, 0)], parts, plane, wide)
    grad_after = tie(grad_hidden, [other])
    other = swap(other, "dp", 0)
    grad_sum_one, grad_attention, terms_one = first_back(
        grad_after, weights_in, normed, normal_one, inverse_one, grad_sum_two, levels, vectors, order
    )
    grad_hidden = tie(grad_hidden, down.send(terms_one))
    inner = scatter_grad(
        scatter_all, [quant_normed], [(0, grad_hidden, 0)], other, terms_one, parts, plane, wide
    )
    grad_after = tie(grad_attention, next(inner))
    grad_context = grad_context_rows(grad_after, weights_out, context, levels)
    grad_context = tie(grad_context, down.send(grad_context))
    sums_before = jnp.zeros((8, 2 * half), F32)
    *grads, token = attend_back(
        qkv, grad_context, ends, lse, sums_before, part_order, columns, 0
    )
    grads_a = grads
    xs = [quant_input, grad_attention]
    products_a = [(0, grad, 0) for grad in grads] + [(1, quant_context, 0)]
    other_a = weight_send(xs, products_a, parts // 2, plane, columns)
    token_a = other_a
    grad_context = tie(grad_context, inner.send(token_a) + down.send(token_a))
    other_a = swap(other_a, "dp", 0)
    *grads, token = attend_back(
        qkv, grad_context, ends, lse, token, part_order, columns, half
    )
    sum_qv = token
    down = run_all(down, token)
    grads[0] = tie(grads[0], inner.send(token) + [down[1]])
    products_b = [(0, grad, 0) for grad in grads] + [(1, quant_context, parts // 2)]
    other_b = weight_send(xs, products_b, parts // 2, plane, columns)
    token = other_b
    other_b = swap(other_b, "dp", 0)
    first_a = scatter_grad(left_over, xs, products_a, other_a, token, parts // 2, plane, columns)
    started = next(first_a)
    first_b = scatter_grad(left_over, xs, products_b, other_b, started[0], parts // 2, plane, columns)
    started = next(first_b) + inner.send(started[0])
    grads[0] = tie(grads[0], started)
    grad_x = grad_input(grads_a + grads, weights_qkv, grad_sum_one, x, levels, order)

    sums = [terms_one[:3], terms_two[:3], sum_qv[:2], sum_hidden.reshape(-1, width)]
    if rows % LANES:
        sums[0], sums[1] = restore(sums[0]), restore(sums[1])
    sums = jnp.concatenate(sums)
    padded = jnp.pad(sums, ((0, -sums.shape[0] % 8), (0, 0)))
    inner, first_a, first_b = [run_all(chain, grad_x) for chain in (inner, first_a, first_b)]
    (down, inner, first), sums = finale(down, inner, first_a + first_b, slopes, padded)
    hidden_all = sums[8 : 8 + sum_hidden.size // width].reshape(-1)
    grad_bias_qv = lax.dynamic_slice_in_dim(sums[6:8], part * columns, columns, 1)
    grad_b_in = lax.dynamic_slice_in_dim(hidden_all, part * b_in.shape[0], b_in.shape[0], 0)
    grad_w_in, grad_w_qkv, grad_w_down, grad_w_out = place_grads(down, inner, first, blocks)
    new_ranges = levels[:4, 0]
    return (
        restore_rows(output),
        restore_rows(grad_x),
        grad_w_qkv,
        grad_bias_qv,
        grad_w_out,
        sums[0],
        sums[1],
        sums[2],
        grad_w_in,
        grad_b_in,
        grad_w_down,
        sums[3],
        sums[4],
        sums[5],
        new_ranges,
    )


def solution(mesh):
    in_specs = (
        P(("dp", "tensor"), None),
        P(("dp", "tensor"), None),
        P("dp", None),
        P(),
        P(None, None, "tensor"),
        P(None, "tensor"),
        P("tensor", None),
        P(),
        P(),
        P(),
        P(None, "tensor"),
        P("tensor"),
        P("tensor", None),
        P(),
        P(),
        P(),
    )
    out_specs = (
        P(("dp", "tensor"), None),
        P(("dp", "tensor"), None),
        P(None, None, "tensor"),
        P(None, "tensor"),
        P("tensor", None),
        P(),
        P(),
        P(),
        P(None, "tensor"),
        P("tensor"),
        P("tensor", None),
        P(),
        P(),
        P(),
        P(),
    )
    return jax.shard_map(
        partial(local, mesh), mesh=mesh, in_specs=in_specs, out_specs=out_specs, check_vma=False
    )
```

```python
from functools import partial

import jax
import jax.numpy as jnp
from jax import lax
from jax.experimental import pallas as pl
from jax.experimental.pallas import tpu as pltpu
from jax.sharding import PartitionSpec as P

HD = 64
SEQ = 512
LANES = 128

EPS = 1e-06
DECAY = 0.9
MASKED = -1e30
MESH = pl.DeviceIdType.MESH
F32 = jnp.float32
BF16 = jnp.bfloat16
MIB = 1024 * 1024


def shape_of(dims, kind):
    return jax.ShapeDtypeStruct(dims, kind)


def params(**rest):
    return pltpu.CompilerParams(vmem_limit_bytes=60 * MIB, **rest)


def in_smem():
    return pl.BlockSpec(memory_space=pltpu.SMEM)


def cost(flops, moved):
    return pl.CostEstimate(flops=int(flops) // 1000, bytes_accessed=int(moved) // 1000, transcendentals=0)


def dot(first, second):
    return jnp.dot(first, second, preferred_element_type=F32)


def dot_cols(first, second):
    return lax.dot_general(first, second, (((1,), (1,)), ((), ())), preferred_element_type=F32)


def dot_rows(first, second):
    return lax.dot_general(first, second, (((0,), (0,)), ((), ())), preferred_element_type=F32)


def flat(block):
    return block.reshape(block.shape[0] * block.shape[1], block.shape[2])


def tie(values, others):
    return lax.optimization_barrier((values, *others))[0]


def swap(values, axis, bit, token=None):
    count = lax.axis_size(axis)
    other = lax.ppermute(values, axis, [(i, i ^ (1 << bit)) for i in range(count)])
    return other if token is None else tie(other, [token])


def far_swap(values, r):
    count = lax.axis_size("dp")
    return lax.ppermute(values, "dp", [(i, i ^ r) for i in range(count)])


def bits_of(axis):
    return lax.axis_size(axis).bit_length() - 1


def plane_orders():
    plane = list(range(1, bits_of("dp")))
    return plane, (plane[::-1], plane)


def run_all(chain, token=None):
    try:
        chain.send(token)
        while True:
            next(chain)
    except StopIteration as done:
        return done.value


def low(values):
    return values.astype(BF16)


def first_split(plane_bits):
    _, orders = plane_orders()
    split = []
    for order in orders:
        bit = order[0] - 1
        split.append([[s for s in range(1 << plane_bits) if (s >> bit) & 1 == away] for away in (0, 1)])
    return split


def scatter_plane(keeps, sends, left_over=False):
    plane, orders = plane_orders()
    left = [[bit for bit in plane[::-1] if bit != order[0]] for order in orders]
    sides = [keep.reshape((2,) * len(left[0]) + keep.shape[1:]) for keep in keeps]
    sends = [send.reshape(side.shape) for side, send in zip(sides, sends)]
    for step in range(len(plane)):
        if step:
            places = [left[i].index(orders[i][step]) for i in range(2)]
            sends = [low(lax.index_in_dim(sides[i], 1, places[i], keepdims=False)) for i in range(2)]
            sides = [lax.index_in_dim(sides[i], 0, places[i], keepdims=False) for i in range(2)]
            for i in range(2):
                left[i].remove(orders[i][step])
        token = yield sends
        others = [swap(sends[i], "dp", orders[i][step], token) for i in range(2)]
        if left_over and step == len(plane) - 2:
            return list(zip(sides, others))
        sides = [side + other.astype(F32) for side, other in zip(sides, others)]
    return sides


def scatter_all(keeps, sends):
    sides = yield from scatter_plane(keeps, sends)
    last = bits_of("tensor") - 1
    for bit in range(last):
        pairs = [values.reshape((-1, 2) + values.shape[1:]) for values in sides]
        send = jnp.concatenate([low(values[:, 1]) for values in pairs])
        token = yield [send]
        others = jnp.split(swap(send, "tensor", bit, token), 2)
        sides = [values[:, 0] + other.astype(F32) for values, other in zip(pairs, others)]
    send = low(sides[1][0])
    token = yield [send]
    return sides[0][0], swap(send, "tensor", last, token)


def at_distance(axis, r):
    me, index = lax.axis_index(axis), 0
    for bit in range(bits_of(axis)):
        index = index + (me // (1 << bit) + (r >> bit)) % 2 * (1 << bit)
    return index


def plane_moves():
    plane = 1 << (bits_of("dp") - 1)
    if plane == 4:
        return [(1, 2), (2, 4)], [(3, 1, 4, 0), (3, 2, 2, 1)]
    return [(slot, 2 * slot) for slot in range(1, plane)], []


class Mover:
    def __init__(self, send, recv, local):
        self.send, self.recv, self.local = send, recv, local
        self.count, self.local_count = 0, 0

    def remote(self, source, target, axis, r):
        i = self.count
        self.count += 1
        return pltpu.make_async_remote_copy(
            src_ref=source,
            dst_ref=target,
            send_sem=self.send.at[i],
            recv_sem=self.recv.at[i],
            device_id={axis: at_distance(axis, r)},
            device_id_type=MESH,
        )

    def own(self, source, target):
        i = self.local_count
        self.local_count += 1
        return pltpu.make_async_copy(source, target, self.local.at[i])


def call_out(distances):
    for axis, r in distances:
        pl.semaphore_signal(
            pltpu.get_barrier_semaphore(),
            inc=1,
            device_id={axis: at_distance(axis, r)},
            device_id_type=MESH,
        )


def await_all(distances):
    pl.semaphore_wait(pltpu.get_barrier_semaphore(), len(distances))


def greet(distances):
    call_out(distances)
    await_all(distances)


def part_distances():
    return [("tensor", r) for r in range(1, 1 << bits_of("tensor"))]


def plane_distances():
    first, second = plane_moves()
    apart = sorted({move[1] for move in first} | {move[2] for move in second} | {1})
    return [("dp", r) for r in apart]


def halves_of(ref, half):
    rows = ref.shape[-2] // 2
    return ref.at[..., half * rows : (half + 1) * rows, :]


def slots(ref, *inner):
    return lambda slot: ref.at[(slot,) + inner]


def low_bit(r):
    return r & -r


class AlongParts:
    def __init__(self, mover, own, place):
        parts = 1 << bits_of("tensor")
        self.copy = mover.own(own, place(0))
        self.moves, self.there = {}, {0}
        for r in range(1, parts):
            rest = r - low_bit(r)
            source = own if rest == 0 else place(rest)
            self.moves[r] = mover.remote(source, place(r), "tensor", low_bit(r))
        self.order = sorted(self.moves, key=lambda r: (bin(r).count("1"), -r))

    def start(self):
        self.copy.start()
        for r in self.order:
            if r == low_bit(r):
                self.moves[r].start()

    def arrive(self, r):
        if r not in self.there:
            self.moves[r].wait_recv()
            self.there.add(r)

    def hand_on(self):
        for r in self.order:
            if r != low_bit(r):
                self.arrive(r - low_bit(r))
                self.moves[r].start()

    def finish(self):
        self.copy.wait()
        for r, move in self.moves.items():
            self.arrive(r)
            move.wait_send()


class OverPlane:
    def __init__(self, mover, held, near, far, given=(), via=None):
        first, second = plane_moves()
        plane = 1 << (bits_of("dp") - 1)
        sources = [held] + (list(given) or [near(slot) for slot, _ in first])
        here = [held] + list(given)
        self.loads = [] if via is None else [mover.own(here[i], via.at[i]) for i in range(len(here))]
        self.copies = [
            mover.own(here[i] if via is None else via.at[i], near(i)) for i in range(len(here))
        ]
        self.first = [] if given else [mover.remote(held, near(slot), "dp", r) for slot, r in first]
        self.second = [
            mover.remote(halves_of(sources[source], half), halves_of(near(slot), half), "dp", r)
            for slot, source, r, half in second
        ]
        sources += [near(slot) for slot in range(len(sources), plane)]
        self.cores = [mover.remote(values, far(i), "dp", 1) for i, values in enumerate(sources)]
        self.early = 1 + len(first)

    def start(self):
        for copy in self.loads or self.copies:
            copy.start()
        for move in self.first:
            move.start()
        self.cores[0].start()

    def relay(self):
        for move in self.first:
            move.wait_recv()
        for move in self.second + self.cores[1 : self.early]:
            move.start()

    def settle(self):
        for load, copy in zip(self.loads, self.copies):
            load.wait()
            copy.start()

    def complete(self):
        for move in self.second:
            move.wait_recv()
        for move in self.cores[self.early :]:
            move.start()

    def finish(self):
        for move in self.first + self.second:
            move.wait_send()
        for move in self.cores:
            move.wait()
        for copy in self.copies:
            copy.wait()


def plane_counts(given):
    first, second = plane_moves()
    plane = 1 << (bits_of("dp") - 1)
    return len(second) + plane + (0 if given else len(first)), 2 + 2 * given


def copy_semaphores(remote, local):
    copies = pltpu.SemaphoreType.DMA
    return [copies((remote,)), copies((remote,)), copies((local,))]


def anywhere():
    return pl.BlockSpec(memory_space=pltpu.HBM)


def all_distances():
    return [("dp", r) for r in range(1, 1 << bits_of("dp"))] + part_distances()


class Peaks:
    def __init__(self, mover, mine, near, mid, far):
        self.mine, self.near, self.mid, self.far = mine, near, mid, far
        self.first = [mover.remote(mine, near.at[r], "dp", r) for r in range(1, near.shape[0])]
        self.second = [mover.remote(mid, far.at[r], axis, r) for axis, r in part_distances()]

    def reach(self, values):
        self.mine[...] = values
        for moves, source, held in (
            (self.first, self.mine, self.near),
            (self.second, self.mid, self.far),
        ):
            for move in moves:
                move.start()
            held[0] = source[...]
            for move in moves:
                move.wait()
            values = jnp.max(held[...], axis=0)
            self.mid[...] = values
        return values


def peak_scratch():
    datas, parts = 1 << bits_of("dp"), 1 << bits_of("tensor")
    tile = (8, LANES)
    return [pltpu.VMEM(dims, F32) for dims in (tile, (datas,) + tile, tile, (parts,) + tile)]


def peak_moves():
    return (1 << bits_of("dp")) + (1 << bits_of("tensor")) - 2


def hosting(body, counts, given, row, peak):
    ins, outs = counts
    sources = sum(1 + count for count in given)

    def kernel(*refs):
        body_ins, (range_ref, before_ref) = refs[:ins], refs[ins : ins + 2]
        held, rest = list(refs[ins + 2 : ins + 2 + sources]), refs[ins + 2 + sources :]
        body_outs, level_ref = rest[:outs], rest[outs]
        sides, rest = rest[outs + 1 : outs + 1 + 2 * len(given)], rest[outs + 1 + 2 * len(given) :]
        body_scratch, vias = rest[: -7 - len(given)], rest[-7 - len(given) : -7]
        mover = Mover(*rest[-3:])
        peaks = Peaks(mover, *rest[-7:-3])
        weights = []
        for i, count in enumerate(given):
            own, *there = [held.pop(0) for _ in range(1 + count)]
            near, far = slots(sides[2 * i]), slots(sides[2 * i + 1])
            weights.append((OverPlane(mover, own, near, far, there, vias[i]), count))
        step, steps = 0, 1
        for i in range(HOST_RANK[body]):
            step = step * pl.num_programs(i) + pl.program_id(i)
            steps = steps * pl.num_programs(i)

        @pl.when(step == 0)
        def _():
            call_out(all_distances())
            if weights:
                await_all(all_distances())
            for weight, count in weights:
                weight.start()
                if count:
                    weight.relay()

        @pl.when(step == steps * 5 // 8)
        def _():
            for weight, count in weights:
                weight.settle()
                if not count:
                    weight.relay()

        body(*body_ins, *body_outs, *body_scratch)

        @pl.when(step == steps - 1)
        def _():
            if not weights:
                await_all(all_distances())
            for weight, _ in weights:
                weight.complete()
            largest = jnp.max(peaks.reach(body_outs[peak][...]), keepdims=True)
            level = DECAY * range_ref[row] + (1.0 - DECAY) * largest
            places = lax.broadcasted_iota(jnp.int32, level_ref.shape, 0)
            level_ref[...] = jnp.where(places == row, level, before_ref[...])
            for weight, _ in weights:
                weight.finish()

    return kernel


def hosted_call(body, weights, cid, ranges, levels, row, peak, *, grid, in_specs, out_specs, out_shape, scratch_shapes=(), **rest):
    plane = 1 << (bits_of("dp") - 1)
    counts = (len(in_specs), len(out_specs))
    given = [len(there) for _, there in weights]
    totals = [sum(column) for column in zip((peak_moves(), 1), *[plane_counts(count) for count in given])]
    small = pl.BlockSpec((8, LANES), lambda *steps: (0, 0))
    out_shape, vias, sources = out_shape + [shape_of((8, LANES), F32)], [], []
    for held, there in weights:
        out_shape += [shape_of((plane,) + held.shape, held.dtype)] * 2
        vias.append(pltpu.VMEM((1 + len(there),) + held.shape, held.dtype))
        sources += [held] + list(there)
    call = pl.pallas_call(
        hosting(body, counts, given, row, peak),
        grid=grid,
        in_specs=in_specs + [in_smem(), small] + [anywhere()] * len(sources),
        out_specs=out_specs + [small] + [anywhere()] * 2 * len(weights),
        out_shape=out_shape,
        scratch_shapes=list(scratch_shapes) + vias + peak_scratch() + copy_semaphores(*totals),
        compiler_params=params(collective_id=cid, has_side_effects=True),
        **rest,
    )

    def run(*args):
        results = call(*args, ranges, levels, *sources)
        return results[: counts[1]], results[counts[1]], results[counts[1] + 1 :]

    return run


def first_gather_kernel(
    first_ref, bias_ref, out_ref, in_ref, near, far, held_bias, near_out, far_out, held_in, held_out, send, recv, own
):
    mover = Mover(send, recv, own)
    parts, plane = near.shape[1], near.shape[0]
    moves, relays = plane_moves()
    along = AlongParts(mover, first_ref, lambda r: near.at[0, r])
    sources = [first_ref] + [near.at[0, r] for r in range(1, parts)]
    over = [[mover.remote(sources[r], near.at[slot, r], "dp", d) for slot, d in moves] for r in range(parts)]
    again = [
        [
            mover.remote(halves_of(near.at[source, r], half), halves_of(near.at[slot, r], half), "dp", d)
            for slot, source, d, half in relays
        ]
        for r in range(parts)
    ]
    cores = [
        [mover.remote(sources[r] if slot == 0 else near.at[slot, r], far.at[slot, r], "dp", 1) for slot in range(plane)]
        for r in range(parts)
    ]
    later = [
        AlongParts(mover, source, lambda r, held=held: held.at[r])
        for source, held in ((bias_ref, held_bias), (out_ref, held_out), (in_ref, held_in))
    ]
    outer = OverPlane(mover, held_out, slots(near_out), slots(far_out))
    greet(part_distances() + plane_distances())
    along.start()
    for move in over[0] + cores[0][:1]:
        move.start()
    along.hand_on()
    for units in later[:2]:
        units.start()
    for r in along.order:
        along.arrive(r)
        for move in over[r] + cores[r][:1]:
            move.start()
    for units in later[:2]:
        units.hand_on()
    later[2].start()
    later[1].finish()
    outer.start()
    later[2].hand_on()
    order = [0] + along.order
    for r in order:
        for i, (slot, _) in enumerate(moves):
            over[r][i].wait_recv()
            cores[r][slot].start()
        for move in again[r]:
            move.start()
    outer.relay()
    for r in order:
        for move in again[r]:
            move.wait_recv()
        for slot in range(1 + len(moves), plane):
            cores[r][slot].start()
    along.finish()
    for r in range(parts):
        for move in over[r] + again[r]:
            move.wait_send()
        for move in cores[r]:
            move.wait()
    outer.complete()
    outer.finish()
    for units in (later[0], later[2]):
        units.finish()


def first_gather(first, biases, outer, inner):
    parts, plane = 1 << bits_of("tensor"), 1 << (bits_of("dp") - 1)
    moves, relays = plane_moves()
    remote = 4 * (parts - 1) + parts * (len(moves) + len(relays) + plane) + plane_counts(0)[0]
    return pl.pallas_call(
        first_gather_kernel,
        in_specs=[pl.BlockSpec(memory_space=pltpu.VMEM)] * 4,
        out_specs=[anywhere()] * 6,
        out_shape=[shape_of((plane, parts) + first.shape, BF16)] * 2
        + [shape_of((parts,) + biases.shape, BF16)]
        + [shape_of((plane, parts) + outer.shape, BF16)] * 2
        + [shape_of((parts,) + inner.shape, BF16)],
        scratch_shapes=[pltpu.VMEM((parts,) + outer.shape, BF16)] + copy_semaphores(remote, 5),
        compiler_params=params(collective_id=3, has_side_effects=True),
        name="first_gather",
    )(first, biases, outer, inner)


CHUNK = 2


def finale_kernel(
    down_sum, down_more, in_sum, in_more, keep_0, more_0, keep_1, more_1, keep_2, more_2, keep_3, more_3,
    slope_q, slope_in, slope_down, sums_ref, near_d, far_d, near_i, far_i, near_q, far_q, sums_out,
    piece_d, piece_i, send_q, recv_q, piece_q, send_p, recv_p, sums_near, sums_mid, sums_far, send, recv, own
):
    mover = Mover(send, recv, own)
    _, orders = plane_orders()
    keeps, mores = (keep_0, keep_1, keep_2, keep_3), (more_0, more_1, more_2, more_3)
    quarter, kinds = keep_0.shape[1:3]
    parts, datas, chunks = 4 * quarter, sums_near.shape[0], kinds // CHUNK
    steps = [
        [mover.remote(send_p.at[k, i], recv_p.at[k, i], "dp", 1 << orders[i % 2][-1]) for i in range(4)]
        for k in range(chunks)
    ]
    along = [
        [mover.remote(send_q.at[k, r - 1], recv_q.at[k, r - 1], axis, r) for axis, r in part_distances()]
        for k in range(chunks)
    ]
    down = OverPlane(mover, piece_d, slots(near_d), slots(far_d))
    inner = OverPlane(mover, piece_i, slots(near_i), slots(far_i))
    first = [
        OverPlane(
            mover,
            piece_q.at[k],
            slots(near_q, pl.ds(k * CHUNK, CHUNK)),
            slots(far_q, pl.ds(k * CHUNK, CHUNK)),
        )
        for k in range(chunks)
    ]
    me = lax.axis_index("dp")
    sum_data = [
        mover.remote(sums_ref.at[at_distance("dp", r)], sums_near.at[r], "dp", r) for r in range(1, datas)
    ]
    sum_back = [mover.remote(sums_out.at[me], sums_out.at[me], "dp", r) for r in range(1, datas)]
    sum_part = [mover.remote(sums_mid, sums_far.at[r], axis, r) for axis, r in part_distances()]

    def kinds_of(k):
        return slice(k * CHUNK, (k + 1) * CHUNK)

    def block(k, r):
        i, j = r // quarter, r % quarter
        here = keeps[i][0, j, kinds_of(k)] + mores[i][0, j, kinds_of(k)].astype(F32)
        return here + recv_p[k, i, j].astype(F32)

    def reach(k):
        total = block(k, 0)
        for r in range(1, parts):
            along[k][r - 1].wait_recv()
            total = total + recv_q[k, r - 1].astype(F32)
        piece_q[k] = low(total * slope_q[kinds_of(k)])
        first[k].start()

    call_out(all_distances())
    for k in range(chunks):
        for i in (3, 2, 1, 0):
            more = mores[i][1, :, kinds_of(k)].astype(F32)
            send_p[k, i] = low(keeps[i][1, :, kinds_of(k)] + more)
    await_all(all_distances())
    for move in sum_data:
        move.start()
    for k in range(chunks):
        for i in (3, 2, 1, 0):
            steps[k][i].start()
    piece_d[...] = low((down_sum[...] + down_more[...].astype(F32)) * slope_down[...])
    piece_i[...] = low((in_sum[...] + in_more[...].astype(F32)) * slope_in[...])
    for k in range(chunks):
        for i in (3, 2, 1, 0):
            steps[k][i].wait_recv()
            for r in range(i * quarter, (i + 1) * quarter):
                if r:
                    send_q[k, r - 1] = low(block(k, r))
                    along[k][r - 1].start()
    down.start()
    inner.start()
    for move in sum_data:
        move.wait()
    sums_near[0] = sums_ref[me]
    sums_mid[...] = jnp.sum(sums_near[...], axis=0)
    for move in sum_part:
        move.start()
    reach(0)
    down.relay()
    inner.relay()
    for k in range(1, chunks):
        reach(k)
        first[k - 1].relay()
    for move in sum_part:
        move.wait()
    sums_far[0] = sums_mid[...]
    sums_out[me] = jnp.sum(sums_far[...], axis=0)
    for move in sum_back:
        move.start()
    first[chunks - 1].relay()
    for unit in [down, inner] + first:
        unit.complete()
    for move in sum_back:
        move.wait()
    for unit in [down, inner] + first:
        unit.finish()
    for group in steps + along:
        for move in group:
            move.wait_send()


def finale(down, inner, first, slopes, sums):
    parts, plane, datas = 1 << bits_of("tensor"), 1 << (bits_of("dp") - 1), 1 << bits_of("dp")
    pieces = [slopes[2], slopes[1], slopes[0]]
    _, quarter, kinds, rows, c = first[0][0].shape
    chunks = kinds // CHUNK
    remote = chunks * (4 + parts - 1) + (2 + chunks) * plane_counts(0)[0] + 2 * (datas - 1) + parts - 1
    dims = sums.shape
    sums = sums.reshape(datas, -1, LANES)
    own = sums.shape[1:]
    vmem = pl.BlockSpec(memory_space=pltpu.VMEM)
    scratch = [pltpu.VMEM(piece.shape, BF16) for piece in pieces[:2]]
    scratch += [pltpu.VMEM((chunks, parts - 1, CHUNK, rows, c), BF16)] * 2
    scratch += [pltpu.VMEM((chunks, CHUNK, rows, c), BF16)]
    scratch += [pltpu.VMEM((chunks, 4, quarter, CHUNK, rows, c), BF16)] * 2
    scratch += [
        pltpu.VMEM(sums.shape, F32),
        pltpu.VMEM(own, F32),
        pltpu.VMEM((parts,) + own, F32),
    ]
    out_shape = []
    for piece in pieces:
        out_shape += [shape_of((plane,) + piece.shape, BF16)] * 2
    args = [*down, *inner]
    for pair in first:
        args += list(pair)
    args += [*slopes, sums]
    results = pl.pallas_call(
        finale_kernel,
        in_specs=[vmem] * len(args),
        out_specs=[anywhere()] * 6 + [vmem],
        out_shape=out_shape + [shape_of(sums.shape, F32)],
        scratch_shapes=scratch + copy_semaphores(remote, 2 + chunks),
        compiler_params=params(collective_id=2, has_side_effects=True),
        name="finale",
    )(*args)
    return [results[2 * i : 2 * i + 2] for i in range(3)], results[6].reshape(dims)


class Order:
    def __init__(self, width):
        self.rows = width // (1 << bits_of("dp"))

    def __getitem__(self, j):
        if self.rows % LANES:
            return j
        plane, each = 1 << (bits_of("dp") - 1), self.rows // LANES
        place = j // each
        return at_distance("dp", place % plane * 2 + place // plane) * each + j % each


def take_blocks(ref, order_ref, here=slice(None)):
    return jnp.concatenate(
        [
            ref[here, pl.ds(pl.multiple_of(order_ref[j] * LANES, LANES), LANES)]
            for j in range(ref.shape[1] // LANES)
        ],
        axis=1,
    )


def put_blocks(ref, order_ref, values):
    for j in range(ref.shape[1] // LANES):
        ref[:, pl.ds(pl.multiple_of(order_ref[j] * LANES, LANES), LANES)] = values[
            :, j * LANES : (j + 1) * LANES
        ]


def fold_peak(values):
    return jnp.max(jnp.abs(values).reshape(-1, 8, LANES), axis=0)


def column_peak(values):
    peak = fold_peak(values[:, :LANES])
    for j in range(1, values.shape[1] // LANES):
        peak = jnp.maximum(peak, fold_peak(values[:, j * LANES : (j + 1) * LANES]))
    return peak


def lane_peak(values):
    return jnp.max(column_peak(values), axis=0, keepdims=True)


def prepare_kernel(
    range_ref, x_ref, qkv_ref, out_ref, in_ref, down_ref, level_ref, quant_ref, *refs
):
    peaks = Peaks(Mover(*refs[-3:-1], None), *refs[-7:-3])
    call_out(all_distances())
    order = Order(x_ref.shape[1])
    rows = 256
    steps = x_ref.shape[0] // rows

    def largest(step, peak):
        here = pl.ds(pl.multiple_of(step * rows, rows), rows)
        return jnp.maximum(peak, column_peak(x_ref[here, :].astype(F32)))

    own = [qkv_ref[j].astype(F32) for j in range(3)]
    own += [ref[0].astype(F32) for ref in (out_ref, in_ref, down_ref)]
    found = [lane_peak(values) for values in own]
    inputs = lax.fori_loop(0, steps, largest, jnp.zeros((8, LANES), F32))
    found.append(jnp.max(inputs, axis=0, keepdims=True))
    found.append(jnp.zeros((1, LANES), F32))
    found = jnp.concatenate(found, axis=0)
    await_all(all_distances())
    reached = jnp.max(peaks.reach(found), axis=1, keepdims=True)
    level = DECAY * range_ref[0] + (1.0 - DECAY) * reached[6:7, :]
    level_ref[...] = jnp.broadcast_to(level, level_ref.shape)
    for i, values in enumerate(own):
        bound = 0.5 * reached[i : i + 1, :]
        tangent = jnp.tanh(values / bound)
        quant, slope = low(bound * tangent), 1.0 - tangent * tangent
        if i < 4:
            refs[4][i] = slope
        else:
            refs[1 + i][0] = slope
        if i < 3:
            refs[0][i] = quant
        else:
            refs[i - 2][0] = quant

    @pl.loop(0, steps)
    def _(step):
        here = pl.ds(pl.multiple_of(step * rows, rows), rows)
        x = take_blocks(x_ref, order, here).astype(F32)
        quant_ref[here, :] = low(level * jnp.tanh(x / level))


def prepare(ranges, x, own):
    vmem = pl.BlockSpec(memory_space=pltpu.VMEM)
    out_shape = [shape_of((8, LANES), F32), shape_of(x.shape, BF16)]
    out_shape += [shape_of(values.shape, BF16) for values in own]
    out_shape += [shape_of((4,) + own[0].shape[1:], F32)]
    out_shape += [shape_of(values.shape, F32) for values in own[2:]]
    levels, quant, *rest = pl.pallas_call(
        prepare_kernel,
        in_specs=[in_smem()] + [vmem] * 5,
        out_specs=[vmem] * 9,
        out_shape=out_shape,
        scratch_shapes=peak_scratch() + copy_semaphores(peak_moves(), 1),
        compiler_params=params(collective_id=0, has_side_effects=True),
        name="prepare",
    )(ranges, x, *own)
    return levels, quant, rest[:4], rest[4:]


def qkv_kernel(x_ref, near_ref, far_ref, b_ref, o_ref):
    half = x_ref.shape[1] // 2
    for i in range(o_ref.shape[0]):
        total = dot(x_ref[:, :half], flat(near_ref[:, i])) + dot(x_ref[:, half:], flat(far_ref[:, i]))
        o_ref[i] = low(total + b_ref[i])


def qkv_rows(x, weights, bias):
    near, far = weights
    plane, parts, kinds, rows, c = near.shape
    tokens, width = x.shape
    weight_spec = pl.BlockSpec((plane, None, kinds, rows, c), lambda r: (0, r, 0, 0, 0))
    return pl.pallas_call(
        qkv_kernel,
        grid=(parts,),
        in_specs=[
            pl.BlockSpec((tokens, width), lambda r: (0, 0)),
            weight_spec,
            weight_spec,
            pl.BlockSpec((kinds, 1, c), lambda r: (0, 0, r)),
        ],
        out_specs=pl.BlockSpec((kinds, tokens, c), lambda r: (0, 0, r)),
        out_shape=shape_of((kinds, tokens, parts * c), BF16),
        compiler_params=params(),
        cost_estimate=cost(2 * tokens * width * kinds * parts * c, 14 * MIB),
        name="qkv",
    )(x, near, far, bias)


def fill_mask(mask_ref, ends_ref):
    row = pl.program_id(0)

    def segments(dims, axis):
        places = lax.broadcasted_iota(jnp.int32, dims, axis)
        count = jnp.zeros(dims, jnp.int32)
        for j in range(ends_ref.shape[1]):
            count = count + (places >= ends_ref[row, j]).astype(jnp.int32)
        return count

    same = segments((SEQ, 1), 0) == segments((1, SEQ), 1)
    mask_ref[...] = jnp.where(same, 0.0, MASKED).astype(F32)


def attend_kernel(
    skip, ends_ref, q_ref, k_ref, v_ref, *refs
):
    o_ref, lse_ref, peak_ref, mask_ref, sums_ref = refs[-5:]
    row, pair = pl.program_id(0), pl.program_id(1)
    factor = HD ** (-0.5)

    @pl.when(pair == 0)
    def _():
        fill_mask(mask_ref, ends_ref)
        sums_ref[...] = jnp.zeros_like(sums_ref) if skip == 0 else refs[0][...].T

    @pl.when((pair == 0) & (row == 0))
    def _():
        peak_ref[...] = jnp.zeros_like(peak_ref) if skip == 0 else refs[1][...]

    rows = SEQ
    lanes = lax.broadcasted_iota(jnp.int32, (rows, LANES), 1)
    for start in range(0, SEQ, rows):
        here = pl.ds(start, rows)
        q = q_ref[here, :] * jnp.asarray(factor, BF16)
        parts = []
        sums = sums_ref[here, :]
        for head in range(LANES // HD):
            own = lanes // HD == head
            scores = dot_cols(jnp.where(own, q, jnp.zeros_like(q)), k_ref[...]) + mask_ref[here, :]
            row_max = jnp.max(scores, axis=-1, keepdims=True)
            exponent = jnp.exp(scores - row_max)
            totals = jnp.sum(exponent, axis=-1, keepdims=True)
            probs = low(exponent * (1.0 / totals))
            parts.append(dot(probs, v_ref[...]))
            sums = jnp.where(lanes == (pair + skip) * (LANES // HD) + head, row_max + jnp.log(totals), sums)
        context = parts[0]
        for head in range(1, LANES // HD):
            context = jnp.where(lanes // HD == head, parts[head], context)
        o_ref[here, :] = context
        sums_ref[here, :] = sums
        peak_ref[...] = jnp.maximum(peak_ref[...], fold_peak(context))

    @pl.when(pair == pl.num_programs(1) - 1)
    def _():
        lse_ref[...] = sums_ref[...].T


def attend_first_kernel(*refs):
    attend_kernel(0, *refs)


def attend_last_kernel(*refs):
    attend_kernel(pl.num_programs(1), *refs)


def attend(qkv, ends, lse=None, peak=None, context=None, weights=(), ranges=None, levels=None):
    _, tokens, width = qkv.shape
    held = tokens // SEQ
    last = context is not None
    skip = width // LANES // 2 if last else 0

    def side(i):
        return pl.BlockSpec((None, SEQ, LANES), lambda r, j: (i, r, j + skip))

    sums = pl.BlockSpec((None, LANES, SEQ), lambda r, j: (r, 0, 0))
    small = pl.BlockSpec((8, LANES), lambda r, j: (0, 0))
    setup = dict(
        grid=(held, width // LANES // 2),
        in_specs=[in_smem(), side(0), side(1), side(2)],
        out_specs=[pl.BlockSpec((SEQ, LANES), lambda r, j: (r, j + skip)), sums, small],
        out_shape=[
            shape_of((tokens, width), F32),
            shape_of((held, LANES, SEQ), F32),
            shape_of((8, LANES), F32),
        ],
        scratch_shapes=[pltpu.VMEM((SEQ, SEQ), F32), pltpu.VMEM((SEQ, LANES), F32)],
        cost_estimate=cost(15e9, 40 * MIB),
        name="attend",
    )
    args = (ends, qkv, qkv, qkv)
    if not last:
        return pl.pallas_call(attend_first_kernel, compiler_params=params(), **setup)(*args)
    setup["in_specs"] += [sums, small, anywhere()]
    run = hosted_call(
        attend_last_kernel, weights, 5, ranges, levels, 1, 2, input_output_aliases={6: 0}, **setup
    )
    return run(*args, lse, peak, context)


def attend_back_kernel(
    c, first, order_ref, ends_ref, q_ref, k_ref, v_ref, g_ref, lse_ref, before_ref, dq_ref, dk_ref,
    dv_ref, sum_ref, mask_ref
):
    pair = pl.program_id(1)

    @pl.when((pair == 0) & (pl.program_id(0) == 0))
    def _():
        sum_ref[...] = before_ref[...]

    factor = HD ** (-0.5)

    @pl.when(pair == 0)
    def _():
        fill_mask(mask_ref, ends_ref)

    lanes = lax.broadcasted_iota(jnp.int32, (SEQ, LANES), 1)
    q, k, v, g = q_ref[...], k_ref[...], v_ref[...], g_ref[...]
    heads, zero = LANES // HD, jnp.zeros((SEQ, LANES), BF16)
    probs, grad_scores = [], []
    for head in range(heads):
        own = lanes // HD == head
        q_own = jnp.where(own, q * jnp.asarray(factor, BF16), zero)
        g_own = jnp.where(own, g, zero)
        logsum = lse_ref[pl.ds((pair + first // LANES) * heads + head, 1), :]
        prob = jnp.exp(dot_cols(k, q_own) + mask_ref[...] - logsum)
        grad_probs = dot_cols(v, g_own)
        mean_grad = jnp.sum(prob * grad_probs, axis=0, keepdims=True)
        probs.append(low(prob))
        grad_scores.append(low(factor * prob * (grad_probs - mean_grad)))
    v_sums = dot(jnp.concatenate(probs, axis=0), g)
    k_sums = dot(jnp.concatenate(grad_scores, axis=0), q)
    q_sums = dot_rows(jnp.concatenate(grad_scores, axis=1), k)

    def join(parts):
        joined = parts[:SEQ]
        for head in range(1, heads):
            joined = jnp.where(lanes // HD == head, parts[head * SEQ : (head + 1) * SEQ], joined)
        return low(joined)

    dq, dv = join(q_sums), join(v_sums)
    dq_ref[...] = dq
    dk_ref[...] = join(k_sums)
    dv_ref[...] = dv
    column = first + pair * LANES
    place = order_ref[column // c] * c + column % c
    here = pl.ds(pl.multiple_of(place, LANES), LANES)
    sum_ref[0:1, here] += jnp.sum(dq.astype(F32), axis=0, keepdims=True)
    sum_ref[1:2, here] += jnp.sum(dv.astype(F32), axis=0, keepdims=True)


def attend_back(qkv, grad, ends, lse, before, part_order, c, first):
    _, tokens, inner = qkv.shape
    width = inner // 2
    held = tokens // SEQ
    skip = first // LANES

    def side(i):
        return pl.BlockSpec((None, SEQ, LANES), lambda r, j: (i, r, j + skip))

    block = pl.BlockSpec((SEQ, LANES), lambda r, j: (r, j))
    sums = pl.BlockSpec((8, inner), lambda r, j: (0, 0))
    return pl.pallas_call(
        partial(attend_back_kernel, c, first),
        grid=(held, width // LANES),
        in_specs=[
            in_smem(),
            in_smem(),
            side(0),
            side(1),
            side(2),
            pl.BlockSpec((SEQ, LANES), lambda r, j: (r, j + skip)),
            pl.BlockSpec((None, LANES, SEQ), lambda r, j: (r, 0, 0)),
            sums,
        ],
        out_specs=[block, block, block, sums],
        out_shape=[shape_of((tokens, width), BF16)] * 3 + [shape_of((8, inner), F32)],
        scratch_shapes=[pltpu.VMEM((SEQ, SEQ), F32)],
        compiler_params=params(),
        cost_estimate=cost(15e9, 50 * MIB),
        name="attend_back",
    )(part_order, ends, qkv, qkv, qkv, grad, lse, before)


def project(values, *sides):
    halves = []
    for refs in (sides[::2], sides[1::2]):
        total, place = None, 0
        for ref in refs:
            c = ref.shape[3]
            for r in range(ref.shape[1]):
                term = dot_cols(values[:, place : place + c], flat(ref[:, r]))
                total = term if total is None else total + term
                place += c
        halves.append(total)
    return jnp.concatenate(halves, axis=1)


def norm_parts(summed):
    center = summed - jnp.mean(summed, axis=-1, keepdims=True)
    inverse = lax.rsqrt(jnp.mean(center * center, axis=-1, keepdims=True) + EPS)
    return center * inverse, inverse


def norm_back(upstream, normal, inverse, gain):
    scaled = upstream * gain
    return inverse * (
        scaled
        - jnp.mean(scaled, axis=-1, keepdims=True)
        - normal * jnp.mean(scaled * normal, axis=-1, keepdims=True)
    )


def add_sums(ref, order_ref, sums):
    @pl.when(pl.program_id(0) == 0)
    def _():
        ref[...] = jnp.zeros_like(ref)

    for i, values in enumerate(sums):
        total = jnp.sum(values, axis=0, keepdims=True)
        for j in range(ref.shape[1] // LANES):
            here = pl.ds(pl.multiple_of(order_ref[j] * LANES, LANES), LANES)
            ref[i : i + 1, here] += total[:, j * LANES : (j + 1) * LANES]


def first_norm_kernel(
    ctx_ref, level_ref, near_ref, far_ref, x_ref, row_ref, quant_ref, normed_ref, normal_ref,
    inverse_ref, peak_ref
):
    level = level_ref[1:2, 0:1]
    quant = low(level * jnp.tanh(ctx_ref[...] / level))
    quant_ref[...] = quant
    order = Order(x_ref.shape[1])
    vectors = take_blocks(row_ref, order)
    summed = take_blocks(x_ref, order).astype(F32) + project(quant, near_ref, far_ref)
    normal, inverse = norm_parts(summed + vectors[0:1, :])
    normed = normal * vectors[1:2, :] + vectors[2:3, :]
    normed_ref[...] = normed
    normal_ref[...] = normal
    inverse_ref[...] = inverse

    @pl.when(pl.program_id(0) == 0)
    def _():
        peak_ref[...] = jnp.zeros_like(peak_ref)

    peak_ref[...] = jnp.maximum(peak_ref[...], column_peak(normed))


def whole(values):
    dims = values.shape
    return pl.BlockSpec(dims, lambda *steps: (0,) * len(dims))


def first_norm(context, level, weights, x, vectors, ranges):
    near, far = weights
    tokens, width = x.shape
    inner = context.shape[1]
    rows = 512

    def block(columns):
        return pl.BlockSpec((rows, columns), lambda t: (t, 0))

    run = hosted_call(
        first_norm_kernel,
        [],
        7,
        ranges,
        level,
        2,
        4,
        grid=(tokens // rows,),
        in_specs=[
            block(inner),
            whole(level),
            whole(near),
            whole(far),
            block(width),
            whole(vectors),
        ],
        out_specs=[
            block(inner),
            block(width),
            block(width),
            block(1),
            pl.BlockSpec((8, LANES), lambda t: (0, 0)),
        ],
        out_shape=[
            shape_of((tokens, inner), BF16),
            shape_of((tokens, width), F32),
            shape_of((tokens, width), F32),
            shape_of((tokens, 1), F32),
            shape_of((8, LANES), F32),
        ],
        cost_estimate=cost(2 * tokens * width * inner, 20 * MIB),
        name="first_norm",
    )
    return run(context, level, near, far, x, vectors)


def hidden_kernel(normed_ref, level_ref, near_ref, far_ref, b_ref, quant_ref, act_ref, slope_ref, peak_ref):
    half = normed_ref.shape[1] // 2

    @pl.when(pl.program_id(0) == 0)
    def _():
        peak_ref[...] = jnp.zeros_like(peak_ref)
        level = level_ref[2:3, 0:1]
        quant_ref[...] = low(level * jnp.tanh(normed_ref[...] / level))

    hidden = dot(quant_ref[:, :half], flat(near_ref[...]))
    hidden = hidden + dot(quant_ref[:, half:], flat(far_ref[...])) + b_ref[...]
    share = 0.5 + 0.5 * lax.erf(hidden * (0.5**0.5))
    active = hidden * share
    act_ref[...] = active
    slope_ref[...] = share + hidden * ((0.5 / jnp.pi) ** 0.5 * jnp.exp(-0.5 * hidden * hidden))
    peak_ref[...] = jnp.maximum(peak_ref[...], column_peak(active))


def hidden_rows(normed, level, weights, bias, held_down, ranges):
    near, far = weights
    plane, parts, rows, c = near.shape
    tokens, width = normed.shape
    step = min(c, 512)
    cuts = c // step
    weight_spec = pl.BlockSpec((plane, None, rows, step), lambda s: (0, s // cuts, 0, s % cuts))
    block = pl.BlockSpec((tokens, step), lambda s: (0, s))
    run = hosted_call(
        hidden_kernel,
        [(held_down, ())],
        6,
        ranges,
        level,
        3,
        3,
        grid=(parts * cuts,),
        in_specs=[
            whole(normed),
            whole(level),
            weight_spec,
            weight_spec,
            pl.BlockSpec((1, step), lambda s: (0, s)),
        ],
        out_specs=[
            pl.BlockSpec((tokens, width), lambda s: (0, 0)),
            block,
            block,
            pl.BlockSpec((8, LANES), lambda s: (0, 0)),
        ],
        out_shape=[
            shape_of((tokens, width), BF16),
            shape_of((tokens, parts * c), F32),
            shape_of((tokens, parts * c), F32),
            shape_of((8, LANES), F32),
        ],
        cost_estimate=cost(2 * tokens * width * parts * c, 50 * MIB),
        name="hidden",
    )
    return run(normed, level, near, far, bias)


def second_norm_kernel(
    order_ref, act_ref, level_ref, near_a, far_a, near_b, far_b, normed_ref, grad_ref, row_ref,
    quant_ref, out_ref, sum_ref, branch_ref, terms_ref
):
    level = level_ref[3:4, 0:1]
    quant = low(level * jnp.tanh(act_ref[...] / level))
    quant_ref[...] = quant
    vectors = take_blocks(row_ref, order_ref)
    summed = normed_ref[...] + project(quant, near_a, far_a, near_b, far_b) + vectors[3:4, :]
    normal, inverse = norm_parts(summed)
    gain = vectors[4:5, :]
    put_blocks(out_ref, order_ref, low(normal * gain + vectors[5:6, :]))
    upstream = take_blocks(grad_ref, order_ref).astype(F32)
    grad_sum = norm_back(upstream, normal, inverse, gain)
    sum_ref[...] = grad_sum
    branch_ref[...] = low(grad_sum)
    add_sums(terms_ref, order_ref, (grad_sum, upstream * normal, upstream))


def second_norm(active, level, weights, normed, grad, vectors, order):
    tokens, width = normed.shape
    inner = active.shape[1]
    rows = 256

    def block(columns):
        return pl.BlockSpec((rows, columns), lambda t: (t, 0))

    return pl.pallas_call(
        second_norm_kernel,
        grid=(tokens // rows,),
        in_specs=[
            in_smem(),
            block(inner),
            whole(level),
            *[whole(side) for side in weights],
            block(width),
            block(width),
            whole(vectors),
        ],
        out_specs=[
            block(inner),
            block(width),
            block(width),
            block(width),
            pl.BlockSpec((8, width), lambda t: (0, 0)),
        ],
        out_shape=[
            shape_of((tokens, inner), BF16),
            shape_of((tokens, width), BF16),
            shape_of((tokens, width), F32),
            shape_of((tokens, width), BF16),
            shape_of((8, width), F32),
        ],
        compiler_params=params(),
        cost_estimate=cost(2 * tokens * width * inner, 80 * MIB),
        name="second_norm",
    )(order, active, level, *weights, normed, grad, vectors)


def weight_specs(xs, products, parts, plane, c):
    tokens, width = xs[0].shape
    count = len(products)
    step = min(c, 1024)
    cuts = c // step
    dims = (plane, parts, count, width // (2 * plane), c)
    in_specs = [
        pl.BlockSpec((tokens, step), lambda r, j, first=first: (0, (r + first) * cuts + j))
        for _, _, first in products
    ]
    out_spec = pl.BlockSpec((plane, None, count, dims[3], step), lambda r, j: (0, r, 0, 0, j))
    estimate = cost(tokens * width * parts * c * count, 20 * MIB)
    return dims, (parts, cuts), in_specs, out_spec, estimate


def turn_once(x_refs, turned_refs):
    @pl.when((pl.program_id(0) == 0) & (pl.program_id(1) == 0))
    def _():
        for x_ref, turned_ref in zip(x_refs, turned_refs):
            turned_ref[...] = x_ref[...].T


def weight_send_kernel(count, which, *refs):
    x_refs, h_refs = refs[:count], refs[count : count + len(which)]
    send_ref, turned = refs[count + len(which)], refs[count + len(which) + 1 :]
    turn_once(x_refs, turned)
    for i, h_ref in enumerate(h_refs):
        h = h_ref[...]
        total = dot(turned[which[i]][...], h)
        send_ref[:, i] = low(total).reshape(send_ref.shape[0], -1, h.shape[1])


def weight_send(xs, products, parts, plane, c):
    dims, grid, in_specs, out_spec, estimate = weight_specs(xs, products, parts, plane, c)
    tokens, width = xs[0].shape
    return pl.pallas_call(
        partial(weight_send_kernel, len(xs), [product[0] for product in products]),
        grid=grid,
        in_specs=[pl.BlockSpec((tokens, width // 2), lambda r, j: (0, 1))] * len(xs) + in_specs,
        out_specs=out_spec,
        out_shape=shape_of(dims, BF16),
        scratch_shapes=[pltpu.VMEM((width // 2, tokens), BF16)] * len(xs),
        compiler_params=params(),
        cost_estimate=estimate,
        name="weight_send",
    )(*xs, *[product[1] for product in products])


def weight_keep_kernel(count, which, split, *refs):
    x_refs, other_ref = refs[:count], refs[count]
    h_refs = refs[count + 1 : count + 1 + len(which)]
    outs, turned = refs[count + 1 + len(which) : -count], refs[-count:]
    half = pl.num_programs(0) // 2
    turn_once(x_refs, turned)
    for side in range(2):

        @pl.when(pl.program_id(0) // half == side)
        def _(side=side):
            keep_ref, send_ref = outs[2 * side : 2 * side + 2]
            for i, h_ref in enumerate(h_refs):
                h = h_ref[...]
                total = dot(turned[which[i]][...], h).reshape(other_ref.shape[0], -1, h.shape[1])
                for j, slot in enumerate(split[side][0]):
                    keep_ref[j, i] = total[slot] + other_ref[slot, i].astype(F32)
                for j, slot in enumerate(split[side][1]):
                    send_ref[j, i] = low(total[slot] + other_ref[slot, i].astype(F32))


def weight_keep(xs, products, other, parts, plane, c):
    dims, (_, cuts), in_specs, out_spec, estimate = weight_specs(xs, products, parts, plane, c)
    tokens, width = xs[0].shape
    half = parts // 2
    block = (plane // 2, None, dims[2], dims[3], c // cuts)
    near = pl.BlockSpec(
        block, lambda r, j: (0, jnp.minimum(r, half - 1), 0, 0, jnp.where(r < half, j, cuts - 1))
    )
    far = pl.BlockSpec(block, lambda r, j: (0, jnp.maximum(r - half, 0), 0, 0, jnp.where(r < half, 0, j)))
    small = (plane // 2, half) + dims[2:]
    which = [product[0] for product in products]
    keep_a, send_a, keep_b, send_b = pl.pallas_call(
        partial(weight_keep_kernel, len(xs), which, first_split(bits_of("dp") - 1)),
        grid=(parts, cuts),
        in_specs=[pl.BlockSpec((tokens, width // 2), lambda r, j: (0, 0))] * len(xs)
        + [out_spec]
        + in_specs,
        out_specs=[near, near, far, far],
        out_shape=[shape_of(small, F32), shape_of(small, BF16)] * 2,
        scratch_shapes=[pltpu.VMEM((width // 2, tokens), BF16)] * len(xs),
        compiler_params=params(),
        cost_estimate=estimate,
        name="weight_keep",
    )(*xs, other, *[product[1] for product in products])
    return [keep_a, keep_b], [send_a, send_b]


def grad_hidden_kernel(
    cuts, order_ref, g_ref, near_a, far_a, near_b, far_b, act_ref, slope_ref, level_ref, o_ref, sum_ref
):
    half = g_ref.shape[1] // 2
    block = pl.program_id(0)
    columns = act_ref.shape[1]
    level = level_ref[3:4, 0:1]

    @pl.when(block == 0)
    def _():
        sum_ref[...] = jnp.zeros_like(sum_ref)

    for side, (near_ref, far_ref) in enumerate(((near_a, far_a), (near_b, far_b))):

        @pl.when(block * 2 // pl.num_programs(0) == side)
        def _(near_ref=near_ref, far_ref=far_ref):
            grad = dot(g_ref[:, :half], flat(near_ref[...])) + dot(g_ref[:, half:], flat(far_ref[...]))
            tangent = jnp.tanh(act_ref[...] / level)
            grad = low(grad * ((1.0 - tangent * tangent) * slope_ref[...]))
            o_ref[...] = grad
            total = jnp.sum(grad.astype(F32), axis=0, keepdims=True)
            start = pl.multiple_of((block % cuts) * columns, LANES)
            sum_ref[pl.ds(order_ref[block // cuts], 1), pl.ds(start, columns)] = total


def grad_hidden_rows(grad, weights, active, slope, level, part_order):
    plane, half, rows, c = weights[0].shape
    parts = 2 * half
    tokens, width = grad.shape
    step = min(c, 1024)
    cuts = c // step
    block = (plane, None, rows, step)
    first = pl.BlockSpec(
        block,
        lambda s: (0, jnp.minimum(s // cuts, half - 1), 0, jnp.where(s < half * cuts, s % cuts, cuts - 1)),
    )
    last = pl.BlockSpec(
        block,
        lambda s: (0, jnp.maximum(s // cuts - half, 0), 0, jnp.where(s < half * cuts, 0, s % cuts)),
    )
    block = pl.BlockSpec((tokens, step), lambda s: (0, s))
    return pl.pallas_call(
        partial(grad_hidden_kernel, cuts),
        grid=(parts * cuts,),
        in_specs=[in_smem(), whole(grad), first, first, last, last, block, block, whole(level)],
        out_specs=[block, pl.BlockSpec((parts, c), lambda s: (0, 0))],
        out_shape=[shape_of((tokens, parts * c), BF16), shape_of((parts, c), F32)],
        compiler_params=params(),
        cost_estimate=cost(2 * tokens * width * parts * c, 34 * MIB),
        name="grad_hidden",
    )(part_order, grad, *weights, active, slope, level)


def first_back_kernel(
    order_ref, g_ref, near_ref, far_ref, normed_ref, normal_ref, inverse_ref, sum_two_ref, level_ref, row_ref,
    sum_ref, low_ref, terms_ref
):
    level = level_ref[2:3, 0:1]
    tangent = jnp.tanh(normed_ref[...] / level)
    grad = project(g_ref[...], near_ref, far_ref) * (1.0 - tangent * tangent) + sum_two_ref[...]
    normal = normal_ref[...]
    gain = take_blocks(row_ref, order_ref)[1:2, :]
    grad_sum = norm_back(grad, normal, inverse_ref[...], gain)
    sum_ref[...] = grad_sum
    low_ref[...] = low(grad_sum)
    add_sums(terms_ref, order_ref, (grad_sum, grad * normal, grad))


def first_back(grad, weights, normed, normal, inverse, sum_two, level, vectors, order):
    near, far = weights
    tokens, width = normed.shape
    inner = grad.shape[1]
    rows = 256

    def block(columns):
        return pl.BlockSpec((rows, columns), lambda t: (t, 0))

    return pl.pallas_call(
        first_back_kernel,
        grid=(tokens // rows,),
        in_specs=[
            in_smem(),
            block(inner),
            whole(near),
            whole(far),
            block(width),
            block(width),
            block(1),
            block(width),
            whole(level),
            whole(vectors),
        ],
        out_specs=[block(width), block(width), pl.BlockSpec((8, width), lambda t: (0, 0))],
        out_shape=[
            shape_of((tokens, width), F32),
            shape_of((tokens, width), BF16),
            shape_of((8, width), F32),
        ],
        compiler_params=params(),
        cost_estimate=cost(2 * tokens * width * inner, 36 * MIB),
        name="first_back",
    )(order, grad, near, far, normed, normal, inverse, sum_two, level, vectors)


def grad_context_kernel(g_ref, near_ref, far_ref, ctx_ref, level_ref, o_ref):
    half = g_ref.shape[1] // 2
    level = level_ref[1:2, 0:1]
    tangent = jnp.tanh(ctx_ref[...] / level)
    grad = dot(g_ref[:, :half], flat(near_ref[...])) + dot(g_ref[:, half:], flat(far_ref[...]))
    o_ref[...] = low(grad * (1.0 - tangent * tangent))


def grad_context_rows(grad, weights, context, level):
    near, far = weights
    plane, parts, rows, c = near.shape
    tokens, width = grad.shape
    weight_spec = pl.BlockSpec((plane, None, rows, c), lambda r: (0, r, 0, 0))
    block = pl.BlockSpec((tokens, c), lambda r: (0, r))
    return pl.pallas_call(
        grad_context_kernel,
        grid=(parts,),
        in_specs=[
            whole(grad),
            weight_spec,
            weight_spec,
            block,
            whole(level),
        ],
        out_specs=block,
        out_shape=shape_of((tokens, parts * c), BF16),
        compiler_params=params(),
        cost_estimate=cost(2 * tokens * width * parts * c, 10 * MIB),
        name="grad_context",
    )(grad, near, far, context, level)


def grad_input_kernel(order_ref, *refs):
    g_refs, (near_ref, far_ref, sum_ref, x_ref, level_ref, o_ref) = refs[:6], refs[6:]
    level = level_ref[0:1, 0:1]
    half = near_ref.shape[1] // 2
    total = None
    for side in range(2):
        for i in range(3):
            term = project(
                g_refs[side * 3 + i][...],
                near_ref.at[:, side * half : (side + 1) * half, i],
                far_ref.at[:, side * half : (side + 1) * half, i],
            )
            total = term if total is None else total + term
    tangent = jnp.tanh(take_blocks(x_ref, order_ref).astype(F32) / level)
    put_blocks(o_ref, order_ref, low(sum_ref[...] + total * (1.0 - tangent * tangent)))


def grad_input(grads, weights, grad_sum, x, level, order):
    near, far = weights
    tokens, width = x.shape
    inner = grads[0].shape[1]
    rows = 256

    def block(columns):
        return pl.BlockSpec((rows, columns), lambda t: (t, 0))

    return pl.pallas_call(
        grad_input_kernel,
        grid=(tokens // rows,),
        in_specs=[in_smem()]
        + [block(inner)] * 6
        + [whole(near), whole(far), block(width), block(width), whole(level)],
        out_specs=block(width),
        out_shape=shape_of((tokens, width), BF16),
        compiler_params=params(),
        cost_estimate=cost(12 * tokens * width * inner, 20 * MIB),
        name="grad_input",
    )(order, *grads, near, far, grad_sum, x, level)


def place_kernel(turned, order_ref, *refs):
    d_refs, i_refs, q_refs = refs[:2], refs[2:4], refs[4:6]
    in_out, qkv_out, *turned_outs = refs[6:]
    step = pl.program_id(0)
    plane, _, rows, _ = i_refs[0].shape
    for core in range(2):
        for j in range(plane):
            here = pl.ds(pl.multiple_of(order_ref[core * plane + j] * rows, rows), rows)
            in_out[0, here, :] = i_refs[core][j, 0].astype(F32)
            if turned:
                turned_outs[0][:, here] = d_refs[core][j, 0].astype(F32).T

            @pl.when(step < 3)
            def _(core=core, j=j, here=here):
                qkv_out[0, here, :] = q_refs[core][j, 0].astype(F32)

            if turned:

                @pl.when(step == 3)
                def _(core=core, j=j, here=here):
                    turned_outs[1][:, here] = q_refs[core][j, 0].astype(F32).T


def place_grads(down, inner, first, blocks):
    plane, _, rows, c = inner[0].shape
    columns = first[0].shape[3]
    width = 2 * plane * rows
    turned = rows % LANES == 0
    cut = c // 4

    def piece(size, index):
        return [pl.BlockSpec((plane, 1, rows, size), index)] * 2

    out_specs = [
        pl.BlockSpec((1, width, cut), lambda p: (0, 0, p)),
        pl.BlockSpec((1, width, columns), lambda p: (jnp.minimum(p, 2), 0, 0)),
    ]
    out_shape = [shape_of((1, width, c), F32), shape_of((3, width, columns), F32)]
    if turned:
        out_specs.append(pl.BlockSpec((cut, width), lambda p: (p, 0)))
        out_specs.append(pl.BlockSpec((columns, width), lambda p: (0, 0)))
        out_shape += [shape_of((c, width), F32), shape_of((columns, width), F32)]
    inner_grad, qkv_grad, *rest = pl.pallas_call(
        partial(place_kernel, turned),
        grid=(4,),
        in_specs=[in_smem()]
        + piece(cut, lambda p: (0, 0, 0, p)) * 2
        + piece(columns, lambda p: (0, p, 0, 0)),
        out_specs=out_specs,
        out_shape=out_shape,
        compiler_params=params(),
        name="place_grads",
    )(blocks.astype(jnp.int32), *down, *inner, *first)
    if not turned:
        back = jnp.zeros((2 * plane,), jnp.int32).at[blocks].set(jnp.arange(2 * plane, dtype=jnp.int32))
        for near, far in (down, [side[:, 3:] for side in first]):
            split = jnp.concatenate([near, far], axis=0)[:, 0]
            rest.append(jnp.take(split, back, axis=0).astype(F32).reshape(width, -1).T)
    return inner_grad[0], qkv_grad, rest[0], rest[1]


def left_over(keeps, sends):
    return scatter_plane(keeps, sends, True)


def scatter_grad(chain, xs, products, other, token, parts, plane, c):
    return chain(*weight_keep([tie(xs[0], [token])] + xs[1:], products, other, parts, plane, c))


HOST_RANK = {first_norm_kernel: 1, attend_last_kernel: 2, hidden_kernel: 1}


def own_block(values, axis):
    rows = values.shape[axis] // lax.axis_size("dp")
    return lax.dynamic_slice_in_dim(values, lax.axis_index("dp") * rows, rows, axis)


def local(
    mesh, layer_input, grad_output, doc_lengths, ranges, w_qkv, bias_qv, w_out, b_out, gain_one,
    shift_one, w_in, b_in, w_down, b_down, gain_two, shift_two
):
    datas, parts = lax.axis_size("dp"), lax.axis_size("tensor")
    data, part = lax.axis_index("dp"), lax.axis_index("tensor")
    plane = datas // 2
    tokens, width = layer_input.shape
    rows = width // datas

    places = jnp.arange(datas)
    distance = (places % plane) * 2 + places // plane
    blocks = data ^ distance
    if rows % LANES == 0:
        per_block = rows // LANES
        order = (blocks[:, None] * per_block + jnp.arange(per_block)).reshape(-1).astype(jnp.int32)
    else:
        order = jnp.arange(width // LANES, dtype=jnp.int32)

    def arrange(values):
        split = values.reshape(values.shape[:-1] + (datas, rows))
        return jnp.take(split, blocks, axis=-2).reshape(values.shape)

    def restore(values):
        split = values.reshape(values.shape[:-1] + (datas, rows))
        back = jnp.zeros((datas,), jnp.int32).at[blocks].set(places.astype(jnp.int32))
        return jnp.take(split, back, axis=-2).reshape(values.shape)

    def arrange_rows(values):
        return values if rows % LANES == 0 else arrange(values)

    def restore_rows(values):
        return values if rows % LANES == 0 else restore(values)

    part_order = (part ^ jnp.arange(parts)).astype(jnp.int32)
    x = arrange_rows(layer_input)
    upstream = arrange_rows(grad_output)
    vectors = jnp.stack([b_out, gain_one, shift_one, b_down, gain_two, shift_two, b_out, b_out])
    vectors = arrange_rows(vectors).astype(F32)

    own = [
        own_block(w_qkv, 1),
        own_block(w_out, 1).T[None],
        own_block(w_in, 0)[None],
        own_block(w_down, 1).T[None],
    ]
    levels, quant_input, quant_own, slopes = prepare(ranges, x, own)
    biases = jnp.concatenate([bias_qv.reshape(-1), b_in])
    count = biases.shape[0]
    biases = jnp.pad(biases, (0, -count % (16 * LANES))).reshape(-1, LANES)
    near, far, biases, near_out, far_out, held_in = first_gather(quant_own[0], biases, *quant_own[1:3])
    weights_qkv, weights_out = (near, far), (near_out, far_out)
    biases = biases.reshape(parts, -1)[:, :count]
    columns = bias_qv.shape[1]
    bias_q = biases[:, :columns].reshape(1, -1)
    bias_v = biases[:, columns : 2 * columns].reshape(1, -1)
    bias_qkv = jnp.stack([bias_q, jnp.zeros_like(bias_q), bias_v]).astype(F32)
    bias_hidden = biases[:, 2 * columns :].reshape(1, -1).astype(F32)

    held = tokens // SEQ
    lengths_here = lax.dynamic_slice_in_dim(doc_lengths, part * held, held, 0)
    ends = jnp.cumsum(lengths_here, axis=1, dtype=jnp.int32)
    half = parts // 2 * columns

    first_moves, _ = plane_moves()

    def over_plane(values, token):
        values = tie(values, [token])
        return [far_swap(values, r) for _, r in first_moves]

    there_in = over_plane(held_in, biases)
    held_a = tie(quant_own[3], [biases])[None]
    for bit in reversed(range(bits_of("tensor") - 1)):
        other = swap(held_a, "tensor", bit)
        held_a = jnp.stack([held_a, other], axis=1).reshape((-1,) + held_a.shape[1:])
    qkv = qkv_rows(quant_input, weights_qkv, bias_qkv)
    held_a = tie(held_a, [qkv])
    there_a = over_plane(held_a, qkv)
    held_b = swap(held_a, "tensor", bits_of("tensor") - 1)
    context, lse, peak = attend(qkv, ends)
    there_in, there_a = [tie(values, [peak]) for values in there_in], [tie(values, [peak]) for values in there_a]
    (context, lse, _), levels, (*weights_in, near_a, far_a) = attend(
        qkv, ends, lse, peak, context, [(held_in, there_in), (held_a, there_a)], ranges, levels
    )
    weights_in = tuple(side[:, :, 0] for side in weights_in)
    weights_out = tuple(side[:, :, 0] for side in weights_out)
    (quant_context, normed, normal_one, inverse_one, _), levels, _ = first_norm(
        context, levels, weights_out, x, vectors, ranges
    )
    held_b = tie(held_b, [levels])
    (quant_normed, active, slope, _), levels, (near_b, far_b) = hidden_rows(
        normed, levels, weights_in, bias_hidden, held_b, ranges
    )
    weights_down = [side[:, :, 0] for side in (near_a, far_a, near_b, far_b)]
    quant_active, output, grad_sum_two, grad_branch, terms_two = second_norm(
        active, levels, weights_down, normed, upstream, vectors, order
    )

    wide = b_in.shape[0]
    other = weight_send([grad_branch], [(0, quant_active, 0)], parts, plane, wide)
    grad_after = tie(grad_branch, [other])
    other = swap(other, "dp", 0)
    grad_hidden, sum_hidden = grad_hidden_rows(
        grad_after, weights_down, active, slope, levels, part_order
    )
    down = scatter_grad(
        scatter_all, [grad_branch], [(0, quant_active, 0)], other, sum_hidden, parts, plane, wide
    )
    grad_hidden = tie(grad_hidden, next(down))
    other = weight_send([quant_normed], [(0, grad_hidden, 0)], parts, plane, wide)
    grad_after = tie(grad_hidden, [other])
    other = swap(other, "dp", 0)
    grad_sum_one, grad_attention, terms_one = first_back(
        grad_after, weights_in, normed, normal_one, inverse_one, grad_sum_two, levels, vectors, order
    )
    grad_hidden = tie(grad_hidden, down.send(terms_one))
    inner = scatter_grad(
        scatter_all, [quant_normed], [(0, grad_hidden, 0)], other, terms_one, parts, plane, wide
    )
    grad_after = tie(grad_attention, next(inner))
    grad_context = grad_context_rows(grad_after, weights_out, context, levels)
    grad_context = tie(grad_context, down.send(grad_context))
    sums_before = jnp.zeros((8, 2 * half), F32)
    *grads, token = attend_back(
        qkv, grad_context, ends, lse, sums_before, part_order, columns, 0
    )
    grads_a = grads
    xs = [quant_input, grad_attention]
    products_a = [(0, grad, 0) for grad in grads] + [(1, quant_context, 0)]
    other_a = weight_send(xs, products_a, parts // 2, plane, columns)
    token_a = other_a
    grad_context = tie(grad_context, inner.send(token_a) + down.send(token_a))
    other_a = swap(other_a, "dp", 0)
    *grads, token = attend_back(
        qkv, grad_context, ends, lse, token, part_order, columns, half
    )
    sum_qv = token
    down = run_all(down, token)
    grads[0] = tie(grads[0], inner.send(token) + [down[1]])
    products_b = [(0, grad, 0) for grad in grads] + [(1, quant_context, parts // 2)]
    other_b = weight_send(xs, products_b, parts // 2, plane, columns)
    token = other_b
    other_b = swap(other_b, "dp", 0)
    first_a = scatter_grad(left_over, xs, products_a, other_a, token, parts // 2, plane, columns)
    started = next(first_a)
    first_b = scatter_grad(left_over, xs, products_b, other_b, started[0], parts // 2, plane, columns)
    started = next(first_b) + inner.send(started[0])
    grads[0] = tie(grads[0], started)
    grad_x = grad_input(grads_a + grads, weights_qkv, grad_sum_one, x, levels, order)

    sums = [terms_one[:3], terms_two[:3], sum_qv[:2], sum_hidden.reshape(-1, width)]
    if rows % LANES:
        sums[0], sums[1] = restore(sums[0]), restore(sums[1])
    sums = jnp.concatenate(sums)
    padded = jnp.pad(sums, ((0, -sums.shape[0] % 8), (0, 0)))
    inner, first_a, first_b = [run_all(chain, grad_x) for chain in (inner, first_a, first_b)]
    (down, inner, first), sums = finale(down, inner, first_a + first_b, slopes, padded)
    hidden_all = sums[8 : 8 + sum_hidden.size // width].reshape(-1)
    grad_bias_qv = lax.dynamic_slice_in_dim(sums[6:8], part * columns, columns, 1)
    grad_b_in = lax.dynamic_slice_in_dim(hidden_all, part * b_in.shape[0], b_in.shape[0], 0)
    grad_w_in, grad_w_qkv, grad_w_down, grad_w_out = place_grads(down, inner, first, blocks)
    new_ranges = levels[:4, 0]
    return (
        restore_rows(output),
        restore_rows(grad_x),
        grad_w_qkv,
        grad_bias_qv,
        grad_w_out,
        sums[0],
        sums[1],
        sums[2],
        grad_w_in,
        grad_b_in,
        grad_w_down,
        sums[3],
        sums[4],
        sums[5],
        new_ranges,
    )


def solution(mesh):
    in_specs = (
        P(("dp", "tensor"), None),
        P(("dp", "tensor"), None),
        P("dp", None),
        P(),
        P(None, None, "tensor"),
        P(None, "tensor"),
        P("tensor", None),
        P(),
        P(),
        P(),
        P(None, "tensor"),
        P("tensor"),
        P("tensor", None),
        P(),
        P(),
        P(),
    )
    out_specs = (
        P(("dp", "tensor"), None),
        P(("dp", "tensor"), None),
        P(None, None, "tensor"),
        P(None, "tensor"),
        P("tensor", None),
        P(),
        P(),
        P(),
        P(None, "tensor"),
        P("tensor"),
        P("tensor", None),
        P(),
        P(),
        P(),
        P(),
    )
    return jax.shard_map(
        partial(local, mesh), mesh=mesh, in_specs=in_specs, out_specs=out_specs, check_vma=False
    )
```

```python
from functools import partial

import jax
import jax.numpy as jnp
from jax import lax
from jax.experimental import pallas as pl
from jax.experimental.pallas import tpu as pltpu
from jax.sharding import PartitionSpec as P

HD = 64
SEQ = 512
LANES = 128

EPS = 1e-06
DECAY = 0.9
MASKED = -1e30
MESH = pl.DeviceIdType.MESH
F32 = jnp.float32
BF16 = jnp.bfloat16
MIB = 1024 * 1024


def shape_of(dims, kind):
    return jax.ShapeDtypeStruct(dims, kind)


def params(**rest):
    return pltpu.CompilerParams(vmem_limit_bytes=60 * MIB, **rest)


def in_smem():
    return pl.BlockSpec(memory_space=pltpu.SMEM)


def cost(flops, moved):
    return pl.CostEstimate(flops=int(flops) // 30, bytes_accessed=int(moved) // 30, transcendentals=0)


def dot(first, second):
    return jnp.dot(first, second, preferred_element_type=F32)


def dot_cols(first, second):
    return lax.dot_general(first, second, (((1,), (1,)), ((), ())), preferred_element_type=F32)


def dot_rows(first, second):
    return lax.dot_general(first, second, (((0,), (0,)), ((), ())), preferred_element_type=F32)


def flat(block):
    return block.reshape(block.shape[0] * block.shape[1], block.shape[2])


def tie(values, others):
    return lax.optimization_barrier((values, *others))[0]


def swap(values, axis, bit, token=None):
    count = lax.axis_size(axis)
    other = lax.ppermute(values, axis, [(i, i ^ (1 << bit)) for i in range(count)])
    return other if token is None else tie(other, [token])


def far_swap(values, r):
    count = lax.axis_size("dp")
    return lax.ppermute(values, "dp", [(i, i ^ r) for i in range(count)])


def bits_of(axis):
    return lax.axis_size(axis).bit_length() - 1


def plane_orders():
    plane = list(range(1, bits_of("dp")))
    return plane, (plane[::-1], plane)


def run_all(chain, token=None):
    try:
        chain.send(token)
        while True:
            next(chain)
    except StopIteration as done:
        return done.value


def low(values):
    return values.astype(BF16)


def first_split(plane_bits):
    _, orders = plane_orders()
    split = []
    for order in orders:
        bit = order[0] - 1
        split.append([[s for s in range(1 << plane_bits) if (s >> bit) & 1 == away] for away in (0, 1)])
    return split


def scatter_plane(keeps, sends, left_over=False):
    plane, orders = plane_orders()
    left = [[bit for bit in plane[::-1] if bit != order[0]] for order in orders]
    sides = [keep.reshape((2,) * len(left[0]) + keep.shape[1:]) for keep in keeps]
    sends = [send.reshape(side.shape) for side, send in zip(sides, sends)]
    for step in range(len(plane)):
        if step:
            places = [left[i].index(orders[i][step]) for i in range(2)]
            sends = [low(lax.index_in_dim(sides[i], 1, places[i], keepdims=False)) for i in range(2)]
            sides = [lax.index_in_dim(sides[i], 0, places[i], keepdims=False) for i in range(2)]
            for i in range(2):
                left[i].remove(orders[i][step])
        token = yield sends
        others = [swap(sends[i], "dp", orders[i][step], token) for i in range(2)]
        if left_over and step == len(plane) - 2:
            return list(zip(sides, others))
        sides = [side + other.astype(F32) for side, other in zip(sides, others)]
    return sides


def scatter_all(keeps, sends):
    sides = yield from scatter_plane(keeps, sends)
    last = bits_of("tensor") - 1
    for bit in range(last):
        pairs = [values.reshape((-1, 2) + values.shape[1:]) for values in sides]
        send = jnp.concatenate([low(values[:, 1]) for values in pairs])
        token = yield [send]
        others = jnp.split(swap(send, "tensor", bit, token), 2)
        sides = [values[:, 0] + other.astype(F32) for values, other in zip(pairs, others)]
    send = low(sides[1][0])
    token = yield [send]
    return sides[0][0], swap(send, "tensor", last, token)


def at_distance(axis, r):
    me, index = lax.axis_index(axis), 0
    for bit in range(bits_of(axis)):
        index = index + (me // (1 << bit) + (r >> bit)) % 2 * (1 << bit)
    return index


def plane_moves():
    plane = 1 << (bits_of("dp") - 1)
    if plane == 4:
        return [(1, 2), (2, 4)], [(3, 1, 4, 0), (3, 2, 2, 1)]
    return [(slot, 2 * slot) for slot in range(1, plane)], []


class Mover:
    def __init__(self, send, recv, local):
        self.send, self.recv, self.local = send, recv, local
        self.count, self.local_count = 0, 0

    def remote(self, source, target, axis, r):
        i = self.count
        self.count += 1
        return pltpu.make_async_remote_copy(
            src_ref=source,
            dst_ref=target,
            send_sem=self.send.at[i],
            recv_sem=self.recv.at[i],
            device_id={axis: at_distance(axis, r)},
            device_id_type=MESH,
        )

    def own(self, source, target):
        i = self.local_count
        self.local_count += 1
        return pltpu.make_async_copy(source, target, self.local.at[i])


def call_out(distances):
    for axis, r in distances:
        pl.semaphore_signal(
            pltpu.get_barrier_semaphore(),
            inc=1,
            device_id={axis: at_distance(axis, r)},
            device_id_type=MESH,
        )


def await_all(distances):
    pl.semaphore_wait(pltpu.get_barrier_semaphore(), len(distances))


def greet(distances):
    call_out(distances)
    await_all(distances)


def part_distances():
    return [("tensor", r) for r in range(1, 1 << bits_of("tensor"))]


def plane_distances():
    first, second = plane_moves()
    apart = sorted({move[1] for move in first} | {move[2] for move in second} | {1})
    return [("dp", r) for r in apart]


def halves_of(ref, half):
    rows = ref.shape[-2] // 2
    return ref.at[..., half * rows : (half + 1) * rows, :]


def slots(ref, *inner):
    return lambda slot: ref.at[(slot,) + inner]


def low_bit(r):
    return r & -r


class AlongParts:
    def __init__(self, mover, own, place):
        parts = 1 << bits_of("tensor")
        self.copy = mover.own(own, place(0))
        self.moves, self.there = {}, {0}
        for r in range(1, parts):
            rest = r - low_bit(r)
            source = own if rest == 0 else place(rest)
            self.moves[r] = mover.remote(source, place(r), "tensor", low_bit(r))
        self.order = sorted(self.moves, key=lambda r: (bin(r).count("1"), -r))

    def start(self):
        self.copy.start()
        for r in self.order:
            if r == low_bit(r):
                self.moves[r].start()

    def arrive(self, r):
        if r not in self.there:
            self.moves[r].wait_recv()
            self.there.add(r)

    def hand_on(self):
        for r in self.order:
            if r != low_bit(r):
                self.arrive(r - low_bit(r))
                self.moves[r].start()

    def finish(self):
        self.copy.wait()
        for r, move in self.moves.items():
            self.arrive(r)
            move.wait_send()


class OverPlane:
    def __init__(self, mover, held, near, far, given=(), via=None):
        first, second = plane_moves()
        plane = 1 << (bits_of("dp") - 1)
        sources = [held] + (list(given) or [near(slot) for slot, _ in first])
        here = [held] + list(given)
        self.loads = [] if via is None else [mover.own(here[i], via.at[i]) for i in range(len(here))]
        self.copies = [
            mover.own(here[i] if via is None else via.at[i], near(i)) for i in range(len(here))
        ]
        self.first = [] if given else [mover.remote(held, near(slot), "dp", r) for slot, r in first]
        self.second = [
            mover.remote(halves_of(sources[source], half), halves_of(near(slot), half), "dp", r)
            for slot, source, r, half in second
        ]
        sources += [near(slot) for slot in range(len(sources), plane)]
        self.cores = [mover.remote(values, far(i), "dp", 1) for i, values in enumerate(sources)]
        self.early = 1 + len(first)

    def start(self):
        for copy in self.loads or self.copies:
            copy.start()
        for move in self.first:
            move.start()
        self.cores[0].start()

    def relay(self):
        for move in self.first:
            move.wait_recv()
        for move in self.second + self.cores[1 : self.early]:
            move.start()

    def settle(self):
        for load, copy in zip(self.loads, self.copies):
            load.wait()
            copy.start()

    def complete(self):
        for move in self.second:
            move.wait_recv()
        for move in self.cores[self.early :]:
            move.start()

    def finish(self):
        for move in self.first + self.second:
            move.wait_send()
        for move in self.cores:
            move.wait()
        for copy in self.copies:
            copy.wait()


def plane_counts(given):
    first, second = plane_moves()
    plane = 1 << (bits_of("dp") - 1)
    return len(second) + plane + (0 if given else len(first)), 2 + 2 * given


def copy_semaphores(remote, local):
    copies = pltpu.SemaphoreType.DMA
    return [copies((remote,)), copies((remote,)), copies((local,))]


def anywhere():
    return pl.BlockSpec(memory_space=pltpu.HBM)


def all_distances():
    return [("dp", r) for r in range(1, 1 << bits_of("dp"))] + part_distances()


class Peaks:
    def __init__(self, mover, mine, near, mid, far):
        self.mine, self.near, self.mid, self.far = mine, near, mid, far
        self.first = [mover.remote(mine, near.at[r], "dp", r) for r in range(1, near.shape[0])]
        self.second = [mover.remote(mid, far.at[r], axis, r) for axis, r in part_distances()]

    def reach(self, values):
        self.mine[...] = values
        for moves, source, held in (
            (self.first, self.mine, self.near),
            (self.second, self.mid, self.far),
        ):
            for move in moves:
                move.start()
            held[0] = source[...]
            for move in moves:
                move.wait()
            values = jnp.max(held[...], axis=0)
            self.mid[...] = values
        return values


def peak_scratch():
    datas, parts = 1 << bits_of("dp"), 1 << bits_of("tensor")
    tile = (8, LANES)
    return [pltpu.VMEM(dims, F32) for dims in (tile, (datas,) + tile, tile, (parts,) + tile)]


def peak_moves():
    return (1 << bits_of("dp")) + (1 << bits_of("tensor")) - 2


def hosting(body, counts, given, row, peak):
    ins, outs = counts
    sources = sum(1 + count for count in given)

    def kernel(*refs):
        body_ins, (range_ref, before_ref) = refs[:ins], refs[ins : ins + 2]
        held, rest = list(refs[ins + 2 : ins + 2 + sources]), refs[ins + 2 + sources :]
        body_outs, level_ref = rest[:outs], rest[outs]
        sides, rest = rest[outs + 1 : outs + 1 + 2 * len(given)], rest[outs + 1 + 2 * len(given) :]
        body_scratch, vias = rest[: -7 - len(given)], rest[-7 - len(given) : -7]
        mover = Mover(*rest[-3:])
        peaks = Peaks(mover, *rest[-7:-3])
        weights = []
        for i, count in enumerate(given):
            own, *there = [held.pop(0) for _ in range(1 + count)]
            near, far = slots(sides[2 * i]), slots(sides[2 * i + 1])
            weights.append((OverPlane(mover, own, near, far, there, vias[i]), count))
        step, steps = 0, 1
        for i in range(HOST_RANK[body]):
            step = step * pl.num_programs(i) + pl.program_id(i)
            steps = steps * pl.num_programs(i)

        @pl.when(step == 0)
        def _():
            call_out(all_distances())
            if weights:
                await_all(all_distances())
            for weight, count in weights:
                weight.start()
                if count:
                    weight.relay()

        @pl.when(step == steps * 5 // 8)
        def _():
            for weight, count in weights:
                weight.settle()
                if not count:
                    weight.relay()

        body(*body_ins, *body_outs, *body_scratch)

        @pl.when(step == steps - 1)
        def _():
            if not weights:
                await_all(all_distances())
            for weight, _ in weights:
                weight.complete()
            largest = jnp.max(peaks.reach(body_outs[peak][...]), keepdims=True)
            level = DECAY * range_ref[row] + (1.0 - DECAY) * largest
            places = lax.broadcasted_iota(jnp.int32, level_ref.shape, 0)
            level_ref[...] = jnp.where(places == row, level, before_ref[...])
            for weight, _ in weights:
                weight.finish()

    return kernel


def hosted_call(body, weights, cid, ranges, levels, row, peak, *, grid, in_specs, out_specs, out_shape, scratch_shapes=(), **rest):
    plane = 1 << (bits_of("dp") - 1)
    counts = (len(in_specs), len(out_specs))
    given = [len(there) for _, there in weights]
    totals = [sum(column) for column in zip((peak_moves(), 1), *[plane_counts(count) for count in given])]
    small = pl.BlockSpec((8, LANES), lambda *steps: (0, 0))
    out_shape, vias, sources = out_shape + [shape_of((8, LANES), F32)], [], []
    for held, there in weights:
        out_shape += [shape_of((plane,) + held.shape, held.dtype)] * 2
        vias.append(pltpu.VMEM((1 + len(there),) + held.shape, held.dtype))
        sources += [held] + list(there)
    call = pl.pallas_call(
        hosting(body, counts, given, row, peak),
        grid=grid,
        in_specs=in_specs + [in_smem(), small] + [anywhere()] * len(sources),
        out_specs=out_specs + [small] + [anywhere()] * 2 * len(weights),
        out_shape=out_shape,
        scratch_shapes=list(scratch_shapes) + vias + peak_scratch() + copy_semaphores(*totals),
        compiler_params=params(collective_id=cid, has_side_effects=True),
        **rest,
    )

    def run(*args):
        results = call(*args, ranges, levels, *sources)
        return results[: counts[1]], results[counts[1]], results[counts[1] + 1 :]

    return run


def first_gather_kernel(
    first_ref, bias_ref, out_ref, in_ref, near, far, held_bias, near_out, far_out, held_in, held_out, send, recv, own
):
    mover = Mover(send, recv, own)
    parts, plane = near.shape[1], near.shape[0]
    moves, relays = plane_moves()
    along = AlongParts(mover, first_ref, lambda r: near.at[0, r])
    sources = [first_ref] + [near.at[0, r] for r in range(1, parts)]
    over = [[mover.remote(sources[r], near.at[slot, r], "dp", d) for slot, d in moves] for r in range(parts)]
    again = [
        [
            mover.remote(halves_of(near.at[source, r], half), halves_of(near.at[slot, r], half), "dp", d)
            for slot, source, d, half in relays
        ]
        for r in range(parts)
    ]
    cores = [
        [mover.remote(sources[r] if slot == 0 else near.at[slot, r], far.at[slot, r], "dp", 1) for slot in range(plane)]
        for r in range(parts)
    ]
    later = [
        AlongParts(mover, source, lambda r, held=held: held.at[r])
        for source, held in ((bias_ref, held_bias), (out_ref, held_out), (in_ref, held_in))
    ]
    outer = OverPlane(mover, held_out, slots(near_out), slots(far_out))
    greet(part_distances() + plane_distances())
    along.start()
    for move in over[0] + cores[0][:1]:
        move.start()
    along.hand_on()
    for units in later[:2]:
        units.start()
    for r in along.order:
        along.arrive(r)
        for move in over[r] + cores[r][:1]:
            move.start()
    for units in later[:2]:
        units.hand_on()
    later[2].start()
    later[1].finish()
    outer.start()
    later[2].hand_on()
    order = [0] + along.order
    for r in order:
        for i, (slot, _) in enumerate(moves):
            over[r][i].wait_recv()
            cores[r][slot].start()
        for move in again[r]:
            move.start()
    outer.relay()
    for r in order:
        for move in again[r]:
            move.wait_recv()
        for slot in range(1 + len(moves), plane):
            cores[r][slot].start()
    along.finish()
    for r in range(parts):
        for move in over[r] + again[r]:
            move.wait_send()
        for move in cores[r]:
            move.wait()
    outer.complete()
    outer.finish()
    for units in (later[0], later[2]):
        units.finish()


def first_gather(first, biases, outer, inner):
    parts, plane = 1 << bits_of("tensor"), 1 << (bits_of("dp") - 1)
    moves, relays = plane_moves()
    remote = 4 * (parts - 1) + parts * (len(moves) + len(relays) + plane) + plane_counts(0)[0]
    return pl.pallas_call(
        first_gather_kernel,
        in_specs=[pl.BlockSpec(memory_space=pltpu.VMEM)] * 4,
        out_specs=[anywhere()] * 6,
        out_shape=[shape_of((plane, parts) + first.shape, BF16)] * 2
        + [shape_of((parts,) + biases.shape, BF16)]
        + [shape_of((plane, parts) + outer.shape, BF16)] * 2
        + [shape_of((parts,) + inner.shape, BF16)],
        scratch_shapes=[pltpu.VMEM((parts,) + outer.shape, BF16)] + copy_semaphores(remote, 5),
        compiler_params=params(collective_id=3, has_side_effects=True),
        name="first_gather",
    )(first, biases, outer, inner)


CHUNK = 2


def finale_kernel(
    down_sum, down_more, in_sum, in_more, keep_0, more_0, keep_1, more_1, keep_2, more_2, keep_3, more_3,
    slope_q, slope_in, slope_down, sums_ref, near_d, far_d, near_i, far_i, near_q, far_q, sums_out,
    piece_d, piece_i, send_q, recv_q, piece_q, send_p, recv_p, sums_near, sums_mid, sums_far, send, recv, own
):
    mover = Mover(send, recv, own)
    _, orders = plane_orders()
    keeps, mores = (keep_0, keep_1, keep_2, keep_3), (more_0, more_1, more_2, more_3)
    quarter, kinds = keep_0.shape[1:3]
    parts, datas, chunks = 4 * quarter, sums_near.shape[0], kinds // CHUNK
    steps = [
        [mover.remote(send_p.at[k, i], recv_p.at[k, i], "dp", 1 << orders[i % 2][-1]) for i in range(4)]
        for k in range(chunks)
    ]
    along = [
        [mover.remote(send_q.at[k, r - 1], recv_q.at[k, r - 1], axis, r) for axis, r in part_distances()]
        for k in range(chunks)
    ]
    down = OverPlane(mover, piece_d, slots(near_d), slots(far_d))
    inner = OverPlane(mover, piece_i, slots(near_i), slots(far_i))
    first = [
        OverPlane(
            mover,
            piece_q.at[k],
            slots(near_q, pl.ds(k * CHUNK, CHUNK)),
            slots(far_q, pl.ds(k * CHUNK, CHUNK)),
        )
        for k in range(chunks)
    ]
    me = lax.axis_index("dp")
    sum_data = [
        mover.remote(sums_ref.at[at_distance("dp", r)], sums_near.at[r], "dp", r) for r in range(1, datas)
    ]
    sum_back = [mover.remote(sums_out.at[me], sums_out.at[me], "dp", r) for r in range(1, datas)]
    sum_part = [mover.remote(sums_mid, sums_far.at[r], axis, r) for axis, r in part_distances()]

    def kinds_of(k):
        return slice(k * CHUNK, (k + 1) * CHUNK)

    def block(k, r):
        i, j = r // quarter, r % quarter
        here = keeps[i][0, j, kinds_of(k)] + mores[i][0, j, kinds_of(k)].astype(F32)
        return here + recv_p[k, i, j].astype(F32)

    def reach(k):
        total = block(k, 0)
        for r in range(1, parts):
            along[k][r - 1].wait_recv()
            total = total + recv_q[k, r - 1].astype(F32)
        piece_q[k] = low(total * slope_q[kinds_of(k)])
        first[k].start()

    call_out(all_distances())
    for k in range(chunks):
        for i in (3, 2, 1, 0):
            more = mores[i][1, :, kinds_of(k)].astype(F32)
            send_p[k, i] = low(keeps[i][1, :, kinds_of(k)] + more)
    await_all(all_distances())
    for move in sum_data:
        move.start()
    for k in range(chunks):
        for i in (3, 2, 1, 0):
            steps[k][i].start()
    piece_d[...] = low((down_sum[...] + down_more[...].astype(F32)) * slope_down[...])
    piece_i[...] = low((in_sum[...] + in_more[...].astype(F32)) * slope_in[...])
    down.start()
    inner.start()
    for k in range(chunks):
        for i in (3, 2, 1, 0):
            steps[k][i].wait_recv()
            for r in range(i * quarter, (i + 1) * quarter):
                if r:
                    send_q[k, r - 1] = low(block(k, r))
                    along[k][r - 1].start()
    for move in sum_data:
        move.wait()
    sums_near[0] = sums_ref[me]
    sums_mid[...] = jnp.sum(sums_near[...], axis=0)
    for move in sum_part:
        move.start()
    reach(0)
    down.relay()
    inner.relay()
    for k in range(1, chunks):
        reach(k)
        first[k - 1].relay()
    for move in sum_part:
        move.wait()
    sums_far[0] = sums_mid[...]
    sums_out[me] = jnp.sum(sums_far[...], axis=0)
    for move in sum_back:
        move.start()
    first[chunks - 1].relay()
    for unit in [down, inner] + first:
        unit.complete()
    for move in sum_back:
        move.wait()
    for unit in [down, inner] + first:
        unit.finish()
    for group in steps + along:
        for move in group:
            move.wait_send()


def finale(down, inner, first, slopes, sums):
    parts, plane, datas = 1 << bits_of("tensor"), 1 << (bits_of("dp") - 1), 1 << bits_of("dp")
    pieces = [slopes[2], slopes[1], slopes[0]]
    _, quarter, kinds, rows, c = first[0][0].shape
    chunks = kinds // CHUNK
    remote = chunks * (4 + parts - 1) + (2 + chunks) * plane_counts(0)[0] + 2 * (datas - 1) + parts - 1
    dims = sums.shape
    sums = sums.reshape(datas, -1, LANES)
    own = sums.shape[1:]
    vmem = pl.BlockSpec(memory_space=pltpu.VMEM)
    scratch = [pltpu.VMEM(piece.shape, BF16) for piece in pieces[:2]]
    scratch += [pltpu.VMEM((chunks, parts - 1, CHUNK, rows, c), BF16)] * 2
    scratch += [pltpu.VMEM((chunks, CHUNK, rows, c), BF16)]
    scratch += [pltpu.VMEM((chunks, 4, quarter, CHUNK, rows, c), BF16)] * 2
    scratch += [
        pltpu.VMEM(sums.shape, F32),
        pltpu.VMEM(own, F32),
        pltpu.VMEM((parts,) + own, F32),
    ]
    out_shape = []
    for piece in pieces:
        out_shape += [shape_of((plane,) + piece.shape, BF16)] * 2
    args = [*down, *inner]
    for pair in first:
        args += list(pair)
    args += [*slopes, sums]
    results = pl.pallas_call(
        finale_kernel,
        in_specs=[vmem] * len(args),
        out_specs=[anywhere()] * 6 + [vmem],
        out_shape=out_shape + [shape_of(sums.shape, F32)],
        scratch_shapes=scratch + copy_semaphores(remote, 2 + chunks),
        compiler_params=params(collective_id=2, has_side_effects=True),
        name="finale",
    )(*args)
    return [results[2 * i : 2 * i + 2] for i in range(3)], results[6].reshape(dims)


class Order:
    def __init__(self, width):
        self.rows = width // (1 << bits_of("dp"))

    def __getitem__(self, j):
        if self.rows % LANES:
            return j
        plane, each = 1 << (bits_of("dp") - 1), self.rows // LANES
        place = j // each
        return at_distance("dp", place % plane * 2 + place // plane) * each + j % each


def take_blocks(ref, order_ref, here=slice(None)):
    return jnp.concatenate(
        [
            ref[here, pl.ds(pl.multiple_of(order_ref[j] * LANES, LANES), LANES)]
            for j in range(ref.shape[1] // LANES)
        ],
        axis=1,
    )


def put_blocks(ref, order_ref, values):
    for j in range(ref.shape[1] // LANES):
        ref[:, pl.ds(pl.multiple_of(order_ref[j] * LANES, LANES), LANES)] = values[
            :, j * LANES : (j + 1) * LANES
        ]


def fold_peak(values):
    return jnp.max(jnp.abs(values).reshape(-1, 8, LANES), axis=0)


def column_peak(values):
    peak = fold_peak(values[:, :LANES])
    for j in range(1, values.shape[1] // LANES):
        peak = jnp.maximum(peak, fold_peak(values[:, j * LANES : (j + 1) * LANES]))
    return peak


def lane_peak(values):
    return jnp.max(column_peak(values), axis=0, keepdims=True)


def prepare_kernel(
    range_ref, x_ref, qkv_ref, out_ref, in_ref, down_ref, level_ref, quant_ref, *refs
):
    peaks = Peaks(Mover(*refs[-3:-1], None), *refs[-7:-3])
    call_out(all_distances())
    order = Order(x_ref.shape[1])
    rows = 256
    steps = x_ref.shape[0] // rows

    def largest(step, peak):
        here = pl.ds(pl.multiple_of(step * rows, rows), rows)
        return jnp.maximum(peak, column_peak(x_ref[here, :].astype(F32)))

    own = [qkv_ref[j].astype(F32) for j in range(3)]
    own += [ref[0].astype(F32) for ref in (out_ref, in_ref, down_ref)]
    found = [lane_peak(values) for values in own]
    inputs = lax.fori_loop(0, steps, largest, jnp.zeros((8, LANES), F32))
    found.append(jnp.max(inputs, axis=0, keepdims=True))
    found.append(jnp.zeros((1, LANES), F32))
    found = jnp.concatenate(found, axis=0)
    await_all(all_distances())
    reached = jnp.max(peaks.reach(found), axis=1, keepdims=True)
    level = DECAY * range_ref[0] + (1.0 - DECAY) * reached[6:7, :]
    level_ref[...] = jnp.broadcast_to(level, level_ref.shape)
    for i, values in enumerate(own):
        bound = 0.5 * reached[i : i + 1, :]
        tangent = jnp.tanh(values / bound)
        quant, slope = low(bound * tangent), 1.0 - tangent * tangent
        if i < 4:
            refs[4][i] = slope
        else:
            refs[1 + i][0] = slope
        if i < 3:
            refs[0][i] = quant
        else:
            refs[i - 2][0] = quant

    @pl.loop(0, steps)
    def _(step):
        here = pl.ds(pl.multiple_of(step * rows, rows), rows)
        x = take_blocks(x_ref, order, here).astype(F32)
        quant_ref[here, :] = low(level * jnp.tanh(x / level))


def prepare(ranges, x, own):
    vmem = pl.BlockSpec(memory_space=pltpu.VMEM)
    out_shape = [shape_of((8, LANES), F32), shape_of(x.shape, BF16)]
    out_shape += [shape_of(values.shape, BF16) for values in own]
    out_shape += [shape_of((4,) + own[0].shape[1:], F32)]
    out_shape += [shape_of(values.shape, F32) for values in own[2:]]
    levels, quant, *rest = pl.pallas_call(
        prepare_kernel,
        in_specs=[in_smem()] + [vmem] * 5,
        out_specs=[vmem] * 9,
        out_shape=out_shape,
        scratch_shapes=peak_scratch() + copy_semaphores(peak_moves(), 1),
        compiler_params=params(collective_id=0, has_side_effects=True),
        name="prepare",
    )(ranges, x, *own)
    return levels, quant, rest[:4], rest[4:]


def qkv_kernel(x_ref, near_ref, far_ref, b_ref, o_ref):
    half = x_ref.shape[1] // 2
    for i in range(o_ref.shape[0]):
        total = dot(x_ref[:, :half], flat(near_ref[:, i])) + dot(x_ref[:, half:], flat(far_ref[:, i]))
        o_ref[i] = low(total + b_ref[i])


def qkv_rows(x, weights, bias):
    near, far = weights
    plane, parts, kinds, rows, c = near.shape
    tokens, width = x.shape
    weight_spec = pl.BlockSpec((plane, None, kinds, rows, c), lambda r: (0, r, 0, 0, 0))
    return pl.pallas_call(
        qkv_kernel,
        grid=(parts,),
        in_specs=[
            pl.BlockSpec((tokens, width), lambda r: (0, 0)),
            weight_spec,
            weight_spec,
            pl.BlockSpec((kinds, 1, c), lambda r: (0, 0, r)),
        ],
        out_specs=pl.BlockSpec((kinds, tokens, c), lambda r: (0, 0, r)),
        out_shape=shape_of((kinds, tokens, parts * c), BF16),
        compiler_params=params(),
        cost_estimate=cost(2 * tokens * width * kinds * parts * c, 14 * MIB),
        name="qkv",
    )(x, near, far, bias)


def fill_mask(mask_ref, ends_ref):
    row = pl.program_id(0)

    def segments(dims, axis):
        places = lax.broadcasted_iota(jnp.int32, dims, axis)
        count = jnp.zeros(dims, jnp.int32)
        for j in range(ends_ref.shape[1]):
            count = count + (places >= ends_ref[row, j]).astype(jnp.int32)
        return count

    same = segments((SEQ, 1), 0) == segments((1, SEQ), 1)
    mask_ref[...] = jnp.where(same, 0.0, MASKED).astype(F32)


def attend_kernel(
    skip, ends_ref, q_ref, k_ref, v_ref, *refs
):
    o_ref, lse_ref, peak_ref, mask_ref, sums_ref = refs[-5:]
    row, pair = pl.program_id(0), pl.program_id(1)
    factor = HD ** (-0.5)

    @pl.when(pair == 0)
    def _():
        fill_mask(mask_ref, ends_ref)
        sums_ref[...] = jnp.zeros_like(sums_ref) if skip == 0 else refs[0][...].T

    @pl.when((pair == 0) & (row == 0))
    def _():
        peak_ref[...] = jnp.zeros_like(peak_ref) if skip == 0 else refs[1][...]

    rows = SEQ
    lanes = lax.broadcasted_iota(jnp.int32, (rows, LANES), 1)
    for start in range(0, SEQ, rows):
        here = pl.ds(start, rows)
        q = q_ref[here, :] * jnp.asarray(factor, BF16)
        parts = []
        sums = sums_ref[here, :]
        for head in range(LANES // HD):
            own = lanes // HD == head
            scores = dot_cols(jnp.where(own, q, jnp.zeros_like(q)), k_ref[...]) + mask_ref[here, :]
            row_max = jnp.max(scores, axis=-1, keepdims=True)
            exponent = jnp.exp(scores - row_max)
            totals = jnp.sum(exponent, axis=-1, keepdims=True)
            probs = low(exponent * (1.0 / totals))
            parts.append(dot(probs, v_ref[...]))
            sums = jnp.where(lanes == (pair + skip) * (LANES // HD) + head, row_max + jnp.log(totals), sums)
        context = parts[0]
        for head in range(1, LANES // HD):
            context = jnp.where(lanes // HD == head, parts[head], context)
        o_ref[here, :] = context
        sums_ref[here, :] = sums
        peak_ref[...] = jnp.maximum(peak_ref[...], fold_peak(context))

    @pl.when(pair == pl.num_programs(1) - 1)
    def _():
        lse_ref[...] = sums_ref[...].T


def attend_first_kernel(*refs):
    attend_kernel(0, *refs)


def attend_last_kernel(*refs):
    attend_kernel(pl.num_programs(1), *refs)


def attend(qkv, ends, lse=None, peak=None, context=None, weights=(), ranges=None, levels=None):
    _, tokens, width = qkv.shape
    held = tokens // SEQ
    last = context is not None
    skip = width // LANES // 2 if last else 0

    def side(i):
        return pl.BlockSpec((None, SEQ, LANES), lambda r, j: (i, r, j + skip))

    sums = pl.BlockSpec((None, LANES, SEQ), lambda r, j: (r, 0, 0))
    small = pl.BlockSpec((8, LANES), lambda r, j: (0, 0))
    setup = dict(
        grid=(held, width // LANES // 2),
        in_specs=[in_smem(), side(0), side(1), side(2)],
        out_specs=[pl.BlockSpec((SEQ, LANES), lambda r, j: (r, j + skip)), sums, small],
        out_shape=[
            shape_of((tokens, width), F32),
            shape_of((held, LANES, SEQ), F32),
            shape_of((8, LANES), F32),
        ],
        scratch_shapes=[pltpu.VMEM((SEQ, SEQ), F32), pltpu.VMEM((SEQ, LANES), F32)],
        cost_estimate=cost(15e9, 40 * MIB),
        name="attend",
    )
    args = (ends, qkv, qkv, qkv)
    if not last:
        return pl.pallas_call(attend_first_kernel, compiler_params=params(), **setup)(*args)
    setup["in_specs"] += [sums, small, anywhere()]
    run = hosted_call(
        attend_last_kernel, weights, 5, ranges, levels, 1, 2, input_output_aliases={6: 0}, **setup
    )
    return run(*args, lse, peak, context)


def attend_back_kernel(
    c, first, order_ref, ends_ref, q_ref, k_ref, v_ref, g_ref, lse_ref, before_ref, dq_ref, dk_ref,
    dv_ref, sum_ref, mask_ref
):
    pair = pl.program_id(1)

    @pl.when((pair == 0) & (pl.program_id(0) == 0))
    def _():
        sum_ref[...] = before_ref[...]

    factor = HD ** (-0.5)

    @pl.when(pair == 0)
    def _():
        fill_mask(mask_ref, ends_ref)

    lanes = lax.broadcasted_iota(jnp.int32, (SEQ, LANES), 1)
    q, k, v, g = q_ref[...], k_ref[...], v_ref[...], g_ref[...]
    heads, zero = LANES // HD, jnp.zeros((SEQ, LANES), BF16)
    probs, grad_scores = [], []
    for head in range(heads):
        own = lanes // HD == head
        q_own = jnp.where(own, q * jnp.asarray(factor, BF16), zero)
        g_own = jnp.where(own, g, zero)
        logsum = lse_ref[pl.ds((pair + first // LANES) * heads + head, 1), :]
        prob = jnp.exp(dot_cols(k, q_own) + mask_ref[...] - logsum)
        grad_probs = dot_cols(v, g_own)
        mean_grad = jnp.sum(prob * grad_probs, axis=0, keepdims=True)
        probs.append(low(prob))
        grad_scores.append(low(factor * prob * (grad_probs - mean_grad)))
    v_sums = dot(jnp.concatenate(probs, axis=0), g)
    k_sums = dot(jnp.concatenate(grad_scores, axis=0), q)
    q_sums = dot_rows(jnp.concatenate(grad_scores, axis=1), k)

    def join(parts):
        joined = parts[:SEQ]
        for head in range(1, heads):
            joined = jnp.where(lanes // HD == head, parts[head * SEQ : (head + 1) * SEQ], joined)
        return low(joined)

    dq, dv = join(q_sums), join(v_sums)
    dq_ref[...] = dq
    dk_ref[...] = join(k_sums)
    dv_ref[...] = dv
    column = first + pair * LANES
    place = order_ref[column // c] * c + column % c
    here = pl.ds(pl.multiple_of(place, LANES), LANES)
    sum_ref[0:1, here] += jnp.sum(dq.astype(F32), axis=0, keepdims=True)
    sum_ref[1:2, here] += jnp.sum(dv.astype(F32), axis=0, keepdims=True)


def attend_back(qkv, grad, ends, lse, before, part_order, c, first):
    _, tokens, inner = qkv.shape
    width = inner // 2
    held = tokens // SEQ
    skip = first // LANES

    def side(i):
        return pl.BlockSpec((None, SEQ, LANES), lambda r, j: (i, r, j + skip))

    block = pl.BlockSpec((SEQ, LANES), lambda r, j: (r, j))
    sums = pl.BlockSpec((8, inner), lambda r, j: (0, 0))
    return pl.pallas_call(
        partial(attend_back_kernel, c, first),
        grid=(held, width // LANES),
        in_specs=[
            in_smem(),
            in_smem(),
            side(0),
            side(1),
            side(2),
            pl.BlockSpec((SEQ, LANES), lambda r, j: (r, j + skip)),
            pl.BlockSpec((None, LANES, SEQ), lambda r, j: (r, 0, 0)),
            sums,
        ],
        out_specs=[block, block, block, sums],
        out_shape=[shape_of((tokens, width), BF16)] * 3 + [shape_of((8, inner), F32)],
        scratch_shapes=[pltpu.VMEM((SEQ, SEQ), F32)],
        compiler_params=params(),
        cost_estimate=cost(15e9, 50 * MIB),
        name="attend_back",
    )(part_order, ends, qkv, qkv, qkv, grad, lse, before)


def project(values, *sides):
    halves = []
    for refs in (sides[::2], sides[1::2]):
        total, place = None, 0
        for ref in refs:
            c = ref.shape[3]
            for r in range(ref.shape[1]):
                term = dot_cols(values[:, place : place + c], flat(ref[:, r]))
                total = term if total is None else total + term
                place += c
        halves.append(total)
    return jnp.concatenate(halves, axis=1)


def norm_parts(summed):
    center = summed - jnp.mean(summed, axis=-1, keepdims=True)
    inverse = lax.rsqrt(jnp.mean(center * center, axis=-1, keepdims=True) + EPS)
    return center * inverse, inverse


def norm_back(upstream, normal, inverse, gain):
    scaled = upstream * gain
    return inverse * (
        scaled
        - jnp.mean(scaled, axis=-1, keepdims=True)
        - normal * jnp.mean(scaled * normal, axis=-1, keepdims=True)
    )


def add_sums(ref, order_ref, sums):
    @pl.when(pl.program_id(0) == 0)
    def _():
        ref[...] = jnp.zeros_like(ref)

    for i, values in enumerate(sums):
        total = jnp.sum(values, axis=0, keepdims=True)
        for j in range(ref.shape[1] // LANES):
            here = pl.ds(pl.multiple_of(order_ref[j] * LANES, LANES), LANES)
            ref[i : i + 1, here] += total[:, j * LANES : (j + 1) * LANES]


def first_norm_kernel(
    ctx_ref, level_ref, near_ref, far_ref, x_ref, row_ref, quant_ref, normed_ref, normal_ref,
    inverse_ref, peak_ref
):
    level = level_ref[1:2, 0:1]
    quant = low(level * jnp.tanh(ctx_ref[...] / level))
    quant_ref[...] = quant
    order = Order(x_ref.shape[1])
    vectors = take_blocks(row_ref, order)
    summed = take_blocks(x_ref, order).astype(F32) + project(quant, near_ref, far_ref)
    normal, inverse = norm_parts(summed + vectors[0:1, :])
    normed = normal * vectors[1:2, :] + vectors[2:3, :]
    normed_ref[...] = normed
    normal_ref[...] = normal
    inverse_ref[...] = inverse

    @pl.when(pl.program_id(0) == 0)
    def _():
        peak_ref[...] = jnp.zeros_like(peak_ref)

    peak_ref[...] = jnp.maximum(peak_ref[...], column_peak(normed))


def whole(values):
    dims = values.shape
    return pl.BlockSpec(dims, lambda *steps: (0,) * len(dims))


def first_norm(context, level, weights, x, vectors, ranges):
    near, far = weights
    tokens, width = x.shape
    inner = context.shape[1]
    rows = 512

    def block(columns):
        return pl.BlockSpec((rows, columns), lambda t: (t, 0))

    run = hosted_call(
        first_norm_kernel,
        [],
        7,
        ranges,
        level,
        2,
        4,
        grid=(tokens // rows,),
        in_specs=[
            block(inner),
            whole(level),
            whole(near),
            whole(far),
            block(width),
            whole(vectors),
        ],
        out_specs=[
            block(inner),
            block(width),
            block(width),
            block(1),
            pl.BlockSpec((8, LANES), lambda t: (0, 0)),
        ],
        out_shape=[
            shape_of((tokens, inner), BF16),
            shape_of((tokens, width), F32),
            shape_of((tokens, width), F32),
            shape_of((tokens, 1), F32),
            shape_of((8, LANES), F32),
        ],
        cost_estimate=cost(2 * tokens * width * inner, 20 * MIB),
        name="first_norm",
    )
    return run(context, level, near, far, x, vectors)


def hidden_kernel(normed_ref, level_ref, near_ref, far_ref, b_ref, quant_ref, act_ref, slope_ref, peak_ref):
    half = normed_ref.shape[1] // 2

    @pl.when(pl.program_id(0) == 0)
    def _():
        peak_ref[...] = jnp.zeros_like(peak_ref)
        level = level_ref[2:3, 0:1]
        quant_ref[...] = low(level * jnp.tanh(normed_ref[...] / level))

    hidden = dot(quant_ref[:, :half], flat(near_ref[...]))
    hidden = hidden + dot(quant_ref[:, half:], flat(far_ref[...])) + b_ref[...]
    share = 0.5 + 0.5 * lax.erf(hidden * (0.5**0.5))
    active = hidden * share
    act_ref[...] = active
    slope_ref[...] = share + hidden * ((0.5 / jnp.pi) ** 0.5 * jnp.exp(-0.5 * hidden * hidden))
    peak_ref[...] = jnp.maximum(peak_ref[...], column_peak(active))


def hidden_rows(normed, level, weights, bias, held_down, ranges):
    near, far = weights
    plane, parts, rows, c = near.shape
    tokens, width = normed.shape
    step = min(c, 512)
    cuts = c // step
    weight_spec = pl.BlockSpec((plane, None, rows, step), lambda s: (0, s // cuts, 0, s % cuts))
    block = pl.BlockSpec((tokens, step), lambda s: (0, s))
    run = hosted_call(
        hidden_kernel,
        [(held_down, ())],
        6,
        ranges,
        level,
        3,
        3,
        grid=(parts * cuts,),
        in_specs=[
            whole(normed),
            whole(level),
            weight_spec,
            weight_spec,
            pl.BlockSpec((1, step), lambda s: (0, s)),
        ],
        out_specs=[
            pl.BlockSpec((tokens, width), lambda s: (0, 0)),
            block,
            block,
            pl.BlockSpec((8, LANES), lambda s: (0, 0)),
        ],
        out_shape=[
            shape_of((tokens, width), BF16),
            shape_of((tokens, parts * c), F32),
            shape_of((tokens, parts * c), F32),
            shape_of((8, LANES), F32),
        ],
        cost_estimate=cost(2 * tokens * width * parts * c, 50 * MIB),
        name="hidden",
    )
    return run(normed, level, near, far, bias)


def second_norm_kernel(
    order_ref, act_ref, level_ref, near_a, far_a, near_b, far_b, normed_ref, grad_ref, row_ref,
    quant_ref, out_ref, sum_ref, branch_ref, terms_ref
):
    level = level_ref[3:4, 0:1]
    quant = low(level * jnp.tanh(act_ref[...] / level))
    quant_ref[...] = quant
    vectors = take_blocks(row_ref, order_ref)
    summed = normed_ref[...] + project(quant, near_a, far_a, near_b, far_b) + vectors[3:4, :]
    normal, inverse = norm_parts(summed)
    gain = vectors[4:5, :]
    put_blocks(out_ref, order_ref, low(normal * gain + vectors[5:6, :]))
    upstream = take_blocks(grad_ref, order_ref).astype(F32)
    grad_sum = norm_back(upstream, normal, inverse, gain)
    sum_ref[...] = grad_sum
    branch_ref[...] = low(grad_sum)
    add_sums(terms_ref, order_ref, (grad_sum, upstream * normal, upstream))


def second_norm(active, level, weights, normed, grad, vectors, order):
    tokens, width = normed.shape
    inner = active.shape[1]
    rows = 256

    def block(columns):
        return pl.BlockSpec((rows, columns), lambda t: (t, 0))

    return pl.pallas_call(
        second_norm_kernel,
        grid=(tokens // rows,),
        in_specs=[
            in_smem(),
            block(inner),
            whole(level),
            *[whole(side) for side in weights],
            block(width),
            block(width),
            whole(vectors),
        ],
        out_specs=[
            block(inner),
            block(width),
            block(width),
            block(width),
            pl.BlockSpec((8, width), lambda t: (0, 0)),
        ],
        out_shape=[
            shape_of((tokens, inner), BF16),
            shape_of((tokens, width), BF16),
            shape_of((tokens, width), F32),
            shape_of((tokens, width), BF16),
            shape_of((8, width), F32),
        ],
        compiler_params=params(),
        cost_estimate=cost(2 * tokens * width * inner, 80 * MIB),
        name="second_norm",
    )(order, active, level, *weights, normed, grad, vectors)


def weight_specs(xs, products, parts, plane, c):
    tokens, width = xs[0].shape
    count = len(products)
    step = min(c, 1024)
    cuts = c // step
    dims = (plane, parts, count, width // (2 * plane), c)
    in_specs = [
        pl.BlockSpec((tokens, step), lambda r, j, first=first: (0, (r + first) * cuts + j))
        for _, _, first in products
    ]
    out_spec = pl.BlockSpec((plane, None, count, dims[3], step), lambda r, j: (0, r, 0, 0, j))
    estimate = cost(tokens * width * parts * c * count, 20 * MIB)
    return dims, (parts, cuts), in_specs, out_spec, estimate


def turn_once(x_refs, turned_refs):
    @pl.when((pl.program_id(0) == 0) & (pl.program_id(1) == 0))
    def _():
        for x_ref, turned_ref in zip(x_refs, turned_refs):
            turned_ref[...] = x_ref[...].T


def weight_send_kernel(count, which, *refs):
    x_refs, h_refs = refs[:count], refs[count : count + len(which)]
    send_ref, turned = refs[count + len(which)], refs[count + len(which) + 1 :]
    turn_once(x_refs, turned)
    for i, h_ref in enumerate(h_refs):
        h = h_ref[...]
        total = dot(turned[which[i]][...], h)
        send_ref[:, i] = low(total).reshape(send_ref.shape[0], -1, h.shape[1])


def weight_send(xs, products, parts, plane, c):
    dims, grid, in_specs, out_spec, estimate = weight_specs(xs, products, parts, plane, c)
    tokens, width = xs[0].shape
    return pl.pallas_call(
        partial(weight_send_kernel, len(xs), [product[0] for product in products]),
        grid=grid,
        in_specs=[pl.BlockSpec((tokens, width // 2), lambda r, j: (0, 1))] * len(xs) + in_specs,
        out_specs=out_spec,
        out_shape=shape_of(dims, BF16),
        scratch_shapes=[pltpu.VMEM((width // 2, tokens), BF16)] * len(xs),
        compiler_params=params(),
        cost_estimate=estimate,
        name="weight_send",
    )(*xs, *[product[1] for product in products])


def weight_keep_kernel(count, which, split, *refs):
    x_refs, other_ref = refs[:count], refs[count]
    h_refs = refs[count + 1 : count + 1 + len(which)]
    outs, turned = refs[count + 1 + len(which) : -count], refs[-count:]
    half = pl.num_programs(0) // 2
    turn_once(x_refs, turned)
    for side in range(2):

        @pl.when(pl.program_id(0) // half == side)
        def _(side=side):
            keep_ref, send_ref = outs[2 * side : 2 * side + 2]
            for i, h_ref in enumerate(h_refs):
                h = h_ref[...]
                total = dot(turned[which[i]][...], h).reshape(other_ref.shape[0], -1, h.shape[1])
                for j, slot in enumerate(split[side][0]):
                    keep_ref[j, i] = total[slot] + other_ref[slot, i].astype(F32)
                for j, slot in enumerate(split[side][1]):
                    send_ref[j, i] = low(total[slot] + other_ref[slot, i].astype(F32))


def weight_keep(xs, products, other, parts, plane, c):
    dims, (_, cuts), in_specs, out_spec, estimate = weight_specs(xs, products, parts, plane, c)
    tokens, width = xs[0].shape
    half = parts // 2
    block = (plane // 2, None, dims[2], dims[3], c // cuts)
    near = pl.BlockSpec(
        block, lambda r, j: (0, jnp.minimum(r, half - 1), 0, 0, jnp.where(r < half, j, cuts - 1))
    )
    far = pl.BlockSpec(block, lambda r, j: (0, jnp.maximum(r - half, 0), 0, 0, jnp.where(r < half, 0, j)))
    small = (plane // 2, half) + dims[2:]
    which = [product[0] for product in products]
    keep_a, send_a, keep_b, send_b = pl.pallas_call(
        partial(weight_keep_kernel, len(xs), which, first_split(bits_of("dp") - 1)),
        grid=(parts, cuts),
        in_specs=[pl.BlockSpec((tokens, width // 2), lambda r, j: (0, 0))] * len(xs)
        + [out_spec]
        + in_specs,
        out_specs=[near, near, far, far],
        out_shape=[shape_of(small, F32), shape_of(small, BF16)] * 2,
        scratch_shapes=[pltpu.VMEM((width // 2, tokens), BF16)] * len(xs),
        compiler_params=params(),
        cost_estimate=estimate,
        name="weight_keep",
    )(*xs, other, *[product[1] for product in products])
    return [keep_a, keep_b], [send_a, send_b]


def grad_hidden_kernel(
    cuts, order_ref, g_ref, near_a, far_a, near_b, far_b, act_ref, slope_ref, level_ref, o_ref, sum_ref
):
    half = g_ref.shape[1] // 2
    block = pl.program_id(0)
    columns = act_ref.shape[1]
    level = level_ref[3:4, 0:1]

    @pl.when(block == 0)
    def _():
        sum_ref[...] = jnp.zeros_like(sum_ref)

    for side, (near_ref, far_ref) in enumerate(((near_a, far_a), (near_b, far_b))):

        @pl.when(block * 2 // pl.num_programs(0) == side)
        def _(near_ref=near_ref, far_ref=far_ref):
            grad = dot(g_ref[:, :half], flat(near_ref[...])) + dot(g_ref[:, half:], flat(far_ref[...]))
            tangent = jnp.tanh(act_ref[...] / level)
            grad = low(grad * ((1.0 - tangent * tangent) * slope_ref[...]))
            o_ref[...] = grad
            total = jnp.sum(grad.astype(F32), axis=0, keepdims=True)
            start = pl.multiple_of((block % cuts) * columns, LANES)
            sum_ref[pl.ds(order_ref[block // cuts], 1), pl.ds(start, columns)] = total


def grad_hidden_rows(grad, weights, active, slope, level, part_order):
    plane, half, rows, c = weights[0].shape
    parts = 2 * half
    tokens, width = grad.shape
    step = min(c, 1024)
    cuts = c // step
    block = (plane, None, rows, step)
    first = pl.BlockSpec(
        block,
        lambda s: (0, jnp.minimum(s // cuts, half - 1), 0, jnp.where(s < half * cuts, s % cuts, cuts - 1)),
    )
    last = pl.BlockSpec(
        block,
        lambda s: (0, jnp.maximum(s // cuts - half, 0), 0, jnp.where(s < half * cuts, 0, s % cuts)),
    )
    block = pl.BlockSpec((tokens, step), lambda s: (0, s))
    return pl.pallas_call(
        partial(grad_hidden_kernel, cuts),
        grid=(parts * cuts,),
        in_specs=[in_smem(), whole(grad), first, first, last, last, block, block, whole(level)],
        out_specs=[block, pl.BlockSpec((parts, c), lambda s: (0, 0))],
        out_shape=[shape_of((tokens, parts * c), BF16), shape_of((parts, c), F32)],
        compiler_params=params(),
        cost_estimate=cost(2 * tokens * width * parts * c, 34 * MIB),
        name="grad_hidden",
    )(part_order, grad, *weights, active, slope, level)


def first_back_kernel(
    order_ref, g_ref, near_ref, far_ref, normed_ref, normal_ref, inverse_ref, sum_two_ref, level_ref, row_ref,
    sum_ref, low_ref, terms_ref
):
    level = level_ref[2:3, 0:1]
    tangent = jnp.tanh(normed_ref[...] / level)
    grad = project(g_ref[...], near_ref, far_ref) * (1.0 - tangent * tangent) + sum_two_ref[...]
    normal = normal_ref[...]
    gain = take_blocks(row_ref, order_ref)[1:2, :]
    grad_sum = norm_back(grad, normal, inverse_ref[...], gain)
    sum_ref[...] = grad_sum
    low_ref[...] = low(grad_sum)
    add_sums(terms_ref, order_ref, (grad_sum, grad * normal, grad))


def first_back(grad, weights, normed, normal, inverse, sum_two, level, vectors, order):
    near, far = weights
    tokens, width = normed.shape
    inner = grad.shape[1]
    rows = 256

    def block(columns):
        return pl.BlockSpec((rows, columns), lambda t: (t, 0))

    return pl.pallas_call(
        first_back_kernel,
        grid=(tokens // rows,),
        in_specs=[
            in_smem(),
            block(inner),
            whole(near),
            whole(far),
            block(width),
            block(width),
            block(1),
            block(width),
            whole(level),
            whole(vectors),
        ],
        out_specs=[block(width), block(width), pl.BlockSpec((8, width), lambda t: (0, 0))],
        out_shape=[
            shape_of((tokens, width), F32),
            shape_of((tokens, width), BF16),
            shape_of((8, width), F32),
        ],
        compiler_params=params(),
        cost_estimate=cost(2 * tokens * width * inner, 36 * MIB),
        name="first_back",
    )(order, grad, near, far, normed, normal, inverse, sum_two, level, vectors)


def grad_context_kernel(g_ref, near_ref, far_ref, ctx_ref, level_ref, o_ref):
    half = g_ref.shape[1] // 2
    level = level_ref[1:2, 0:1]
    tangent = jnp.tanh(ctx_ref[...] / level)
    grad = dot(g_ref[:, :half], flat(near_ref[...])) + dot(g_ref[:, half:], flat(far_ref[...]))
    o_ref[...] = low(grad * (1.0 - tangent * tangent))


def grad_context_rows(grad, weights, context, level):
    near, far = weights
    plane, parts, rows, c = near.shape
    tokens, width = grad.shape
    weight_spec = pl.BlockSpec((plane, None, rows, c), lambda r: (0, r, 0, 0))
    block = pl.BlockSpec((tokens, c), lambda r: (0, r))
    return pl.pallas_call(
        grad_context_kernel,
        grid=(parts,),
        in_specs=[
            whole(grad),
            weight_spec,
            weight_spec,
            block,
            whole(level),
        ],
        out_specs=block,
        out_shape=shape_of((tokens, parts * c), BF16),
        compiler_params=params(),
        cost_estimate=cost(2 * tokens * width * parts * c, 10 * MIB),
        name="grad_context",
    )(grad, near, far, context, level)


def grad_input_kernel(order_ref, *refs):
    g_refs, (near_ref, far_ref, sum_ref, x_ref, level_ref, o_ref) = refs[:6], refs[6:]
    level = level_ref[0:1, 0:1]
    half = near_ref.shape[1] // 2
    total = None
    for side in range(2):
        for i in range(3):
            term = project(
                g_refs[side * 3 + i][...],
                near_ref.at[:, side * half : (side + 1) * half, i],
                far_ref.at[:, side * half : (side + 1) * half, i],
            )
            total = term if total is None else total + term
    tangent = jnp.tanh(take_blocks(x_ref, order_ref).astype(F32) / level)
    put_blocks(o_ref, order_ref, low(sum_ref[...] + total * (1.0 - tangent * tangent)))


def grad_input(grads, weights, grad_sum, x, level, order):
    near, far = weights
    tokens, width = x.shape
    inner = grads[0].shape[1]
    rows = 256

    def block(columns):
        return pl.BlockSpec((rows, columns), lambda t: (t, 0))

    return pl.pallas_call(
        grad_input_kernel,
        grid=(tokens // rows,),
        in_specs=[in_smem()]
        + [block(inner)] * 6
        + [whole(near), whole(far), block(width), block(width), whole(level)],
        out_specs=block(width),
        out_shape=shape_of((tokens, width), BF16),
        compiler_params=params(),
        cost_estimate=cost(12 * tokens * width * inner, 20 * MIB),
        name="grad_input",
    )(order, *grads, near, far, grad_sum, x, level)


def place_kernel(turned, order_ref, *refs):
    d_refs, i_refs, q_refs = refs[:2], refs[2:4], refs[4:6]
    in_out, qkv_out, *turned_outs = refs[6:]
    step = pl.program_id(0)
    plane, _, rows, _ = i_refs[0].shape
    for core in range(2):
        for j in range(plane):
            here = pl.ds(pl.multiple_of(order_ref[core * plane + j] * rows, rows), rows)
            in_out[0, here, :] = i_refs[core][j, 0].astype(F32)
            if turned:
                turned_outs[0][:, here] = d_refs[core][j, 0].astype(F32).T

            @pl.when(step < 3)
            def _(core=core, j=j, here=here):
                qkv_out[0, here, :] = q_refs[core][j, 0].astype(F32)

            if turned:

                @pl.when(step == 3)
                def _(core=core, j=j, here=here):
                    turned_outs[1][:, here] = q_refs[core][j, 0].astype(F32).T


def place_grads(down, inner, first, blocks):
    plane, _, rows, c = inner[0].shape
    columns = first[0].shape[3]
    width = 2 * plane * rows
    turned = rows % LANES == 0
    cut = c // 4

    def piece(size, index):
        return [pl.BlockSpec((plane, 1, rows, size), index)] * 2

    out_specs = [
        pl.BlockSpec((1, width, cut), lambda p: (0, 0, p)),
        pl.BlockSpec((1, width, columns), lambda p: (jnp.minimum(p, 2), 0, 0)),
    ]
    out_shape = [shape_of((1, width, c), F32), shape_of((3, width, columns), F32)]
    if turned:
        out_specs.append(pl.BlockSpec((cut, width), lambda p: (p, 0)))
        out_specs.append(pl.BlockSpec((columns, width), lambda p: (0, 0)))
        out_shape += [shape_of((c, width), F32), shape_of((columns, width), F32)]
    inner_grad, qkv_grad, *rest = pl.pallas_call(
        partial(place_kernel, turned),
        grid=(4,),
        in_specs=[in_smem()]
        + piece(cut, lambda p: (0, 0, 0, p)) * 2
        + piece(columns, lambda p: (0, p, 0, 0)),
        out_specs=out_specs,
        out_shape=out_shape,
        compiler_params=params(),
        name="place_grads",
    )(blocks.astype(jnp.int32), *down, *inner, *first)
    if not turned:
        back = jnp.zeros((2 * plane,), jnp.int32).at[blocks].set(jnp.arange(2 * plane, dtype=jnp.int32))
        for near, far in (down, [side[:, 3:] for side in first]):
            split = jnp.concatenate([near, far], axis=0)[:, 0]
            rest.append(jnp.take(split, back, axis=0).astype(F32).reshape(width, -1).T)
    return inner_grad[0], qkv_grad, rest[0], rest[1]


def left_over(keeps, sends):
    return scatter_plane(keeps, sends, True)


def scatter_grad(chain, xs, products, other, token, parts, plane, c):
    return chain(*weight_keep([tie(xs[0], [token])] + xs[1:], products, other, parts, plane, c))


HOST_RANK = {first_norm_kernel: 1, attend_last_kernel: 2, hidden_kernel: 1}


def own_block(values, axis):
    rows = values.shape[axis] // lax.axis_size("dp")
    return lax.dynamic_slice_in_dim(values, lax.axis_index("dp") * rows, rows, axis)


def local(
    mesh, layer_input, grad_output, doc_lengths, ranges, w_qkv, bias_qv, w_out, b_out, gain_one,
    shift_one, w_in, b_in, w_down, b_down, gain_two, shift_two
):
    datas, parts = lax.axis_size("dp"), lax.axis_size("tensor")
    data, part = lax.axis_index("dp"), lax.axis_index("tensor")
    plane = datas // 2
    tokens, width = layer_input.shape
    rows = width // datas

    places = jnp.arange(datas)
    distance = (places % plane) * 2 + places // plane
    blocks = data ^ distance
    if rows % LANES == 0:
        per_block = rows // LANES
        order = (blocks[:, None] * per_block + jnp.arange(per_block)).reshape(-1).astype(jnp.int32)
    else:
        order = jnp.arange(width // LANES, dtype=jnp.int32)

    def arrange(values):
        split = values.reshape(values.shape[:-1] + (datas, rows))
        return jnp.take(split, blocks, axis=-2).reshape(values.shape)

    def restore(values):
        split = values.reshape(values.shape[:-1] + (datas, rows))
        back = jnp.zeros((datas,), jnp.int32).at[blocks].set(places.astype(jnp.int32))
        return jnp.take(split, back, axis=-2).reshape(values.shape)

    def arrange_rows(values):
        return values if rows % LANES == 0 else arrange(values)

    def restore_rows(values):
        return values if rows % LANES == 0 else restore(values)

    part_order = (part ^ jnp.arange(parts)).astype(jnp.int32)
    x = arrange_rows(layer_input)
    upstream = arrange_rows(grad_output)
    vectors = jnp.stack([b_out, gain_one, shift_one, b_down, gain_two, shift_two, b_out, b_out])
    vectors = arrange_rows(vectors).astype(F32)

    own = [
        own_block(w_qkv, 1),
        own_block(w_out, 1).T[None],
        own_block(w_in, 0)[None],
        own_block(w_down, 1).T[None],
    ]
    levels, quant_input, quant_own, slopes = prepare(ranges, x, own)
    biases = jnp.concatenate([bias_qv.reshape(-1), b_in])
    count = biases.shape[0]
    biases = jnp.pad(biases, (0, -count % (16 * LANES))).reshape(-1, LANES)
    near, far, biases, near_out, far_out, held_in = first_gather(quant_own[0], biases, *quant_own[1:3])
    weights_qkv, weights_out = (near, far), (near_out, far_out)
    biases = biases.reshape(parts, -1)[:, :count]
    columns = bias_qv.shape[1]
    bias_q = biases[:, :columns].reshape(1, -1)
    bias_v = biases[:, columns : 2 * columns].reshape(1, -1)
    bias_qkv = jnp.stack([bias_q, jnp.zeros_like(bias_q), bias_v]).astype(F32)
    bias_hidden = biases[:, 2 * columns :].reshape(1, -1).astype(F32)

    held = tokens // SEQ
    lengths_here = lax.dynamic_slice_in_dim(doc_lengths, part * held, held, 0)
    ends = jnp.cumsum(lengths_here, axis=1, dtype=jnp.int32)
    half = parts // 2 * columns

    first_moves, _ = plane_moves()

    def over_plane(values, token):
        values = tie(values, [token])
        return [far_swap(values, r) for _, r in first_moves]

    there_in = over_plane(held_in, biases)
    held_a = tie(quant_own[3], [biases])[None]
    for bit in reversed(range(bits_of("tensor") - 1)):
        other = swap(held_a, "tensor", bit)
        held_a = jnp.stack([held_a, other], axis=1).reshape((-1,) + held_a.shape[1:])
    qkv = qkv_rows(quant_input, weights_qkv, bias_qkv)
    held_a = tie(held_a, [qkv])
    there_a = over_plane(held_a, qkv)
    held_b = swap(held_a, "tensor", bits_of("tensor") - 1)
    context, lse, peak = attend(qkv, ends)
    there_in, there_a = [tie(values, [peak]) for values in there_in], [tie(values, [peak]) for values in there_a]
    (context, lse, _), levels, (*weights_in, near_a, far_a) = attend(
        qkv, ends, lse, peak, context, [(held_in, there_in), (held_a, there_a)], ranges, levels
    )
    weights_in = tuple(side[:, :, 0] for side in weights_in)
    weights_out = tuple(side[:, :, 0] for side in weights_out)
    (quant_context, normed, normal_one, inverse_one, _), levels, _ = first_norm(
        context, levels, weights_out, x, vectors, ranges
    )
    held_b = tie(held_b, [levels])
    (quant_normed, active, slope, _), levels, (near_b, far_b) = hidden_rows(
        normed, levels, weights_in, bias_hidden, held_b, ranges
    )
    weights_down = [side[:, :, 0] for side in (near_a, far_a, near_b, far_b)]
    quant_active, output, grad_sum_two, grad_branch, terms_two = second_norm(
        active, levels, weights_down, normed, upstream, vectors, order
    )

    wide = b_in.shape[0]
    other = weight_send([grad_branch], [(0, quant_active, 0)], parts, plane, wide)
    grad_after = tie(grad_branch, [other])
    other = swap(other, "dp", 0)
    grad_hidden, sum_hidden = grad_hidden_rows(
        grad_after, weights_down, active, slope, levels, part_order
    )
    down = scatter_grad(
        scatter_all, [grad_branch], [(0, quant_active, 0)], other, sum_hidden, parts, plane, wide
    )
    grad_hidden = tie(grad_hidden, next(down))
    other = weight_send([quant_normed], [(0, grad_hidden, 0)], parts, plane, wide)
    grad_after = tie(grad_hidden, [other])
    other = swap(other, "dp", 0)
    grad_sum_one, grad_attention, terms_one = first_back(
        grad_after, weights_in, normed, normal_one, inverse_one, grad_sum_two, levels, vectors, order
    )
    grad_hidden = tie(grad_hidden, down.send(terms_one))
    inner = scatter_grad(
        scatter_all, [quant_normed], [(0, grad_hidden, 0)], other, terms_one, parts, plane, wide
    )
    grad_after = tie(grad_attention, next(inner))
    grad_context = grad_context_rows(grad_after, weights_out, context, levels)
    grad_context = tie(grad_context, down.send(grad_context))
    sums_before = jnp.zeros((8, 2 * half), F32)
    *grads, token = attend_back(
        qkv, grad_context, ends, lse, sums_before, part_order, columns, 0
    )
    grads_a = grads
    xs = [quant_input, grad_attention]
    products_a = [(0, grad, 0) for grad in grads] + [(1, quant_context, 0)]
    other_a = weight_send(xs, products_a, parts // 2, plane, columns)
    token_a = other_a
    grad_context = tie(grad_context, inner.send(token_a) + down.send(token_a))
    other_a = swap(other_a, "dp", 0)
    *grads, token = attend_back(
        qkv, grad_context, ends, lse, token, part_order, columns, half
    )
    sum_qv = token
    down = run_all(down, token)
    grads[0] = tie(grads[0], inner.send(token) + [down[1]])
    products_b = [(0, grad, 0) for grad in grads] + [(1, quant_context, parts // 2)]
    other_b = weight_send(xs, products_b, parts // 2, plane, columns)
    token = other_b
    other_b = swap(other_b, "dp", 0)
    first_a = scatter_grad(left_over, xs, products_a, other_a, token, parts // 2, plane, columns)
    started = next(first_a)
    first_b = scatter_grad(left_over, xs, products_b, other_b, started[0], parts // 2, plane, columns)
    started = next(first_b) + inner.send(started[0])
    grads[0] = tie(grads[0], started)
    grad_x = grad_input(grads_a + grads, weights_qkv, grad_sum_one, x, levels, order)

    sums = [terms_one[:3], terms_two[:3], sum_qv[:2], sum_hidden.reshape(-1, width)]
    if rows % LANES:
        sums[0], sums[1] = restore(sums[0]), restore(sums[1])
    sums = jnp.concatenate(sums)
    padded = jnp.pad(sums, ((0, -sums.shape[0] % 8), (0, 0)))
    inner, first_a, first_b = [run_all(chain, grad_x) for chain in (inner, first_a, first_b)]
    (down, inner, first), sums = finale(down, inner, first_a + first_b, slopes, padded)
    hidden_all = sums[8 : 8 + sum_hidden.size // width].reshape(-1)
    grad_bias_qv = lax.dynamic_slice_in_dim(sums[6:8], part * columns, columns, 1)
    grad_b_in = lax.dynamic_slice_in_dim(hidden_all, part * b_in.shape[0], b_in.shape[0], 0)
    grad_w_in, grad_w_qkv, grad_w_down, grad_w_out = place_grads(down, inner, first, blocks)
    new_ranges = levels[:4, 0]
    return (
        restore_rows(output),
        restore_rows(grad_x),
        grad_w_qkv,
        grad_bias_qv,
        grad_w_out,
        sums[0],
        sums[1],
        sums[2],
        grad_w_in,
        grad_b_in,
        grad_w_down,
        sums[3],
        sums[4],
        sums[5],
        new_ranges,
    )


def solution(mesh):
    in_specs = (
        P(("dp", "tensor"), None),
        P(("dp", "tensor"), None),
        P("dp", None),
        P(),
        P(None, None, "tensor"),
        P(None, "tensor"),
        P("tensor", None),
        P(),
        P(),
        P(),
        P(None, "tensor"),
        P("tensor"),
        P("tensor", None),
        P(),
        P(),
        P(),
    )
    out_specs = (
        P(("dp", "tensor"), None),
        P(("dp", "tensor"), None),
        P(None, None, "tensor"),
        P(None, "tensor"),
        P("tensor", None),
        P(),
        P(),
        P(),
        P(None, "tensor"),
        P("tensor"),
        P("tensor", None),
        P(),
        P(),
        P(),
        P(),
    )
    return jax.shard_map(
        partial(local, mesh), mesh=mesh, in_specs=in_specs, out_specs=out_specs, check_vma=False
    )
```
